128 devices in a mesh: dp: 32 (over x_hi, y, z), vocab: 4 (over x_lo, core).
Axes of the slice: x: 4 (x_hi: 2, x_lo: 2; x = x_hi * 2 + x_lo), y: 4, z: 4, core: 2. Of those that a mesh axis runs over, the one named last changes fastest.
Arguments:
- token_ids: int32 [2, 8192], P(None, ('dp', 'vocab')), may hold values from 0 to 50264
- box_coords: int32 [4, 2, 8192], P(None, None, ('dp', 'vocab')), may hold values from 0 to 1023
- intersection_flags: int32 [2, 8192], P(None, ('dp', 'vocab')), may hold values from 0 to 1, as said below
- masked_rows: int32 [2, 1024], P(None, ('dp', 'vocab')), may hold values from 0 to 63, as said below
- masked_labels: int32 [2, 1024], P(None, ('dp', 'vocab')), may hold values from 0 to 50264
- word_table: float32 [768, 50304], P('dp', 'vocab'), may hold values from -0.21650635 to 0.21650635
- word_table_momentum: float32 [768, 50304], P('dp', 'vocab'), may hold values from -1.5258789e-05 to 1.5258789e-05
- word_table_average: float32 [768, 50304], P('dp', 'vocab'), may hold values from -0.4375 to 0.4375
- position_table: float32 [640, 960], P(('dp', 'vocab')), may hold values from -0.4375 to 0.4375
- position_table_momentum: float32 [640, 960], P(('dp', 'vocab')), may hold values from -0.0004272461 to 0.0004272461
- position_table_average: float32 [640, 960], P(('dp', 'vocab')), may hold values from -0.4375 to 0.4375
- box_table: float32 [4, 1024, 128], P(None, ('dp', 'vocab')), may hold values from -0.4375 to 0.4375
- box_table_momentum: float32 [4, 1024, 128], P(None, ('dp', 'vocab')), may hold values from -1.5258789e-05 to 1.5258789e-05
- box_table_average: float32 [4, 1024, 128], P(None, ('dp', 'vocab')), may hold values from -0.4375 to 0.4375
- text_weights: float32 [768, 6144], P(None, ('dp', 'vocab')), may hold values from -0.109375 to 0.109375
- text_weights_momentum: float32 [768, 6144], P(None, ('dp', 'vocab')), may hold values from -1.5258789e-05 to 1.5258789e-05
- text_weights_average: float32 [768, 6144], P(None, ('dp', 'vocab')), may hold values from -0.109375 to 0.109375
- text_down: float32 [3072, 768], P(('dp', 'vocab')), may hold values from -0.109375 to 0.109375
- text_down_momentum: float32 [3072, 768], P(('dp', 'vocab')), may hold values from -1.5258789e-05 to 1.5258789e-05
- text_down_average: float32 [3072, 768], P(('dp', 'vocab')), may hold values from -0.109375 to 0.109375
- layout_weights: float32 [192, 1536], P(None, ('dp', 'vocab')), may hold values from -0.21875 to 0.21875
- layout_weights_momentum: float32 [192, 1536], P(None, ('dp', 'vocab')), may hold values from -1.5258789e-05 to 1.5258789e-05
- layout_weights_average: float32 [192, 1536], P(None, ('dp', 'vocab')), may hold values from -0.21875 to 0.21875
- layout_down: float32 [2, 768, 192], P(None, ('dp', 'vocab')), may hold values from -0.21875 to 0.21875
- layout_down_momentum: float32 [2, 768, 192], P(None, ('dp', 'vocab')), may hold values from -1.5258789e-05 to 1.5258789e-05
- layout_down_average: float32 [2, 768, 192], P(None, ('dp', 'vocab')), may hold values from -0.21875 to 0.21875
- head_dense: float32 [960, 768], P(None, ('dp', 'vocab')), may hold values from -0.1875 to 0.1875
- head_dense_momentum: float32 [960, 768], P(None, ('dp', 'vocab')), may hold values from -1.5258789e-05 to 1.5258789e-05
- head_dense_average: float32 [960, 768], P(None, ('dp', 'vocab')), may hold values from -0.1875 to 0.1875
- norm_vectors: float32 [15744], P(('dp', 'vocab')), may hold values from -1 to 2.4
- norm_vectors_momentum: float32 [15744], P(('dp', 'vocab')), may hold values from -7.6293945e-05 to 7.6293945e-05
- norm_vectors_average: float32 [15744], P(('dp', 'vocab')), may hold values from 0.5 to 1.5
Outputs:
- word_table_next: float32 [768, 50304], P('dp', 'vocab')
- word_table_momentum_next: float32 [768, 50304], P('dp', 'vocab')
- word_table_average_next: float32 [768, 50304], P('dp', 'vocab')
- position_table_next: float32 [640, 960], P(('dp', 'vocab'))
- position_table_momentum_next: float32 [640, 960], P(('dp', 'vocab'))
- position_table_average_next: float32 [640, 960], P(('dp', 'vocab'))
- box_table_next: float32 [4, 1024, 128], P(None, ('dp', 'vocab'))
- box_table_momentum_next: float32 [4, 1024, 128], P(None, ('dp', 'vocab'))
- box_table_average_next: float32 [4, 1024, 128], P(None, ('dp', 'vocab'))
- text_weights_next: float32 [768, 6144], P(None, ('dp', 'vocab'))
- text_weights_momentum_next: float32 [768, 6144], P(None, ('dp', 'vocab'))
- text_weights_average_next: float32 [768, 6144], P(None, ('dp', 'vocab'))
- text_down_next: float32 [3072, 768], P(('dp', 'vocab'))
- text_down_momentum_next: float32 [3072, 768], P(('dp', 'vocab'))
- text_down_average_next: float32 [3072, 768], P(('dp', 'vocab'))
- layout_weights_next: float32 [192, 1536], P(None, ('dp', 'vocab'))
- layout_weights_momentum_next: float32 [192, 1536], P(None, ('dp', 'vocab'))
- layout_weights_average_next: float32 [192, 1536], P(None, ('dp', 'vocab'))
- layout_down_next: float32 [2, 768, 192], P(None, ('dp', 'vocab'))
- layout_down_momentum_next: float32 [2, 768, 192], P(None, ('dp', 'vocab'))
- layout_down_average_next: float32 [2, 768, 192], P(None, ('dp', 'vocab'))
- head_dense_next: float32 [960, 768], P(None, ('dp', 'vocab'))
- head_dense_momentum_next: float32 [960, 768], P(None, ('dp', 'vocab'))
- head_dense_average_next: float32 [960, 768], P(None, ('dp', 'vocab'))
- norm_vectors_next: float32 [15744], P(('dp', 'vocab'))
- norm_vectors_momentum_next: float32 [15744], P(('dp', 'vocab'))
- norm_vectors_average_next: float32 [15744], P(('dp', 'vocab'))
- loss_sum: float32 [], replicated
- masked_count: float32 [], replicated
- grad_norm: float32 [], replicated
The draws below stay inside these ranges and needn't reach their ends.
Inputs may be any that keep to these rules, and one draw needn't show every extreme that they name: `intersection_flags`: 1 marks a token that a later block of its document already holds; slots at such tokens are not counted. `masked_rows`: in a micro-batch, the 8 entries of one device are distinct rows of that device's block of 64 tokens.
All inputs are finite; a program needn't handle non-finite values.
Results may differ from the reference program's by a relative error of at most 0.017.
Values may be sent and summed in bfloat16 or wider, within the bound.
A program may use at most 320 MiB of HBM per device.

```python
import math
import jax
import jax.numpy as jnp
import numpy as np
from jax import lax

D = 768
FF = 3072
DL = 192
FFL = 768
BOX_W = 128
HEADS = 12
VOCAB = 50304
VOCAB_REAL = 50265
POS_ROWS = 640
BOX_ROWS = 1024
MB = 2
TOK_MB = 64
SPAN = 256
TOKENS = 8192
SLOTS = 8
SLOTS_ALL = 1024
VEC = 15744
PARAMS_REST = 9559424


def vector_layout():
    gain_parts = []
    ramp_parts = []
    groups = [([D] * 7 + [FF] + [D] * 3, [1, 0, 0, 0, 0, 1, 0, 0, 0, 1, 0]), ([DL] * 7 + [FFL] + [DL] * 3, [1, 0, 0, 0, 0, 1, 0, 0, 0, 1, 0]), ([D] * 3, [0, 1, 0])]
    for lengths, marks in groups:
        for length, mark in zip(lengths, marks):
            gain_parts.append(np.full(length, mark, np.float32))
            ramp_parts.append(np.linspace(0.0, 1.0, length, dtype=np.float32))
    return (np.concatenate(gain_parts), np.concatenate(ramp_parts))


def draw_word_table(key, part):
    key = jax.random.fold_in(key, 11)
    column = jnp.arange(VOCAB, dtype=jnp.float32) / (VOCAB - 1)
    ramp = 1.0 + 2.0 * column
    values = jax.random.truncated_normal(key, -4.0, 4.0, (D, VOCAB), jnp.float32)
    return values * ramp[None, :] * (0.5 / math.sqrt(D))


def draw_norm_vectors(key, part):
    key = jax.random.fold_in(key, 7)
    gain_mask, ramp = vector_layout()
    first_key, second_key = jax.random.split(key)
    gains = (0.6 + 1.2 * jnp.asarray(ramp)) * jax.random.uniform(first_key, (VEC,), jnp.float32, 0.85, 1.15)
    biases = 0.4 * jax.random.truncated_normal(second_key, -2.5, 2.5, (VEC,), jnp.float32)
    return jnp.where(jnp.asarray(gain_mask) > 0.5, gains, biases)


def draw_intersection_flags(key, part):
    key = jax.random.fold_in(key, 13)
    device_count = TOKENS // TOK_MB
    device = jnp.arange(TOKENS) // TOK_MB
    draws = jax.random.randint(key, (MB, TOKENS), 0, 3 * (device_count - 1))
    return (draws < 2 * (device_count - 1 - device)[None, :]).astype(jnp.int32)


def draw_masked_rows(key, part):
    key = jax.random.fold_in(key, 17)
    device_count = SLOTS_ALL // SLOTS
    scores = jax.random.randint(key, (MB, device_count, TOK_MB), 0, 1 << 20) * TOK_MB + jnp.arange(TOK_MB)
    order = jnp.argsort(scores, axis=-1)
    return order[:, :, :SLOTS].reshape(MB, SLOTS_ALL).astype(jnp.int32)


def plant(array, rng, least, high):
    longest = array.shape.index(max(array.shape))
    spots = []
    for shift in (0, 1):
        where = [jax.random.randint(jax.random.fold_in(rng, axis), (), 0, length) for axis, length in enumerate(array.shape)]
        where[longest] = (where[longest] + shift) % array.shape[longest]
        spots.append(tuple(where))
    return array.at[spots[0]].set(least).at[spots[1]].set(high)


def block_levels(key, extent, shards, least, high):
    def one(axis_at, blocks):
        steps = jax.random.uniform(jax.random.fold_in(jax.random.fold_in(key, 6), axis_at), (blocks,), jnp.float32, least / len(shards), high / len(shards))
        return jnp.repeat(jnp.exp(steps), extent[axis_at] // blocks).reshape((-1,) + (1,) * (len(extent) - axis_at - 1))

    factor_of = one(*shards[0])
    for cut in shards[1:]:
        factor_of = factor_of * one(*cut)
    return factor_of


def rank_table(number_of, lean):
    portions = [(1 << 20) // math.isqrt(rank ** lean) + 1 for rank in range(1, number_of + 1)]
    spread = 1 + sum(portions) // (1 << 30)
    return np.cumsum(np.array([max(1, weight // spread) for weight in portions]))


def ranked_ids(own_key, dims, number_of, lean):
    listing = rank_table(number_of, lean)
    pick = jax.random.randint(jax.random.fold_in(own_key, 1), dims, 0, int(listing[number_of - 1]))
    standing = jnp.searchsorted(jnp.asarray(listing, jnp.int32), pick, side="right")
    return jax.random.permutation(jax.random.fold_in(own_key, 2), number_of)[standing].astype(jnp.int32)


def noise(rng, shape, deviation, limit, cuts=(), held_as=jnp.bfloat16):
    drawn = jax.random.normal(rng, shape, jnp.float32) * deviation
    if len(cuts) > 0:
        drawn = block_levels(rng, shape, cuts, -0.22, 0.18) * drawn
    return jnp.clip(drawn, min=-limit, max=limit).astype(held_as)


def setup_inputs(seed: int = 0) -> dict:
    streams_of = jax.random.split(jax.random.key(seed), 33)
    token_ids = plant(ranked_ids(streams_of[0], (MB, TOKENS), VOCAB_REAL, 2), jax.random.fold_in(streams_of[0], 3), 0, VOCAB_REAL - 1).astype(jnp.int32)
    box_coords = plant(jax.random.randint(streams_of[1], (4, MB, TOKENS), 0, BOX_ROWS), jax.random.fold_in(streams_of[1], 1), 0, BOX_ROWS - 1).astype(jnp.int32)
    intersection_flags = draw_intersection_flags(jax.random.fold_in(streams_of[32], 71), 0)
    masked_rows = draw_masked_rows(jax.random.fold_in(streams_of[32], 71), 0)
    masked_labels = plant(jax.random.randint(streams_of[4], (MB, SLOTS_ALL), 0, VOCAB_REAL), jax.random.fold_in(streams_of[4], 1), 0, VOCAB_REAL - 1).astype(jnp.int32)
    word_table = draw_word_table(jax.random.fold_in(streams_of[32], 71), 0)
    word_table_momentum = noise(streams_of[6], (D, VOCAB), (1e-6), 1.52587890625e-05, ((0, 32), (1, 4)), jnp.float32)
    word_table_average = noise(streams_of[7], (D, VOCAB), 0.03, 0.4375, ((0, 32), (1, 4)), jnp.float32)
    position_table = noise(streams_of[8], (POS_ROWS, D + DL), 0.03, 0.4375, ((0, 128),), jnp.float32)
    position_table_momentum = noise(streams_of[9], (POS_ROWS, D + DL), (0.2 / (D * VOCAB + PARAMS_REST) ** 0.5), 0.0004272461, ((0, 128),), jnp.float32)
    position_table_average = noise(streams_of[10], (POS_ROWS, D + DL), 0.03, 0.4375, ((0, 128),), jnp.float32)
    box_table = noise(streams_of[11], (4, BOX_ROWS, BOX_W), 0.03, 0.4375, ((1, 128),), jnp.float32)
    box_table_momentum = noise(streams_of[12], (4, BOX_ROWS, BOX_W), (1e-6), 1.52587890625e-05, ((1, 128),), jnp.float32)
    box_table_average = noise(streams_of[13], (4, BOX_ROWS, BOX_W), 0.03, 0.4375, ((1, 128),), jnp.float32)
    text_weights = noise(streams_of[14], (D, 4 * D + FF), (4 * D) ** -0.5, 0.109375, ((1, 128),), jnp.float32)
    text_weights_momentum = noise(streams_of[15], (D, 4 * D + FF), (1e-6), 1.52587890625e-05, ((1, 128),), jnp.float32)
    text_weights_average = noise(streams_of[16], (D, 4 * D + FF), (4 * D) ** -0.5, 0.109375, ((1, 128),), jnp.float32)
    text_down = noise(streams_of[17], (FF, D), FF ** -0.5, 0.109375, ((0, 128),), jnp.float32)
    text_down_momentum = noise(streams_of[18], (FF, D), (1e-6), 1.52587890625e-05, ((0, 128),), jnp.float32)
    text_down_average = noise(streams_of[19], (FF, D), FF ** -0.5, 0.109375, ((0, 128),), jnp.float32)
    layout_weights = noise(streams_of[20], (DL, 4 * DL + FFL), (4 * DL) ** -0.5, 0.21875, ((1, 128),), jnp.float32)
    layout_weights_momentum = noise(streams_of[21], (DL, 4 * DL + FFL), (1e-6), 1.52587890625e-05, ((1, 128),), jnp.float32)
    layout_weights_average = noise(streams_of[22], (DL, 4 * DL + FFL), (4 * DL) ** -0.5, 0.21875, ((1, 128),), jnp.float32)
    layout_down = noise(streams_of[23], (2, FFL, DL), FFL ** -0.5, 0.21875, ((1, 128),), jnp.float32)
    layout_down_momentum = noise(streams_of[24], (2, FFL, DL), (1e-6), 1.52587890625e-05, ((1, 128),), jnp.float32)
    layout_down_average = noise(streams_of[25], (2, FFL, DL), FFL ** -0.5, 0.21875, ((1, 128),), jnp.float32)
    head_dense = noise(streams_of[26], (D + DL, D), (D + DL) ** -0.5, 0.1875, ((1, 128),), jnp.float32)
    head_dense_momentum = noise(streams_of[27], (D + DL, D), (1e-6), 1.52587890625e-05, ((1, 128),), jnp.float32)
    head_dense_average = noise(streams_of[28], (D + DL, D), (D + DL) ** -0.5, 0.1875, ((1, 128),), jnp.float32)
    norm_vectors = draw_norm_vectors(jax.random.fold_in(streams_of[32], 71), 0)
    norm_vectors_momentum = noise(streams_of[30], (VEC,), (5e-6), 7.62939453125e-05, ((0, 128),), jnp.float32)
    norm_vectors_average = jnp.clip(1.0 + 0.1 * jax.random.normal(streams_of[31], (VEC,), jnp.float32), 0.5, 1.5)
    return dict(token_ids=token_ids, box_coords=box_coords, intersection_flags=intersection_flags, masked_rows=masked_rows, masked_labels=masked_labels, word_table=word_table, word_table_momentum=word_table_momentum, word_table_average=word_table_average, position_table=position_table, position_table_momentum=position_table_momentum, position_table_average=position_table_average, box_table=box_table, box_table_momentum=box_table_momentum, box_table_average=box_table_average, text_weights=text_weights, text_weights_momentum=text_weights_momentum, text_weights_average=text_weights_average, text_down=text_down, text_down_momentum=text_down_momentum, text_down_average=text_down_average, layout_weights=layout_weights, layout_weights_momentum=layout_weights_momentum, layout_weights_average=layout_weights_average, layout_down=layout_down, layout_down_momentum=layout_down_momentum, layout_down_average=layout_down_average, head_dense=head_dense, head_dense_momentum=head_dense_momentum, head_dense_average=head_dense_average, norm_vectors=norm_vectors, norm_vectors_momentum=norm_vectors_momentum, norm_vectors_average=norm_vectors_average)


NORM_EPSILON = 1e-05
MOMENTUM = 0.9
AVERAGE_KEEP = 0.9
RATE = 1500.0
CLIP = 0.05
HIGHEST = lax.Precision.HIGHEST

@jax.custom_vjp
def low(v):
    return lax.optimization_barrier(v.astype(jnp.bfloat16)).astype(jnp.float32)

@jax.custom_vjp
def low_back(v):
    return v

def low_keep(v):
    return (low(v), None)

def low_pass(kept, grad):
    return (grad,)

def back_keep(v):
    return (v, None)

def back_low(kept, grad):
    return (low(grad),)
low.defvjp(low_keep, low_pass)
low_back.defvjp(back_keep, back_low)

def product(left, right):
    return jnp.dot(left, right, precision=HIGHEST)

def norm_apply(values, gain, bias):
    centred = values - lax.optimization_barrier(jnp.mean(values, -1, keepdims=True))
    variance = lax.optimization_barrier(jnp.mean(centred * centred, -1, keepdims=True))
    return centred * lax.rsqrt(variance + NORM_EPSILON) * gain + bias

def gelu_exact(values):
    return jax.nn.gelu(values, approximate=False)

def carve_vector(vector, width, hidden):
    lengths = [width] * 7 + [hidden] + [width] * 3
    pieces = []
    offset = 0
    for length in lengths:
        pieces.append(vector[offset:offset + length])
        offset += length
    return pieces

def stream_open(embed_sum, pieces, w_in, width):
    normed = norm_apply(embed_sum, pieces[0], pieces[1])
    bias_row = jnp.concatenate([pieces[2], jnp.zeros_like(pieces[2]), pieces[3]])
    raw = low(low_back(product(low(normed), w_in[:, :3 * width]) + bias_row))
    return (normed, raw)

def stream_close(normed, attended, pieces, w_in, w_down, width):
    mid = normed + low_back(product(attended, w_in[:, 3 * width:4 * width]) + pieces[4])
    first = norm_apply(mid, pieces[5], pieces[6])
    pre_act = low_back(product(low(first), w_in[:, 4 * width:]) + pieces[7])
    second = low_back(product(low(gelu_exact(pre_act)), w_down) + pieces[8])
    return norm_apply(first + second, pieces[9], pieces[10])

def attend(raws, widths):
    seq_count = TOKENS // SPAN
    scores = 0.0
    split_parts = []
    for raw, width in zip(raws, widths):
        parts = raw.reshape(seq_count, SPAN, 3, HEADS, width // HEADS)
        split_parts.append(parts)
        scores = scores + jnp.einsum('sqhd,skhd->shqk', parts[:, :, 0], parts[:, :, 1], precision=HIGHEST) * (width // HEADS) ** (-0.5)
    probs = low(jax.nn.softmax(low_back(scores), axis=-1))
    results = []
    for parts, width in zip(split_parts, widths):
        mixed = jnp.einsum('shqk,skhd->sqhd', probs, parts[:, :, 2], precision=HIGHEST)
        results.append(low(low_back(mixed.reshape(TOKENS, width))))
    return results

def forward(weights, token_ids, box_coords, global_rows, masked_labels, counted):
    word_table, position_table, box_table, text_weights, text_down, layout_weights, layout_down, head_dense, norm_vectors = [low(w) for w in weights]
    text_length = 10 * D + FF
    layout_length = 10 * DL + FFL
    text_pieces = carve_vector(norm_vectors[:text_length], D, FF)
    layout_pieces = carve_vector(norm_vectors[text_length:text_length + layout_length], DL, FFL)
    head_part = norm_vectors[text_length + layout_length:]
    head_bias, head_gain, head_shift = (head_part[:D], head_part[D:2 * D], head_part[2 * D:])
    position_rows = position_table[jnp.arange(TOKENS) % SPAN]
    loss_sum = jnp.zeros((), jnp.float32)
    for micro in range(MB):
        text_sum = low_back(word_table[:, token_ids[micro]].T + position_rows[:, :D])
        left, upper, right, lower = [box_coords[coord, micro] for coord in range(4)]
        spatial = low_back(jnp.concatenate([box_table[0][left], box_table[1][upper], box_table[0][right], box_table[1][lower], box_table[2][jnp.abs(lower - upper)], box_table[3][jnp.abs(right - left)]], 1))
        layout_sum = low_back(position_rows[:, D:] + product(spatial, layout_down[1]))
        text_normed, text_raw = stream_open(text_sum, text_pieces, text_weights, D)
        layout_normed, layout_raw = stream_open(layout_sum, layout_pieces, layout_weights, DL)
        text_att, layout_att = attend([text_raw, layout_raw], [D, DL])
        text_final = stream_close(text_normed, text_att, text_pieces, text_weights, text_down, D)
        layout_final = stream_close(layout_normed, layout_att, layout_pieces, layout_weights, layout_down[0], DL)
        joined = low(jnp.concatenate([text_final, layout_final], 1)[global_rows[micro]])
        dense = low_back(product(joined, head_dense) + head_bias)
        picked = low(norm_apply(gelu_exact(dense), head_gain, head_shift))
        logits = low_back(product(picked, word_table))
        log_total = jax.nn.logsumexp(logits, axis=-1)
        target = jnp.take_along_axis(logits, masked_labels[micro][:, None], 1)[:, 0]
        loss_sum = loss_sum + jnp.sum(counted[micro] * (log_total - target))
    return loss_sum

def reference(token_ids, box_coords, intersection_flags, masked_rows, masked_labels, word_table, word_table_momentum, word_table_average, position_table, position_table_momentum, position_table_average, box_table, box_table_momentum, box_table_average, text_weights, text_weights_momentum, text_weights_average, text_down, text_down_momentum, text_down_average, layout_weights, layout_weights_momentum, layout_weights_average, layout_down, layout_down_momentum, layout_down_average, head_dense, head_dense_momentum, head_dense_average, norm_vectors, norm_vectors_momentum, norm_vectors_average):
    triples = [(word_table, word_table_momentum, word_table_average), (position_table, position_table_momentum, position_table_average), (box_table, box_table_momentum, box_table_average), (text_weights, text_weights_momentum, text_weights_average), (text_down, text_down_momentum, text_down_average), (layout_weights, layout_weights_momentum, layout_weights_average), (layout_down, layout_down_momentum, layout_down_average), (head_dense, head_dense_momentum, head_dense_average), (norm_vectors, norm_vectors_momentum, norm_vectors_average)]
    masters = [entry[0] for entry in triples]
    global_rows = (masked_rows + (jnp.arange(SLOTS_ALL) // SLOTS)[None, :] * TOK_MB).astype(jnp.int32)
    counted = (jnp.take_along_axis(intersection_flags, global_rows, 1) == 0).astype(jnp.float32)
    masked_count = jnp.sum(counted)

    def objective(*weights):
        loss_sum = forward(weights, token_ids, box_coords, global_rows, masked_labels, counted)
        return (loss_sum / masked_count, loss_sum)
    value, pullback, loss_sum = jax.vjp(objective, *masters, has_aux=True)
    grads = pullback(jnp.ones((), jnp.float32))
    square_total = jnp.zeros((), jnp.float32)
    for grad in grads:
        square_total = square_total + jnp.sum(grad * grad)
    grad_norm = jnp.sqrt(square_total)
    factor = jnp.minimum(1.0, CLIP / grad_norm)
    results = []
    for (master, momentum, average), grad in zip(triples, grads):
        clipped = factor * grad
        momentum_next = MOMENTUM * momentum + clipped
        master_next = master - RATE * (clipped + MOMENTUM * momentum_next)
        average_next = AVERAGE_KEEP * average + (1.0 - AVERAGE_KEEP) * master_next
        results += [master_next, momentum_next, average_next]
    return (results[0], results[1], results[2], results[3], results[4], results[5], results[6], results[7], results[8], results[9], results[10], results[11], results[12], results[13], results[14], results[15], results[16], results[17], results[18], results[19], results[20], results[21], results[22], results[23], results[24], results[25], results[26], loss_sum, masked_count, grad_norm)
```

```python
import functools

import jax
import jax.numpy as jnp
from jax import lax
from jax.experimental import pallas as pl
from jax.experimental.pallas import tpu as pltpu
from jax.sharding import PartitionSpec as P

AXES = ("dp", "vocab")
MESH = pl.DeviceIdType.MESH
ORDERS = (("z", "y", "x"), ("y", "x", "z"), ("x", "z", "y"))


def my_place():
    dp = lax.axis_index("dp")
    vocab = lax.axis_index("vocab")
    return {
        "x": (dp // 16) * 2 + vocab // 2,
        "y": (dp // 4) % 4,
        "z": dp % 4,
        "c": vocab % 2,
    }


def moved(place, dim, step):
    other = dict(place)
    other[dim] = (1 - place["c"]) if dim == "c" else (place[dim] + step + 4) % 4
    return other


def device_of(place):
    return (
        (place["x"] // 2) * 16 + place["y"] * 4 + place["z"],
        (place["x"] % 2) * 2 + place["c"],
    )


def greet(place, steps=(1, 3)):
    barrier = pltpu.get_barrier_semaphore()
    peers = [moved(place, dim, step) for dim in "xyz" for step in steps]
    peers.append(moved(place, "c", 1))
    for peer in peers:
        pl.semaphore_signal(barrier, inc=1, device_id=device_of(peer), device_id_type=MESH)
    pl.semaphore_wait(barrier, len(peers))


def remote(src, dst, send, recv, place):
    return pltpu.make_async_remote_copy(
        src_ref=src,
        dst_ref=dst,
        send_sem=send,
        recv_sem=recv,
        device_id=device_of(place),
        device_id_type=MESH,
    )


def lanes_at(ref, lanes):
    return slice(None) if lanes is None else pl.ds(*lanes)


def block_view(ref, place, dims, lanes, core=None):
    high, low = (pl.ds(0, 2), pl.ds(0, 2)) if "x" in dims else (place["x"] // 2, place["x"] % 2)
    mid = pl.ds(0, 4) if "y" in dims else place["y"]
    deep = pl.ds(0, 4) if "z" in dims else place["z"]
    where = (high, mid, deep, low)
    if core is not None:
        where += (core,)
    return ref.at[where + (slice(None), lanes_at(ref, lanes))]


def halves(lanes, number):
    if lanes is None or lanes[1] < 256:
        return (lanes, False) if number % 2 == 0 else (False, lanes)
    half = lanes[1] // 256 * 128
    return (lanes[0], half), (lanes[0] + half, lanes[1] - half)


def gather_kernel(pieces, count, *refs):
    ins, outs = refs[:count], refs[count : 2 * count]
    own_sem, core_sems, ring_send, ring_recv, pass_send, pass_recv = refs[2 * count :]
    place = my_place()
    sibling = moved(place, "c", 1)
    greet(place)

    def spot(number, origin, dims, lanes):
        return block_view(outs[number], origin, dims, lanes, place["c"])

    copies, crosses = [], []
    for number in range(count):
        here = block_view(outs[number], place, "", None, place["c"])
        copy = pltpu.make_async_copy(ins[number], here, own_sem.at[number])
        copy.start()
        copies.append(copy)
        cross = remote(ins[number], here, core_sems.at[0, number], core_sems.at[1, number], sibling)
        cross.start()
        crosses.append(cross)
    rings, passes = {}, []

    def send(phase, piece, way, src, dst, target):
        copy = remote(
            src, dst, ring_send.at[phase, way, piece], ring_recv.at[phase, way, piece], target
        )
        copy.start()
        rings[(phase, way, piece)] = copy

    def hand_over(phase, piece, way, where):
        copy = remote(
            where, where, pass_send.at[phase, way, piece], pass_recv.at[phase, way, piece], sibling
        )
        copy.start()
        passes.append(copy)

    def begin(phase, piece):
        number, lanes, order = pieces[piece]
        dim, dims = ORDERS[order][phase], ORDERS[order][:phase]
        where = spot(number, place, dims, lanes)
        src = ins[number].at[:, lanes_at(ins[number], lanes)] if phase == 0 else where
        for way, step in ((0, 1), (1, -1)):
            send(phase, piece, way, src, where, moved(place, dim, step))

    for piece in range(len(pieces)):
        begin(0, piece)
    for copy in copies:
        copy.wait()
    for phase in range(3):
        for piece, (number, lanes, order) in enumerate(pieces):
            dim, dims = ORDERS[order][phase], ORDERS[order][:phase]
            parts = halves(lanes, piece)
            for way, step in ((0, 1), (1, -1)):
                rings[(phase, way, piece)].wait_recv()
                origin = moved(place, dim, -step)
                if parts[way] is not False:
                    onward = spot(number, origin, dims, parts[way])
                    send(phase, piece, 2 + way, onward, onward, moved(place, dim, step))
                hand_over(phase, piece, way, spot(number, origin, dims, lanes))
        for piece, (number, lanes, order) in enumerate(pieces):
            dim, dims = ORDERS[order][phase], ORDERS[order][:phase]
            parts = halves(lanes, piece)
            for way in range(2):
                if parts[way] is not False:
                    rings[(phase, 2 + way, piece)].wait_recv()
            if phase < 2:
                begin(phase + 1, piece)
            hand_over(phase, piece, 2, spot(number, moved(place, dim, 2), dims, lanes))
    for copy in rings.values():
        copy.wait_send()
    for copy in crosses + passes:
        copy.wait()


def gather_all(arrays, pieces, collective_id):
    count, total = len(arrays), len(pieces)
    outs = pl.pallas_call(
        functools.partial(gather_kernel, pieces, count),
        out_shape=[jax.ShapeDtypeStruct((2, 4, 4, 2, 2) + a.shape, a.dtype) for a in arrays],
        in_specs=[pl.BlockSpec(memory_space=pl.ANY)] * count,
        out_specs=[pl.BlockSpec(memory_space=pl.ANY)] * count,
        scratch_shapes=[
            pltpu.SemaphoreType.DMA((count,)),
            pltpu.SemaphoreType.DMA((2, count)),
            pltpu.SemaphoreType.DMA((3, 4, total)),
            pltpu.SemaphoreType.DMA((3, 4, total)),
            pltpu.SemaphoreType.DMA((3, 3, total)),
            pltpu.SemaphoreType.DMA((3, 3, total)),
        ],
        compiler_params=pltpu.CompilerParams(collective_id=collective_id, has_side_effects=True),
    )(*arrays)
    return [o.reshape((128,) + a.shape) for o, a in zip(outs, arrays)]


def open_shape(dims):
    shape = ()
    if "x" in dims:
        shape += (2,)
    if "y" in dims:
        shape += (4,)
    if "z" in dims:
        shape += (4,)
    if "x" in dims:
        shape += (2,)
    return shape


def blocks_in(dims):
    total = 1
    for size in open_shape(dims):
        total *= size
    return total


def walk(flat, dims, place):
    high, mid, deep, low = place["x"] // 2, place["y"], place["z"], place["x"] % 2
    inner = ()
    if "x" in dims:
        low = flat % 2
        flat = flat // 2
        inner = (low,)
    if "z" in dims:
        deep = flat % 4
        flat = flat // 4
        inner = (deep,) + inner
    if "y" in dims:
        mid = flat % 4
        flat = flat // 4
        inner = (mid,) + inner
    if "x" in dims:
        high = flat
        inner = (high,) + inner
    return (high, mid, deep, low), inner


def reduce_kernel(sources, pieces, count, *refs):
    total = len(pieces)
    ins = refs[: len(sources)]
    refs = refs[len(sources) :]
    outs, accs, crosses = refs[:count], refs[count : 2 * count], refs[2 * count : 3 * count]
    refs = refs[3 * count :]
    slots = refs[: 12 * total]
    own_sem, core_sems, ring_send, ring_recv = refs[12 * total :]
    place = my_place()
    sibling = moved(place, "c", 1)
    greet(place)

    def slot(phase, way, piece):
        return slots[(phase * 4 + way) * total + piece]

    def add(number, lanes, at, dims, others):
        acc = accs[number]

        def body(flat, carry):
            block, inner = walk(flat, dims, at)
            where = block + (slice(None), lanes_at(acc, lanes))
            value = acc[where].astype(jnp.float32)
            for other, index in others:
                value = value + (other[inner] if index is None else other[block + index]).astype(
                    jnp.float32
                )
            acc[where] = value.astype(acc.dtype)
            return carry

        lax.fori_loop(0, blocks_in(dims), body, 0)

    started = []
    first = {}
    for piece, (number, lanes, order) in enumerate(pieces):
        for index, (owner, high, mids) in enumerate(sources):
            if owner != number:
                continue
            copies = []
            for core, target in ((sibling["c"], "cross"), (place["c"], "own")):
                where = (slice(None), slice(None), slice(None), slice(None), core)
                src = ins[index].at[where + (slice(None), lanes_at(ins[index], lanes))]
                at = (
                    pl.ds(*high),
                    pl.ds(*mids),
                    slice(None),
                    slice(None),
                    slice(None),
                    lanes_at(accs[number], lanes),
                )
                if target == "cross":
                    copy = remote(
                        src,
                        crosses[number].at[at],
                        core_sems.at[0, piece, index],
                        core_sems.at[1, piece, index],
                        sibling,
                    )
                else:
                    copy = pltpu.make_async_copy(src, accs[number].at[at], own_sem.at[piece, index])
                copy.start()
                copies.append(copy)
            started.append(copies[0])
            first.setdefault(piece, []).append(copies)
    rings = {}

    def send(phase, way, piece, src, step):
        number, lanes, order = pieces[piece]
        copy = remote(
            src,
            slot(phase, way, piece),
            ring_send.at[phase, way, piece],
            ring_recv.at[phase, way, piece],
            moved(place, ORDERS[order][phase], step),
        )
        copy.start()
        rings[(phase, way, piece)] = copy
        started.append(copy)

    def begin(phase, piece):
        number, lanes, order = pieces[piece]
        dim, rest = ORDERS[order][phase], ORDERS[order][phase + 1 :]
        parts = halves(lanes, piece)
        for way, step in ((0, 1), (1, -1)):
            if parts[way] is not False:
                there = moved(place, dim, 2)
                send(phase, way, piece, block_view(accs[number], there, rest, parts[way]), step)

    for piece, (number, lanes, order) in enumerate(pieces):
        for cross, own in first[piece]:
            own.wait()
            cross.wait_recv()
        add(number, lanes, place, "xyz", [(crosses[number], (slice(None), lanes_at(accs[number], lanes)))])
        begin(0, piece)
    for phase in range(3):
        for piece, (number, lanes, order) in enumerate(pieces):
            dim, rest = ORDERS[order][phase], ORDERS[order][phase + 1 :]
            parts = halves(lanes, piece)
            for way, step in ((0, 1), (1, -1)):
                there = moved(place, dim, step)
                if parts[way] is not False:
                    rings[(phase, way, piece)].wait_recv()
                    add(number, parts[way], there, rest, [(slot(phase, way, piece), None)])
                send(phase, 2 + way, piece, block_view(accs[number], there, rest, lanes), step)
        for piece, (number, lanes, order) in enumerate(pieces):
            rest = ORDERS[order][phase + 1 :]
            for way in range(2):
                rings[(phase, 2 + way, piece)].wait_recv()
            others = [slot(phase, 2 + way, piece) for way in range(2)]
            if phase < 2:
                add(number, lanes, place, rest, [(other, None) for other in others])
                begin(phase + 1, piece)
            else:
                block, inner = walk(0, "", place)
                where = (slice(None), lanes_at(accs[number], lanes))
                value = accs[number][block + where].astype(jnp.float32)
                for other in others:
                    value = value + other[...].astype(jnp.float32)
                outs[number][where] = value
    for copy in started:
        copy.wait_send()


def reduce_all(arrays, sources, pieces, collective_id):
    shapes = {}
    views = []
    for array, (owner, high, mids) in zip(arrays, sources):
        shapes[owner] = array.shape[1:]
        views.append(array.reshape((high[1], mids[1], 4, 2, 2) + array.shape[1:]))
    count, total = len(shapes), len(pieces)
    dtype = arrays[0].dtype
    scratch = [pltpu.VMEM((2, 4, 4, 2) + shapes[n], dtype) for n in range(count)] * 2
    for phase in range(3):
        for way in range(4):
            for piece, (number, lanes, order) in enumerate(pieces):
                rest = ORDERS[order][phase + 1 :]
                rows, width = shapes[number]
                part = halves(lanes, piece)[way] if way < 2 else lanes
                if part is False:
                    scratch.append(pltpu.VMEM((8, 128), dtype))
                else:
                    wide = width if part is None else part[1]
                    scratch.append(pltpu.VMEM(open_shape(rest) + (rows, wide), dtype))
    scratch += [
        pltpu.SemaphoreType.DMA((total, len(arrays))),
        pltpu.SemaphoreType.DMA((2, total, len(arrays))),
        pltpu.SemaphoreType.DMA((3, 4, total)),
        pltpu.SemaphoreType.DMA((3, 4, total)),
    ]
    return pl.pallas_call(
        functools.partial(reduce_kernel, sources, pieces, count),
        out_shape=[jax.ShapeDtypeStruct(shapes[n], jnp.float32) for n in range(count)],
        in_specs=[pl.BlockSpec(memory_space=pl.ANY)] * len(arrays),
        out_specs=[pl.BlockSpec(memory_space=pltpu.VMEM)] * count,
        scratch_shapes=scratch,
        compiler_params=pltpu.CompilerParams(
            collective_id=collective_id, has_side_effects=True, vmem_limit_bytes=56 * 1024 * 1024
        ),
    )(*views)


def view(ref, place, open_dims, rows):
    start, count = rows
    if "x" in open_dims:
        high, low = pl.ds(0, 2), pl.ds(0, 2)
    else:
        high, low = place["x"] // 2, place["x"] % 2
    mid = pl.ds(0, 4) if "y" in open_dims else place["y"]
    deep = pl.ds(0, 4) if "z" in open_dims else place["z"]
    core = pl.ds(0, 2) if "c" in open_dims else place["c"]
    return ref.at[high, mid, deep, low, core, pl.ds(start, count), :]


def slot_gather_kernel(pieces, count, *refs):
    ins, outs = refs[:count], refs[count : 2 * count]
    own_sem, core_send, core_recv, ring_send, ring_recv, pass_send, pass_recv = refs[2 * count :]
    place = my_place()
    sibling = moved(place, "c", 1)
    greet(place, (1, 2, 3))


    closing = []
    locals_ = []
    for number in range(count):
        whole = (0, ins[number].shape[0])
        copy = pltpu.make_async_copy(ins[number], view(outs[number], place, "", whole), own_sem.at[number])
        copy.start()
        locals_.append(copy)
        cross = remote(ins[number], view(outs[number], place, "", whole),
                       core_send.at[number], core_recv.at[number], sibling)
        cross.start()
        closing.append(cross)
    started = {}
    forwarded = []

    def land(phase):
        for split, pieces_of in enumerate(pieces):
            order = ORDERS[split]
            dim = order[phase]
            for step in (1, 2, 3):
                origin = moved(place, dim, -step)
                for index, (number, rows) in pieces_of:
                    started[(phase, split, step, index)].wait_recv()
                    spot = view(outs[number], origin, order[:phase], rows)
                    onward = remote(spot, spot, pass_send.at[phase, step - 1, index],
                                    pass_recv.at[phase, step - 1, index], sibling)
                    onward.start()
                    forwarded.append(onward)

    for phase in range(3):
        if phase:
            land(phase - 1)
        for split, pieces_of in enumerate(pieces):
            order = ORDERS[split]
            dim = order[phase]
            for step in (1, 2, 3):
                target = moved(place, dim, step)
                for index, (number, rows) in pieces_of:
                    spot = view(outs[number], place, order[:phase], rows)
                    src = ins[number].at[pl.ds(*rows), :] if phase == 0 else spot
                    copy = remote(src, spot, ring_send.at[phase, step - 1, index],
                                  ring_recv.at[phase, step - 1, index], target)
                    copy.start()
                    started[(phase, split, step, index)] = copy
        if phase == 0:
            for copy in locals_:
                copy.wait()
    land(2)
    for copy in started.values():
        copy.wait_send()
    for copy in forwarded + closing:
        copy.wait()


def number_pieces(splits):
    index = 0
    result = []
    for split in splits:
        rows = []
        for piece in split:
            rows.append((index, piece))
            index += 1
        result.append(rows)
    return result, index


def gather_slots(arrays, splits, collective_id):
    pieces, total = number_pieces(splits)
    count = len(arrays)
    outs = pl.pallas_call(
        functools.partial(slot_gather_kernel, pieces, count),
        out_shape=[jax.ShapeDtypeStruct((2, 4, 4, 2, 2) + a.shape, a.dtype) for a in arrays],
        in_specs=[pl.BlockSpec(memory_space=pl.ANY)] * count,
        out_specs=[pl.BlockSpec(memory_space=pl.ANY)] * count,
        scratch_shapes=[
            pltpu.SemaphoreType.DMA((count,)),
            pltpu.SemaphoreType.DMA((count,)),
            pltpu.SemaphoreType.DMA((count,)),
            pltpu.SemaphoreType.DMA((3, 3, total)),
            pltpu.SemaphoreType.DMA((3, 3, total)),
            pltpu.SemaphoreType.DMA((3, 3, total)),
            pltpu.SemaphoreType.DMA((3, 3, total)),
        ],
        compiler_params=pltpu.CompilerParams(collective_id=collective_id, has_side_effects=True),
    )(*arrays)
    return [o.reshape((128,) + a.shape) for o, a in zip(outs, arrays)]


def block_at(ref, place, dims, rows, lead=()):
    start, count = rows
    high, low = (pl.ds(0, 2), pl.ds(0, 2)) if "x" in dims else (place["x"] // 2, place["x"] % 2)
    mid = pl.ds(0, 4) if "y" in dims else place["y"]
    deep = pl.ds(0, 4) if "z" in dims else place["z"]
    return ref.at[high, mid, deep, low, pl.ds(start, count), :]


def spot_of(flat, dims, place):
    spot = {"xh": place["x"] // 2, "y": place["y"], "z": place["z"], "xl": place["x"] % 2}
    if "x" in dims:
        spot["xl"] = flat % 2
        flat = flat // 2
    if "z" in dims:
        spot["z"] = flat % 4
        flat = flat // 4
    if "y" in dims:
        spot["y"] = flat % 4
        flat = flat // 4
    if "x" in dims:
        spot["xh"] = flat
    return spot


def open_index(spot, dims):
    index = ()
    if "x" in dims:
        index += (spot["xh"],)
    if "y" in dims:
        index += (spot["y"],)
    if "z" in dims:
        index += (spot["z"],)
    if "x" in dims:
        index += (spot["xl"],)
    return index


def slot_reduce_kernel(pieces, count, total, *refs):
    ins, outs = refs[:count], refs[count : 2 * count]
    refs = refs[2 * count :]
    accs, crosses = refs[:count], refs[count : 2 * count]
    rings = [refs[2 * count + phase * total : 2 * count + (phase + 1) * total] for phase in range(3)]
    own_sem, core_send, core_recv, ring_send, ring_recv = refs[2 * count + 3 * total :]
    place = my_place()
    sibling = moved(place, "c", 1)
    greet(place, (1, 2, 3))


    def add_into(number, rows, place, dims, others):
        start, length = rows
        acc = accs[number]

        def body(flat, carry):
            spot = spot_of(flat, dims, place)
            where = (spot["xh"], spot["y"], spot["z"], spot["xl"], pl.ds(start, length), slice(None))
            value = acc[where].astype(jnp.float32)
            for other in others:
                value = value + other(spot)
            acc[where] = value.astype(acc.dtype)
            return carry

        lax.fori_loop(0, blocks_in(dims), body, 0)

    crossing = {}
    for split, pieces_of in enumerate(pieces):
        for index, (number, rows) in pieces_of:
            cross = remote(
                view(ins[number], sibling, "xyz", rows),
                block_at(crosses[number], place, "xyz", rows),
                core_send.at[index], core_recv.at[index], sibling,
            )
            cross.start()
            own = pltpu.make_async_copy(
                view(ins[number], place, "xyz", rows),
                block_at(accs[number], place, "xyz", rows),
                own_sem.at[index],
            )
            own.start()
            crossing[index] = (cross, own)
    sends = []
    rounds = {}

    def launch(phase, split, pieces_of):
        order = ORDERS[split]
        dim = order[phase]
        rest = "".join(order[phase + 1 :])
        for step in (1, 2, 3):
            there = moved(place, dim, step)
            target = there
            for index, (number, rows) in pieces_of:
                copy = remote(
                    block_at(accs[number], there, rest, rows),
                    rings[phase][index].at[step - 1],
                    ring_send.at[phase, step - 1, index],
                    ring_recv.at[phase, step - 1, index],
                    target,
                )
                copy.start()
                rounds[(phase, step, index)] = copy

    for split, pieces_of in enumerate(pieces):
        for index, (number, rows) in pieces_of:
            cross, own = crossing[index]
            own.wait()
            cross.wait_recv()
            start, length = rows

            def other(spot, number=number, start=start, length=length):
                return crosses[number][spot["xh"], spot["y"], spot["z"], spot["xl"], pl.ds(start, length), :].astype(jnp.float32)

            add_into(number, rows, place, "xyz", [other])
        launch(0, split, pieces_of)
    for phase in range(3):
        for split, pieces_of in enumerate(pieces):
            order = ORDERS[split]
            rest = "".join(order[phase + 1 :])
            for index, (number, rows) in pieces_of:
                others = []
                for step in (1, 2, 3):
                    rounds[(phase, step, index)].wait_recv()

                    def other(spot, step=step, index=index, rest=rest):
                        return rings[phase][index][(step - 1,) + open_index(spot, rest)].astype(jnp.float32)

                    others.append(other)
                if phase < 2:
                    add_into(number, rows, place, rest, others)
                else:
                    start, length = rows
                    spot = spot_of(0, "", place)
                    value = accs[number][spot["xh"], spot["y"], spot["z"], spot["xl"], pl.ds(start, length), :].astype(jnp.float32)
                    for item in others:
                        value = value + item(spot)
                    outs[number][pl.ds(start, length), :] = value
            if phase < 2:
                launch(phase + 1, split, pieces_of)
    for cross, own in crossing.values():
        cross.wait_send()
    for copy in rounds.values():
        copy.wait_send()


def reduce_slots(arrays, splits, collective_id):
    pieces, total = number_pieces(splits)
    count = len(arrays)
    shapes = [a.shape[1:] for a in arrays]
    dtype = arrays[0].dtype
    arrays = [a.reshape((2, 4, 4, 2, 2) + s) for a, s in zip(arrays, shapes)]
    scratch = [pltpu.VMEM((2, 4, 4, 2) + s, dtype) for s in shapes] * 2
    for phase in range(3):
        for split, pieces_of in enumerate(pieces):
            rest = "".join(ORDERS[split][phase + 1 :])
            for index, (number, rows) in pieces_of:
                scratch.append(pltpu.VMEM((3,) + open_shape(rest) + (rows[1], shapes[number][1]), dtype))
    scratch += [
        pltpu.SemaphoreType.DMA((total,)),
        pltpu.SemaphoreType.DMA((total,)),
        pltpu.SemaphoreType.DMA((total,)),
        pltpu.SemaphoreType.DMA((3, 3, total)),
        pltpu.SemaphoreType.DMA((3, 3, total)),
    ]
    return pl.pallas_call(
        functools.partial(slot_reduce_kernel, pieces, count, total),
        out_shape=[jax.ShapeDtypeStruct(s, jnp.float32) for s in shapes],
        in_specs=[pl.BlockSpec(memory_space=pl.ANY)] * count,
        out_specs=[pl.BlockSpec(memory_space=pltpu.VMEM)] * count,
        scratch_shapes=scratch,
        compiler_params=pltpu.CompilerParams(
            collective_id=collective_id, has_side_effects=True, vmem_limit_bytes=56 * 1024 * 1024
        ),
    )(*arrays)


def merge_parts(parts):
    top = parts[0][0]
    for part in parts[1:]:
        top = jnp.maximum(top, part[0])
    total = 0.0
    target = 0.0
    for part in parts:
        total = total + part[1] * jnp.exp(part[0] - top)
        target = target + part[2]
    return top, total, target


def stats_kernel(in_ref, out_ref, core_slots, ring_slots, core_sems, ring_send, ring_recv):
    place = my_place()
    greet(place, (1, 2, 3))

    def parts_of(ref, index):
        return tuple(ref[index, pl.ds(16 * row, 16), :] for row in range(3))

    def put(ref, index, parts):
        for row in range(3):
            ref[index, pl.ds(16 * row, 16), :] = parts[row]

    put(core_slots, place["c"], tuple(in_ref[pl.ds(16 * row, 16), :] for row in range(3)))
    cross = pltpu.make_async_remote_copy(
        src_ref=core_slots.at[place["c"]],
        dst_ref=core_slots.at[place["c"]],
        send_sem=core_sems.at[0],
        recv_sem=core_sems.at[1],
        device_id=device_of(moved(place, "c", 1)),
        device_id_type=pl.DeviceIdType.MESH,
    )
    cross.start()
    cross.wait()
    merged = merge_parts([parts_of(core_slots, number) for number in range(2)])
    for phase, dim in enumerate("xyz"):
        slots = ring_slots.at[phase]
        put(slots, place[dim], merged)
        copies = []
        for step in (1, 2, 3):
            copy = pltpu.make_async_remote_copy(
                src_ref=slots.at[place[dim]],
                dst_ref=slots.at[place[dim]],
                send_sem=ring_send.at[phase, step - 1],
                recv_sem=ring_recv.at[phase, step - 1],
                device_id=device_of(moved(place, dim, step)),
                device_id_type=pl.DeviceIdType.MESH,
            )
            copy.start()
            copies.append(copy)
        for copy in copies:
            copy.wait()
        merged = merge_parts([parts_of(slots, number) for number in range(4)])
    for row in range(3):
        out_ref[pl.ds(16 * row, 16), :] = merged[row]


def merge_stats(stats, collective_id):
    return pl.pallas_call(
        stats_kernel,
        out_shape=jax.ShapeDtypeStruct((48, 128), jnp.float32),
        in_specs=[pl.BlockSpec(memory_space=pltpu.VMEM)],
        out_specs=pl.BlockSpec(memory_space=pltpu.VMEM),
        scratch_shapes=[
            pltpu.VMEM((2, 48, 128), jnp.float32),
            pltpu.VMEM((3, 4, 48, 128), jnp.float32),
            pltpu.SemaphoreType.DMA((2,)),
            pltpu.SemaphoreType.DMA((3, 3)),
            pltpu.SemaphoreType.DMA((3, 3)),
        ],
        compiler_params=pltpu.CompilerParams(collective_id=collective_id, has_side_effects=True),
    )(stats)


HEADS = 12
NORM_EPSILON = 1e-05
MOMENTUM = 0.9
AVERAGE_KEEP = 0.9
RATE = 1500.0
CLIP = 0.05
TABLE_OF = (0, 1, 0, 1, 2, 3)
LOW = jnp.bfloat16
SPAN_LOW = 256
HEAD_BLOCK = 512
TOKEN_BLOCK = 1024


def pick_kernel(levels, rows, table_ref, high_ref, low_ref, out_ref):
    low = low_ref[...]
    high = high_ref[...]
    count = low.shape[1]
    hot = (lax.broadcasted_iota(jnp.int32, (SPAN_LOW, count), 0) == low).astype(LOW)
    total = jnp.zeros((rows, count), jnp.float32)
    group = 5
    for first in range(0, levels, group):
        found = jnp.dot(
            table_ref[pl.ds(first * rows, group * rows), :], hot, preferred_element_type=jnp.float32
        )
        for level in range(group):
            total = total + jnp.where(
                high == first + level, found[level * rows : (level + 1) * rows], 0.0
            )
    value = total.astype(LOW)
    for piece in range(count // 128):
        out_ref[piece] = value[:, piece * 128 : (piece + 1) * 128]


def pick_columns(table_levels, high, low, rows):
    levels = table_levels.shape[0] // rows
    tokens = high.shape[1]
    return pl.pallas_call(
        functools.partial(pick_kernel, levels, rows),
        grid=(tokens // TOKEN_BLOCK,),
        out_shape=jax.ShapeDtypeStruct((tokens // 128, rows, 128), LOW),
        in_specs=[
            pl.BlockSpec(table_levels.shape, lambda step: (0, 0)),
            pl.BlockSpec((1, TOKEN_BLOCK), lambda step: (0, step)),
            pl.BlockSpec((1, TOKEN_BLOCK), lambda step: (0, step)),
        ],
        out_specs=pl.BlockSpec((TOKEN_BLOCK // 128, rows, 128), lambda step: (step, 0, 0)),
        compiler_params=pltpu.CompilerParams(vmem_limit_bytes=32 * 1024 * 1024),
    )(table_levels, high, low)


def spread_kernel(levels, rows, grad_ref, high_ref, low_ref, out_ref, spread_ref):
    step = pl.program_id(0)

    @pl.when(step == 0)
    def _():
        out_ref[...] = jnp.zeros_like(out_ref)

    low = low_ref[...]
    high = high_ref[...]
    count = low.shape[1]
    hot = (lax.broadcasted_iota(jnp.int32, (SPAN_LOW, count), 0) == low).astype(LOW)
    grad = jnp.concatenate([grad_ref[piece] for piece in range(count // 128)], 1).astype(jnp.float32)
    pair = 2
    for first in range(0, levels, pair):
        spread_ref[pl.ds(first * rows, pair * rows), :] = jnp.concatenate(
            [jnp.where(high == first + level, grad, 0.0) for level in range(pair)], 0
        ).astype(LOW)
    group = 10 * rows
    for first in range(0, levels * rows, group):
        out_ref[pl.ds(first, group), :] += lax.dot_general(
            spread_ref[pl.ds(first, group), :],
            hot,
            (((1,), (1,)), ((), ())),
            preferred_element_type=jnp.float32,
        )


def spread_columns(grads, high, low, levels):
    rows = grads.shape[1]
    tokens = high.shape[1]
    return pl.pallas_call(
        functools.partial(spread_kernel, levels, rows),
        grid=(tokens // TOKEN_BLOCK,),
        out_shape=jax.ShapeDtypeStruct((levels * rows, SPAN_LOW), jnp.float32),
        in_specs=[
            pl.BlockSpec((TOKEN_BLOCK // 128, rows, 128), lambda step: (step, 0, 0)),
            pl.BlockSpec((1, TOKEN_BLOCK), lambda step: (0, step)),
            pl.BlockSpec((1, TOKEN_BLOCK), lambda step: (0, step)),
        ],
        out_specs=pl.BlockSpec((levels * rows, SPAN_LOW), lambda step: (0, 0)),
        scratch_shapes=[pltpu.VMEM((levels * rows, TOKEN_BLOCK), LOW)],
        compiler_params=pltpu.CompilerParams(vmem_limit_bytes=32 * 1024 * 1024),
    )(grads, high, low)


def plain_product(left, right):
    return jnp.dot(left, right, preferred_element_type=jnp.float32)


def rows_product(left, right):
    return lax.dot_general(
        left, right, (((0,), (0,)), ((), ())), preferred_element_type=jnp.float32
    )


def cols_product(left, right):
    return lax.dot_general(
        left, right, (((1,), (1,)), ((), ())), preferred_element_type=jnp.float32
    )


def column_sum(values):
    return jnp.sum(values.astype(jnp.float32), 0)


def norm_apply(values, gain, bias):
    centred = values - jnp.mean(values, -1, keepdims=True)
    variance = jnp.mean(centred * centred, -1, keepdims=True)
    return centred * lax.rsqrt(variance + NORM_EPSILON) * gain + bias


def norm_back(values, gain, bias, grad):
    outcome, pullback = jax.vjp(norm_apply, values, gain, bias)
    return pullback(grad)


def gelu_exact(values):
    return jax.nn.gelu(values, approximate=False)


def carve_vector(vector, width, hidden):
    lengths = [width] * 7 + [hidden] + [width] * 3
    pieces = []
    offset = 0
    for length in lengths:
        pieces.append(vector[offset : offset + length])
        offset += length
    return pieces


def split_heads(block):
    return block.reshape(block.shape[:-1] + (HEADS, block.shape[-1] // HEADS))


def take_rows(hot, values):
    return lax.dot_general(
        hot, values, (((1,), (0,)), ((), ())),
        precision=lax.Precision.HIGHEST, preferred_element_type=jnp.float32,
    )


def put_rows(hot, values):
    return lax.dot_general(
        hot, values, (((0,), (0,)), ((), ())),
        precision=lax.Precision.HIGHEST, preferred_element_type=jnp.float32,
    )


def thirds(number):
    return [(number, (256 * k, 256), k) for k in range(3)]


GATHER_PIECES = thirds(0) + thirds(1) + [(2, None, 0), (3, None, 2), (4, None, 1), (5, None, 2)]
REDUCE_PIECES = (
    thirds(0)
    + thirds(1)
    + [(2, None, 0), (3, None, 2), (4, None, 1), (5, None, 1), (6, None, 2), (7, None, 2), (8, None, 0)]
)
WHOLE = ((0, 2), (0, 4))
REDUCE_SOURCES = [
    (0, (0, 1), (0, 1)),
    (0, (0, 1), (1, 2)),
    (0, (0, 1), (3, 1)),
    (0, (1, 1), (0, 4)),
] + [(number,) + WHOLE for number in range(1, 9)]
SLOT_SPLITS = [[(0, (0, 16))], [(1, (0, 16))], [(2, (0, 16))]]


def fetch(masters):
    word, position, box, text, down, layout, layout_down, head, vector = [
        m.astype(LOW) for m in masters
    ]
    misc = jnp.concatenate(
        [
            layout.T,
            layout_down[0],
            layout_down[1],
            jnp.pad(vector, (0, 192 - vector.shape[0]))[None],
        ],
        0,
    )
    text, down, head, position, misc, box = gather_all(
        [text.T, down, head.T, position, misc, box.reshape(32, 128)], GATHER_PIECES, 2
    )
    return dict(
        text=text.reshape(6144, 768),
        down=down.reshape(3072, 768),
        head=head.reshape(768, 960),
        box=box.reshape(128, 4, 8, 128).transpose(1, 0, 2, 3).reshape(4, 1024, 128),
        layout=misc[:, :12].reshape(1536, 192),
        layout_down=misc[:, 12:18].reshape(768, 192),
        box_proj=misc[:, 18:24].reshape(768, 192),
        position=position.reshape(640, 960),
        vector=misc[:, 24, :123].reshape(15744),
    )


def reduce_weights(grads):
    shards = reduce_all(
        [
            grads["query"].reshape(16, 48, 768),
            grads["key_value"].reshape(32, 48, 768),
            grads["out"].reshape(16, 48, 768),
            grads["up"].reshape(64, 48, 768),
            grads["down"].reshape(128, 24, 768),
            grads["head"].reshape(128, 6, 960),
            grads["position"].reshape(128, 5, 960),
            grads["layout"].reshape(128, 12, 192),
            grads["layout_down"].reshape(128, 6, 192),
            grads["box_proj"].reshape(128, 6, 192),
            grads["box"].reshape(4, 128, 8, 128).transpose(1, 0, 2, 3).reshape(128, 32, 128),
            grads["vector"].reshape(128, 1, 123),
        ],
        REDUCE_SOURCES,
        REDUCE_PIECES,
        6,
    )
    text, down, head, position, layout, layout_down, box_proj, box, vector = shards
    return [
        position,
        box.reshape(4, 8, 128),
        text.T,
        down,
        layout.T,
        jnp.stack([layout_down, box_proj]),
        head.T,
        vector[0],
    ]


def close_forward(normed, attended_low, pieces, w_out, w_up, w_down):
    mid = normed + (cols_product(attended_low, w_out) + pieces[4])
    first = norm_apply(mid, pieces[5], pieces[6])
    first_low = first.astype(LOW)
    pre_act = cols_product(first_low, w_up) + pieces[7]
    act_low = gelu_exact(pre_act).astype(LOW)
    out_mid = first + (plain_product(act_low, w_down) + pieces[8])
    final = norm_apply(out_mid, pieces[9], pieces[10])
    return final, (mid, first_low, pre_act, act_low, out_mid)


def close_backward(grad_final, attended_low, pieces, w_out, w_up, w_down, kept):
    mid, first_low, pre_act, act_low, out_mid = kept
    d_out, d_gain2, d_shift2 = norm_back(out_mid, pieces[9], pieces[10], grad_final)
    d_branch2 = d_out.astype(LOW)
    d_down = rows_product(act_low, d_branch2)
    outcome, gelu_pull = jax.vjp(gelu_exact, pre_act)
    d_pre = gelu_pull(cols_product(d_branch2, w_down))[0].astype(LOW)
    d_up = rows_product(d_pre, first_low)
    d_first = d_out + plain_product(d_pre, w_up)
    d_mid, d_gain1, d_shift1 = norm_back(mid, pieces[5], pieces[6], d_first)
    d_branch1 = d_mid.astype(LOW)
    d_out_w = rows_product(d_branch1, attended_low)
    d_attended = plain_product(d_branch1, w_out).astype(LOW)
    tail = [
        column_sum(d_branch1),
        d_gain1,
        d_shift1,
        column_sum(d_pre),
        column_sum(d_branch2),
        d_gain2,
        d_shift2,
    ]
    return d_mid, d_attended, d_out_w, d_up, d_down, tail


def on_device(
    token_ids,
    box_coords,
    intersection_flags,
    masked_rows,
    masked_labels,
    *weights,
):
    triples = [tuple(weights[3 * n : 3 * n + 3]) for n in range(9)]
    masters = [entry[0] for entry in triples]
    word_table = masters[0]
    dp = lax.axis_index("dp")
    vocab = lax.axis_index("vocab")
    shard_width = word_table.shape[1]
    table_rows = word_table.shape[0]
    levels = -(-shard_width // SPAN_LOW)

    row_hot = masked_rows[:, :, None] == jnp.arange(64)[None, None, :]
    counted = jnp.sum(jnp.where(row_hot & (intersection_flags == 0)[:, None, :], 1, 0), 2)
    slot_hot = jnp.concatenate(
        [
            jnp.pad(row_hot[0], ((0, 0), (0, 64))),
            jnp.pad(row_hot[1], ((0, 0), (64, 0))),
        ],
        0,
    )
    slot_hot_wide = slot_hot.astype(jnp.float32)

    notes = jnp.concatenate(
        [
            token_ids.reshape(1, 128),
            jnp.concatenate(
                [masked_labels.reshape(1, 16), counted.reshape(1, 16), jnp.zeros((1, 96), jnp.int32)], 1
            ),
        ],
        0,
    )
    notes_all = lax.all_to_all(
        jnp.broadcast_to(notes[None], (128,) + notes.shape), AXES, 0, 0, tiled=True
    )
    ids_all = notes_all[:, 0, :].reshape(1, 16384)
    labels_all = notes_all[:, 1, :16].reshape(2048)
    counted_all = notes_all[:, 1, 16:32].reshape(2048).astype(jnp.float32)
    total_count = jnp.sum(counted_all)

    local_ids = ids_all - vocab * shard_width
    ids_high = local_ids >> 8
    ids_low = local_ids & 255
    table_low = word_table.astype(LOW)
    table_levels = (
        jnp.pad(table_low, ((0, 0), (0, levels * SPAN_LOW - shard_width)))
        .reshape(table_rows, levels, SPAN_LOW)
        .transpose(1, 0, 2)
        .reshape(levels * table_rows, SPAN_LOW)
    )
    found = pick_columns(table_levels, ids_high, ids_low, table_rows)
    found = lax.all_to_all(found, AXES, 0, 0, tiled=True)
    embedded = jnp.sum(found.reshape(32, 4, 24, 128).astype(jnp.float32), 1).reshape(768, 128).T

    table_blocks = (
        jnp.pad(table_low, ((0, 0), (0, 32 * HEAD_BLOCK - shard_width)))
        .reshape(table_rows, 32, HEAD_BLOCK)
        .transpose(1, 0, 2)
    )
    table_head = lax.all_to_all(table_blocks, "dp", 0, 0, tiled=True).reshape(768, HEAD_BLOCK)

    full = fetch(masters)
    vector = full["vector"].astype(jnp.float32)
    text_pieces = carve_vector(vector[:10752], 768, 3072)
    layout_pieces = carve_vector(vector[10752:13440], 192, 768)
    head_bias, head_gain, head_shift = vector[13440:14208], vector[14208:14976], vector[14976:]
    position_own = lax.dynamic_slice_in_dim(full["position"], vocab * 64, 64, 0).astype(jnp.float32)
    position_rows = jnp.concatenate([position_own, position_own], 0)
    text_sum = embedded + position_rows[:, :768]
    boxes = box_coords.reshape(4, 128)
    box_index = [
        boxes[0],
        boxes[1],
        boxes[2],
        boxes[3],
        jnp.abs(boxes[3] - boxes[1]),
        jnp.abs(boxes[2] - boxes[0]),
    ]
    box_hots = [(index[:, None] == jnp.arange(1024)[None, :]).astype(LOW) for index in box_index]
    spatial_low = jnp.concatenate(
        [plain_product(box_hots[n], full["box"][TABLE_OF[n]]) for n in range(6)], 1
    ).astype(LOW)
    layout_sum = position_rows[:, 768:] + plain_product(spatial_low, full["box_proj"])

    sums = [text_sum, layout_sum]
    widths = [768, 192]
    pieces = [text_pieces, layout_pieces]
    w_ins = [full["text"], full["layout"]]
    w_downs = [full["down"], full["layout_down"]]
    normed, normed_low, slot_normed, slot_low, keys, values, queries = [], [], [], [], [], [], []
    for n in range(2):
        width = widths[n]
        here = norm_apply(sums[n], pieces[n][0], pieces[n][1])
        here_low = here.astype(LOW)
        normed.append(here)
        normed_low.append(here_low)
        slot_here = take_rows(slot_hot_wide, here)
        slot_normed.append(slot_here)
        slot_low.append(slot_here.astype(LOW))
        kv_bias = jnp.concatenate([jnp.zeros_like(pieces[n][3]), pieces[n][3]])
        kv = (cols_product(here_low, w_ins[n][width : 3 * width]) + kv_bias).astype(LOW)
        keys.append(kv[:, :width].reshape(2, 64, width))
        values.append(kv[:, width:].reshape(2, 64, width))
        queries.append((cols_product(slot_low[n], w_ins[n][:width]) + pieces[n][2]).astype(LOW))

    scales = [(width // HEADS) ** (-0.5) for width in widths]
    query_group = lax.all_gather(jnp.concatenate(queries, 1), "vocab", axis=0)
    query_group = query_group.reshape(4, 2, 8, 960).transpose(1, 0, 2, 3).reshape(2, 32, 960)
    query_parts = [query_group[:, :, :768], query_group[:, :, 768:]]
    scores = 0.0
    for n in range(2):
        scores = scores + jnp.einsum(
            "mqhd,mkhd->mhqk",
            split_heads(query_parts[n]),
            split_heads(keys[n]),
            preferred_element_type=jnp.float32,
        ) * scales[n]
    score_top = jnp.max(scores, -1)
    score_exp = jnp.exp(scores - score_top[..., None])
    score_sum = jnp.sum(score_exp, -1)
    score_low = score_exp.astype(LOW)
    mixed = [
        jnp.einsum(
            "mhqk,mkhd->mqhd",
            score_low,
            split_heads(values[n]),
            preferred_element_type=jnp.float32,
        ).reshape(2, 32, widths[n])
        for n in range(2)
    ]
    partial = jnp.concatenate(
        mixed
        + [
            score_top.transpose(0, 2, 1),
            score_sum.transpose(0, 2, 1),
            jnp.zeros((2, 32, 40), jnp.float32),
        ],
        2,
    )
    partial = partial.reshape(2, 4, 8, 1024).transpose(1, 0, 2, 3).reshape(4, 16, 1024)
    partial = lax.all_to_all(partial, "vocab", 0, 0, tiled=True)
    tops = partial[:, :, 960:972]
    top = jnp.max(tops, 0)
    shares = jnp.exp(tops - top)
    share_sum = jnp.sum(shares * partial[:, :, 972:984], 0)
    log_total = top + jnp.log(share_sum)
    shares = shares / share_sum
    attended = [
        jnp.sum(split_heads(partial[:, :, :768]) * shares[..., None], 0).reshape(16, 768),
        jnp.sum(split_heads(partial[:, :, 768:960]) * shares[..., None], 0).reshape(16, 192),
    ]
    attended_low = [a.astype(LOW) for a in attended]
    finals, kepts = [], []
    for n in range(2):
        width = widths[n]
        final, kept = close_forward(
            slot_normed[n],
            attended_low[n],
            pieces[n],
            w_ins[n][3 * width : 4 * width],
            w_ins[n][4 * width :],
            w_downs[n],
        )
        finals.append(final)
        kepts.append(kept)
    joined_low = jnp.concatenate(finals, 1).astype(LOW)
    dense = cols_product(joined_low, full["head"]) + head_bias
    activated = gelu_exact(dense)
    picked_low = norm_apply(activated, head_gain, head_shift).astype(LOW)
    picked_all = gather_slots(
        [picked_low[:, 256 * k : 256 * (k + 1)] for k in range(3)], SLOT_SPLITS, 3
    )
    picked_all = jnp.concatenate([p.reshape(2048, 256) for p in picked_all], 1)
    column = lax.broadcasted_iota(jnp.int32, (1, HEAD_BLOCK), 1)
    valid = column < shard_width - dp * HEAD_BLOCK
    logits = jnp.where(valid, plain_product(picked_all, table_head), -1e30)
    row_max = jnp.max(logits, 1)
    row_sum = jnp.sum(jnp.where(valid, jnp.exp(logits - row_max[:, None]), 0.0), 1)
    label_hot = valid & (
        (labels_all - vocab * shard_width - dp * HEAD_BLOCK)[:, None] == column
    )
    target = jnp.sum(jnp.where(label_hot, logits, 0.0), 1)
    stats = jnp.concatenate(
        [row_max.reshape(16, 128), row_sum.reshape(16, 128), target.reshape(16, 128)], 0
    )
    stats = merge_stats(stats, 4)
    row_log = (stats[:16] + jnp.log(stats[16:32])).reshape(2048)
    loss_total = jnp.sum(counted_all * (row_log - stats[32:].reshape(2048)))
    d_logits = (
        (counted_all / total_count)[:, None]
        * (
            jnp.where(valid, jnp.exp(logits - row_log[:, None]), 0.0)
            - label_hot.astype(jnp.float32)
        )
    ).astype(LOW)
    d_picked_part = cols_product(d_logits, table_head).astype(LOW)
    d_picked = reduce_slots(
        [d_picked_part[:, 256 * k : 256 * (k + 1)].reshape(128, 16, 256) for k in range(3)],
        SLOT_SPLITS,
        5,
    )
    d_picked = jnp.concatenate(d_picked, 1)
    table_head_grad = rows_product(picked_all, d_logits).astype(LOW).reshape(32, 24, HEAD_BLOCK)
    table_head_grad = lax.all_to_all(table_head_grad, "dp", 0, 0, tiled=True)

    d_activated, d_head_gain, d_head_shift = norm_back(activated, head_gain, head_shift, d_picked)
    outcome, gelu_pull = jax.vjp(gelu_exact, dense)
    d_dense = gelu_pull(d_activated)[0].astype(LOW)
    d_head = rows_product(d_dense, joined_low)
    d_joined = plain_product(d_dense, full["head"])
    d_finals = [d_joined[:, :768], d_joined[:, 768:]]
    closed = []
    for n in range(2):
        width = widths[n]
        closed.append(
            close_backward(
                d_finals[n],
                attended_low[n],
                pieces[n],
                w_ins[n][3 * width : 4 * width],
                w_ins[n][4 * width :],
                w_downs[n],
                kepts[n],
            )
        )
    delta = 0.0
    for n in range(2):
        delta = delta + jnp.sum(
            split_heads(closed[n][1].astype(jnp.float32) * attended[n]), -1
        )
    back = jnp.concatenate(
        [
            closed[0][1].astype(jnp.float32),
            closed[1][1].astype(jnp.float32),
            log_total,
            delta,
            jnp.zeros((16, 40), jnp.float32),
        ],
        1,
    )
    back = lax.all_gather(back, "vocab", axis=0)
    back = back.reshape(4, 2, 8, 1024).transpose(1, 0, 2, 3).reshape(2, 32, 1024)
    d_attended = [back[:, :, :768].astype(LOW), back[:, :, 768:960].astype(LOW)]
    log_group = back[:, :, 960:972].transpose(0, 2, 1)
    delta_group = back[:, :, 972:984].transpose(0, 2, 1)
    probs = jnp.exp(scores - log_group[..., None])
    probs_low = probs.astype(LOW)
    d_probs = 0.0
    for n in range(2):
        d_probs = d_probs + jnp.einsum(
            "mqhd,mkhd->mhqk",
            split_heads(d_attended[n]),
            split_heads(values[n]),
            preferred_element_type=jnp.float32,
        )
    d_scores = (probs * (d_probs - delta_group[..., None])).astype(LOW)
    query_grads, kv_grads = [], []
    for n in range(2):
        query_grads.append(
            (
                jnp.einsum(
                    "mhqk,mkhd->mqhd",
                    d_scores,
                    split_heads(keys[n]),
                    preferred_element_type=jnp.float32,
                )
                * scales[n]
            ).reshape(2, 32, widths[n])
        )
        key_grad = (
            jnp.einsum(
                "mhqk,mqhd->mkhd",
                d_scores,
                split_heads(query_parts[n]),
                preferred_element_type=jnp.float32,
            )
            * scales[n]
        ).reshape(128, widths[n])
        value_grad = jnp.einsum(
            "mhqk,mqhd->mkhd",
            probs_low,
            split_heads(d_attended[n]),
            preferred_element_type=jnp.float32,
        ).reshape(128, widths[n])
        kv_grads.append(jnp.concatenate([key_grad, value_grad], 1).astype(LOW))
    query_grad = jnp.concatenate(query_grads + [jnp.zeros((2, 32, 64), jnp.float32)], 2)
    query_grad = query_grad.reshape(2, 4, 8, 1024).transpose(1, 0, 2, 3).reshape(4, 16, 1024)
    query_grad = jnp.sum(lax.all_to_all(query_grad, "vocab", 0, 0, tiled=True), 0)
    d_queries = [query_grad[:, :768].astype(LOW), query_grad[:, 768:960].astype(LOW)]

    weight_grads, vector_grads, d_lows = [], [], []
    for n in range(2):
        width = widths[n]
        d_mid, d_att, d_out_w, d_up, d_down, tail = closed[n]
        d_slot = d_mid + plain_product(d_queries[n], w_ins[n][:width])
        d_normed = plain_product(kv_grads[n], w_ins[n][width : 3 * width]) + put_rows(
            slot_hot_wide, d_slot
        )
        d_embed, d_gain0, d_shift0 = norm_back(sums[n], pieces[n][0], pieces[n][1], d_normed)
        d_lows.append(d_embed.astype(LOW))
        weight_grads.append(
            [
                rows_product(d_queries[n], slot_low[n]).astype(LOW),
                rows_product(kv_grads[n], normed_low[n]).astype(LOW),
                d_out_w.astype(LOW),
                d_up.astype(LOW),
            ]
        )
        vector_grads.append(
            jnp.concatenate(
                [d_gain0, d_shift0, column_sum(d_queries[n]), column_sum(kv_grads[n][:, width:])]
                + tail
            )
        )
    d_text_blocks = jnp.broadcast_to(
        d_lows[0].T.reshape(32, 1, 24, 128), (32, 4, 24, 128)
    ).reshape(128, 24, 128)
    d_text_all = lax.all_to_all(d_text_blocks, AXES, 0, 0, tiled=True)
    table_grad = (
        spread_columns(d_text_all, ids_high, ids_low, levels)
        .reshape(levels, table_rows, SPAN_LOW)
        .transpose(1, 0, 2)
        .reshape(table_rows, levels * SPAN_LOW)[:, :shard_width]
    )
    table_grad = table_grad + table_head_grad.transpose(1, 0, 2).reshape(
        table_rows, 32 * HEAD_BLOCK
    )[:, :shard_width].astype(jnp.float32)

    d_both = jnp.concatenate(d_lows, 1).astype(jnp.float32)
    d_positions = lax.dynamic_update_slice_in_dim(
        jnp.zeros((640, 960), jnp.float32), d_both[:64] + d_both[64:], vocab * 64, 0
    )
    d_spatial = cols_product(d_lows[1], full["box_proj"]).astype(LOW)
    spatial_grads = [
        rows_product(box_hots[n], d_spatial[:, n * 128 : (n + 1) * 128]) for n in range(6)
    ]
    d_box = jnp.stack(
        [
            spatial_grads[0] + spatial_grads[2],
            spatial_grads[1] + spatial_grads[3],
            spatial_grads[4],
            spatial_grads[5],
        ]
    )
    shards = reduce_weights(
        dict(
            query=weight_grads[0][0],
            key_value=weight_grads[0][1],
            out=weight_grads[0][2],
            up=weight_grads[0][3],
            down=closed[0][4].astype(LOW),
            head=d_head.astype(LOW),
            box=d_box.astype(LOW),
            layout=jnp.concatenate(weight_grads[1], 0),
            layout_down=closed[1][4].astype(LOW),
            box_proj=rows_product(spatial_low, d_lows[1]).astype(LOW),
            position=d_positions.astype(LOW),
            vector=jnp.concatenate(
                vector_grads + [column_sum(d_dense), d_head_gain, d_head_shift]
            ).astype(LOW),
        )
    )
    all_grads = [table_grad] + shards
    square_sum = jnp.zeros((), jnp.float32)
    for grad in all_grads:
        square_sum = square_sum + jnp.sum(grad * grad)
    norm_stats = jnp.zeros((48, 128), jnp.float32).at[16:32].set(square_sum)
    grad_norm = jnp.sqrt(merge_stats(norm_stats, 7)[16, 0])
    factor = jnp.minimum(1.0, CLIP / grad_norm)
    results = []
    for (master, momentum, average), grad in zip(triples, all_grads):
        clipped = factor * grad
        momentum_next = MOMENTUM * momentum + clipped
        master_next = master - RATE * (clipped + MOMENTUM * momentum_next)
        average_next = AVERAGE_KEEP * average + (1.0 - AVERAGE_KEEP) * master_next
        results += [master_next, momentum_next, average_next]
    return tuple(results + [loss_total, total_count, grad_norm])


TOKEN_SPEC = P(None, AXES)
WEIGHT_SPECS = (
    P("dp", "vocab"),
    P(AXES, None),
    P(None, AXES, None),
    P(None, AXES),
    P(AXES, None),
    P(None, AXES),
    P(None, AXES, None),
    P(None, AXES),
    P(AXES),
)


def solution(mesh):
    weight_specs = tuple(spec for spec in WEIGHT_SPECS for _ in range(3))
    in_specs = (TOKEN_SPEC, P(None, None, AXES), TOKEN_SPEC, TOKEN_SPEC, TOKEN_SPEC) + weight_specs
    out_specs = weight_specs + (P(), P(), P())
    return jax.shard_map(
        on_device, mesh=mesh, in_specs=in_specs, out_specs=out_specs, check_vma=False
    )
```

```python
import functools

import jax
import jax.numpy as jnp
from jax import lax
from jax.experimental import pallas as pl
from jax.experimental.pallas import tpu as pltpu
from jax.sharding import PartitionSpec as P

AXES = ("dp", "vocab")
MESH = pl.DeviceIdType.MESH
LONG = pl.CostEstimate(flops=60_000_000_000, bytes_accessed=200_000_000, transcendentals=0)
ORDERS = (("z", "y", "x"), ("y", "x", "z"), ("x", "z", "y"))


def my_place():
    dp = lax.axis_index("dp")
    vocab = lax.axis_index("vocab")
    return {
        "x": (dp // 16) * 2 + vocab // 2,
        "y": (dp // 4) % 4,
        "z": dp % 4,
        "c": vocab % 2,
    }


def moved(place, dim, step):
    other = dict(place)
    other[dim] = (1 - place["c"]) if dim == "c" else (place[dim] + step + 4) % 4
    return other


def device_of(place):
    return (
        (place["x"] // 2) * 16 + place["y"] * 4 + place["z"],
        (place["x"] % 2) * 2 + place["c"],
    )


def greet(place, steps=(1, 3)):
    barrier = pltpu.get_barrier_semaphore()
    peers = [moved(place, dim, step) for dim in "xyz" for step in steps]
    peers.append(moved(place, "c", 1))
    for peer in peers:
        pl.semaphore_signal(barrier, inc=1, device_id=device_of(peer), device_id_type=MESH)
    pl.semaphore_wait(barrier, len(peers))


def remote(src, dst, send, recv, place):
    return pltpu.make_async_remote_copy(
        src_ref=src,
        dst_ref=dst,
        send_sem=send,
        recv_sem=recv,
        device_id=device_of(place),
        device_id_type=MESH,
    )


def lanes_at(ref, lanes):
    return slice(None) if lanes is None else pl.ds(*lanes)


def block_view(ref, place, dims, lanes, core=None):
    high, low = (pl.ds(0, 2), pl.ds(0, 2)) if "x" in dims else (place["x"] // 2, place["x"] % 2)
    mid = pl.ds(0, 4) if "y" in dims else place["y"]
    deep = pl.ds(0, 4) if "z" in dims else place["z"]
    where = (high, mid, deep, low)
    if core is not None:
        where += (core,)
    return ref.at[where + (slice(None), lanes_at(ref, lanes))]


def halves(lanes, number):
    if lanes is None or lanes[1] < 256:
        return (lanes, False) if number % 2 == 0 else (False, lanes)
    half = lanes[1] // 256 * 128
    return (lanes[0], half), (lanes[0] + half, lanes[1] - half)


def gather_kernel(pieces, count, *refs):
    ins, outs = refs[:count], refs[count : 2 * count]
    own_sem, core_sems, ring_send, ring_recv, pass_send, pass_recv = refs[2 * count :]
    place = my_place()
    sibling = moved(place, "c", 1)
    greet(place)

    def spot(number, origin, dims, lanes):
        return block_view(outs[number], origin, dims, lanes, place["c"])

    copies, crosses = [], []
    for number in range(count):
        here = block_view(outs[number], place, "", None, place["c"])
        copy = pltpu.make_async_copy(ins[number], here, own_sem.at[number])
        copy.start()
        copies.append(copy)
        cross = remote(ins[number], here, core_sems.at[0, number], core_sems.at[1, number], sibling)
        cross.start()
        crosses.append(cross)
    rings, passes = {}, []

    def send(phase, piece, way, src, dst, target):
        copy = remote(
            src, dst, ring_send.at[phase, way, piece], ring_recv.at[phase, way, piece], target
        )
        copy.start()
        rings[(phase, way, piece)] = copy

    def hand_over(phase, piece, way, where):
        copy = remote(
            where, where, pass_send.at[phase, way, piece], pass_recv.at[phase, way, piece], sibling
        )
        copy.start()
        passes.append(copy)

    def begin(phase, piece):
        number, lanes, order = pieces[piece]
        dim, dims = ORDERS[order][phase], ORDERS[order][:phase]
        where = spot(number, place, dims, lanes)
        src = ins[number].at[:, lanes_at(ins[number], lanes)] if phase == 0 else where
        for way, step in ((0, 1), (1, -1)):
            send(phase, piece, way, src, where, moved(place, dim, step))

    for piece in range(len(pieces)):
        begin(0, piece)
    for copy in copies:
        copy.wait()
    for phase in range(3):
        for piece, (number, lanes, order) in enumerate(pieces):
            dim, dims = ORDERS[order][phase], ORDERS[order][:phase]
            parts = halves(lanes, piece)
            for way, step in ((0, 1), (1, -1)):
                rings[(phase, way, piece)].wait_recv()
                origin = moved(place, dim, -step)
                if parts[way] is not False:
                    onward = spot(number, origin, dims, parts[way])
                    send(phase, piece, 2 + way, onward, onward, moved(place, dim, step))
                hand_over(phase, piece, way, spot(number, origin, dims, lanes))
        for piece, (number, lanes, order) in enumerate(pieces):
            dim, dims = ORDERS[order][phase], ORDERS[order][:phase]
            parts = halves(lanes, piece)
            for way in range(2):
                if parts[way] is not False:
                    rings[(phase, 2 + way, piece)].wait_recv()
            if phase < 2:
                begin(phase + 1, piece)
            hand_over(phase, piece, 2, spot(number, moved(place, dim, 2), dims, lanes))
    for copy in rings.values():
        copy.wait_send()
    for copy in crosses + passes:
        copy.wait()


def gather_all(arrays, pieces, collective_id):
    count, total = len(arrays), len(pieces)
    outs = pl.pallas_call(
        functools.partial(gather_kernel, pieces, count),
        out_shape=[jax.ShapeDtypeStruct((2, 4, 4, 2, 2) + a.shape, a.dtype) for a in arrays],
        in_specs=[pl.BlockSpec(memory_space=pl.ANY)] * count,
        out_specs=[pl.BlockSpec(memory_space=pl.ANY)] * count,
        scratch_shapes=[
            pltpu.SemaphoreType.DMA((count,)),
            pltpu.SemaphoreType.DMA((2, count)),
            pltpu.SemaphoreType.DMA((3, 4, total)),
            pltpu.SemaphoreType.DMA((3, 4, total)),
            pltpu.SemaphoreType.DMA((3, 3, total)),
            pltpu.SemaphoreType.DMA((3, 3, total)),
        ],
        cost_estimate=LONG,
        compiler_params=pltpu.CompilerParams(collective_id=collective_id, has_side_effects=True),
    )(*arrays)
    return [o.reshape((128,) + a.shape) for o, a in zip(outs, arrays)]


def open_shape(dims):
    shape = ()
    if "x" in dims:
        shape += (2,)
    if "y" in dims:
        shape += (4,)
    if "z" in dims:
        shape += (4,)
    if "x" in dims:
        shape += (2,)
    return shape


def chunks_of(dims, place):
    high, mid, deep, low = place["x"] // 2, place["y"], place["z"], place["x"] % 2
    every = slice(None)
    if dims == "":
        return 1, lambda flat: ((high, mid, deep, low), ())
    inner = (every if "y" in dims else mid, every if "z" in dims else deep)
    if "x" in dims and "y" in dims and "z" in dims:
        return 8, lambda flat: ((flat // 4, flat % 4, every, every), (flat // 4, flat % 4))
    if "x" in dims:
        return 2, lambda flat: ((flat,) + inner + (every,), (flat,))
    if "y" in dims and "z" in dims:
        return 4, lambda flat: ((high, flat, every, low), (flat,))
    return 1, lambda flat: ((high,) + inner + (low,), ())


def reduce_kernel(sources, pieces, count, *refs):
    total = len(pieces)
    ins = refs[: len(sources)]
    refs = refs[len(sources) :]
    outs, square_ref, refs = refs[:count], refs[count], refs[count + 1 :]
    accs, crosses, refs = refs[:count], refs[count : 2 * count], refs[2 * count :]
    slots = refs[: 12 * total]
    own_sem, core_sems, ring_send, ring_recv = refs[12 * total :]
    place = my_place()
    sibling = moved(place, "c", 1)
    greet(place)

    def slot(phase, way, piece):
        return slots[(phase * 4 + way) * total + piece]

    def add(number, lanes, at, dims, others):
        acc = accs[number]

        count, chunk = chunks_of(dims, at)

        def body(flat, carry):
            block, inner = chunk(flat)
            where = block + (slice(None), lanes_at(acc, lanes))
            parts = [
                other[inner] if index is None else other[block + index] for other, index in others
            ]
            if len(parts) == 1:
                acc[where] = acc[where] + parts[0]
            else:
                wide = [part.astype(jnp.float32) for part in [acc[where]] + parts]
                acc[where] = sum(wide).astype(acc.dtype)
            return carry

        if count == 1:
            body(0, 0)
        else:
            lax.fori_loop(0, count, body, 0)

    started = []
    first = {}
    for piece, (number, lanes, order) in enumerate(pieces):
        for index, (owner, high, mids) in enumerate(sources):
            if owner != number:
                continue
            copies = []
            for core, target in ((sibling["c"], "cross"), (place["c"], "own")):
                where = (slice(None), slice(None), slice(None), slice(None), core)
                src = ins[index].at[where + (slice(None), lanes_at(ins[index], lanes))]
                at = (
                    pl.ds(*high),
                    pl.ds(*mids),
                    slice(None),
                    slice(None),
                    slice(None),
                    lanes_at(accs[number], lanes),
                )
                if target == "cross":
                    copy = remote(
                        src,
                        crosses[number].at[at],
                        core_sems.at[0, piece, index],
                        core_sems.at[1, piece, index],
                        sibling,
                    )
                else:
                    copy = pltpu.make_async_copy(src, accs[number].at[at], own_sem.at[piece, index])
                copy.start()
                copies.append(copy)
            started.append(copies[0])
            first.setdefault(piece, []).append(copies)
    rings = {}

    def send(phase, way, piece, src, step):
        number, lanes, order = pieces[piece]
        copy = remote(
            src,
            slot(phase, way, piece),
            ring_send.at[phase, way, piece],
            ring_recv.at[phase, way, piece],
            moved(place, ORDERS[order][phase], step),
        )
        copy.start()
        rings[(phase, way, piece)] = copy
        started.append(copy)

    def begin(phase, piece):
        number, lanes, order = pieces[piece]
        dim, rest = ORDERS[order][phase], ORDERS[order][phase + 1 :]
        parts = halves(lanes, piece)
        for way, step in ((0, 1), (1, -1)):
            if parts[way] is not False:
                there = moved(place, dim, 2)
                send(phase, way, piece, block_view(accs[number], there, rest, parts[way]), step)

    for piece, (number, lanes, order) in enumerate(pieces):
        for cross, own in first[piece]:
            own.wait()
            cross.wait_recv()
        add(number, lanes, place, "xyz", [(crosses[number], (slice(None), lanes_at(accs[number], lanes)))])
        begin(0, piece)
    for phase in range(3):
        for piece, (number, lanes, order) in enumerate(pieces):
            dim, rest = ORDERS[order][phase], ORDERS[order][phase + 1 :]
            parts = halves(lanes, piece)
            for way, step in ((0, 1), (1, -1)):
                there = moved(place, dim, step)
                if parts[way] is not False:
                    rings[(phase, way, piece)].wait_recv()
                    add(number, parts[way], there, rest, [(slot(phase, way, piece), None)])
                send(phase, 2 + way, piece, block_view(accs[number], there, rest, lanes), step)
        for piece, (number, lanes, order) in enumerate(pieces):
            rest = ORDERS[order][phase + 1 :]
            for way in range(2):
                rings[(phase, 2 + way, piece)].wait_recv()
            others = [slot(phase, 2 + way, piece) for way in range(2)]
            if phase < 2:
                add(number, lanes, place, rest, [(other, None) for other in others])
                begin(phase + 1, piece)
            else:
                block = (place["x"] // 2, place["y"], place["z"], place["x"] % 2)
                where = (slice(None), lanes_at(accs[number], lanes))
                value = accs[number][block + where].astype(jnp.float32)
                for other in others:
                    value = value + other[...].astype(jnp.float32)
                outs[number][where] = value
    total_square = jnp.zeros((1, 1), jnp.float32)
    for number in range(count):
        value = outs[number][...]
        total_square = total_square + jnp.sum(
            jnp.sum(value * value, 1, keepdims=True), 0, keepdims=True
        )
    square_ref[...] = jnp.broadcast_to(total_square, square_ref.shape)
    for copy in started:
        copy.wait_send()


def reduce_all(arrays, sources, pieces, collective_id):
    shapes = {}
    views = []
    for array, (owner, high, mids) in zip(arrays, sources):
        shapes[owner] = array.shape[1:]
        views.append(array.reshape((high[1], mids[1], 4, 2, 2) + array.shape[1:]))
    count, total = len(shapes), len(pieces)
    dtype = arrays[0].dtype
    scratch = [pltpu.VMEM((2, 4, 4, 2) + shapes[n], dtype) for n in range(count)] * 2
    for phase in range(3):
        for way in range(4):
            for piece, (number, lanes, order) in enumerate(pieces):
                rest = ORDERS[order][phase + 1 :]
                rows, width = shapes[number]
                part = halves(lanes, piece)[way] if way < 2 else lanes
                if part is False:
                    scratch.append(pltpu.VMEM((8, 128), dtype))
                else:
                    wide = width if part is None else part[1]
                    scratch.append(pltpu.VMEM(open_shape(rest) + (rows, wide), dtype))
    scratch += [
        pltpu.SemaphoreType.DMA((total, len(arrays))),
        pltpu.SemaphoreType.DMA((2, total, len(arrays))),
        pltpu.SemaphoreType.DMA((3, 4, total)),
        pltpu.SemaphoreType.DMA((3, 4, total)),
    ]
    return pl.pallas_call(
        functools.partial(reduce_kernel, sources, pieces, count),
        out_shape=[
            jax.ShapeDtypeStruct(shape, jnp.float32)
            for shape in [shapes[n] for n in range(count)] + [(16, 128)]
        ],
        in_specs=[pl.BlockSpec(memory_space=pl.ANY)] * len(arrays),
        out_specs=[pl.BlockSpec(memory_space=pltpu.VMEM)] * (count + 1),
        scratch_shapes=scratch,
        cost_estimate=LONG,
        compiler_params=pltpu.CompilerParams(
            collective_id=collective_id, has_side_effects=True, vmem_limit_bytes=56 * 1024 * 1024
        ),
    )(*views)


def blocks_in(dims):
    total = 1
    for size in open_shape(dims):
        total *= size
    return total


def view(ref, place, open_dims, rows):
    start, count = rows
    if "x" in open_dims:
        high, low = pl.ds(0, 2), pl.ds(0, 2)
    else:
        high, low = place["x"] // 2, place["x"] % 2
    mid = pl.ds(0, 4) if "y" in open_dims else place["y"]
    deep = pl.ds(0, 4) if "z" in open_dims else place["z"]
    core = pl.ds(0, 2) if "c" in open_dims else place["c"]
    return ref.at[high, mid, deep, low, core, pl.ds(start, count), :]


def slot_gather_kernel(pieces, count, *refs):
    ins, outs = refs[:count], refs[count : 2 * count]
    own_sem, core_send, core_recv, ring_send, ring_recv, pass_send, pass_recv = refs[2 * count :]
    place = my_place()
    sibling = moved(place, "c", 1)
    greet(place, (1, 2, 3))


    closing = []
    locals_ = []
    for number in range(count):
        whole = (0, ins[number].shape[0])
        copy = pltpu.make_async_copy(ins[number], view(outs[number], place, "", whole), own_sem.at[number])
        copy.start()
        locals_.append(copy)
        cross = remote(ins[number], view(outs[number], place, "", whole),
                       core_send.at[number], core_recv.at[number], sibling)
        cross.start()
        closing.append(cross)
    started = {}
    forwarded = []

    def land(phase):
        for split, pieces_of in enumerate(pieces):
            order = ORDERS[split]
            dim = order[phase]
            for step in (1, 2, 3):
                origin = moved(place, dim, -step)
                for index, (number, rows) in pieces_of:
                    started[(phase, split, step, index)].wait_recv()
                    spot = view(outs[number], origin, order[:phase], rows)
                    onward = remote(spot, spot, pass_send.at[phase, step - 1, index],
                                    pass_recv.at[phase, step - 1, index], sibling)
                    onward.start()
                    forwarded.append(onward)

    for phase in range(3):
        if phase:
            land(phase - 1)
        for split, pieces_of in enumerate(pieces):
            order = ORDERS[split]
            dim = order[phase]
            for step in (1, 2, 3):
                target = moved(place, dim, step)
                for index, (number, rows) in pieces_of:
                    spot = view(outs[number], place, order[:phase], rows)
                    src = ins[number].at[pl.ds(*rows), :] if phase == 0 else spot
                    copy = remote(src, spot, ring_send.at[phase, step - 1, index],
                                  ring_recv.at[phase, step - 1, index], target)
                    copy.start()
                    started[(phase, split, step, index)] = copy
        if phase == 0:
            for copy in locals_:
                copy.wait()
    land(2)
    for copy in started.values():
        copy.wait_send()
    for copy in forwarded + closing:
        copy.wait()


def number_pieces(splits):
    index = 0
    result = []
    for split in splits:
        rows = []
        for piece in split:
            rows.append((index, piece))
            index += 1
        result.append(rows)
    return result, index


def gather_slots(arrays, splits, collective_id):
    pieces, total = number_pieces(splits)
    count = len(arrays)
    outs = pl.pallas_call(
        functools.partial(slot_gather_kernel, pieces, count),
        out_shape=[jax.ShapeDtypeStruct((2, 4, 4, 2, 2) + a.shape, a.dtype) for a in arrays],
        in_specs=[pl.BlockSpec(memory_space=pl.ANY)] * count,
        out_specs=[pl.BlockSpec(memory_space=pl.ANY)] * count,
        scratch_shapes=[
            pltpu.SemaphoreType.DMA((count,)),
            pltpu.SemaphoreType.DMA((count,)),
            pltpu.SemaphoreType.DMA((count,)),
            pltpu.SemaphoreType.DMA((3, 3, total)),
            pltpu.SemaphoreType.DMA((3, 3, total)),
            pltpu.SemaphoreType.DMA((3, 3, total)),
            pltpu.SemaphoreType.DMA((3, 3, total)),
        ],
        compiler_params=pltpu.CompilerParams(collective_id=collective_id, has_side_effects=True),
    )(*arrays)
    return [o.reshape((128,) + a.shape) for o, a in zip(outs, arrays)]


def block_at(ref, place, dims, rows, lead=()):
    start, count = rows
    high, low = (pl.ds(0, 2), pl.ds(0, 2)) if "x" in dims else (place["x"] // 2, place["x"] % 2)
    mid = pl.ds(0, 4) if "y" in dims else place["y"]
    deep = pl.ds(0, 4) if "z" in dims else place["z"]
    return ref.at[high, mid, deep, low, pl.ds(start, count), :]


def spot_of(flat, dims, place):
    spot = {"xh": place["x"] // 2, "y": place["y"], "z": place["z"], "xl": place["x"] % 2}
    if "x" in dims:
        spot["xl"] = flat % 2
        flat = flat // 2
    if "z" in dims:
        spot["z"] = flat % 4
        flat = flat // 4
    if "y" in dims:
        spot["y"] = flat % 4
        flat = flat // 4
    if "x" in dims:
        spot["xh"] = flat
    return spot


def open_index(spot, dims):
    index = ()
    if "x" in dims:
        index += (spot["xh"],)
    if "y" in dims:
        index += (spot["y"],)
    if "z" in dims:
        index += (spot["z"],)
    if "x" in dims:
        index += (spot["xl"],)
    return index


def slot_reduce_kernel(pieces, count, total, *refs):
    ins, outs = refs[:count], refs[count : 2 * count]
    refs = refs[2 * count :]
    accs, crosses = refs[:count], refs[count : 2 * count]
    rings = [refs[2 * count + phase * total : 2 * count + (phase + 1) * total] for phase in range(3)]
    own_sem, core_send, core_recv, ring_send, ring_recv = refs[2 * count + 3 * total :]
    place = my_place()
    sibling = moved(place, "c", 1)
    greet(place, (1, 2, 3))


    def add_into(number, rows, place, dims, others):
        start, length = rows
        acc = accs[number]

        def body(flat, carry):
            spot = spot_of(flat, dims, place)
            where = (spot["xh"], spot["y"], spot["z"], spot["xl"], pl.ds(start, length), slice(None))
            value = acc[where].astype(jnp.float32)
            for other in others:
                value = value + other(spot)
            acc[where] = value.astype(acc.dtype)
            return carry

        lax.fori_loop(0, blocks_in(dims), body, 0)

    crossing = {}
    for split, pieces_of in enumerate(pieces):
        for index, (number, rows) in pieces_of:
            cross = remote(
                view(ins[number], sibling, "xyz", rows),
                block_at(crosses[number], place, "xyz", rows),
                core_send.at[index], core_recv.at[index], sibling,
            )
            cross.start()
            own = pltpu.make_async_copy(
                view(ins[number], place, "xyz", rows),
                block_at(accs[number], place, "xyz", rows),
                own_sem.at[index],
            )
            own.start()
            crossing[index] = (cross, own)
    sends = []
    rounds = {}

    def launch(phase, split, pieces_of):
        order = ORDERS[split]
        dim = order[phase]
        rest = "".join(order[phase + 1 :])
        for step in (1, 2, 3):
            there = moved(place, dim, step)
            target = there
            for index, (number, rows) in pieces_of:
                copy = remote(
                    block_at(accs[number], there, rest, rows),
                    rings[phase][index].at[step - 1],
                    ring_send.at[phase, step - 1, index],
                    ring_recv.at[phase, step - 1, index],
                    target,
                )
                copy.start()
                rounds[(phase, step, index)] = copy

    for split, pieces_of in enumerate(pieces):
        for index, (number, rows) in pieces_of:
            cross, own = crossing[index]
            own.wait()
            cross.wait_recv()
            start, length = rows

            def other(spot, number=number, start=start, length=length):
                return crosses[number][spot["xh"], spot["y"], spot["z"], spot["xl"], pl.ds(start, length), :].astype(jnp.float32)

            add_into(number, rows, place, "xyz", [other])
        launch(0, split, pieces_of)
    for phase in range(3):
        for split, pieces_of in enumerate(pieces):
            order = ORDERS[split]
            rest = "".join(order[phase + 1 :])
            for index, (number, rows) in pieces_of:
                others = []
                for step in (1, 2, 3):
                    rounds[(phase, step, index)].wait_recv()

                    def other(spot, step=step, index=index, rest=rest):
                        return rings[phase][index][(step - 1,) + open_index(spot, rest)].astype(jnp.float32)

                    others.append(other)
                if phase < 2:
                    add_into(number, rows, place, rest, others)
                else:
                    start, length = rows
                    spot = spot_of(0, "", place)
                    value = accs[number][spot["xh"], spot["y"], spot["z"], spot["xl"], pl.ds(start, length), :].astype(jnp.float32)
                    for item in others:
                        value = value + item(spot)
                    outs[number][pl.ds(start, length), :] = value
            if phase < 2:
                launch(phase + 1, split, pieces_of)
    for cross, own in crossing.values():
        cross.wait_send()
    for copy in rounds.values():
        copy.wait_send()


def reduce_slots(arrays, splits, collective_id):
    pieces, total = number_pieces(splits)
    count = len(arrays)
    shapes = [a.shape[1:] for a in arrays]
    dtype = arrays[0].dtype
    arrays = [a.reshape((2, 4, 4, 2, 2) + s) for a, s in zip(arrays, shapes)]
    scratch = [pltpu.VMEM((2, 4, 4, 2) + s, dtype) for s in shapes] * 2
    for phase in range(3):
        for split, pieces_of in enumerate(pieces):
            rest = "".join(ORDERS[split][phase + 1 :])
            for index, (number, rows) in pieces_of:
                scratch.append(pltpu.VMEM((3,) + open_shape(rest) + (rows[1], shapes[number][1]), dtype))
    scratch += [
        pltpu.SemaphoreType.DMA((total,)),
        pltpu.SemaphoreType.DMA((total,)),
        pltpu.SemaphoreType.DMA((total,)),
        pltpu.SemaphoreType.DMA((3, 3, total)),
        pltpu.SemaphoreType.DMA((3, 3, total)),
    ]
    return pl.pallas_call(
        functools.partial(slot_reduce_kernel, pieces, count, total),
        out_shape=[jax.ShapeDtypeStruct(s, jnp.float32) for s in shapes],
        in_specs=[pl.BlockSpec(memory_space=pl.ANY)] * count,
        out_specs=[pl.BlockSpec(memory_space=pltpu.VMEM)] * count,
        scratch_shapes=scratch,
        compiler_params=pltpu.CompilerParams(
            collective_id=collective_id, has_side_effects=True, vmem_limit_bytes=56 * 1024 * 1024
        ),
    )(*arrays)


def merge_parts(parts):
    top = parts[0][0]
    for part in parts[1:]:
        top = jnp.maximum(top, part[0])
    total = 0.0
    target = 0.0
    for part in parts:
        total = total + part[1] * jnp.exp(part[0] - top)
        target = target + part[2]
    return top, total, target


def stats_kernel(in_ref, out_ref, core_slots, ring_slots, core_sems, ring_send, ring_recv):
    place = my_place()
    greet(place, (1, 2, 3))

    def parts_of(ref, index):
        return tuple(ref[index, pl.ds(16 * row, 16), :] for row in range(3))

    def put(ref, index, parts):
        for row in range(3):
            ref[index, pl.ds(16 * row, 16), :] = parts[row]

    put(core_slots, place["c"], tuple(in_ref[pl.ds(16 * row, 16), :] for row in range(3)))
    cross = pltpu.make_async_remote_copy(
        src_ref=core_slots.at[place["c"]],
        dst_ref=core_slots.at[place["c"]],
        send_sem=core_sems.at[0],
        recv_sem=core_sems.at[1],
        device_id=device_of(moved(place, "c", 1)),
        device_id_type=pl.DeviceIdType.MESH,
    )
    cross.start()
    cross.wait()
    merged = merge_parts([parts_of(core_slots, number) for number in range(2)])
    for phase, dim in enumerate("xyz"):
        slots = ring_slots.at[phase]
        put(slots, place[dim], merged)
        copies = []
        for step in (1, 2, 3):
            copy = pltpu.make_async_remote_copy(
                src_ref=slots.at[place[dim]],
                dst_ref=slots.at[place[dim]],
                send_sem=ring_send.at[phase, step - 1],
                recv_sem=ring_recv.at[phase, step - 1],
                device_id=device_of(moved(place, dim, step)),
                device_id_type=pl.DeviceIdType.MESH,
            )
            copy.start()
            copies.append(copy)
        for copy in copies:
            copy.wait()
        merged = merge_parts([parts_of(slots, number) for number in range(4)])
    for row in range(3):
        out_ref[pl.ds(16 * row, 16), :] = merged[row]


def merge_stats(stats, collective_id):
    return pl.pallas_call(
        stats_kernel,
        out_shape=jax.ShapeDtypeStruct((48, 128), jnp.float32),
        in_specs=[pl.BlockSpec(memory_space=pltpu.VMEM)],
        out_specs=pl.BlockSpec(memory_space=pltpu.VMEM),
        scratch_shapes=[
            pltpu.VMEM((2, 48, 128), jnp.float32),
            pltpu.VMEM((3, 4, 48, 128), jnp.float32),
            pltpu.SemaphoreType.DMA((2,)),
            pltpu.SemaphoreType.DMA((3, 3)),
            pltpu.SemaphoreType.DMA((3, 3)),
        ],
        compiler_params=pltpu.CompilerParams(collective_id=collective_id, has_side_effects=True),
    )(stats)


MOMENTUM = 0.9
AVERAGE_KEEP = 0.9
RATE = 1500.0
CLIP = 0.05
LOW = jnp.bfloat16
SPAN_LOW = 256
HEAD_BLOCK = 512
TOKEN_BLOCK = 1024


def pick_kernel(levels, rows, table_ref, high_ref, low_ref, out_ref):
    low = low_ref[...]
    high = high_ref[...]
    count = low.shape[1]
    hot = (lax.broadcasted_iota(jnp.int32, (SPAN_LOW, count), 0) == low).astype(LOW)
    total = jnp.zeros((rows, count), jnp.float32)
    group = 5
    for first in range(0, levels, group):
        found = jnp.dot(
            table_ref[pl.ds(first * rows, group * rows), :], hot, preferred_element_type=jnp.float32
        )
        for level in range(group):
            total = total + jnp.where(
                high == first + level, found[level * rows : (level + 1) * rows], 0.0
            )
    value = total.astype(LOW)
    for piece in range(count // 128):
        out_ref[piece] = value[:, piece * 128 : (piece + 1) * 128]


def pick_columns(table_levels, high, low, rows):
    levels = table_levels.shape[0] // rows
    tokens = high.shape[1]
    return pl.pallas_call(
        functools.partial(pick_kernel, levels, rows),
        grid=(tokens // TOKEN_BLOCK,),
        out_shape=jax.ShapeDtypeStruct((tokens // 128, rows, 128), LOW),
        in_specs=[
            pl.BlockSpec(table_levels.shape, lambda step: (0, 0)),
            pl.BlockSpec((1, TOKEN_BLOCK), lambda step: (0, step)),
            pl.BlockSpec((1, TOKEN_BLOCK), lambda step: (0, step)),
        ],
        out_specs=pl.BlockSpec((TOKEN_BLOCK // 128, rows, 128), lambda step: (step, 0, 0)),
        compiler_params=pltpu.CompilerParams(vmem_limit_bytes=32 * 1024 * 1024),
    )(table_levels, high, low)


def spread_kernel(levels, rows, grad_ref, high_ref, low_ref, out_ref, spread_ref):
    step = pl.program_id(0)

    @pl.when(step == 0)
    def _():
        out_ref[...] = jnp.zeros_like(out_ref)

    low = low_ref[...]
    high = high_ref[...]
    count = low.shape[1]
    hot = (lax.broadcasted_iota(jnp.int32, (SPAN_LOW, count), 0) == low).astype(LOW)
    grad = jnp.concatenate([grad_ref[piece] for piece in range(count // 128)], 1).astype(jnp.float32)
    pair = 2
    for first in range(0, levels, pair):
        spread_ref[pl.ds(first * rows, pair * rows), :] = jnp.concatenate(
            [jnp.where(high == first + level, grad, 0.0) for level in range(pair)], 0
        ).astype(LOW)
    group = 10 * rows
    for first in range(0, levels * rows, group):
        out_ref[pl.ds(first, group), :] += lax.dot_general(
            spread_ref[pl.ds(first, group), :],
            hot,
            (((1,), (1,)), ((), ())),
            preferred_element_type=jnp.float32,
        )


def spread_columns(grads, high, low, levels):
    rows = grads.shape[1]
    tokens = high.shape[1]
    return pl.pallas_call(
        functools.partial(spread_kernel, levels, rows),
        grid=(tokens // TOKEN_BLOCK,),
        out_shape=jax.ShapeDtypeStruct((levels * rows, SPAN_LOW), jnp.float32),
        in_specs=[
            pl.BlockSpec((TOKEN_BLOCK // 128, rows, 128), lambda step: (step, 0, 0)),
            pl.BlockSpec((1, TOKEN_BLOCK), lambda step: (0, step)),
            pl.BlockSpec((1, TOKEN_BLOCK), lambda step: (0, step)),
        ],
        out_specs=pl.BlockSpec((levels * rows, SPAN_LOW), lambda step: (0, 0)),
        scratch_shapes=[pltpu.VMEM((levels * rows, TOKEN_BLOCK), LOW)],
        compiler_params=pltpu.CompilerParams(vmem_limit_bytes=32 * 1024 * 1024),
    )(grads, high, low)


HEADS = 12
NORM_EPSILON = 1e-05
ROOT_HALF = 0.5**0.5
PEAK = 0.3989422804014327
WIDTHS = (768, 192)
HEAD_SIZES = (64, 16)
SCALES = (0.125, 0.25)
QUERY_LANES = ((0, 768), (768, 192))
NEGATIVE = -1e30


def plain_product(left, right):
    return jnp.dot(left, right, preferred_element_type=jnp.float32)


def rows_product(left, right):
    return lax.dot_general(
        left, right, (((0,), (0,)), ((), ())), preferred_element_type=jnp.float32
    )


def cols_product(left, right):
    return lax.dot_general(
        left, right, (((1,), (1,)), ((), ())), preferred_element_type=jnp.float32
    )


def exact_product(left, right):
    return jnp.dot(
        left, right, precision=lax.Precision.HIGHEST, preferred_element_type=jnp.float32
    )


def total_rows(values):
    return jnp.sum(values.astype(jnp.float32), 0, keepdims=True)


def normalised(values):
    centred = values - jnp.mean(values, -1, keepdims=True)
    scale = lax.rsqrt(jnp.mean(centred * centred, -1, keepdims=True) + NORM_EPSILON)
    return centred * scale, scale


def norm_apply(values, gain, bias):
    return normalised(values)[0] * gain + bias


def norm_back(values, gain, grad):
    unit, scale = normalised(values)
    inner = grad * gain
    result = scale * (
        inner
        - jnp.mean(inner, -1, keepdims=True)
        - unit * jnp.mean(inner * unit, -1, keepdims=True)
    )
    return result, total_rows(grad * unit), total_rows(grad)


def gelu_value(values):
    return 0.5 * values * (1.0 + lax.erf(values * ROOT_HALF))


def gelu_slope(values):
    return 0.5 * (1.0 + lax.erf(values * ROOT_HALF)) + values * PEAK * jnp.exp(
        -0.5 * values * values
    )


def row_of(ref, row):
    return ref[row : row + 1, :]


def hidden_bias(ref):
    return jnp.concatenate([row_of(ref, row) for row in range(7, 11)], 1)


def head_of(rows, stream):
    lanes = lax.broadcasted_iota(jnp.int32, (rows, WIDTHS[stream]), 1)
    return lanes // HEAD_SIZES[stream]


def stack_heads(values, stream):
    heads = head_of(values.shape[0], stream)
    zero = jnp.zeros_like(values)
    return jnp.concatenate([jnp.where(heads == h, values, zero) for h in range(HEADS)], 0)


def fold_heads(values, stream):
    rows = values.shape[0] // HEADS
    heads = head_of(rows, stream)
    total = jnp.zeros((rows, values.shape[1]), jnp.float32)
    for h in range(HEADS):
        total = total + jnp.where(heads == h, values[h * rows : (h + 1) * rows], 0.0)
    return total


def lane_heads(stream):
    rows = lax.broadcasted_iota(jnp.int32, (128, WIDTHS[stream]), 0)
    return (rows == head_of(128, stream)).astype(jnp.float32)


def head_lanes(stream):
    rows = lax.broadcasted_iota(jnp.int32, (WIDTHS[stream], 128), 0) // HEAD_SIZES[stream]
    return (rows == lax.broadcasted_iota(jnp.int32, (WIDTHS[stream], 128), 1)).astype(jnp.float32)


def stack_columns(values):
    return jnp.concatenate([values[:, h : h + 1] for h in range(HEADS)], 0)


def one_micro_batch(rows):
    row = lax.broadcasted_iota(jnp.int32, (rows, 128), 0)
    key = lax.broadcasted_iota(jnp.int32, (rows, 128), 1)
    return (row // 8) % 2 == key // 64


def coupled_scores(stacks, key_refs):
    return sum(
        cols_product(stacks[n], key_refs[n][...]) * SCALES[n] for n in range(2)
    )


def open_kernel(
    found_ref, position_ref, index_ref, box_ref, proj_ref, qkv_ref, layout_ref,
    text_vec, layout_vec, slot_ref,
    text_sum_ref, layout_sum_ref, spatial_ref, key_text, value_text, key_layout, value_layout,
    query_ref, slot_text, slot_layout,
):
    found = found_ref[...].astype(jnp.float32).reshape(32, 4, 24, 128)
    embedded = (found[:, 0] + found[:, 1] + found[:, 2] + found[:, 3]).reshape(768, 128).T
    place = position_ref[...]
    place = jnp.concatenate([place, place], 0)
    text_sum = embedded + place[:, :768]
    text_sum_ref[...] = text_sum
    tables = (0, 1, 0, 1, 2, 3)
    number = lax.broadcasted_iota(jnp.int32, (128, 1024), 1)
    for k in range(6):
        hot = (number == index_ref[:, k : k + 1]).astype(LOW)
        rows = box_ref[pl.ds(1024 * tables[k], 1024), :]
        spatial_ref[:, pl.ds(128 * k, 128)] = plain_product(hot, rows).astype(LOW)
    layout_sum = place[:, 768:] + plain_product(spatial_ref[...], proj_ref[...])
    layout_sum_ref[...] = layout_sum
    query_ref[...] = jnp.zeros_like(query_ref)
    qkv = qkv_ref[...].reshape(2304, 768)
    weights = (qkv, layout_ref[pl.ds(0, 576), :])
    sums, vecs = (text_sum, layout_sum), (text_vec, layout_vec)
    keys, values, slots = (key_text, key_layout), (value_text, value_layout), (slot_text, slot_layout)
    for n in range(2):
        width, weight, vec = WIDTHS[n], weights[n], vecs[n]
        normed = norm_apply(sums[n], row_of(vec, 0), row_of(vec, 1))
        low = normed.astype(LOW)
        keys[n][...] = cols_product(low, weight[width : 2 * width]).astype(LOW)
        values[n][...] = (cols_product(low, weight[2 * width :]) + row_of(vec, 3)).astype(LOW)
        slot = exact_product(slot_ref[...], normed)
        slots[n][...] = slot
        start, size = QUERY_LANES[n]
        query_ref[:, pl.ds(start, size)] = (
            cols_product(slot.astype(LOW), weight[:width]) + row_of(vec, 2)
        ).astype(LOW)


def score_kernel(query_ref, key_text, value_text, key_layout, value_layout, out_ref):
    stacks = [
        stack_heads(query_ref[:, pl.ds(*QUERY_LANES[n])], n) for n in range(2)
    ]
    mask = one_micro_batch(64 * HEADS)
    scores = jnp.where(mask, coupled_scores(stacks, (key_text, key_layout)), NEGATIVE)
    top = jnp.max(scores, -1, keepdims=True)
    powers = jnp.where(mask, jnp.exp(scores - top), 0.0)
    total = jnp.sum(powers, -1, keepdims=True)
    low = powers.astype(LOW)
    out_ref[:, pl.ds(768, 256)] = jnp.zeros((64, 256), jnp.float32)
    for n, values in enumerate((value_text, value_layout)):
        out_ref[:, pl.ds(*QUERY_LANES[n])] = fold_heads(plain_product(low, values[...]), n)
    lane = lax.broadcasted_iota(jnp.int32, (64, 128), 1)
    tops = jnp.zeros((64, 128), jnp.float32)
    totals = jnp.ones((64, 128), jnp.float32)
    for h in range(HEADS):
        tops = jnp.where(lane == h, top[64 * h : 64 * h + 64], tops)
        totals = jnp.where(lane == h, total[64 * h : 64 * h + 64], totals)
    out_ref[:, pl.ds(1024, 128)] = tops
    out_ref[:, pl.ds(1152, 128)] = totals


def close_kernel(
    parts_ref, slot_text, slot_layout, out_w, up_w, down_w, layout_ref, layout_down,
    text_vec, layout_vec, head_ref, head_vec,
    att_text, att_layout, log_ref, mid_text, mid_layout, pre_text, pre_layout,
    end_text, end_layout, joined_ref, dense_ref, pick0, pick1, pick2,
):
    tops = [parts_ref[j, :, pl.ds(1024, 128)] for j in range(4)]
    top = jnp.maximum(jnp.maximum(tops[0], tops[1]), jnp.maximum(tops[2], tops[3]))
    shares = [jnp.exp(item - top) for item in tops]
    total = sum(shares[j] * parts_ref[j, :, pl.ds(1152, 128)] for j in range(4))
    log_ref[...] = top + jnp.log(total)
    shares = [item / total for item in shares]
    joined_ref[...] = jnp.zeros_like(joined_ref)
    streams = (
        (slot_text, text_vec, out_w, up_w, down_w, att_text, mid_text, pre_text, end_text),
        (slot_layout, layout_vec, layout_ref, layout_ref, layout_down, att_layout, mid_layout,
         pre_layout, end_layout),
    )
    for n, (slot, vec, out_r, up_r, down_r, att_r, mid_r, pre_r, end_r) in enumerate(streams):
        width = WIDTHS[n]
        spread = lane_heads(n)
        att = sum(
            parts_ref[j, :, pl.ds(*QUERY_LANES[n])] * exact_product(shares[j], spread)
            for j in range(4)
        )
        att_r[...] = att
        if n == 0:
            out_m, up_m = out_r[...].reshape(768, 768), up_r[...].reshape(3072, 768)
        else:
            out_m, up_m = out_r[pl.ds(576, 192), :], up_r[pl.ds(768, 768), :]
        mid = slot[...] + (cols_product(att.astype(LOW), out_m) + row_of(vec, 4))
        mid_r[...] = mid
        first = norm_apply(mid, row_of(vec, 5), row_of(vec, 6))
        pre = cols_product(first.astype(LOW), up_m) + hidden_bias(vec)
        pre_r[...] = pre
        end = first + (
            plain_product(gelu_value(pre).astype(LOW), down_r[...]) + row_of(vec, 11)
        )
        end_r[...] = end
        joined_ref[:, pl.ds(*QUERY_LANES[n])] = norm_apply(
            end, row_of(vec, 12), row_of(vec, 13)
        ).astype(LOW)
    dense = cols_product(joined_ref[:, pl.ds(0, 960)], head_ref[...]) + row_of(head_vec, 0)
    dense_ref[...] = dense
    picked = norm_apply(gelu_value(dense), row_of(head_vec, 1), row_of(head_vec, 2)).astype(LOW)
    for k, ref in enumerate((pick0, pick1, pick2)):
        ref[...] = picked[:, 256 * k : 256 * k + 256]


def close_back_kernel(
    grad0, grad1, grad2, dense_ref, joined_ref, att_text, att_layout, log_ref, mid_text, mid_layout,
    pre_text, pre_layout, end_text, end_layout, out_w, up_w, down_w, layout_ref, layout_down,
    text_vec, layout_vec, head_ref, head_vec,
    back_ref, d_mid_text, d_mid_layout, d_head, d_out, d_up, d_down, d_layout, d_layout_down,
    d_text_vec, d_layout_vec, d_head_vec,
):
    d_picked = jnp.concatenate([grad0[...], grad1[...], grad2[...]], 1)
    dense = dense_ref[...]
    d_active, d_gain, d_shift = norm_back(gelu_value(dense), row_of(head_vec, 1), d_picked)
    d_dense = (d_active * gelu_slope(dense)).astype(LOW)
    d_head_vec[0:1, :] = total_rows(d_dense)
    d_head_vec[1:2, :] = d_gain
    d_head_vec[2:3, :] = d_shift
    d_head[...] = rows_product(d_dense, joined_ref[:, pl.ds(0, 960)]).astype(LOW)
    d_joined = plain_product(d_dense, head_ref[...])
    back_ref[:, pl.ds(768, 256)] = jnp.zeros((16, 256), jnp.float32)
    delta = jnp.zeros((16, 128), jnp.float32)
    streams = (
        (text_vec, out_w, up_w, down_w, att_text, mid_text, pre_text, end_text,
         d_mid_text, d_out, d_up, d_down, d_text_vec),
        (layout_vec, layout_ref, layout_ref, layout_down, att_layout, mid_layout, pre_layout,
         end_layout, d_mid_layout, d_layout, d_layout, d_layout_down, d_layout_vec),
    )
    for n, (vec, out_r, up_r, down_r, att_r, mid_r, pre_r, end_r, d_mid_r, d_out_r, d_up_r,
            d_down_r, d_vec) in enumerate(streams):
        width = WIDTHS[n]
        if n == 0:
            out_m, up_m = out_r[...].reshape(768, 768), up_r[...].reshape(3072, 768)
        else:
            out_m, up_m = out_r[pl.ds(576, 192), :], up_r[pl.ds(768, 768), :]
        d_end, d_gain2, d_shift2 = norm_back(
            end_r[...], row_of(vec, 12), d_joined[:, QUERY_LANES[n][0] : sum(QUERY_LANES[n])]
        )
        d_branch2 = d_end.astype(LOW)
        mid, pre = mid_r[...], pre_r[...]
        low = gelu_value(pre).astype(LOW)
        d_pre = (cols_product(d_branch2, down_r[...]) * gelu_slope(pre)).astype(LOW)
        first_low = norm_apply(mid, row_of(vec, 5), row_of(vec, 6)).astype(LOW)
        for k in range(4):
            part = slice(width * k, width * (k + 1))
            d_down_r[pl.ds(width * k, width), :] = rows_product(low[:, part], d_branch2).astype(LOW)
            up_at = pl.ds(width * k, width) if n == 0 else pl.ds(192 + width * k, width)
            d_up_r[up_at, :] = rows_product(d_pre[:, part], first_low).astype(LOW)
            d_vec[7 + k : 8 + k, :] = total_rows(d_pre[:, part])
        d_first = d_end + plain_product(d_pre, up_m)
        d_mid, d_gain1, d_shift1 = norm_back(mid, row_of(vec, 5), d_first)
        d_mid_r[...] = d_mid
        d_branch1 = d_mid.astype(LOW)
        att = att_r[...]
        d_out_r[pl.ds(0, width), :] = rows_product(d_branch1, att.astype(LOW)).astype(LOW)
        d_att = plain_product(d_branch1, out_m).astype(LOW).astype(jnp.float32)
        back_ref[:, pl.ds(*QUERY_LANES[n])] = d_att
        delta = delta + exact_product(d_att * att, head_lanes(n))
        d_vec[0:4, :] = jnp.zeros((4, width), jnp.float32)
        for row, value in (
            (4, total_rows(d_branch1)),
            (5, d_gain1),
            (6, d_shift1),
            (11, total_rows(d_branch2)),
            (12, d_gain2),
            (13, d_shift2),
        ):
            d_vec[row : row + 1, :] = value
    back_ref[:, pl.ds(1024, 128)] = log_ref[...]
    back_ref[:, pl.ds(1152, 128)] = delta


def score_back_kernel(
    back_ref, query_ref, key_text, value_text, key_layout, value_layout,
    d_query, d_key_text, d_value_text, d_key_layout, d_value_layout,
):
    keys, values = (key_text, key_layout), (value_text, value_layout)
    stacks = [stack_heads(query_ref[:, pl.ds(*QUERY_LANES[n])], n) for n in range(2)]
    grads = [stack_heads(back_ref[:, pl.ds(*QUERY_LANES[n])], n).astype(LOW) for n in range(2)]
    logs = stack_columns(back_ref[:, pl.ds(1024, 128)])
    delta = stack_columns(back_ref[:, pl.ds(1152, 128)])
    mask = one_micro_batch(64 * HEADS)
    probs = jnp.where(mask, jnp.exp(jnp.where(mask, coupled_scores(stacks, keys) - logs, 0.0)), 0.0)
    d_probs = sum(cols_product(grads[n], values[n][...]) for n in range(2))
    d_scores = (probs * (d_probs - delta)).astype(LOW)
    low = probs.astype(LOW)
    d_query[:, pl.ds(768, 256)] = jnp.zeros((64, 256), jnp.float32)
    d_keys, d_values = (d_key_text, d_key_layout), (d_value_text, d_value_layout)
    for n in range(2):
        d_query[:, pl.ds(*QUERY_LANES[n])] = (
            fold_heads(plain_product(d_scores, keys[n][...]), n) * SCALES[n]
        )
        d_keys[n][...] = (rows_product(d_scores, stacks[n]) * SCALES[n]).astype(LOW)
        d_values[n][...] = rows_product(low, grads[n]).astype(LOW)


def open_back_kernel(
    parts_ref, d_key_text, d_value_text, d_key_layout, d_value_layout, d_mid_text, d_mid_layout,
    text_sum, layout_sum, slot_text, slot_layout, qkv_ref, layout_ref, proj_ref, spatial_ref,
    index_ref, text_vec, layout_vec, slot_turned,
    d_query_w, d_kv_w, d_layout, d_embedded, d_position, d_box, d_proj, d_text_vec, d_layout_vec,
):
    qkv = qkv_ref[...].reshape(2304, 768)
    streams = (
        (qkv, d_key_text, d_value_text, d_mid_text, text_sum, slot_text, text_vec, d_text_vec),
        (layout_ref[pl.ds(0, 576), :], d_key_layout, d_value_layout, d_mid_layout, layout_sum,
         slot_layout, layout_vec, d_layout_vec),
    )
    lows = []
    for n, (weight, d_key_r, d_value_r, d_mid_r, sum_r, slot_r, vec, d_vec) in enumerate(streams):
        width = WIDTHS[n]
        lanes = pl.ds(*QUERY_LANES[n])
        d_query = sum(parts_ref[j, :, lanes] for j in range(4)).astype(LOW)
        d_key, d_value = d_key_r[...], d_value_r[...]
        d_slot = d_mid_r[...] + plain_product(d_query, weight[:width])
        d_normed = (
            plain_product(d_key, weight[width : 2 * width])
            + plain_product(d_value, weight[2 * width :])
            + exact_product(slot_turned[...], d_slot)
        )
        sums = sum_r[...]
        low = norm_apply(sums, row_of(vec, 0), row_of(vec, 1)).astype(LOW)
        d_sum, d_gain, d_shift = norm_back(sums, row_of(vec, 0), d_normed)
        d_vec[...] = jnp.zeros_like(d_vec)
        for row, value in ((0, d_gain), (1, d_shift), (2, total_rows(d_query)), (3, total_rows(d_value))):
            d_vec[row : row + 1, :] = value
        slot_low = slot_r[...].astype(LOW)
        grads = (rows_product(d_query, slot_low), rows_product(d_key, low), rows_product(d_value, low))
        if n == 0:
            d_query_w[...] = grads[0].astype(LOW)
            d_kv_w[pl.ds(0, 768), :] = grads[1].astype(LOW)
            d_kv_w[pl.ds(768, 768), :] = grads[2].astype(LOW)
        else:
            for k in range(3):
                d_layout[pl.ds(192 * k, 192), :] = grads[k].astype(LOW)
        d_low = d_sum.astype(LOW)
        lows.append(d_low)
        wide = d_low.astype(jnp.float32)
        d_position[:, lanes] = wide[:64] + wide[64:]
        if n == 0:
            d_embedded[...] = wide.T.astype(LOW)
    d_spatial = cols_product(lows[1], proj_ref[...]).astype(LOW)
    d_proj[...] = rows_product(spatial_ref[...], lows[1]).astype(LOW)
    number = lax.broadcasted_iota(jnp.int32, (128, 1024), 1)
    for table, users in enumerate(((0, 2), (1, 3), (4,), (5,))):
        total = 0.0
        for k in users:
            hot = (number == index_ref[:, k : k + 1]).astype(LOW)
            total = total + rows_product(hot, d_spatial[:, 128 * k : 128 * k + 128])
        d_box[pl.ds(1024 * table, 1024), :] = total.astype(LOW)


def local_call(kernel, inputs, outputs, name):
    specs, arrays = [], []

    def spec(shape, index):
        return pl.BlockSpec(shape, lambda step: index, pipeline_mode=pl.Buffered(1))

    for item in inputs:
        array, shape, index = item if isinstance(item, tuple) else (item, item.shape, None)
        specs.append(spec(shape, index or (0,) * len(shape)))
        arrays.append(array)
    return pl.pallas_call(
        kernel,
        name=name,
        grid=(1,),
        out_shape=[jax.ShapeDtypeStruct(shape, dtype) for shape, dtype in outputs],
        in_specs=specs,
        out_specs=[spec(shape, (0,) * len(shape)) for shape, dtype in outputs],
        compiler_params=pltpu.CompilerParams(vmem_limit_bytes=56 * 1024 * 1024),
    )(*arrays)


def thirds(number):
    return [(number, (256 * k, 256), k) for k in range(3)]


GATHER_PIECES = thirds(0) + thirds(1) + [(2, None, 0), (3, None, 2), (4, None, 1), (5, None, 2)]
REDUCE_PIECES = (
    thirds(0)
    + thirds(1)
    + [(2, None, 0), (3, None, 2), (4, None, 1), (5, None, 1), (6, None, 2), (7, None, 2), (8, None, 0)]
)
WHOLE = ((0, 2), (0, 4))
REDUCE_SOURCES = [
    (0, (0, 1), (0, 1)),
    (0, (0, 1), (1, 2)),
    (0, (0, 1), (3, 1)),
    (0, (1, 1), (0, 4)),
] + [(number,) + WHOLE for number in range(1, 9)]
SLOT_SPLITS = [[(0, (0, 16))], [(1, (0, 16))], [(2, (0, 16))]]


def fetch(masters):
    word, position, box, text, down, layout, layout_down, head, vector = [
        m.astype(LOW) for m in masters
    ]
    misc = jnp.concatenate(
        [
            layout.T,
            layout_down[0],
            layout_down[1],
            jnp.pad(vector, (0, 192 - vector.shape[0]))[None],
        ],
        0,
    )
    text, down, head, position, misc, box = gather_all(
        [text.T, down, head.T, position, misc, box.reshape(32, 128)], GATHER_PIECES, 2
    )
    return dict(
        text=text,
        down=down.reshape(3072, 768),
        head=head.reshape(768, 960),
        box=box.reshape(128, 4, 8, 128).transpose(1, 0, 2, 3).reshape(4096, 128),
        layout=misc[:, :12].reshape(1536, 192),
        layout_down=misc[:, 12:18].reshape(768, 192),
        box_proj=misc[:, 18:24].reshape(768, 192),
        position=position.reshape(640, 960),
        vector=misc[:, 24, :123].reshape(15744),
    )


def reduce_weights(grads):
    shards = reduce_all(
        [
            grads["query"].reshape(16, 48, 768),
            grads["key_value"].reshape(32, 48, 768),
            grads["out"].reshape(16, 48, 768),
            grads["up"].reshape(64, 48, 768),
            grads["down"].reshape(128, 24, 768),
            grads["head"].reshape(128, 6, 960),
            grads["position"].reshape(128, 5, 960),
            grads["layout"].reshape(128, 12, 192),
            grads["layout_down"].reshape(128, 6, 192),
            grads["box_proj"].reshape(128, 6, 192),
            grads["box"].reshape(4, 128, 8, 128).transpose(1, 0, 2, 3).reshape(128, 32, 128),
            grads["vector"].reshape(128, 1, 123),
        ],
        REDUCE_SOURCES,
        REDUCE_PIECES,
        6,
    )
    text, down, head, position, layout, layout_down, box_proj, box, vector, square = shards
    return square, [
        position,
        box.reshape(4, 8, 128),
        text.T,
        down,
        layout.T,
        jnp.stack([layout_down, box_proj]),
        head.T,
        vector[0],
    ]


def on_device(
    token_ids,
    box_coords,
    intersection_flags,
    masked_rows,
    masked_labels,
    *weights,
):
    triples = [tuple(weights[3 * n : 3 * n + 3]) for n in range(9)]
    masters = [entry[0] for entry in triples]
    word_table = masters[0]
    dp = lax.axis_index("dp")
    vocab = lax.axis_index("vocab")
    shard_width = word_table.shape[1]
    table_rows = word_table.shape[0]
    levels = -(-shard_width // SPAN_LOW)

    row_hot = masked_rows[:, :, None] == jnp.arange(64)[None, None, :]
    counted = jnp.sum(jnp.where(row_hot & (intersection_flags == 0)[:, None, :], 1, 0), 2)
    slot_hot = jnp.concatenate(
        [
            jnp.pad(row_hot[0], ((0, 0), (0, 64))),
            jnp.pad(row_hot[1], ((0, 0), (64, 0))),
        ],
        0,
    )
    slot_hot_wide = slot_hot.astype(jnp.float32)
    f32 = jnp.float32

    notes = jnp.concatenate(
        [
            token_ids.reshape(1, 128),
            jnp.concatenate(
                [masked_labels.reshape(1, 16), counted.reshape(1, 16), jnp.zeros((1, 96), jnp.int32)], 1
            ),
        ],
        0,
    )
    notes_all = lax.all_to_all(
        jnp.broadcast_to(notes[None], (128,) + notes.shape), AXES, 0, 0, tiled=True
    )
    ids_all = notes_all[:, 0, :].reshape(1, 16384)
    labels_all = notes_all[:, 1, :16].reshape(2048)
    counted_all = notes_all[:, 1, 16:32].reshape(2048).astype(jnp.float32)
    total_count = jnp.sum(counted_all)

    local_ids = ids_all - vocab * shard_width
    ids_high = local_ids >> 8
    ids_low = local_ids & 255
    table_low = word_table.astype(LOW)
    table_levels = (
        jnp.pad(table_low, ((0, 0), (0, levels * SPAN_LOW - shard_width)))
        .reshape(table_rows, levels, SPAN_LOW)
        .transpose(1, 0, 2)
        .reshape(levels * table_rows, SPAN_LOW)
    )
    found = pick_columns(table_levels, ids_high, ids_low, table_rows)
    found, masters = lax.optimization_barrier((found, masters))
    found = lax.all_to_all(found, AXES, 0, 0, tiled=True)

    table_blocks = (
        jnp.pad(table_low, ((0, 0), (0, 32 * HEAD_BLOCK - shard_width)))
        .reshape(table_rows, 32, HEAD_BLOCK)
        .transpose(1, 0, 2)
    )
    table_head = lax.all_to_all(table_blocks, "dp", 0, 0, tiled=True).reshape(768, HEAD_BLOCK)

    full = fetch(masters)
    vector = full["vector"].astype(jnp.float32)
    text_vec = vector[:10752].reshape(14, 768)
    layout_vec = vector[10752:13440].reshape(14, 192)
    head_vec = vector[13440:].reshape(3, 768)
    position_own = lax.dynamic_slice_in_dim(full["position"], vocab * 64, 64, 0).astype(f32)
    boxes = box_coords.reshape(4, 128)
    box_index = jnp.stack(
        [
            boxes[0],
            boxes[1],
            boxes[2],
            boxes[3],
            jnp.abs(boxes[3] - boxes[1]),
            jnp.abs(boxes[2] - boxes[0]),
            boxes[0],
            boxes[0],
        ],
        1,
    )
    qkv = (full["text"], (48, 48, 768), (0, 0, 0))
    out_w = (full["text"], (16, 48, 768), (3, 0, 0))
    up_w = (full["text"], (64, 48, 768), (1, 0, 0))
    text_sum, layout_sum, spatial, *kv, query, slot_text, slot_layout = local_call(
        open_kernel,
        [
            found,
            position_own,
            box_index,
            full["box"],
            full["box_proj"],
            qkv,
            full["layout"],
            text_vec,
            layout_vec,
            slot_hot_wide,
        ],
        [
            ((128, 768), f32),
            ((128, 192), f32),
            ((128, 768), LOW),
            ((128, 768), LOW),
            ((128, 768), LOW),
            ((128, 192), LOW),
            ((128, 192), LOW),
            ((16, 1024), LOW),
            ((16, 768), f32),
            ((16, 192), f32),
        ],
        "open_streams",
    )
    query_all = lax.all_gather(query, "vocab", axis=0, tiled=True)
    (partial,) = local_call(score_kernel, [query_all, *kv], [((64, 1280), f32)], "partial_attention")
    partial = lax.all_to_all(partial.reshape(4, 16, 1280), "vocab", 0, 0, tiled=True)
    weights_close = [out_w, up_w, full["down"], full["layout"], full["layout_down"]]
    vectors_close = [text_vec, layout_vec, full["head"], head_vec]
    (att_text, att_layout, log_total, mid_text, mid_layout, pre_text, pre_layout, end_text,
     end_layout, joined, dense, *picked) = local_call(
        close_kernel,
        [partial, slot_text, slot_layout] + weights_close + vectors_close,
        [
            ((16, 768), f32),
            ((16, 192), f32),
            ((16, 128), f32),
            ((16, 768), f32),
            ((16, 192), f32),
            ((16, 3072), f32),
            ((16, 768), f32),
            ((16, 768), f32),
            ((16, 192), f32),
            ((16, 1024), LOW),
            ((16, 768), f32),
            ((16, 256), LOW),
            ((16, 256), LOW),
            ((16, 256), LOW),
        ],
        "close_streams",
    )
    picked_all = gather_slots(picked, SLOT_SPLITS, 3)
    picked_all = jnp.concatenate([p.reshape(2048, 256) for p in picked_all], 1)
    column = lax.broadcasted_iota(jnp.int32, (1, HEAD_BLOCK), 1)
    valid = column < shard_width - dp * HEAD_BLOCK
    logits = jnp.where(valid, plain_product(picked_all, table_head), -1e30)
    row_max = jnp.max(logits, 1)
    row_sum = jnp.sum(jnp.where(valid, jnp.exp(logits - row_max[:, None]), 0.0), 1)
    label_hot = valid & (
        (labels_all - vocab * shard_width - dp * HEAD_BLOCK)[:, None] == column
    )
    target = jnp.sum(jnp.where(label_hot, logits, 0.0), 1)
    stats = jnp.concatenate(
        [row_max.reshape(16, 128), row_sum.reshape(16, 128), target.reshape(16, 128)], 0
    )
    stats = merge_stats(stats, 4)
    row_log = (stats[:16] + jnp.log(stats[16:32])).reshape(2048)
    loss_total = jnp.sum(counted_all * (row_log - stats[32:].reshape(2048)))
    d_logits = (
        (counted_all / total_count)[:, None]
        * (
            jnp.where(valid, jnp.exp(logits - row_log[:, None]), 0.0)
            - label_hot.astype(jnp.float32)
        )
    ).astype(LOW)
    d_picked_part = cols_product(d_logits, table_head).astype(LOW)
    d_picked = reduce_slots(
        [d_picked_part[:, 256 * k : 256 * (k + 1)].reshape(128, 16, 256) for k in range(3)],
        SLOT_SPLITS,
        5,
    )
    table_head_grad = rows_product(picked_all, d_logits).astype(LOW).reshape(32, 24, HEAD_BLOCK)
    table_head_grad = lax.all_to_all(table_head_grad, "dp", 0, 0, tiled=True)

    (back, d_mid_text, d_mid_layout, d_head, d_out, d_up, d_down, d_layout_close, d_layout_down,
     d_text_vec, d_layout_vec, d_head_vec) = local_call(
        close_back_kernel,
        list(d_picked)
        + [dense, joined, att_text, att_layout, log_total, mid_text, mid_layout, pre_text]
        + [pre_layout, end_text, end_layout]
        + weights_close
        + vectors_close,
        [
            ((16, 1280), f32),
            ((16, 768), f32),
            ((16, 192), f32),
            ((768, 960), LOW),
            ((768, 768), LOW),
            ((3072, 768), LOW),
            ((3072, 768), LOW),
            ((960, 192), LOW),
            ((768, 192), LOW),
            ((14, 768), f32),
            ((14, 192), f32),
            ((3, 768), f32),
        ],
        "close_streams_back",
    )
    back = lax.all_gather(back, "vocab", axis=0, tiled=True)
    d_query, *d_kv = local_call(
        score_back_kernel,
        [back, query_all, *kv],
        [
            ((64, 1024), f32),
            ((128, 768), LOW),
            ((128, 768), LOW),
            ((128, 192), LOW),
            ((128, 192), LOW),
        ],
        "attention_back",
    )
    d_query = lax.all_to_all(d_query.reshape(4, 16, 1024), "vocab", 0, 0, tiled=True)
    (d_query_w, d_kv_w, d_layout_open, d_embedded, d_position, d_box, d_proj, d_text_open,
     d_layout_vec_open) = local_call(
        open_back_kernel,
        [d_query, *d_kv, d_mid_text, d_mid_layout, text_sum, layout_sum, slot_text, slot_layout]
        + [qkv, full["layout"], full["box_proj"], spatial, box_index, text_vec, layout_vec]
        + [slot_hot_wide.T],
        [
            ((768, 768), LOW),
            ((1536, 768), LOW),
            ((576, 192), LOW),
            ((768, 128), LOW),
            ((64, 960), f32),
            ((4096, 128), LOW),
            ((768, 192), LOW),
            ((14, 768), f32),
            ((14, 192), f32),
        ],
        "open_streams_back",
    )
    d_text_blocks = jnp.broadcast_to(
        d_embedded.reshape(32, 1, 24, 128), (32, 4, 24, 128)
    ).reshape(128, 24, 128)
    d_text_all = lax.all_to_all(d_text_blocks, AXES, 0, 0, tiled=True)
    table_grad = (
        spread_columns(d_text_all, ids_high, ids_low, levels)
        .reshape(levels, table_rows, SPAN_LOW)
        .transpose(1, 0, 2)
        .reshape(table_rows, levels * SPAN_LOW)[:, :shard_width]
    )
    table_grad = table_grad + table_head_grad.transpose(1, 0, 2).reshape(
        table_rows, 32 * HEAD_BLOCK
    )[:, :shard_width].astype(jnp.float32)

    d_positions = lax.dynamic_update_slice_in_dim(
        jnp.zeros((640, 960), LOW), d_position.astype(LOW), vocab * 64, 0
    )
    square, shards = reduce_weights(
        dict(
            query=d_query_w,
            key_value=d_kv_w,
            out=d_out,
            up=d_up,
            down=d_down,
            head=d_head,
            box=d_box,
            layout=jnp.concatenate([d_layout_open, d_layout_close], 0),
            layout_down=d_layout_down,
            box_proj=d_proj,
            position=d_positions,
            vector=jnp.concatenate(
                [
                    (d_text_vec + d_text_open).reshape(10752),
                    (d_layout_vec + d_layout_vec_open).reshape(2688),
                    d_head_vec.reshape(2304),
                ]
            ).astype(LOW),
        )
    )
    all_grads = [table_grad] + shards
    norm_stats = jnp.concatenate(
        [
            jnp.zeros((16, 128), f32),
            square + jnp.sum(table_grad * table_grad),
            jnp.zeros((16, 128), f32),
        ],
        0,
    )
    grad_norm = jnp.sqrt(merge_stats(norm_stats, 7)[16, 0])
    factor = jnp.minimum(1.0, CLIP / grad_norm)
    results = []
    for (master, momentum, average), grad in zip(triples, all_grads):
        clipped = factor * grad
        momentum_next = MOMENTUM * momentum + clipped
        master_next = master - RATE * (clipped + MOMENTUM * momentum_next)
        average_next = AVERAGE_KEEP * average + (1.0 - AVERAGE_KEEP) * master_next
        results += [master_next, momentum_next, average_next]
    return tuple(results + [loss_total, total_count, grad_norm])


TOKEN_SPEC = P(None, AXES)
WEIGHT_SPECS = (
    P("dp", "vocab"),
    P(AXES, None),
    P(None, AXES, None),
    P(None, AXES),
    P(AXES, None),
    P(None, AXES),
    P(None, AXES, None),
    P(None, AXES),
    P(AXES),
)


def solution(mesh):
    weight_specs = tuple(spec for spec in WEIGHT_SPECS for _ in range(3))
    in_specs = (TOKEN_SPEC, P(None, None, AXES), TOKEN_SPEC, TOKEN_SPEC, TOKEN_SPEC) + weight_specs
    out_specs = weight_specs + (P(), P(), P())
    return jax.shard_map(
        on_device, mesh=mesh, in_specs=in_specs, out_specs=out_specs, check_vma=False
    )
```

```python
import functools

import jax
import jax.numpy as jnp
from jax import lax
from jax.experimental import pallas as pl
from jax.experimental.pallas import tpu as pltpu
from jax.sharding import PartitionSpec as P

AXES = ("dp", "vocab")
MESH = pl.DeviceIdType.MESH
LONG = pl.CostEstimate(flops=60_000_000_000, bytes_accessed=200_000_000, transcendentals=0)
ORDERS = (("z", "y", "x"), ("y", "x", "z"), ("x", "z", "y"))


def my_place():
    dp = lax.axis_index("dp")
    vocab = lax.axis_index("vocab")
    return {
        "x": (dp // 16) * 2 + vocab // 2,
        "y": (dp // 4) % 4,
        "z": dp % 4,
        "c": vocab % 2,
    }


def moved(place, dim, step):
    other = dict(place)
    other[dim] = (1 - place["c"]) if dim == "c" else (place[dim] + step + 4) % 4
    return other


def device_of(place):
    return (
        (place["x"] // 2) * 16 + place["y"] * 4 + place["z"],
        (place["x"] % 2) * 2 + place["c"],
    )


def greet(place, steps=(1, 3)):
    barrier = pltpu.get_barrier_semaphore()
    peers = [moved(place, dim, step) for dim in "xyz" for step in steps]
    peers.append(moved(place, "c", 1))
    for peer in peers:
        pl.semaphore_signal(barrier, inc=1, device_id=device_of(peer), device_id_type=MESH)
    pl.semaphore_wait(barrier, len(peers))


def remote(src, dst, send, recv, place):
    return pltpu.make_async_remote_copy(
        src_ref=src,
        dst_ref=dst,
        send_sem=send,
        recv_sem=recv,
        device_id=device_of(place),
        device_id_type=MESH,
    )


def lanes_at(ref, lanes):
    return slice(None) if lanes is None else pl.ds(*lanes)


def block_view(ref, place, dims, lanes, core=None):
    high, low = (pl.ds(0, 2), pl.ds(0, 2)) if "x" in dims else (place["x"] // 2, place["x"] % 2)
    mid = pl.ds(0, 4) if "y" in dims else place["y"]
    deep = pl.ds(0, 4) if "z" in dims else place["z"]
    where = (high, mid, deep, low)
    if core is not None:
        where += (core,)
    return ref.at[where + (slice(None), lanes_at(ref, lanes))]


def halves(lanes, number):
    if lanes is None or lanes[1] < 256:
        return (lanes, False) if number % 2 == 0 else (False, lanes)
    half = lanes[1] // 256 * 128
    return (lanes[0], half), (lanes[0] + half, lanes[1] - half)


def gather_kernel(pieces, count, *refs):
    ins, outs = refs[:count], refs[count : 2 * count]
    own_sem, core_sems, ring_send, ring_recv, pass_send, pass_recv = refs[2 * count :]
    place = my_place()
    sibling = moved(place, "c", 1)
    greet(place)

    def spot(number, origin, dims, lanes):
        return block_view(outs[number], origin, dims, lanes, place["c"])

    copies, crosses = [], []
    for number in range(count):
        here = block_view(outs[number], place, "", None, place["c"])
        copy = pltpu.make_async_copy(ins[number], here, own_sem.at[number])
        copy.start()
        copies.append(copy)
        cross = remote(ins[number], here, core_sems.at[0, number], core_sems.at[1, number], sibling)
        cross.start()
        crosses.append(cross)
    rings, passes = {}, []

    def send(phase, piece, way, src, dst, target):
        copy = remote(
            src, dst, ring_send.at[phase, way, piece], ring_recv.at[phase, way, piece], target
        )
        copy.start()
        rings[(phase, way, piece)] = copy

    def hand_over(phase, piece, way, where):
        copy = remote(
            where, where, pass_send.at[phase, way, piece], pass_recv.at[phase, way, piece], sibling
        )
        copy.start()
        passes.append(copy)

    def begin(phase, piece):
        number, lanes, order = pieces[piece]
        dim, dims = ORDERS[order][phase], ORDERS[order][:phase]
        where = spot(number, place, dims, lanes)
        src = ins[number].at[:, lanes_at(ins[number], lanes)] if phase == 0 else where
        for way, step in ((0, 1), (1, -1)):
            send(phase, piece, way, src, where, moved(place, dim, step))

    for piece in range(len(pieces)):
        begin(0, piece)
    for copy in copies:
        copy.wait()
    for phase in range(3):
        for piece, (number, lanes, order) in enumerate(pieces):
            dim, dims = ORDERS[order][phase], ORDERS[order][:phase]
            parts = halves(lanes, piece)
            for way, step in ((0, 1), (1, -1)):
                rings[(phase, way, piece)].wait_recv()
                origin = moved(place, dim, -step)
                if parts[way] is not False:
                    onward = spot(number, origin, dims, parts[way])
                    send(phase, piece, 2 + way, onward, onward, moved(place, dim, step))
                hand_over(phase, piece, way, spot(number, origin, dims, lanes))
        for piece, (number, lanes, order) in enumerate(pieces):
            dim, dims = ORDERS[order][phase], ORDERS[order][:phase]
            parts = halves(lanes, piece)
            for way in range(2):
                if parts[way] is not False:
                    rings[(phase, 2 + way, piece)].wait_recv()
            if phase < 2:
                begin(phase + 1, piece)
            hand_over(phase, piece, 2, spot(number, moved(place, dim, 2), dims, lanes))
    for copy in rings.values():
        copy.wait_send()
    for copy in crosses + passes:
        copy.wait()


def gather_all(arrays, pieces, collective_id):
    count, total = len(arrays), len(pieces)
    outs = pl.pallas_call(
        functools.partial(gather_kernel, pieces, count),
        out_shape=[jax.ShapeDtypeStruct((2, 4, 4, 2, 2) + a.shape, a.dtype) for a in arrays],
        in_specs=[pl.BlockSpec(memory_space=pl.ANY)] * count,
        out_specs=[pl.BlockSpec(memory_space=pl.ANY)] * count,
        scratch_shapes=[
            pltpu.SemaphoreType.DMA((count,)),
            pltpu.SemaphoreType.DMA((2, count)),
            pltpu.SemaphoreType.DMA((3, 4, total)),
            pltpu.SemaphoreType.DMA((3, 4, total)),
            pltpu.SemaphoreType.DMA((3, 3, total)),
            pltpu.SemaphoreType.DMA((3, 3, total)),
        ],
        cost_estimate=LONG,
        compiler_params=pltpu.CompilerParams(collective_id=collective_id, has_side_effects=True),
    )(*arrays)
    return [o.reshape((128,) + a.shape) for o, a in zip(outs, arrays)]


def open_shape(dims):
    shape = ()
    if "x" in dims:
        shape += (2,)
    if "y" in dims:
        shape += (4,)
    if "z" in dims:
        shape += (4,)
    if "x" in dims:
        shape += (2,)
    return shape


def chunks_of(dims, place):
    high, mid, deep, low = place["x"] // 2, place["y"], place["z"], place["x"] % 2
    every = slice(None)
    if dims == "":
        return 1, lambda flat: ((high, mid, deep, low), ())
    inner = (every if "y" in dims else mid, every if "z" in dims else deep)
    if "x" in dims and "y" in dims and "z" in dims:
        return 8, lambda flat: ((flat // 4, flat % 4, every, every), (flat // 4, flat % 4))
    if "x" in dims:
        return 2, lambda flat: ((flat,) + inner + (every,), (flat,))
    if "y" in dims and "z" in dims:
        return 4, lambda flat: ((high, flat, every, low), (flat,))
    return 1, lambda flat: ((high,) + inner + (low,), ())


def reduce_kernel(sources, pieces, count, *refs):
    total = len(pieces)
    ins = refs[: len(sources)]
    refs = refs[len(sources) :]
    outs, square_ref, refs = refs[:count], refs[count], refs[count + 1 :]
    accs, crosses, refs = refs[:count], refs[count : 2 * count], refs[2 * count :]
    slots = refs[: 12 * total]
    own_sem, core_sems, ring_send, ring_recv = refs[12 * total :]
    place = my_place()
    sibling = moved(place, "c", 1)
    greet(place)

    def slot(phase, way, piece):
        return slots[(phase * 4 + way) * total + piece]

    def add(number, lanes, at, dims, others):
        acc = accs[number]

        count, chunk = chunks_of(dims, at)

        def body(flat, carry):
            block, inner = chunk(flat)
            where = block + (slice(None), lanes_at(acc, lanes))
            parts = [
                other[inner] if index is None else other[block + index] for other, index in others
            ]
            if len(parts) == 1:
                acc[where] = acc[where] + parts[0]
            else:
                wide = [part.astype(jnp.float32) for part in [acc[where]] + parts]
                acc[where] = sum(wide).astype(acc.dtype)
            return carry

        if count == 1:
            body(0, 0)
        else:
            lax.fori_loop(0, count, body, 0)

    started = []
    first = {}
    for piece, (number, lanes, order) in enumerate(pieces):
        for index, (owner, high, mids) in enumerate(sources):
            if owner != number:
                continue
            copies = []
            for core, target in ((sibling["c"], "cross"), (place["c"], "own")):
                where = (slice(None), slice(None), slice(None), slice(None), core)
                src = ins[index].at[where + (slice(None), lanes_at(ins[index], lanes))]
                at = (
                    pl.ds(*high),
                    pl.ds(*mids),
                    slice(None),
                    slice(None),
                    slice(None),
                    lanes_at(accs[number], lanes),
                )
                if target == "cross":
                    copy = remote(
                        src,
                        crosses[number].at[at],
                        core_sems.at[0, piece, index],
                        core_sems.at[1, piece, index],
                        sibling,
                    )
                else:
                    copy = pltpu.make_async_copy(src, accs[number].at[at], own_sem.at[piece, index])
                copy.start()
                copies.append(copy)
            started.append(copies[0])
            first.setdefault(piece, []).append(copies)
    rings = {}

    def send(phase, way, piece, src, step):
        number, lanes, order = pieces[piece]
        copy = remote(
            src,
            slot(phase, way, piece),
            ring_send.at[phase, way, piece],
            ring_recv.at[phase, way, piece],
            moved(place, ORDERS[order][phase], step),
        )
        copy.start()
        rings[(phase, way, piece)] = copy
        started.append(copy)

    def begin(phase, piece):
        number, lanes, order = pieces[piece]
        dim, rest = ORDERS[order][phase], ORDERS[order][phase + 1 :]
        parts = halves(lanes, piece)
        for way, step in ((0, 1), (1, -1)):
            if parts[way] is not False:
                there = moved(place, dim, 2)
                send(phase, way, piece, block_view(accs[number], there, rest, parts[way]), step)

    for piece, (number, lanes, order) in enumerate(pieces):
        for cross, own in first[piece]:
            own.wait()
            cross.wait_recv()
        add(number, lanes, place, "xyz", [(crosses[number], (slice(None), lanes_at(accs[number], lanes)))])
        begin(0, piece)
    for phase in range(3):
        for piece, (number, lanes, order) in enumerate(pieces):
            dim, rest = ORDERS[order][phase], ORDERS[order][phase + 1 :]
            parts = halves(lanes, piece)
            for way, step in ((0, 1), (1, -1)):
                there = moved(place, dim, step)
                if parts[way] is not False:
                    rings[(phase, way, piece)].wait_recv()
                    add(number, parts[way], there, rest, [(slot(phase, way, piece), None)])
                send(phase, 2 + way, piece, block_view(accs[number], there, rest, lanes), step)
        for piece, (number, lanes, order) in enumerate(pieces):
            rest = ORDERS[order][phase + 1 :]
            for way in range(2):
                rings[(phase, 2 + way, piece)].wait_recv()
            others = [slot(phase, 2 + way, piece) for way in range(2)]
            if phase < 2:
                add(number, lanes, place, rest, [(other, None) for other in others])
                begin(phase + 1, piece)
            else:
                block = (place["x"] // 2, place["y"], place["z"], place["x"] % 2)
                where = (slice(None), lanes_at(accs[number], lanes))
                value = accs[number][block + where].astype(jnp.float32)
                for other in others:
                    value = value + other[...].astype(jnp.float32)
                outs[number][where] = value
    total_square = jnp.zeros((1, 1), jnp.float32)
    for number in range(count):
        value = outs[number][...]
        total_square = total_square + jnp.sum(
            jnp.sum(value * value, 1, keepdims=True), 0, keepdims=True
        )
    square_ref[...] = jnp.broadcast_to(total_square, square_ref.shape)
    for copy in started:
        copy.wait_send()


def reduce_all(arrays, sources, pieces, collective_id):
    shapes = {}
    views = []
    for array, (owner, high, mids) in zip(arrays, sources):
        shapes[owner] = array.shape[1:]
        views.append(array.reshape((high[1], mids[1], 4, 2, 2) + array.shape[1:]))
    count, total = len(shapes), len(pieces)
    dtype = arrays[0].dtype
    scratch = [pltpu.VMEM((2, 4, 4, 2) + shapes[n], dtype) for n in range(count)] * 2
    for phase in range(3):
        for way in range(4):
            for piece, (number, lanes, order) in enumerate(pieces):
                rest = ORDERS[order][phase + 1 :]
                rows, width = shapes[number]
                part = halves(lanes, piece)[way] if way < 2 else lanes
                if part is False:
                    scratch.append(pltpu.VMEM((8, 128), dtype))
                else:
                    wide = width if part is None else part[1]
                    scratch.append(pltpu.VMEM(open_shape(rest) + (rows, wide), dtype))
    scratch += [
        pltpu.SemaphoreType.DMA((total, len(arrays))),
        pltpu.SemaphoreType.DMA((2, total, len(arrays))),
        pltpu.SemaphoreType.DMA((3, 4, total)),
        pltpu.SemaphoreType.DMA((3, 4, total)),
    ]
    return pl.pallas_call(
        functools.partial(reduce_kernel, sources, pieces, count),
        out_shape=[
            jax.ShapeDtypeStruct(shape, jnp.float32)
            for shape in [shapes[n] for n in range(count)] + [(16, 128)]
        ],
        in_specs=[pl.BlockSpec(memory_space=pl.ANY)] * len(arrays),
        out_specs=[pl.BlockSpec(memory_space=pltpu.VMEM)] * (count + 1),
        scratch_shapes=scratch,
        cost_estimate=LONG,
        compiler_params=pltpu.CompilerParams(
            collective_id=collective_id, has_side_effects=True, vmem_limit_bytes=56 * 1024 * 1024
        ),
    )(*views)


def merge_parts(parts):
    top = parts[0][0]
    for part in parts[1:]:
        top = jnp.maximum(top, part[0])
    total = 0.0
    target = 0.0
    for part in parts:
        total = total + part[1] * jnp.exp(part[0] - top)
        target = target + part[2]
    return top, total, target


def stats_kernel(in_ref, out_ref, core_slots, ring_slots, core_sems, ring_send, ring_recv):
    place = my_place()
    greet(place, (1, 2, 3))

    def parts_of(ref, index):
        return tuple(ref[index, pl.ds(16 * row, 16), :] for row in range(3))

    def put(ref, index, parts):
        for row in range(3):
            ref[index, pl.ds(16 * row, 16), :] = parts[row]

    put(core_slots, place["c"], tuple(in_ref[pl.ds(16 * row, 16), :] for row in range(3)))
    cross = pltpu.make_async_remote_copy(
        src_ref=core_slots.at[place["c"]],
        dst_ref=core_slots.at[place["c"]],
        send_sem=core_sems.at[0],
        recv_sem=core_sems.at[1],
        device_id=device_of(moved(place, "c", 1)),
        device_id_type=pl.DeviceIdType.MESH,
    )
    cross.start()
    cross.wait()
    merged = merge_parts([parts_of(core_slots, number) for number in range(2)])
    for phase, dim in enumerate("xyz"):
        slots = ring_slots.at[phase]
        put(slots, place[dim], merged)
        copies = []
        for step in (1, 2, 3):
            copy = pltpu.make_async_remote_copy(
                src_ref=slots.at[place[dim]],
                dst_ref=slots.at[place[dim]],
                send_sem=ring_send.at[phase, step - 1],
                recv_sem=ring_recv.at[phase, step - 1],
                device_id=device_of(moved(place, dim, step)),
                device_id_type=pl.DeviceIdType.MESH,
            )
            copy.start()
            copies.append(copy)
        for copy in copies:
            copy.wait()
        merged = merge_parts([parts_of(slots, number) for number in range(4)])
    for row in range(3):
        out_ref[pl.ds(16 * row, 16), :] = merged[row]


def merge_stats(stats, collective_id):
    return pl.pallas_call(
        stats_kernel,
        out_shape=jax.ShapeDtypeStruct((48, 128), jnp.float32),
        in_specs=[pl.BlockSpec(memory_space=pltpu.VMEM)],
        out_specs=pl.BlockSpec(memory_space=pltpu.VMEM),
        scratch_shapes=[
            pltpu.VMEM((2, 48, 128), jnp.float32),
            pltpu.VMEM((3, 4, 48, 128), jnp.float32),
            pltpu.SemaphoreType.DMA((2,)),
            pltpu.SemaphoreType.DMA((3, 3)),
            pltpu.SemaphoreType.DMA((3, 3)),
        ],
        compiler_params=pltpu.CompilerParams(collective_id=collective_id, has_side_effects=True),
    )(stats)


MOMENTUM = 0.9
AVERAGE_KEEP = 0.9
RATE = 1500.0
CLIP = 0.05
LOW = jnp.bfloat16
SPAN_LOW = 256
TOKEN_BLOCK = 1024


def pick_kernel(levels, rows, table_ref, high_ref, low_ref, out_ref):
    low = low_ref[...]
    high = high_ref[...]
    count = low.shape[1]
    hot = (lax.broadcasted_iota(jnp.int32, (SPAN_LOW, count), 0) == low).astype(LOW)
    total = jnp.zeros((rows, count), jnp.float32)
    group = 5
    for first in range(0, levels, group):
        found = jnp.dot(
            table_ref[pl.ds(first * rows, group * rows), :], hot, preferred_element_type=jnp.float32
        )
        for level in range(group):
            total = total + jnp.where(
                high == first + level, found[level * rows : (level + 1) * rows], 0.0
            )
    value = total.astype(LOW)
    for piece in range(count // 128):
        out_ref[piece] = value[:, piece * 128 : (piece + 1) * 128]


def pick_columns(table_levels, high, low, rows):
    levels = table_levels.shape[0] // rows
    tokens = high.shape[1]
    return pl.pallas_call(
        functools.partial(pick_kernel, levels, rows),
        grid=(tokens // TOKEN_BLOCK,),
        out_shape=jax.ShapeDtypeStruct((tokens // 128, rows, 128), LOW),
        in_specs=[
            pl.BlockSpec(table_levels.shape, lambda step: (0, 0)),
            pl.BlockSpec((1, TOKEN_BLOCK), lambda step: (0, step)),
            pl.BlockSpec((1, TOKEN_BLOCK), lambda step: (0, step)),
        ],
        out_specs=pl.BlockSpec((TOKEN_BLOCK // 128, rows, 128), lambda step: (step, 0, 0)),
        compiler_params=pltpu.CompilerParams(vmem_limit_bytes=32 * 1024 * 1024),
    )(table_levels, high, low)


def spread_kernel(levels, rows, grad_ref, high_ref, low_ref, out_ref, spread_ref):
    step = pl.program_id(0)

    @pl.when(step == 0)
    def _():
        out_ref[...] = jnp.zeros_like(out_ref)

    low = low_ref[...]
    high = high_ref[...]
    count = low.shape[1]
    hot = (lax.broadcasted_iota(jnp.int32, (SPAN_LOW, count), 0) == low).astype(LOW)
    grad = jnp.concatenate([grad_ref[piece] for piece in range(count // 128)], 1).astype(jnp.float32)
    pair = 2
    for first in range(0, levels, pair):
        spread_ref[pl.ds(first * rows, pair * rows), :] = jnp.concatenate(
            [jnp.where(high == first + level, grad, 0.0) for level in range(pair)], 0
        ).astype(LOW)
    group = 10 * rows
    for first in range(0, levels * rows, group):
        out_ref[pl.ds(first, group), :] += lax.dot_general(
            spread_ref[pl.ds(first, group), :],
            hot,
            (((1,), (1,)), ((), ())),
            preferred_element_type=jnp.float32,
        )


def spread_columns(grads, high, low, levels):
    rows = grads.shape[1]
    tokens = high.shape[1]
    return pl.pallas_call(
        functools.partial(spread_kernel, levels, rows),
        grid=(tokens // TOKEN_BLOCK,),
        out_shape=jax.ShapeDtypeStruct((levels * rows, SPAN_LOW), jnp.float32),
        in_specs=[
            pl.BlockSpec((TOKEN_BLOCK // 128, rows, 128), lambda step: (step, 0, 0)),
            pl.BlockSpec((1, TOKEN_BLOCK), lambda step: (0, step)),
            pl.BlockSpec((1, TOKEN_BLOCK), lambda step: (0, step)),
        ],
        out_specs=pl.BlockSpec((levels * rows, SPAN_LOW), lambda step: (0, 0)),
        scratch_shapes=[pltpu.VMEM((levels * rows, TOKEN_BLOCK), LOW)],
        compiler_params=pltpu.CompilerParams(vmem_limit_bytes=32 * 1024 * 1024),
    )(grads, high, low)


HEADS = 12
NORM_EPSILON = 1e-05
ROOT_HALF = 0.5**0.5
PEAK = 0.3989422804014327
WIDTHS = (768, 192)
HEAD_SIZES = (64, 16)
SCALES = (0.125, 0.25)
QUERY_LANES = ((0, 768), (768, 192))
NEGATIVE = -1e30


def plain_product(left, right):
    return jnp.dot(left, right, preferred_element_type=jnp.float32)


def rows_product(left, right):
    return lax.dot_general(
        left, right, (((0,), (0,)), ((), ())), preferred_element_type=jnp.float32
    )


def cols_product(left, right):
    return lax.dot_general(
        left, right, (((1,), (1,)), ((), ())), preferred_element_type=jnp.float32
    )


def exact_product(left, right):
    return jnp.dot(
        left, right, precision=lax.Precision.HIGHEST, preferred_element_type=jnp.float32
    )


def total_rows(values):
    return jnp.sum(values.astype(jnp.float32), 0, keepdims=True)


def normalised(values):
    centred = values - jnp.mean(values, -1, keepdims=True)
    scale = lax.rsqrt(jnp.mean(centred * centred, -1, keepdims=True) + NORM_EPSILON)
    return centred * scale, scale


def norm_apply(values, gain, bias):
    return normalised(values)[0] * gain + bias


def norm_back(values, gain, grad):
    unit, scale = normalised(values)
    inner = grad * gain
    result = scale * (
        inner
        - jnp.mean(inner, -1, keepdims=True)
        - unit * jnp.mean(inner * unit, -1, keepdims=True)
    )
    return result, total_rows(grad * unit), total_rows(grad)


def gelu_value(values):
    return 0.5 * values * (1.0 + lax.erf(values * ROOT_HALF))


def gelu_slope(values):
    return 0.5 * (1.0 + lax.erf(values * ROOT_HALF)) + values * PEAK * jnp.exp(
        -0.5 * values * values
    )


def row_of(ref, row):
    return ref[row : row + 1, :]


def hidden_bias(ref):
    return jnp.concatenate([row_of(ref, row) for row in range(7, 11)], 1)


def head_of(rows, stream):
    lanes = lax.broadcasted_iota(jnp.int32, (rows, WIDTHS[stream]), 1)
    return lanes // HEAD_SIZES[stream]


def stack_heads(values, stream):
    heads = head_of(values.shape[0], stream)
    zero = jnp.zeros_like(values)
    return jnp.concatenate([jnp.where(heads == h, values, zero) for h in range(HEADS)], 0)


def fold_heads(values, stream):
    rows = values.shape[0] // HEADS
    heads = head_of(rows, stream)
    total = jnp.zeros((rows, values.shape[1]), jnp.float32)
    for h in range(HEADS):
        total = total + jnp.where(heads == h, values[h * rows : (h + 1) * rows], 0.0)
    return total


def lane_heads(stream):
    rows = lax.broadcasted_iota(jnp.int32, (128, WIDTHS[stream]), 0)
    return (rows == head_of(128, stream)).astype(jnp.float32)


def head_lanes(stream):
    rows = lax.broadcasted_iota(jnp.int32, (WIDTHS[stream], 128), 0) // HEAD_SIZES[stream]
    return (rows == lax.broadcasted_iota(jnp.int32, (WIDTHS[stream], 128), 1)).astype(jnp.float32)


def stack_columns(values):
    return jnp.concatenate([values[:, h : h + 1] for h in range(HEADS)], 0)


def one_micro_batch(rows):
    row = lax.broadcasted_iota(jnp.int32, (rows, 128), 0)
    key = lax.broadcasted_iota(jnp.int32, (rows, 128), 1)
    return (row // 8) % 2 == key // 64


def coupled_scores(stacks, key_refs):
    return sum(
        cols_product(stacks[n], key_refs[n][...]) * SCALES[n] for n in range(2)
    )


def open_kernel(
    found_ref, position_ref, index_ref, box_ref, proj_ref, qkv_ref, layout_ref,
    text_vec, layout_vec, slot_ref,
    text_sum_ref, layout_sum_ref, spatial_ref, key_text, value_text, key_layout, value_layout,
    query_ref, slot_text, slot_layout,
):
    found = found_ref[...].astype(jnp.float32).reshape(32, 4, 24, 128)
    embedded = (found[:, 0] + found[:, 1] + found[:, 2] + found[:, 3]).reshape(768, 128).T
    place = position_ref[...]
    place = jnp.concatenate([place, place], 0)
    text_sum = embedded + place[:, :768]
    text_sum_ref[...] = text_sum
    tables = (0, 1, 0, 1, 2, 3)
    number = lax.broadcasted_iota(jnp.int32, (128, 1024), 1)
    for k in range(6):
        hot = (number == index_ref[:, k : k + 1]).astype(LOW)
        rows = box_ref[pl.ds(1024 * tables[k], 1024), :]
        spatial_ref[:, pl.ds(128 * k, 128)] = plain_product(hot, rows).astype(LOW)
    layout_sum = place[:, 768:] + plain_product(spatial_ref[...], proj_ref[...])
    layout_sum_ref[...] = layout_sum
    query_ref[...] = jnp.zeros_like(query_ref)
    qkv = qkv_ref[...].reshape(2304, 768)
    weights = (qkv, layout_ref[pl.ds(0, 576), :])
    sums, vecs = (text_sum, layout_sum), (text_vec, layout_vec)
    keys, values, slots = (key_text, key_layout), (value_text, value_layout), (slot_text, slot_layout)
    for n in range(2):
        width, weight, vec = WIDTHS[n], weights[n], vecs[n]
        normed = norm_apply(sums[n], row_of(vec, 0), row_of(vec, 1))
        low = normed.astype(LOW)
        keys[n][...] = cols_product(low, weight[width : 2 * width]).astype(LOW)
        values[n][...] = (cols_product(low, weight[2 * width :]) + row_of(vec, 3)).astype(LOW)
        slot = exact_product(slot_ref[...], normed)
        slots[n][...] = slot
        start, size = QUERY_LANES[n]
        query_ref[:, pl.ds(start, size)] = (
            cols_product(slot.astype(LOW), weight[:width]) + row_of(vec, 2)
        ).astype(LOW)


def score_kernel(query_ref, key_text, value_text, key_layout, value_layout, out_ref):
    stacks = [
        stack_heads(query_ref[:, pl.ds(*QUERY_LANES[n])], n) for n in range(2)
    ]
    mask = one_micro_batch(64 * HEADS)
    scores = jnp.where(mask, coupled_scores(stacks, (key_text, key_layout)), NEGATIVE)
    top = jnp.max(scores, -1, keepdims=True)
    powers = jnp.where(mask, jnp.exp(scores - top), 0.0)
    total = jnp.sum(powers, -1, keepdims=True)
    low = powers.astype(LOW)
    out_ref[:, pl.ds(768, 256)] = jnp.zeros((64, 256), jnp.float32)
    for n, values in enumerate((value_text, value_layout)):
        out_ref[:, pl.ds(*QUERY_LANES[n])] = fold_heads(plain_product(low, values[...]), n)
    lane = lax.broadcasted_iota(jnp.int32, (64, 128), 1)
    tops = jnp.zeros((64, 128), jnp.float32)
    totals = jnp.ones((64, 128), jnp.float32)
    for h in range(HEADS):
        tops = jnp.where(lane == h, top[64 * h : 64 * h + 64], tops)
        totals = jnp.where(lane == h, total[64 * h : 64 * h + 64], totals)
    out_ref[:, pl.ds(1024, 128)] = tops
    out_ref[:, pl.ds(1152, 128)] = totals


def close_kernel(
    parts_ref, slot_text, slot_layout, out_w, up_w, down_w, layout_ref, layout_down,
    text_vec, layout_vec, head_ref, head_vec,
    att_text, att_layout, log_ref, mid_text, mid_layout, pre_text, pre_layout,
    end_text, end_layout, joined_ref, dense_ref, pick_ref,
):
    tops = [parts_ref[j, :, pl.ds(1024, 128)] for j in range(4)]
    top = jnp.maximum(jnp.maximum(tops[0], tops[1]), jnp.maximum(tops[2], tops[3]))
    shares = [jnp.exp(item - top) for item in tops]
    total = sum(shares[j] * parts_ref[j, :, pl.ds(1152, 128)] for j in range(4))
    log_ref[...] = top + jnp.log(total)
    shares = [item / total for item in shares]
    joined_ref[...] = jnp.zeros_like(joined_ref)
    streams = (
        (slot_text, text_vec, out_w, up_w, down_w, att_text, mid_text, pre_text, end_text),
        (slot_layout, layout_vec, layout_ref, layout_ref, layout_down, att_layout, mid_layout,
         pre_layout, end_layout),
    )
    for n, (slot, vec, out_r, up_r, down_r, att_r, mid_r, pre_r, end_r) in enumerate(streams):
        width = WIDTHS[n]
        spread = lane_heads(n)
        att = sum(
            parts_ref[j, :, pl.ds(*QUERY_LANES[n])] * exact_product(shares[j], spread)
            for j in range(4)
        )
        att_r[...] = att
        if n == 0:
            out_m, up_m = out_r[...].reshape(768, 768), up_r[...].reshape(3072, 768)
        else:
            out_m, up_m = out_r[pl.ds(576, 192), :], up_r[pl.ds(768, 768), :]
        mid = slot[...] + (cols_product(att.astype(LOW), out_m) + row_of(vec, 4))
        mid_r[...] = mid
        first = norm_apply(mid, row_of(vec, 5), row_of(vec, 6))
        pre = cols_product(first.astype(LOW), up_m) + hidden_bias(vec)
        pre_r[...] = pre
        end = first + (
            plain_product(gelu_value(pre).astype(LOW), down_r[...]) + row_of(vec, 11)
        )
        end_r[...] = end
        joined_ref[:, pl.ds(*QUERY_LANES[n])] = norm_apply(
            end, row_of(vec, 12), row_of(vec, 13)
        ).astype(LOW)
    dense = cols_product(joined_ref[:, pl.ds(0, 960)], head_ref[...]) + row_of(head_vec, 0)
    dense_ref[...] = dense
    pick_ref[...] = norm_apply(
        gelu_value(dense), row_of(head_vec, 1), row_of(head_vec, 2)
    ).astype(LOW)


def close_back_kernel(
    grad_ref, dense_ref, joined_ref, att_text, att_layout, log_ref, mid_text, mid_layout,
    pre_text, pre_layout, end_text, end_layout, out_w, up_w, down_w, layout_ref, layout_down,
    text_vec, layout_vec, head_ref, head_vec,
    back_ref, d_mid_text, d_mid_layout, d_head, d_out, d_up, d_down, d_layout, d_layout_down,
    d_text_vec, d_layout_vec, d_head_vec,
):
    dense = dense_ref[...]
    d_active, d_gain, d_shift = norm_back(gelu_value(dense), row_of(head_vec, 1), grad_ref[...])
    d_dense = (d_active * gelu_slope(dense)).astype(LOW)
    d_head_vec[0:1, :] = total_rows(d_dense)
    d_head_vec[1:2, :] = d_gain
    d_head_vec[2:3, :] = d_shift
    d_head[...] = rows_product(d_dense, joined_ref[:, pl.ds(0, 960)]).astype(LOW)
    d_joined = plain_product(d_dense, head_ref[...])
    back_ref[:, pl.ds(768, 256)] = jnp.zeros((16, 256), jnp.float32)
    delta = jnp.zeros((16, 128), jnp.float32)
    streams = (
        (text_vec, out_w, up_w, down_w, att_text, mid_text, pre_text, end_text,
         d_mid_text, d_out, d_up, d_down, d_text_vec),
        (layout_vec, layout_ref, layout_ref, layout_down, att_layout, mid_layout, pre_layout,
         end_layout, d_mid_layout, d_layout, d_layout, d_layout_down, d_layout_vec),
    )
    for n, (vec, out_r, up_r, down_r, att_r, mid_r, pre_r, end_r, d_mid_r, d_out_r, d_up_r,
            d_down_r, d_vec) in enumerate(streams):
        width = WIDTHS[n]
        if n == 0:
            out_m, up_m = out_r[...].reshape(768, 768), up_r[...].reshape(3072, 768)
        else:
            out_m, up_m = out_r[pl.ds(576, 192), :], up_r[pl.ds(768, 768), :]
        d_end, d_gain2, d_shift2 = norm_back(
            end_r[...], row_of(vec, 12), d_joined[:, QUERY_LANES[n][0] : sum(QUERY_LANES[n])]
        )
        d_branch2 = d_end.astype(LOW)
        mid, pre = mid_r[...], pre_r[...]
        low = gelu_value(pre).astype(LOW)
        d_pre = (cols_product(d_branch2, down_r[...]) * gelu_slope(pre)).astype(LOW)
        first_low = norm_apply(mid, row_of(vec, 5), row_of(vec, 6)).astype(LOW)
        for k in range(4):
            part = slice(width * k, width * (k + 1))
            d_down_r[pl.ds(width * k, width), :] = rows_product(low[:, part], d_branch2).astype(LOW)
            up_at = pl.ds(width * k, width) if n == 0 else pl.ds(192 + width * k, width)
            d_up_r[up_at, :] = rows_product(d_pre[:, part], first_low).astype(LOW)
            d_vec[7 + k : 8 + k, :] = total_rows(d_pre[:, part])
        d_first = d_end + plain_product(d_pre, up_m)
        d_mid, d_gain1, d_shift1 = norm_back(mid, row_of(vec, 5), d_first)
        d_mid_r[...] = d_mid
        d_branch1 = d_mid.astype(LOW)
        att = att_r[...]
        d_out_r[pl.ds(0, width), :] = rows_product(d_branch1, att.astype(LOW)).astype(LOW)
        d_att = plain_product(d_branch1, out_m).astype(LOW).astype(jnp.float32)
        back_ref[:, pl.ds(*QUERY_LANES[n])] = d_att
        delta = delta + exact_product(d_att * att, head_lanes(n))
        d_vec[0:4, :] = jnp.zeros((4, width), jnp.float32)
        for row, value in (
            (4, total_rows(d_branch1)),
            (5, d_gain1),
            (6, d_shift1),
            (11, total_rows(d_branch2)),
            (12, d_gain2),
            (13, d_shift2),
        ):
            d_vec[row : row + 1, :] = value
    back_ref[:, pl.ds(1024, 128)] = log_ref[...]
    back_ref[:, pl.ds(1152, 128)] = delta


def score_back_kernel(
    back_ref, query_ref, key_text, value_text, key_layout, value_layout,
    d_query, d_key_text, d_value_text, d_key_layout, d_value_layout,
):
    keys, values = (key_text, key_layout), (value_text, value_layout)
    stacks = [stack_heads(query_ref[:, pl.ds(*QUERY_LANES[n])], n) for n in range(2)]
    grads = [stack_heads(back_ref[:, pl.ds(*QUERY_LANES[n])], n).astype(LOW) for n in range(2)]
    logs = stack_columns(back_ref[:, pl.ds(1024, 128)])
    delta = stack_columns(back_ref[:, pl.ds(1152, 128)])
    mask = one_micro_batch(64 * HEADS)
    probs = jnp.where(mask, jnp.exp(jnp.where(mask, coupled_scores(stacks, keys) - logs, 0.0)), 0.0)
    d_probs = sum(cols_product(grads[n], values[n][...]) for n in range(2))
    d_scores = (probs * (d_probs - delta)).astype(LOW)
    low = probs.astype(LOW)
    d_query[:, pl.ds(768, 256)] = jnp.zeros((64, 256), jnp.float32)
    d_keys, d_values = (d_key_text, d_key_layout), (d_value_text, d_value_layout)
    for n in range(2):
        d_query[:, pl.ds(*QUERY_LANES[n])] = (
            fold_heads(plain_product(d_scores, keys[n][...]), n) * SCALES[n]
        )
        d_keys[n][...] = (rows_product(d_scores, stacks[n]) * SCALES[n]).astype(LOW)
        d_values[n][...] = rows_product(low, grads[n]).astype(LOW)


def open_back_kernel(
    parts_ref, d_key_text, d_value_text, d_key_layout, d_value_layout, d_mid_text, d_mid_layout,
    text_sum, layout_sum, slot_text, slot_layout, qkv_ref, layout_ref, proj_ref, spatial_ref,
    index_ref, text_vec, layout_vec, slot_turned,
    d_query_w, d_kv_w, d_layout, d_embedded, d_position, d_box, d_proj, d_text_vec, d_layout_vec,
):
    qkv = qkv_ref[...].reshape(2304, 768)
    streams = (
        (qkv, d_key_text, d_value_text, d_mid_text, text_sum, slot_text, text_vec, d_text_vec),
        (layout_ref[pl.ds(0, 576), :], d_key_layout, d_value_layout, d_mid_layout, layout_sum,
         slot_layout, layout_vec, d_layout_vec),
    )
    lows = []
    for n, (weight, d_key_r, d_value_r, d_mid_r, sum_r, slot_r, vec, d_vec) in enumerate(streams):
        width = WIDTHS[n]
        lanes = pl.ds(*QUERY_LANES[n])
        d_query = sum(parts_ref[j, :, lanes] for j in range(4)).astype(LOW)
        d_key, d_value = d_key_r[...], d_value_r[...]
        d_slot = d_mid_r[...] + plain_product(d_query, weight[:width])
        d_normed = (
            plain_product(d_key, weight[width : 2 * width])
            + plain_product(d_value, weight[2 * width :])
            + exact_product(slot_turned[...], d_slot)
        )
        sums = sum_r[...]
        low = norm_apply(sums, row_of(vec, 0), row_of(vec, 1)).astype(LOW)
        d_sum, d_gain, d_shift = norm_back(sums, row_of(vec, 0), d_normed)
        d_vec[...] = jnp.zeros_like(d_vec)
        for row, value in ((0, d_gain), (1, d_shift), (2, total_rows(d_query)), (3, total_rows(d_value))):
            d_vec[row : row + 1, :] = value
        slot_low = slot_r[...].astype(LOW)
        grads = (rows_product(d_query, slot_low), rows_product(d_key, low), rows_product(d_value, low))
        if n == 0:
            d_query_w[...] = grads[0].astype(LOW)
            d_kv_w[pl.ds(0, 768), :] = grads[1].astype(LOW)
            d_kv_w[pl.ds(768, 768), :] = grads[2].astype(LOW)
        else:
            for k in range(3):
                d_layout[pl.ds(192 * k, 192), :] = grads[k].astype(LOW)
        d_low = d_sum.astype(LOW)
        lows.append(d_low)
        wide = d_low.astype(jnp.float32)
        d_position[:, lanes] = wide[:64] + wide[64:]
        if n == 0:
            d_embedded[...] = wide.T.astype(LOW)
    d_spatial = cols_product(lows[1], proj_ref[...]).astype(LOW)
    d_proj[...] = rows_product(spatial_ref[...], lows[1]).astype(LOW)
    number = lax.broadcasted_iota(jnp.int32, (128, 1024), 1)
    for table, users in enumerate(((0, 2), (1, 3), (4,), (5,))):
        total = 0.0
        for k in users:
            hot = (number == index_ref[:, k : k + 1]).astype(LOW)
            total = total + rows_product(hot, d_spatial[:, 128 * k : 128 * k + 128])
        d_box[pl.ds(1024 * table, 1024), :] = total.astype(LOW)


def local_call(kernel, inputs, outputs, name):
    specs, arrays = [], []

    def spec(shape, index):
        return pl.BlockSpec(shape, lambda step: index, pipeline_mode=pl.Buffered(1))

    for item in inputs:
        array, shape, index = item if isinstance(item, tuple) else (item, item.shape, None)
        specs.append(spec(shape, index or (0,) * len(shape)))
        arrays.append(array)
    return pl.pallas_call(
        kernel,
        name=name,
        grid=(1,),
        out_shape=[jax.ShapeDtypeStruct(shape, dtype) for shape, dtype in outputs],
        in_specs=specs,
        out_specs=[spec(shape, (0,) * len(shape)) for shape, dtype in outputs],
        compiler_params=pltpu.CompilerParams(vmem_limit_bytes=56 * 1024 * 1024),
    )(*arrays)


PLANES = (("y", "z"), ("x", "z"), ("x", "y"))
LINES = ("x", "y", "z")
HEAD_BLOCK = 512
PLANE_STEPS = [(a, b) for a in range(4) for b in range(4) if (a, b) != (0, 0)]


def plane_peer(place, plane, a, b):
    return moved(moved(place, plane[0], a), plane[1], b)


def head_peers(place):
    peers = [
        plane_peer(place, plane, a, b)
        for plane in PLANES
        for a, b in PLANE_STEPS
        if (a and b) or plane == ("y", "z")
    ]
    peers += [moved(place, "x", step) for step in (1, 2, 3)]
    peers += [moved(moved(place, "x", step), "c", 1) for step in range(4)]
    return peers


def merge_logs(logs):
    top = logs[0]
    for item in logs[1:]:
        top = jnp.maximum(top, item)
    total = jnp.exp(logs[0] - top)
    for item in logs[1:]:
        total = total + jnp.exp(item - top)
    return top + jnp.log(total)


def head_kernel(
    limit_width, pick_ref, table_ref, label_ref, weight_ref, count_ref,
    grad_ref, d_table_ref, loss_ref,
    picked, table, logits, d_logits, part, acc, cross, near, far, line_in, plane_in, own_sem,
    plane_send, plane_recv, line_send, line_recv, pass_send, pass_recv,
    near_send, near_recv, far_send, far_recv, core_send, core_recv,
    back_send, back_recv, last_send, last_recv,
):
    place = my_place()
    sibling = moved(place, "c", 1)
    barrier = pltpu.get_barrier_semaphore()
    peers = head_peers(place)
    for peer in peers:
        pl.semaphore_signal(barrier, inc=1, device_id=device_of(peer), device_id_type=MESH)
    own = pltpu.make_async_copy(
        pick_ref, block_view(picked, place, "", None, place["c"]), own_sem
    )
    own.start()
    pl.semaphore_wait(barrier, len(peers))
    sends = []

    def go(copy):
        copy.start()
        sends.append(copy)
        return copy

    def third(k):
        return (256 * k, 256)

    flights = {}
    for k in range(3):
        here = block_view(picked, place, "", third(k), place["c"])
        for a, b in PLANE_STEPS:
            n = 4 * a + b - 1
            flights[(k, n)] = go(
                remote(
                    pick_ref.at[:, pl.ds(*third(k))], here, plane_send.at[k, n],
                    plane_recv.at[k, n], plane_peer(place, PLANES[k], a, b),
                )
            )
    table[...] = table_ref[...].astype(jnp.float32).T.astype(LOW)
    own.wait()
    lines, passes = {}, []

    def hand_over(k, n, where):
        passes.append(go(remote(where, where, pass_send.at[k, n], pass_recv.at[k, n], sibling)))

    for k in range(3):
        for a, b in PLANE_STEPS:
            flights[(k, 4 * a + b - 1)].wait_recv()
        sheet = block_view(picked, place, PLANES[k], third(k), place["c"])
        for step in (1, 2, 3):
            lines[(k, step)] = go(
                remote(
                    sheet, sheet, line_send.at[k, step - 1], line_recv.at[k, step - 1],
                    moved(place, LINES[k], step),
                )
            )
        hand_over(k, 0, sheet)
    for step in (1, 3, 2):
        for k in range(3):
            lines[(k, step)].wait_recv()
            origin = moved(place, LINES[k], -step)
            hand_over(k, step, block_view(picked, origin, PLANES[k], third(k), place["c"]))
    for copy in passes:
        copy.wait_recv()

    limit = limit_width - lax.axis_index("dp") * HEAD_BLOCK
    row = lax.broadcasted_iota(jnp.int32, (HEAD_BLOCK, 256), 0)
    valid = row < limit
    mine = place["x"] * 2 + place["c"]
    for chunk in range(8):
        high, mid = chunk // 4, chunk % 4
        lanes = pl.ds(256 * chunk, 256)
        values = cols_product(table[...], picked[high, mid].reshape(256, 768))
        values = jnp.where(valid, values, NEGATIVE)
        logits[:, lanes] = values
        top = jnp.max(values, 0, keepdims=True)
        total = jnp.sum(jnp.where(valid, jnp.exp(values - top), 0.0), 0, keepdims=True)
        hot = valid & (row == label_ref[:, lanes])
        near[mine, 0, :, lanes] = top + jnp.log(jnp.maximum(total, 1e-30))
        near[mine, 1, :, lanes] = jnp.sum(jnp.where(hot, values, 0.0), 0, keepdims=True)
    meets = []
    for n in range(1, 8):
        peer = moved(place, "x", n // 2)
        if n % 2:
            peer = moved(peer, "c", 1)
        meets.append(
            go(remote(near.at[mine], near.at[mine], near_send.at[n - 1], near_recv.at[n - 1], peer))
        )
    for copy in meets:
        copy.wait_recv()
    spot = place["y"] * 4 + place["z"]
    far[spot, 0] = merge_logs([near[n, 0] for n in range(8)])
    far[spot, 1] = sum(near[n, 1] for n in range(8))
    meets = []
    for a, b in PLANE_STEPS:
        n = 4 * a + b - 1
        peer = plane_peer(place, ("y", "z"), a, b)
        meets.append(go(remote(far.at[spot], far.at[spot], far_send.at[n], far_recv.at[n], peer)))
    for copy in meets:
        copy.wait_recv()
    log_total = merge_logs([far[n, 0] for n in range(16)])
    target = sum(far[n, 1] for n in range(16))
    loss = jnp.sum(count_ref[...] * (log_total - target), 1, keepdims=True)
    loss_ref[...] = jnp.broadcast_to(loss, loss_ref.shape)

    crossings = []
    for chunk in range(8):
        high, mid = chunk // 4, chunk % 4
        lanes = pl.ds(256 * chunk, 256)
        here = slice(256 * chunk, 256 * chunk + 256)
        hot = (valid & (row == label_ref[:, lanes])).astype(jnp.float32)
        powers = jnp.where(valid, jnp.exp(logits[:, lanes] - log_total[:, here]), 0.0)
        low = (weight_ref[:, lanes] * (powers - hot)).astype(LOW)
        d_logits[:, lanes] = low
        part[high, mid] = rows_product(low, table[...]).astype(LOW).reshape(4, 2, 2, 16, 768)
        crossings.append(
            go(
                remote(
                    part.at[high, mid, :, :, sibling["c"]], cross.at[high, mid],
                    core_send.at[chunk], core_recv.at[chunk], sibling,
                )
            )
        )
    for chunk in range(8):
        high, mid = chunk // 4, chunk % 4
        crossings[chunk].wait_recv()
        acc[high, mid] = part[high, mid, :, :, place["c"]] + cross[high, mid]

    legs = {}
    for k in range(3):
        for step in (1, 3, 2):
            there = moved(place, LINES[k], step)
            legs[(k, step)] = go(
                remote(
                    block_view(acc, there, PLANES[k], third(k)), line_in[k].at[step - 1],
                    back_send.at[k, step - 1], back_recv.at[k, step - 1], there,
                )
            )
    d_table = jnp.zeros((HEAD_BLOCK, 768), jnp.float32)
    for chunk in range(8):
        d_table = d_table + plain_product(
            d_logits[:, pl.ds(256 * chunk, 256)], picked[chunk // 4, chunk % 4].reshape(256, 768)
        )
    d_table_ref[...] = d_table.T.astype(LOW)
    ends = {}
    for k in range(3):
        for step in (1, 2, 3):
            legs[(k, step)].wait_recv()
        count, chunk_of = chunks_of("".join(PLANES[k]), place)
        for flat in range(count):
            block, inner = chunk_of(flat)
            where = block + (slice(None), pl.ds(*third(k)))
            total = acc[where].astype(jnp.float32)
            for step in (1, 2, 3):
                total = total + line_in[k][(step - 1,) + inner].astype(jnp.float32)
            acc[where] = total.astype(LOW)
        for a, b in PLANE_STEPS:
            n = 4 * a + b - 1
            there = plane_peer(place, PLANES[k], a, b)
            ends[(k, n)] = go(
                remote(
                    block_view(acc, there, "", third(k)), plane_in.at[k, n],
                    last_send.at[k, n], last_recv.at[k, n], there,
                )
            )
    home = (place["x"] // 2, place["y"], place["z"], place["x"] % 2)
    for k in range(3):
        total = acc[home + (slice(None), pl.ds(*third(k)))].astype(jnp.float32)
        for n in range(15):
            ends[(k, n)].wait_recv()
            total = total + plane_in[k, n].astype(jnp.float32)
        grad_ref[:, pl.ds(*third(k))] = total
    for copy in sends:
        copy.wait_send()


def head_step(picked, table, labels, weights, counts, width, collective_id):
    sems = pltpu.SemaphoreType.DMA
    everyone = (2, 4, 4, 2, 2, 16, 768)
    half = (2, 4, 4, 2, 16, 768)
    line_slots = [
        pltpu.VMEM((3,) + open_shape("".join(PLANES[k])) + (16, 256), LOW) for k in range(3)
    ]

    def kernel(*refs):
        head_kernel(width, *refs[:17], refs[17:20], *refs[20:])

    return pl.pallas_call(
        kernel,
        out_shape=[
            jax.ShapeDtypeStruct((16, 768), jnp.float32),
            jax.ShapeDtypeStruct((768, HEAD_BLOCK), LOW),
            jax.ShapeDtypeStruct((8, 128), jnp.float32),
        ],
        in_specs=[pl.BlockSpec(memory_space=pltpu.VMEM)] * 5,
        out_specs=[pl.BlockSpec(memory_space=pltpu.VMEM)] * 3,
        scratch_shapes=[
            pltpu.VMEM(everyone, LOW),
            pltpu.VMEM((HEAD_BLOCK, 768), LOW),
            pltpu.VMEM((HEAD_BLOCK, 2048), jnp.float32),
            pltpu.VMEM((HEAD_BLOCK, 2048), LOW),
            pltpu.VMEM(everyone, LOW),
            pltpu.VMEM(half, LOW),
            pltpu.VMEM(half, LOW),
            pltpu.VMEM((8, 2, 1, 2048), jnp.float32),
            pltpu.VMEM((16, 2, 1, 2048), jnp.float32),
        ]
        + line_slots
        + [
            pltpu.VMEM((3, 15, 16, 256), LOW),
            sems(()),
            sems((3, 15)),
            sems((3, 15)),
            sems((3, 3)),
            sems((3, 3)),
            sems((3, 4)),
            sems((3, 4)),
            sems((7,)),
            sems((7,)),
            sems((15,)),
            sems((15,)),
            sems((8,)),
            sems((8,)),
            sems((3, 3)),
            sems((3, 3)),
            sems((3, 15)),
            sems((3, 15)),
        ],
        compiler_params=pltpu.CompilerParams(
            collective_id=collective_id, has_side_effects=True, vmem_limit_bytes=56 * 1024 * 1024
        ),
    )(picked, table, labels, weights, counts)


def thirds(number):
    return [(number, (256 * k, 256), k) for k in range(3)]


GATHER_PIECES = thirds(0) + thirds(1) + [(2, None, 0), (3, None, 2), (4, None, 1), (5, None, 2)]
REDUCE_PIECES = (
    thirds(0)
    + thirds(1)
    + [(2, None, 0), (3, None, 2), (4, None, 1), (5, None, 1), (6, None, 2), (7, None, 2), (8, None, 0)]
)
WHOLE = ((0, 2), (0, 4))
REDUCE_SOURCES = [
    (0, (0, 1), (0, 1)),
    (0, (0, 1), (1, 2)),
    (0, (0, 1), (3, 1)),
    (0, (1, 1), (0, 4)),
] + [(number,) + WHOLE for number in range(1, 9)]


def fetch(masters):
    word, position, box, text, down, layout, layout_down, head, vector = [
        m.astype(LOW) for m in masters
    ]
    misc = jnp.concatenate(
        [
            layout.T,
            layout_down[0],
            layout_down[1],
            jnp.pad(vector, (0, 192 - vector.shape[0]))[None],
        ],
        0,
    )
    text, down, head, position, misc, box = gather_all(
        [text.T, down, head.T, position, misc, box.reshape(32, 128)], GATHER_PIECES, 2
    )
    return dict(
        text=text,
        down=down.reshape(3072, 768),
        head=head.reshape(768, 960),
        box=box.reshape(128, 4, 8, 128).transpose(1, 0, 2, 3).reshape(4096, 128),
        layout=misc[:, :12].reshape(1536, 192),
        layout_down=misc[:, 12:18].reshape(768, 192),
        box_proj=misc[:, 18:24].reshape(768, 192),
        position=position.reshape(640, 960),
        vector=misc[:, 24, :123].reshape(15744),
    )


def reduce_weights(grads):
    shards = reduce_all(
        [
            grads["query"].reshape(16, 48, 768),
            grads["key_value"].reshape(32, 48, 768),
            grads["out"].reshape(16, 48, 768),
            grads["up"].reshape(64, 48, 768),
            grads["down"].reshape(128, 24, 768),
            grads["head"].reshape(128, 6, 960),
            grads["position"].reshape(128, 5, 960),
            grads["layout"].reshape(128, 12, 192),
            grads["layout_down"].reshape(128, 6, 192),
            grads["box_proj"].reshape(128, 6, 192),
            grads["box"].reshape(4, 128, 8, 128).transpose(1, 0, 2, 3).reshape(128, 32, 128),
            grads["vector"].reshape(128, 1, 123),
        ],
        REDUCE_SOURCES,
        REDUCE_PIECES,
        6,
    )
    text, down, head, position, layout, layout_down, box_proj, box, vector, square = shards
    return square, [
        position,
        box.reshape(4, 8, 128),
        text.T,
        down,
        layout.T,
        jnp.stack([layout_down, box_proj]),
        head.T,
        vector[0],
    ]


def on_device(
    token_ids,
    box_coords,
    intersection_flags,
    masked_rows,
    masked_labels,
    *weights,
):
    triples = [tuple(weights[3 * n : 3 * n + 3]) for n in range(9)]
    masters = [entry[0] for entry in triples]
    word_table = masters[0]
    dp = lax.axis_index("dp")
    vocab = lax.axis_index("vocab")
    shard_width = word_table.shape[1]
    table_rows = word_table.shape[0]
    levels = -(-shard_width // SPAN_LOW)

    row_hot = masked_rows[:, :, None] == jnp.arange(64)[None, None, :]
    counted = jnp.sum(jnp.where(row_hot & (intersection_flags == 0)[:, None, :], 1, 0), 2)
    slot_hot = jnp.concatenate(
        [
            jnp.pad(row_hot[0], ((0, 0), (0, 64))),
            jnp.pad(row_hot[1], ((0, 0), (64, 0))),
        ],
        0,
    )
    slot_hot_wide = slot_hot.astype(jnp.float32)
    f32 = jnp.float32

    notes = jnp.concatenate(
        [
            token_ids.reshape(1, 128),
            jnp.concatenate(
                [masked_labels.reshape(1, 16), counted.reshape(1, 16), jnp.zeros((1, 96), jnp.int32)], 1
            ),
        ],
        0,
    )
    notes_all = lax.all_to_all(
        jnp.broadcast_to(notes[None], (128,) + notes.shape), AXES, 0, 0, tiled=True
    )
    ids_all = notes_all[:, 0, :].reshape(1, 16384)
    labels_all = notes_all[:, 1, :16].reshape(2048)
    counted_all = notes_all[:, 1, 16:32].reshape(2048).astype(jnp.float32)
    total_count = jnp.sum(counted_all)

    local_ids = ids_all - vocab * shard_width
    ids_high = local_ids >> 8
    ids_low = local_ids & 255
    table_low = word_table.astype(LOW)
    table_levels = (
        jnp.pad(table_low, ((0, 0), (0, levels * SPAN_LOW - shard_width)))
        .reshape(table_rows, levels, SPAN_LOW)
        .transpose(1, 0, 2)
        .reshape(levels * table_rows, SPAN_LOW)
    )
    found = pick_columns(table_levels, ids_high, ids_low, table_rows)
    found, masters = lax.optimization_barrier((found, masters))
    found = lax.all_to_all(found, AXES, 0, 0, tiled=True)

    table_blocks = (
        jnp.pad(table_low, ((0, 0), (0, 32 * HEAD_BLOCK - shard_width)))
        .reshape(table_rows, 32, HEAD_BLOCK)
        .transpose(1, 0, 2)
    )
    table_head = lax.all_to_all(table_blocks, "dp", 0, 0, tiled=True).reshape(768, HEAD_BLOCK)

    full = fetch(masters)
    vector = full["vector"].astype(jnp.float32)
    text_vec = vector[:10752].reshape(14, 768)
    layout_vec = vector[10752:13440].reshape(14, 192)
    head_vec = vector[13440:].reshape(3, 768)
    position_own = lax.dynamic_slice_in_dim(full["position"], vocab * 64, 64, 0).astype(f32)
    boxes = box_coords.reshape(4, 128)
    box_index = jnp.stack(
        [
            boxes[0],
            boxes[1],
            boxes[2],
            boxes[3],
            jnp.abs(boxes[3] - boxes[1]),
            jnp.abs(boxes[2] - boxes[0]),
            boxes[0],
            boxes[0],
        ],
        1,
    )
    qkv = (full["text"], (48, 48, 768), (0, 0, 0))
    out_w = (full["text"], (16, 48, 768), (3, 0, 0))
    up_w = (full["text"], (64, 48, 768), (1, 0, 0))
    text_sum, layout_sum, spatial, *kv, query, slot_text, slot_layout = local_call(
        open_kernel,
        [
            found,
            position_own,
            box_index,
            full["box"],
            full["box_proj"],
            qkv,
            full["layout"],
            text_vec,
            layout_vec,
            slot_hot_wide,
        ],
        [
            ((128, 768), f32),
            ((128, 192), f32),
            ((128, 768), LOW),
            ((128, 768), LOW),
            ((128, 768), LOW),
            ((128, 192), LOW),
            ((128, 192), LOW),
            ((16, 1024), LOW),
            ((16, 768), f32),
            ((16, 192), f32),
        ],
        "open_streams",
    )
    query_all = lax.all_gather(query, "vocab", axis=0, tiled=True)
    (partial,) = local_call(score_kernel, [query_all, *kv], [((64, 1280), f32)], "partial_attention")
    partial = lax.all_to_all(partial.reshape(4, 16, 1280), "vocab", 0, 0, tiled=True)
    weights_close = [out_w, up_w, full["down"], full["layout"], full["layout_down"]]
    vectors_close = [text_vec, layout_vec, full["head"], head_vec]
    (att_text, att_layout, log_total, mid_text, mid_layout, pre_text, pre_layout, end_text,
     end_layout, joined, dense, picked) = local_call(
        close_kernel,
        [partial, slot_text, slot_layout] + weights_close + vectors_close,
        [
            ((16, 768), f32),
            ((16, 192), f32),
            ((16, 128), f32),
            ((16, 768), f32),
            ((16, 192), f32),
            ((16, 3072), f32),
            ((16, 768), f32),
            ((16, 768), f32),
            ((16, 192), f32),
            ((16, 1024), LOW),
            ((16, 768), f32),
            ((16, 768), LOW),
        ],
        "close_streams",
    )
    d_picked, table_head_grad, loss = head_step(
        picked,
        table_head,
        (labels_all - vocab * shard_width - dp * HEAD_BLOCK)[None],
        (counted_all / total_count)[None],
        counted_all[None],
        shard_width,
        3,
    )
    loss_total = loss[0, 0]
    table_head_grad = lax.all_to_all(
        table_head_grad.reshape(32, 24, HEAD_BLOCK), "dp", 0, 0, tiled=True
    )
    (back, d_mid_text, d_mid_layout, d_head, d_out, d_up, d_down, d_layout_close, d_layout_down,
     d_text_vec, d_layout_vec, d_head_vec) = local_call(
        close_back_kernel,
        [d_picked, dense, joined, att_text, att_layout, log_total, mid_text, mid_layout]
        + [pre_text, pre_layout, end_text, end_layout]
        + weights_close
        + vectors_close,
        [
            ((16, 1280), f32),
            ((16, 768), f32),
            ((16, 192), f32),
            ((768, 960), LOW),
            ((768, 768), LOW),
            ((3072, 768), LOW),
            ((3072, 768), LOW),
            ((960, 192), LOW),
            ((768, 192), LOW),
            ((14, 768), f32),
            ((14, 192), f32),
            ((3, 768), f32),
        ],
        "close_streams_back",
    )
    back = lax.all_gather(back, "vocab", axis=0, tiled=True)
    d_query, *d_kv = local_call(
        score_back_kernel,
        [back, query_all, *kv],
        [
            ((64, 1024), f32),
            ((128, 768), LOW),
            ((128, 768), LOW),
            ((128, 192), LOW),
            ((128, 192), LOW),
        ],
        "attention_back",
    )
    d_query = lax.all_to_all(d_query.reshape(4, 16, 1024), "vocab", 0, 0, tiled=True)
    (d_query_w, d_kv_w, d_layout_open, d_embedded, d_position, d_box, d_proj, d_text_open,
     d_layout_vec_open) = local_call(
        open_back_kernel,
        [d_query, *d_kv, d_mid_text, d_mid_layout, text_sum, layout_sum, slot_text, slot_layout]
        + [qkv, full["layout"], full["box_proj"], spatial, box_index, text_vec, layout_vec]
        + [slot_hot_wide.T],
        [
            ((768, 768), LOW),
            ((1536, 768), LOW),
            ((576, 192), LOW),
            ((768, 128), LOW),
            ((64, 960), f32),
            ((4096, 128), LOW),
            ((768, 192), LOW),
            ((14, 768), f32),
            ((14, 192), f32),
        ],
        "open_streams_back",
    )
    d_text_blocks = jnp.broadcast_to(
        d_embedded.reshape(32, 1, 24, 128), (32, 4, 24, 128)
    ).reshape(128, 24, 128)
    d_text_all = lax.all_to_all(d_text_blocks, AXES, 0, 0, tiled=True)
    table_grad = (
        spread_columns(d_text_all, ids_high, ids_low, levels)
        .reshape(levels, table_rows, SPAN_LOW)
        .transpose(1, 0, 2)
        .reshape(table_rows, levels * SPAN_LOW)[:, :shard_width]
    )
    table_grad = table_grad + table_head_grad.transpose(1, 0, 2).reshape(
        table_rows, 32 * HEAD_BLOCK
    )[:, :shard_width].astype(jnp.float32)

    d_positions = lax.dynamic_update_slice_in_dim(
        jnp.zeros((640, 960), LOW), d_position.astype(LOW), vocab * 64, 0
    )
    square, shards = reduce_weights(
        dict(
            query=d_query_w,
            key_value=d_kv_w,
            out=d_out,
            up=d_up,
            down=d_down,
            head=d_head,
            box=d_box,
            layout=jnp.concatenate([d_layout_open, d_layout_close], 0),
            layout_down=d_layout_down,
            box_proj=d_proj,
            position=d_positions,
            vector=jnp.concatenate(
                [
                    (d_text_vec + d_text_open).reshape(10752),
                    (d_layout_vec + d_layout_vec_open).reshape(2688),
                    d_head_vec.reshape(2304),
                ]
            ).astype(LOW),
        )
    )
    all_grads = [table_grad] + shards
    norm_stats = jnp.concatenate(
        [
            jnp.zeros((16, 128), f32),
            square + jnp.sum(table_grad * table_grad),
            jnp.zeros((16, 128), f32),
        ],
        0,
    )
    grad_norm = jnp.sqrt(merge_stats(norm_stats, 7)[16, 0])
    factor = jnp.minimum(1.0, CLIP / grad_norm)
    results = []
    for (master, momentum, average), grad in zip(triples, all_grads):
        clipped = factor * grad
        momentum_next = MOMENTUM * momentum + clipped
        master_next = master - RATE * (clipped + MOMENTUM * momentum_next)
        average_next = AVERAGE_KEEP * average + (1.0 - AVERAGE_KEEP) * master_next
        results += [master_next, momentum_next, average_next]
    return tuple(results + [loss_total, total_count, grad_norm])


TOKEN_SPEC = P(None, AXES)
WEIGHT_SPECS = (
    P("dp", "vocab"),
    P(AXES, None),
    P(None, AXES, None),
    P(None, AXES),
    P(AXES, None),
    P(None, AXES),
    P(None, AXES, None),
    P(None, AXES),
    P(AXES),
)


def solution(mesh):
    weight_specs = tuple(spec for spec in WEIGHT_SPECS for _ in range(3))
    in_specs = (TOKEN_SPEC, P(None, None, AXES), TOKEN_SPEC, TOKEN_SPEC, TOKEN_SPEC) + weight_specs
    out_specs = weight_specs + (P(), P(), P())
    return jax.shard_map(
        on_device, mesh=mesh, in_specs=in_specs, out_specs=out_specs, check_vma=False
    )
```

```python
import functools

import jax
import jax.numpy as jnp
from jax import lax
from jax.experimental import pallas as pl
from jax.experimental.pallas import tpu as pltpu
from jax.sharding import PartitionSpec as P

AXES = ("dp", "vocab")
MESH = pl.DeviceIdType.MESH
LONG = pl.CostEstimate(flops=60_000_000_000, bytes_accessed=200_000_000, transcendentals=0)
ORDERS = (("z", "y", "x"), ("y", "x", "z"), ("x", "z", "y"))


def my_place():
    dp = lax.axis_index("dp")
    vocab = lax.axis_index("vocab")
    return {
        "x": (dp // 16) * 2 + vocab // 2,
        "y": (dp // 4) % 4,
        "z": dp % 4,
        "c": vocab % 2,
    }


def moved(place, dim, step):
    other = dict(place)
    other[dim] = (1 - place["c"]) if dim == "c" else (place[dim] + step + 4) % 4
    return other


def device_of(place):
    return (
        (place["x"] // 2) * 16 + place["y"] * 4 + place["z"],
        (place["x"] % 2) * 2 + place["c"],
    )


def greet(place, steps=(1, 3)):
    barrier = pltpu.get_barrier_semaphore()
    peers = [moved(place, dim, step) for dim in "xyz" for step in steps]
    peers.append(moved(place, "c", 1))
    for peer in peers:
        pl.semaphore_signal(barrier, inc=1, device_id=device_of(peer), device_id_type=MESH)
    pl.semaphore_wait(barrier, len(peers))


def remote(src, dst, send, recv, place):
    return pltpu.make_async_remote_copy(
        src_ref=src,
        dst_ref=dst,
        send_sem=send,
        recv_sem=recv,
        device_id=device_of(place),
        device_id_type=MESH,
    )


def lanes_at(ref, lanes):
    return slice(None) if lanes is None else pl.ds(*lanes)


def block_view(ref, place, dims, lanes, core=None):
    high, low = (pl.ds(0, 2), pl.ds(0, 2)) if "x" in dims else (place["x"] // 2, place["x"] % 2)
    mid = pl.ds(0, 4) if "y" in dims else place["y"]
    deep = pl.ds(0, 4) if "z" in dims else place["z"]
    where = (high, mid, deep, low)
    if core is not None:
        where += (core,)
    return ref.at[where + (slice(None), lanes_at(ref, lanes))]


def halves(lanes, number):
    if lanes is None or lanes[1] < 256:
        return (lanes, False) if number % 2 == 0 else (False, lanes)
    half = lanes[1] // 256 * 128
    return (lanes[0], half), (lanes[0] + half, lanes[1] - half)


def open_shape(dims):
    shape = ()
    if "x" in dims:
        shape += (2,)
    if "y" in dims:
        shape += (4,)
    if "z" in dims:
        shape += (4,)
    if "x" in dims:
        shape += (2,)
    return shape


def chunks_of(dims, place):
    high, mid, deep, low = place["x"] // 2, place["y"], place["z"], place["x"] % 2
    every = slice(None)
    if dims == "":
        return 1, lambda flat: ((high, mid, deep, low), ())
    inner = (every if "y" in dims else mid, every if "z" in dims else deep)
    if "x" in dims and "y" in dims and "z" in dims:
        return 8, lambda flat: ((flat // 4, flat % 4, every, every), (flat // 4, flat % 4))
    if "x" in dims:
        return 2, lambda flat: ((flat,) + inner + (every,), (flat,))
    if "y" in dims and "z" in dims:
        return 4, lambda flat: ((high, flat, every, low), (flat,))
    return 1, lambda flat: ((high,) + inner + (low,), ())


MOMENTUM = 0.9
AVERAGE_KEEP = 0.9
RATE = 1500.0
CLIP = 0.05
LOW = jnp.bfloat16
SPAN_LOW = 256
TOKEN_BLOCK = 1024


HEADS = 12
NORM_EPSILON = 1e-05
ROOT_HALF = 0.5**0.5
PEAK = 0.3989422804014327
WIDTHS = (768, 192)
HEAD_SIZES = (64, 16)
SCALES = (0.125, 0.25)
QUERY_LANES = ((0, 768), (768, 192))
NEGATIVE = -1e30


def plain_product(left, right):
    return jnp.dot(left, right, preferred_element_type=jnp.float32)


def rows_product(left, right):
    return lax.dot_general(
        left, right, (((0,), (0,)), ((), ())), preferred_element_type=jnp.float32
    )


def cols_product(left, right):
    return lax.dot_general(
        left, right, (((1,), (1,)), ((), ())), preferred_element_type=jnp.float32
    )


def exact_product(left, right):
    return jnp.dot(
        left, right, precision=lax.Precision.HIGHEST, preferred_element_type=jnp.float32
    )


def total_rows(values):
    return jnp.sum(values.astype(jnp.float32), 0, keepdims=True)


def normalised(values):
    centred = values - jnp.mean(values, -1, keepdims=True)
    scale = lax.rsqrt(jnp.mean(centred * centred, -1, keepdims=True) + NORM_EPSILON)
    return centred * scale, scale


def norm_apply(values, gain, bias):
    return normalised(values)[0] * gain + bias


def norm_back(values, gain, grad):
    unit, scale = normalised(values)
    inner = grad * gain
    result = scale * (
        inner
        - jnp.mean(inner, -1, keepdims=True)
        - unit * jnp.mean(inner * unit, -1, keepdims=True)
    )
    return result, total_rows(grad * unit), total_rows(grad)


def gelu_value(values):
    return 0.5 * values * (1.0 + lax.erf(values * ROOT_HALF))


def gelu_slope(values):
    return 0.5 * (1.0 + lax.erf(values * ROOT_HALF)) + values * PEAK * jnp.exp(
        -0.5 * values * values
    )


def row_of(ref, row):
    return ref[row : row + 1, :]


def hidden_bias(ref):
    return jnp.concatenate([row_of(ref, row) for row in range(7, 11)], 1)


def head_of(rows, stream):
    lanes = lax.broadcasted_iota(jnp.int32, (rows, WIDTHS[stream]), 1)
    return lanes // HEAD_SIZES[stream]


def stack_heads(values, stream):
    heads = head_of(values.shape[0], stream)
    zero = jnp.zeros_like(values)
    return jnp.concatenate([jnp.where(heads == h, values, zero) for h in range(HEADS)], 0)


def fold_heads(values, stream):
    rows = values.shape[0] // HEADS
    heads = head_of(rows, stream)
    total = jnp.zeros((rows, values.shape[1]), jnp.float32)
    for h in range(HEADS):
        total = total + jnp.where(heads == h, values[h * rows : (h + 1) * rows], 0.0)
    return total


def lane_heads(stream):
    rows = lax.broadcasted_iota(jnp.int32, (128, WIDTHS[stream]), 0)
    return (rows == head_of(128, stream)).astype(jnp.float32)


def head_lanes(stream):
    rows = lax.broadcasted_iota(jnp.int32, (WIDTHS[stream], 128), 0) // HEAD_SIZES[stream]
    return (rows == lax.broadcasted_iota(jnp.int32, (WIDTHS[stream], 128), 1)).astype(jnp.float32)


def stack_columns(values):
    return jnp.concatenate([values[:, h : h + 1] for h in range(HEADS)], 0)


def one_micro_batch(rows):
    row = lax.broadcasted_iota(jnp.int32, (rows, 128), 0)
    key = lax.broadcasted_iota(jnp.int32, (rows, 128), 1)
    return (row // 8) % 2 == key // 64


def coupled_scores(stacks, key_refs):
    return sum(
        cols_product(stacks[n], key_refs[n][...]) * SCALES[n] for n in range(2)
    )


def open_kernel(
    found_ref, position_ref, index_ref, box_ref, proj_ref, qkv_ref, layout_ref,
    text_vec, layout_vec, slot_ref,
    text_sum_ref, layout_sum_ref, spatial_ref, key_text, value_text, key_layout, value_layout,
    query_ref, slot_text, slot_layout,
):
    found = found_ref[...].astype(jnp.float32).reshape(32, 4, 24, 128)
    embedded = (found[:, 0] + found[:, 1] + found[:, 2] + found[:, 3]).reshape(768, 128).T
    place = position_ref[...]
    place = jnp.concatenate([place, place], 0)
    text_sum = embedded + place[:, :768]
    text_sum_ref[...] = text_sum
    tables = (0, 1, 0, 1, 2, 3)
    number = lax.broadcasted_iota(jnp.int32, (128, 1024), 1)
    for k in range(6):
        hot = (number == index_ref[:, k : k + 1]).astype(LOW)
        rows = box_ref[pl.ds(1024 * tables[k], 1024), :]
        spatial_ref[:, pl.ds(128 * k, 128)] = plain_product(hot, rows).astype(LOW)
    layout_sum = place[:, 768:] + plain_product(spatial_ref[...], proj_ref[...])
    layout_sum_ref[...] = layout_sum
    query_ref[...] = jnp.zeros_like(query_ref)
    qkv = qkv_ref[...].reshape(2304, 768)
    weights = (qkv, layout_ref[pl.ds(0, 576), :])
    sums, vecs = (text_sum, layout_sum), (text_vec, layout_vec)
    keys, values, slots = (key_text, key_layout), (value_text, value_layout), (slot_text, slot_layout)
    for n in range(2):
        width, weight, vec = WIDTHS[n], weights[n], vecs[n]
        normed = norm_apply(sums[n], row_of(vec, 0), row_of(vec, 1))
        low = normed.astype(LOW)
        keys[n][...] = cols_product(low, weight[width : 2 * width]).astype(LOW)
        values[n][...] = (cols_product(low, weight[2 * width :]) + row_of(vec, 3)).astype(LOW)
        slot = exact_product(slot_ref[...], normed)
        slots[n][...] = slot
        start, size = QUERY_LANES[n]
        query_ref[:, pl.ds(start, size)] = (
            cols_product(slot.astype(LOW), weight[:width]) + row_of(vec, 2)
        ).astype(LOW)


def score_kernel(query_ref, key_text, value_text, key_layout, value_layout, out_ref):
    stacks = [
        stack_heads(query_ref[:, pl.ds(*QUERY_LANES[n])], n) for n in range(2)
    ]
    mask = one_micro_batch(64 * HEADS)
    scores = jnp.where(mask, coupled_scores(stacks, (key_text, key_layout)), NEGATIVE)
    top = jnp.max(scores, -1, keepdims=True)
    powers = jnp.where(mask, jnp.exp(scores - top), 0.0)
    total = jnp.sum(powers, -1, keepdims=True)
    low = powers.astype(LOW)
    out_ref[:, pl.ds(768, 256)] = jnp.zeros((64, 256), jnp.float32)
    for n, values in enumerate((value_text, value_layout)):
        out_ref[:, pl.ds(*QUERY_LANES[n])] = fold_heads(plain_product(low, values[...]), n)
    lane = lax.broadcasted_iota(jnp.int32, (64, 128), 1)
    tops = jnp.zeros((64, 128), jnp.float32)
    totals = jnp.ones((64, 128), jnp.float32)
    for h in range(HEADS):
        tops = jnp.where(lane == h, top[64 * h : 64 * h + 64], tops)
        totals = jnp.where(lane == h, total[64 * h : 64 * h + 64], totals)
    out_ref[:, pl.ds(1024, 128)] = tops
    out_ref[:, pl.ds(1152, 128)] = totals


def close_kernel(
    parts_ref, slot_text, slot_layout, out_w, up_w, down_w, layout_ref, layout_down,
    text_vec, layout_vec, head_ref, head_vec,
    att_text, att_layout, log_ref, mid_text, mid_layout, pre_text, pre_layout,
    end_text, end_layout, joined_ref, dense_ref, pick_ref,
):
    tops = [parts_ref[j, :, pl.ds(1024, 128)] for j in range(4)]
    top = jnp.maximum(jnp.maximum(tops[0], tops[1]), jnp.maximum(tops[2], tops[3]))
    shares = [jnp.exp(item - top) for item in tops]
    total = sum(shares[j] * parts_ref[j, :, pl.ds(1152, 128)] for j in range(4))
    log_ref[...] = top + jnp.log(total)
    shares = [item / total for item in shares]
    joined_ref[...] = jnp.zeros_like(joined_ref)
    streams = (
        (slot_text, text_vec, out_w, up_w, down_w, att_text, mid_text, pre_text, end_text),
        (slot_layout, layout_vec, layout_ref, layout_ref, layout_down, att_layout, mid_layout,
         pre_layout, end_layout),
    )
    for n, (slot, vec, out_r, up_r, down_r, att_r, mid_r, pre_r, end_r) in enumerate(streams):
        width = WIDTHS[n]
        spread = lane_heads(n)
        att = sum(
            parts_ref[j, :, pl.ds(*QUERY_LANES[n])] * exact_product(shares[j], spread)
            for j in range(4)
        )
        att_r[...] = att
        if n == 0:
            out_m, up_m = out_r[...].reshape(768, 768), up_r[...].reshape(3072, 768)
        else:
            out_m, up_m = out_r[pl.ds(576, 192), :], up_r[pl.ds(768, 768), :]
        mid = slot[...] + (cols_product(att.astype(LOW), out_m) + row_of(vec, 4))
        mid_r[...] = mid
        first = norm_apply(mid, row_of(vec, 5), row_of(vec, 6))
        pre = cols_product(first.astype(LOW), up_m) + hidden_bias(vec)
        pre_r[...] = pre
        end = first + (
            plain_product(gelu_value(pre).astype(LOW), down_r[...]) + row_of(vec, 11)
        )
        end_r[...] = end
        joined_ref[:, pl.ds(*QUERY_LANES[n])] = norm_apply(
            end, row_of(vec, 12), row_of(vec, 13)
        ).astype(LOW)
    dense = cols_product(joined_ref[:, pl.ds(0, 960)], head_ref[...]) + row_of(head_vec, 0)
    dense_ref[...] = dense
    pick_ref[...] = norm_apply(
        gelu_value(dense), row_of(head_vec, 1), row_of(head_vec, 2)
    ).astype(LOW)


def close_back_kernel(
    grad_ref, dense_ref, joined_ref, att_text, att_layout, log_ref, mid_text, mid_layout,
    pre_text, pre_layout, end_text, end_layout, out_w, up_w, down_w, layout_ref, layout_down,
    text_vec, layout_vec, head_ref, head_vec,
    back_ref, d_mid_text, d_mid_layout, d_head, d_out, d_up, d_down, d_layout, d_layout_down,
    d_text_vec, d_layout_vec, d_head_vec,
):
    dense = dense_ref[...]
    d_active, d_gain, d_shift = norm_back(gelu_value(dense), row_of(head_vec, 1), grad_ref[...])
    d_dense = (d_active * gelu_slope(dense)).astype(LOW)
    d_head_vec[0:1, :] = total_rows(d_dense)
    d_head_vec[1:2, :] = d_gain
    d_head_vec[2:3, :] = d_shift
    d_head[...] = rows_product(d_dense, joined_ref[:, pl.ds(0, 960)]).astype(LOW)
    d_joined = plain_product(d_dense, head_ref[...])
    back_ref[:, pl.ds(768, 256)] = jnp.zeros((16, 256), jnp.float32)
    delta = jnp.zeros((16, 128), jnp.float32)
    streams = (
        (text_vec, out_w, up_w, down_w, att_text, mid_text, pre_text, end_text,
         d_mid_text, d_out, d_up, d_down, d_text_vec),
        (layout_vec, layout_ref, layout_ref, layout_down, att_layout, mid_layout, pre_layout,
         end_layout, d_mid_layout, d_layout, d_layout, d_layout_down, d_layout_vec),
    )
    for n, (vec, out_r, up_r, down_r, att_r, mid_r, pre_r, end_r, d_mid_r, d_out_r, d_up_r,
            d_down_r, d_vec) in enumerate(streams):
        width = WIDTHS[n]
        if n == 0:
            out_m, up_m = out_r[...].reshape(768, 768), up_r[...].reshape(3072, 768)
        else:
            out_m, up_m = out_r[pl.ds(576, 192), :], up_r[pl.ds(768, 768), :]
        d_end, d_gain2, d_shift2 = norm_back(
            end_r[...], row_of(vec, 12), d_joined[:, QUERY_LANES[n][0] : sum(QUERY_LANES[n])]
        )
        d_branch2 = d_end.astype(LOW)
        mid, pre = mid_r[...], pre_r[...]
        low = gelu_value(pre).astype(LOW)
        d_pre = (cols_product(d_branch2, down_r[...]) * gelu_slope(pre)).astype(LOW)
        first_low = norm_apply(mid, row_of(vec, 5), row_of(vec, 6)).astype(LOW)
        for k in range(4):
            part = slice(width * k, width * (k + 1))
            d_down_r[pl.ds(width * k, width), :] = rows_product(low[:, part], d_branch2).astype(LOW)
            up_at = pl.ds(width * k, width) if n == 0 else pl.ds(192 + width * k, width)
            d_up_r[up_at, :] = rows_product(d_pre[:, part], first_low).astype(LOW)
            d_vec[7 + k : 8 + k, :] = total_rows(d_pre[:, part])
        d_first = d_end + plain_product(d_pre, up_m)
        d_mid, d_gain1, d_shift1 = norm_back(mid, row_of(vec, 5), d_first)
        d_mid_r[...] = d_mid
        d_branch1 = d_mid.astype(LOW)
        att = att_r[...]
        d_out_r[pl.ds(0, width), :] = rows_product(d_branch1, att.astype(LOW)).astype(LOW)
        d_att = plain_product(d_branch1, out_m).astype(LOW).astype(jnp.float32)
        back_ref[:, pl.ds(*QUERY_LANES[n])] = d_att
        delta = delta + exact_product(d_att * att, head_lanes(n))
        d_vec[0:4, :] = jnp.zeros((4, width), jnp.float32)
        for row, value in (
            (4, total_rows(d_branch1)),
            (5, d_gain1),
            (6, d_shift1),
            (11, total_rows(d_branch2)),
            (12, d_gain2),
            (13, d_shift2),
        ):
            d_vec[row : row + 1, :] = value
    back_ref[:, pl.ds(1024, 128)] = log_ref[...]
    back_ref[:, pl.ds(1152, 128)] = delta


def score_back_kernel(
    back_ref, query_ref, key_text, value_text, key_layout, value_layout,
    d_query, d_key_text, d_value_text, d_key_layout, d_value_layout,
):
    keys, values = (key_text, key_layout), (value_text, value_layout)
    stacks = [stack_heads(query_ref[:, pl.ds(*QUERY_LANES[n])], n) for n in range(2)]
    grads = [stack_heads(back_ref[:, pl.ds(*QUERY_LANES[n])], n).astype(LOW) for n in range(2)]
    logs = stack_columns(back_ref[:, pl.ds(1024, 128)])
    delta = stack_columns(back_ref[:, pl.ds(1152, 128)])
    mask = one_micro_batch(64 * HEADS)
    probs = jnp.where(mask, jnp.exp(jnp.where(mask, coupled_scores(stacks, keys) - logs, 0.0)), 0.0)
    d_probs = sum(cols_product(grads[n], values[n][...]) for n in range(2))
    d_scores = (probs * (d_probs - delta)).astype(LOW)
    low = probs.astype(LOW)
    d_query[:, pl.ds(768, 256)] = jnp.zeros((64, 256), jnp.float32)
    d_keys, d_values = (d_key_text, d_key_layout), (d_value_text, d_value_layout)
    for n in range(2):
        d_query[:, pl.ds(*QUERY_LANES[n])] = (
            fold_heads(plain_product(d_scores, keys[n][...]), n) * SCALES[n]
        )
        d_keys[n][...] = (rows_product(d_scores, stacks[n]) * SCALES[n]).astype(LOW)
        d_values[n][...] = rows_product(low, grads[n]).astype(LOW)


def open_back_kernel(
    parts_ref, d_key_text, d_value_text, d_key_layout, d_value_layout, d_mid_text, d_mid_layout,
    text_sum, layout_sum, slot_text, slot_layout, qkv_ref, layout_ref, proj_ref, spatial_ref,
    index_ref, text_vec, layout_vec, slot_turned,
    d_query_w, d_kv_w, d_layout, d_embedded, d_position, d_box, d_proj, d_text_vec, d_layout_vec,
):
    qkv = qkv_ref[...].reshape(2304, 768)
    streams = (
        (qkv, d_key_text, d_value_text, d_mid_text, text_sum, slot_text, text_vec, d_text_vec),
        (layout_ref[pl.ds(0, 576), :], d_key_layout, d_value_layout, d_mid_layout, layout_sum,
         slot_layout, layout_vec, d_layout_vec),
    )
    lows = []
    for n, (weight, d_key_r, d_value_r, d_mid_r, sum_r, slot_r, vec, d_vec) in enumerate(streams):
        width = WIDTHS[n]
        lanes = pl.ds(*QUERY_LANES[n])
        d_query = sum(parts_ref[j, :, lanes] for j in range(4)).astype(LOW)
        d_key, d_value = d_key_r[...], d_value_r[...]
        d_slot = d_mid_r[...] + plain_product(d_query, weight[:width])
        d_normed = (
            plain_product(d_key, weight[width : 2 * width])
            + plain_product(d_value, weight[2 * width :])
            + exact_product(slot_turned[...], d_slot)
        )
        sums = sum_r[...]
        low = norm_apply(sums, row_of(vec, 0), row_of(vec, 1)).astype(LOW)
        d_sum, d_gain, d_shift = norm_back(sums, row_of(vec, 0), d_normed)
        d_vec[...] = jnp.zeros_like(d_vec)
        for row, value in ((0, d_gain), (1, d_shift), (2, total_rows(d_query)), (3, total_rows(d_value))):
            d_vec[row : row + 1, :] = value
        slot_low = slot_r[...].astype(LOW)
        grads = (rows_product(d_query, slot_low), rows_product(d_key, low), rows_product(d_value, low))
        if n == 0:
            d_query_w[...] = grads[0].astype(LOW)
            d_kv_w[pl.ds(0, 768), :] = grads[1].astype(LOW)
            d_kv_w[pl.ds(768, 768), :] = grads[2].astype(LOW)
        else:
            for k in range(3):
                d_layout[pl.ds(192 * k, 192), :] = grads[k].astype(LOW)
        d_low = d_sum.astype(LOW)
        lows.append(d_low)
        wide = d_low.astype(jnp.float32)
        d_position[:, lanes] = wide[:64] + wide[64:]
        if n == 0:
            d_embedded[...] = wide.T.astype(LOW)
    d_spatial = cols_product(lows[1], proj_ref[...]).astype(LOW)
    d_proj[...] = rows_product(spatial_ref[...], lows[1]).astype(LOW)
    number = lax.broadcasted_iota(jnp.int32, (128, 1024), 1)
    for table, users in enumerate(((0, 2), (1, 3), (4,), (5,))):
        total = 0.0
        for k in users:
            hot = (number == index_ref[:, k : k + 1]).astype(LOW)
            total = total + rows_product(hot, d_spatial[:, 128 * k : 128 * k + 128])
        d_box[pl.ds(1024 * table, 1024), :] = total.astype(LOW)


def local_call(kernel, inputs, outputs, name):
    specs, arrays = [], []

    def spec(shape, index):
        return pl.BlockSpec(shape, lambda step: index, pipeline_mode=pl.Buffered(1))

    for item in inputs:
        array, shape, index = item if isinstance(item, tuple) else (item, item.shape, None)
        specs.append(spec(shape, index or (0,) * len(shape)))
        arrays.append(array)
    return pl.pallas_call(
        kernel,
        name=name,
        grid=(1,),
        out_shape=[jax.ShapeDtypeStruct(shape, dtype) for shape, dtype in outputs],
        in_specs=specs,
        out_specs=[spec(shape, (0,) * len(shape)) for shape, dtype in outputs],
        compiler_params=pltpu.CompilerParams(vmem_limit_bytes=56 * 1024 * 1024),
    )(*arrays)


PLANES = (("y", "z"), ("x", "z"), ("x", "y"))
LINES = ("x", "y", "z")
HEAD_BLOCK = 512
PLANE_STEPS = [(a, b) for a in range(4) for b in range(4) if (a, b) != (0, 0)]


def plane_peer(place, plane, a, b):
    return moved(moved(place, plane[0], a), plane[1], b)


def head_peers(place):
    peers = [
        plane_peer(place, plane, a, b)
        for plane in PLANES
        for a, b in PLANE_STEPS
        if (a and b) or plane == ("y", "z")
    ]
    peers += [moved(place, "x", step) for step in (1, 2, 3)]
    peers += [moved(moved(place, "x", step), "c", 1) for step in range(4)]
    return peers


def merge_logs(logs):
    top = logs[0]
    for item in logs[1:]:
        top = jnp.maximum(top, item)
    total = jnp.exp(logs[0] - top)
    for item in logs[1:]:
        total = total + jnp.exp(item - top)
    return top + jnp.log(total)


def head_kernel(
    limit_width, pick_ref, table_ref, label_ref, weight_ref, count_ref,
    grad_ref, d_table_ref, loss_ref,
    picked, table, logits, d_logits, part, acc, cross, near, far, line_in, plane_in, own_sem,
    plane_send, plane_recv, line_send, line_recv, pass_send, pass_recv,
    near_send, near_recv, far_send, far_recv, core_send, core_recv,
    back_send, back_recv, last_send, last_recv,
):
    place = my_place()
    sibling = moved(place, "c", 1)
    barrier = pltpu.get_barrier_semaphore()
    peers = head_peers(place)
    for peer in peers:
        pl.semaphore_signal(barrier, inc=1, device_id=device_of(peer), device_id_type=MESH)
    own = pltpu.make_async_copy(
        pick_ref, block_view(picked, place, "", None, place["c"]), own_sem
    )
    own.start()
    pl.semaphore_wait(barrier, len(peers))
    sends = []

    def go(copy):
        copy.start()
        sends.append(copy)
        return copy

    def third(k):
        return (256 * k, 256)

    flights = {}
    for k in range(3):
        here = block_view(picked, place, "", third(k), place["c"])
        for a, b in PLANE_STEPS:
            n = 4 * a + b - 1
            flights[(k, n)] = go(
                remote(
                    pick_ref.at[:, pl.ds(*third(k))], here, plane_send.at[k, n],
                    plane_recv.at[k, n], plane_peer(place, PLANES[k], a, b),
                )
            )
    table[...] = table_ref[...].astype(jnp.float32).T.astype(LOW)
    own.wait()
    lines, passes = {}, []

    def hand_over(k, n, where):
        passes.append(go(remote(where, where, pass_send.at[k, n], pass_recv.at[k, n], sibling)))

    for k in range(3):
        for a, b in PLANE_STEPS:
            flights[(k, 4 * a + b - 1)].wait_recv()
        sheet = block_view(picked, place, PLANES[k], third(k), place["c"])
        for step in (1, 2, 3):
            lines[(k, step)] = go(
                remote(
                    sheet, sheet, line_send.at[k, step - 1], line_recv.at[k, step - 1],
                    moved(place, LINES[k], step),
                )
            )
        hand_over(k, 0, sheet)
    for step in (1, 3, 2):
        for k in range(3):
            lines[(k, step)].wait_recv()
            origin = moved(place, LINES[k], -step)
            hand_over(k, step, block_view(picked, origin, PLANES[k], third(k), place["c"]))
    for copy in passes:
        copy.wait_recv()

    limit = limit_width - lax.axis_index("dp") * HEAD_BLOCK
    row = lax.broadcasted_iota(jnp.int32, (HEAD_BLOCK, 256), 0)
    valid = row < limit
    mine = place["x"] * 2 + place["c"]
    for chunk in range(8):
        high, mid = chunk // 4, chunk % 4
        lanes = pl.ds(256 * chunk, 256)
        values = cols_product(table[...], picked[high, mid].reshape(256, 768))
        values = jnp.where(valid, values, NEGATIVE)
        logits[:, lanes] = values
        top = jnp.max(values, 0, keepdims=True)
        total = jnp.sum(jnp.where(valid, jnp.exp(values - top), 0.0), 0, keepdims=True)
        hot = valid & (row == label_ref[:, lanes])
        near[mine, 0, :, lanes] = top + jnp.log(jnp.maximum(total, 1e-30))
        near[mine, 1, :, lanes] = jnp.sum(jnp.where(hot, values, 0.0), 0, keepdims=True)
    meets = []
    for n in range(1, 8):
        peer = moved(place, "x", n // 2)
        if n % 2:
            peer = moved(peer, "c", 1)
        meets.append(
            go(remote(near.at[mine], near.at[mine], near_send.at[n - 1], near_recv.at[n - 1], peer))
        )
    for copy in meets:
        copy.wait_recv()
    spot = place["y"] * 4 + place["z"]
    far[spot, 0] = merge_logs([near[n, 0] for n in range(8)])
    far[spot, 1] = sum(near[n, 1] for n in range(8))
    meets = []
    for a, b in PLANE_STEPS:
        n = 4 * a + b - 1
        peer = plane_peer(place, ("y", "z"), a, b)
        meets.append(go(remote(far.at[spot], far.at[spot], far_send.at[n], far_recv.at[n], peer)))
    for copy in meets:
        copy.wait_recv()
    log_total = merge_logs([far[n, 0] for n in range(16)])
    target = sum(far[n, 1] for n in range(16))
    loss = jnp.sum(count_ref[...] * (log_total - target), 1, keepdims=True)
    loss_ref[...] = jnp.broadcast_to(loss, loss_ref.shape)

    crossings = []
    for chunk in range(8):
        high, mid = chunk // 4, chunk % 4
        lanes = pl.ds(256 * chunk, 256)
        here = slice(256 * chunk, 256 * chunk + 256)
        hot = (valid & (row == label_ref[:, lanes])).astype(jnp.float32)
        powers = jnp.where(valid, jnp.exp(logits[:, lanes] - log_total[:, here]), 0.0)
        low = (weight_ref[:, lanes] * (powers - hot)).astype(LOW)
        d_logits[:, lanes] = low
        part[high, mid] = rows_product(low, table[...]).astype(LOW).reshape(4, 2, 2, 16, 768)
        crossings.append(
            go(
                remote(
                    part.at[high, mid, :, :, sibling["c"]], cross.at[high, mid],
                    core_send.at[chunk], core_recv.at[chunk], sibling,
                )
            )
        )
    for chunk in range(8):
        high, mid = chunk // 4, chunk % 4
        crossings[chunk].wait_recv()
        acc[high, mid] = part[high, mid, :, :, place["c"]] + cross[high, mid]

    legs = {}
    for k in range(3):
        for step in (1, 3, 2):
            there = moved(place, LINES[k], step)
            legs[(k, step)] = go(
                remote(
                    block_view(acc, there, PLANES[k], third(k)), line_in[k].at[step - 1],
                    back_send.at[k, step - 1], back_recv.at[k, step - 1], there,
                )
            )
    d_table = jnp.zeros((HEAD_BLOCK, 768), jnp.float32)
    for chunk in range(8):
        d_table = d_table + plain_product(
            d_logits[:, pl.ds(256 * chunk, 256)], picked[chunk // 4, chunk % 4].reshape(256, 768)
        )
    d_table_ref[...] = d_table.T.astype(LOW)
    ends = {}
    for k in range(3):
        for step in (1, 2, 3):
            legs[(k, step)].wait_recv()
        count, chunk_of = chunks_of("".join(PLANES[k]), place)
        for flat in range(count):
            block, inner = chunk_of(flat)
            where = block + (slice(None), pl.ds(*third(k)))
            total = acc[where].astype(jnp.float32)
            for step in (1, 2, 3):
                total = total + line_in[k][(step - 1,) + inner].astype(jnp.float32)
            acc[where] = total.astype(LOW)
        for a, b in PLANE_STEPS:
            n = 4 * a + b - 1
            there = plane_peer(place, PLANES[k], a, b)
            ends[(k, n)] = go(
                remote(
                    block_view(acc, there, "", third(k)), plane_in.at[k, n],
                    last_send.at[k, n], last_recv.at[k, n], there,
                )
            )
    home = (place["x"] // 2, place["y"], place["z"], place["x"] % 2)
    for k in range(3):
        total = acc[home + (slice(None), pl.ds(*third(k)))].astype(jnp.float32)
        for n in range(15):
            ends[(k, n)].wait_recv()
            total = total + plane_in[k, n].astype(jnp.float32)
        grad_ref[:, pl.ds(*third(k))] = total
    for copy in sends:
        copy.wait_send()


def head_step(picked, table, labels, weights, counts, width, collective_id):
    sems = pltpu.SemaphoreType.DMA
    everyone = (2, 4, 4, 2, 2, 16, 768)
    half = (2, 4, 4, 2, 16, 768)
    line_slots = [
        pltpu.VMEM((3,) + open_shape("".join(PLANES[k])) + (16, 256), LOW) for k in range(3)
    ]

    def kernel(*refs):
        head_kernel(width, *refs[:17], refs[17:20], *refs[20:])

    return pl.pallas_call(
        kernel,
        out_shape=[
            jax.ShapeDtypeStruct((16, 768), jnp.float32),
            jax.ShapeDtypeStruct((768, HEAD_BLOCK), LOW),
            jax.ShapeDtypeStruct((8, 128), jnp.float32),
        ],
        in_specs=[pl.BlockSpec(memory_space=pltpu.VMEM)] * 5,
        out_specs=[pl.BlockSpec(memory_space=pltpu.VMEM)] * 3,
        scratch_shapes=[
            pltpu.VMEM(everyone, LOW),
            pltpu.VMEM((HEAD_BLOCK, 768), LOW),
            pltpu.VMEM((HEAD_BLOCK, 2048), jnp.float32),
            pltpu.VMEM((HEAD_BLOCK, 2048), LOW),
            pltpu.VMEM(everyone, LOW),
            pltpu.VMEM(half, LOW),
            pltpu.VMEM(half, LOW),
            pltpu.VMEM((8, 2, 1, 2048), jnp.float32),
            pltpu.VMEM((16, 2, 1, 2048), jnp.float32),
        ]
        + line_slots
        + [
            pltpu.VMEM((3, 15, 16, 256), LOW),
            sems(()),
            sems((3, 15)),
            sems((3, 15)),
            sems((3, 3)),
            sems((3, 3)),
            sems((3, 4)),
            sems((3, 4)),
            sems((7,)),
            sems((7,)),
            sems((15,)),
            sems((15,)),
            sems((8,)),
            sems((8,)),
            sems((3, 3)),
            sems((3, 3)),
            sems((3, 15)),
            sems((3, 15)),
        ],
        compiler_params=pltpu.CompilerParams(
            collective_id=collective_id, has_side_effects=True, vmem_limit_bytes=56 * 1024 * 1024
        ),
    )(picked, table, labels, weights, counts)


def device_at(number):
    return number // 4, number % 4


def start_kernel(
    pieces, count, width, notes_ref, levels_ref, blocks_ref, *refs
):
    ins, refs = refs[:count], refs[count:]
    notes_out, found_out, table_out = refs[:3]
    outs, refs = refs[3 : 3 + count], refs[3 + count :]
    notes_all, found, note_sems, found_sems, table_sems = refs[:5]
    plane_send, plane_recv, ring_send, ring_recv, pass_send, pass_recv = refs[5:]
    place = my_place()
    sibling = moved(place, "c", 1)
    me = lax.axis_index("dp") * 4 + lax.axis_index("vocab")
    own_dp, own_vocab = device_at(me)
    barrier = pltpu.get_barrier_semaphore()

    def greet_one(step, carry):
        pl.semaphore_signal(
            barrier, inc=1, device_id=device_at((me + step) % 128), device_id_type=MESH
        )
        return carry

    lax.fori_loop(1, 128, greet_one, 0)
    pl.semaphore_wait(barrier, 127)

    def to_device(src, dst, sems, device):
        return pltpu.make_async_remote_copy(
            src_ref=src, dst_ref=dst, send_sem=sems.at[0], recv_sem=sems.at[1],
            device_id=device, device_id_type=MESH,
        )

    planes = []
    for piece, (number, lanes, order) in enumerate(pieces):
        here = block_view(outs[number], place, "", lanes, place["c"])
        src = ins[number].at[:, lanes_at(ins[number], lanes)]
        pltpu.make_async_copy(src, here, plane_recv.at[piece]).start()
        for a, b in PLANE_STEPS:
            copy = remote(
                src, here, plane_send.at[piece, 4 * a + b - 1], plane_recv.at[piece],
                plane_peer(place, PLANES[order], a, b),
            )
            copy.start()
            planes.append(copy)
    own_note = pltpu.make_async_copy(notes_ref, notes_all.at[me], note_sems.at[1])
    own_note.start()

    def send_note(step, carry):
        to_device(notes_ref, notes_all.at[me], note_sems, device_at((me + step) % 128)).start()
        return carry

    lax.fori_loop(1, 128, send_note, 0)

    pltpu.make_async_copy(
        blocks_ref.at[own_dp], table_out.at[own_dp], table_sems.at[1]
    ).start()

    def send_block(step, carry):
        other = (own_dp + step) % 32
        to_device(
            blocks_ref.at[other], table_out.at[own_dp], table_sems, (other, own_vocab)
        ).start()
        return carry

    lax.fori_loop(1, 32, send_block, 0)

    rows = found.shape[1]
    levels = levels_ref.shape[0] // rows

    def pick(step, carry):
        block = (step + me // 8) % 16
        ids = jnp.concatenate([notes_all[block * 8 + n, 0:1, :] for n in range(8)], 1)
        local = ids - own_vocab * width
        high = jnp.where((local >= 0) & (local < width), local >> 8, -1)
        low = local & 255
        hot = (lax.broadcasted_iota(jnp.int32, (SPAN_LOW, 1024), 0) == low).astype(LOW)
        total = jnp.zeros((rows, 1024), jnp.float32)
        group = 5
        for first in range(0, levels, group):
            values = jnp.dot(
                levels_ref[pl.ds(first * rows, group * rows), :],
                hot,
                preferred_element_type=jnp.float32,
            )
            for level in range(group):
                total = total + jnp.where(
                    high == first + level, values[level * rows : (level + 1) * rows], 0.0
                )
        total = total.astype(LOW)
        for n in range(8):
            there = block * 8 + n
            found[there] = total[:, 128 * n : 128 * n + 128]

            @pl.when(there != me)
            def _():
                to_device(
                    found.at[there], found_out.at[me], found_sems, device_at(there)
                ).start()

        return carry

    rings, passes = {}, []

    def spot(number, origin, dims, lanes):
        return block_view(outs[number], origin, dims, lanes, place["c"])

    def send(way, piece, src, target):
        copy = remote(src, src, ring_send.at[way, piece], ring_recv.at[way, piece], target)
        copy.start()
        rings[(way, piece)] = copy

    def hand_over(way, piece, where):
        copy = remote(where, where, pass_send.at[way, piece], pass_recv.at[way, piece], sibling)
        copy.start()
        passes.append(copy)

    for piece, (number, lanes, order) in enumerate(pieces):
        sheet = spot(number, place, PLANES[order], lanes)
        pltpu.make_async_copy(sheet, sheet, plane_recv.at[piece]).wait()
        for way, step in ((0, 1), (1, -1)):
            send(way, piece, sheet, moved(place, LINES[order], step))
        hand_over(2, piece, sheet)
    pltpu.make_async_copy(notes_all, notes_all, note_sems.at[1]).wait()
    lax.fori_loop(0, 8, pick, 0)
    for piece, (number, lanes, order) in enumerate(pieces):
        dim, dims = LINES[order], PLANES[order]
        parts = halves(lanes, piece)
        for way, step in ((0, 1), (1, -1)):
            rings[(way, piece)].wait_recv()
            origin = moved(place, dim, -step)
            if parts[way] is not False:
                send(2 + way, piece, spot(number, origin, dims, parts[way]), moved(place, dim, step))
            hand_over(way, piece, spot(number, origin, dims, lanes))
    lax.fori_loop(8, 16, pick, 0)
    own_found = pltpu.make_async_copy(found.at[me], found_out.at[me], found_sems.at[1])
    own_found.start()
    for piece, (number, lanes, order) in enumerate(pieces):
        parts = halves(lanes, piece)
        for way in range(2):
            if parts[way] is not False:
                rings[(2 + way, piece)].wait_recv()
        far = moved(place, LINES[order], 2)
        hand_over(3, piece, spot(number, far, PLANES[order], lanes))
    notes_out[...] = notes_all[...]
    pltpu.make_async_copy(found_out, found_out, found_sems.at[1]).wait()
    pltpu.make_async_copy(table_out, table_out, table_sems.at[1]).wait()
    for sems, ref, size in (
        (note_sems, notes_all, 127), (found_sems, found, 127), (table_sems, blocks_ref, 31)
    ):
        sent = ref.at[pl.ds(0, size)]
        pltpu.make_async_copy(sent, sent, sems.at[0]).wait()
    for copy in planes + list(rings.values()):
        copy.wait_send()
    for copy in passes:
        copy.wait()


def start_step(notes, levels, blocks, arrays, pieces, width, collective_id):
    count, total = len(arrays), len(pieces)
    sems = pltpu.SemaphoreType.DMA
    anywhere = pl.BlockSpec(memory_space=pl.ANY)
    local = pl.BlockSpec(memory_space=pltpu.VMEM)
    rows = blocks.shape[1]
    notes_all, found, table, *outs = pl.pallas_call(
        functools.partial(start_kernel, pieces, count, width),
        out_shape=[
            jax.ShapeDtypeStruct((128,) + notes.shape, jnp.int32),
            jax.ShapeDtypeStruct((128, rows, 128), LOW),
            jax.ShapeDtypeStruct(blocks.shape, LOW),
        ]
        + [jax.ShapeDtypeStruct((2, 4, 4, 2, 2) + a.shape, a.dtype) for a in arrays],
        in_specs=[local, local, anywhere] + [anywhere] * count,
        out_specs=[local, anywhere, anywhere] + [anywhere] * count,
        scratch_shapes=[
            pltpu.VMEM((128,) + notes.shape, jnp.int32),
            pltpu.VMEM((128, rows, 128), LOW),
            sems((2,)),
            sems((2,)),
            sems((2,)),
            sems((total, 15)),
            sems((total,)),
            sems((4, total)),
            sems((4, total)),
            sems((4, total)),
            sems((4, total)),
        ],
        cost_estimate=LONG,
        compiler_params=pltpu.CompilerParams(
            collective_id=collective_id, has_side_effects=True, vmem_limit_bytes=40 * 1024 * 1024
        ),
    )(notes, levels, blocks, *arrays)
    return notes_all, found, table, [o.reshape((128,) + a.shape) for o, a in zip(outs, arrays)]


def finish_kernel(sources, pieces, count, width, *refs):
    total = len(pieces)
    ins, refs = refs[: len(sources)], refs[len(sources) :]
    text_ref, notes_ref, head_ref, refs = refs[0], refs[1], refs[2], refs[3:]
    outs, table_ref, square_ref, refs = refs[:count], refs[count], refs[count + 1], refs[count + 2 :]
    accs, crosses, refs = refs[:count], refs[count : 2 * count], refs[2 * count :]
    slots, planes, refs = refs[: 4 * total], refs[4 * total : 5 * total], refs[5 * total :]
    text_all, spread, near, far = refs[:4]
    own_sem, core_sems, line_sems, plane_sems, text_sems, near_sems, far_sems = refs[4:]
    place = my_place()
    sibling = moved(place, "c", 1)
    me = lax.axis_index("dp") * 4 + lax.axis_index("vocab")
    own_dp, own_vocab = device_at(me)
    barrier = pltpu.get_barrier_semaphore()

    def greet_one(step, carry):
        pl.semaphore_signal(
            barrier, inc=1, device_id=device_at((me + step) % 128), device_id_type=MESH
        )
        return carry

    lax.fori_loop(1, 128, greet_one, 0)
    pl.semaphore_wait(barrier, 127)
    started = []

    def go(src, dst, sems, index, target):
        copy = remote(src, dst, sems.at[(0,) + index], sems.at[(1,) + index], target)
        copy.start()
        started.append(copy)
        return copy

    def add(number, lanes, at, dims, others):
        acc = accs[number]
        count, chunk = chunks_of(dims, at)

        def body(flat, carry):
            block, inner = chunk(flat)
            where = block + (slice(None), lanes_at(acc, lanes))
            parts = [
                other[inner] if index is None else other[block + index] for other, index in others
            ]
            if len(parts) == 1:
                acc[where] = acc[where] + parts[0]
            else:
                wide = [part.astype(jnp.float32) for part in [acc[where]] + parts]
                acc[where] = sum(wide).astype(acc.dtype)
            return carry

        if count == 1:
            body(0, 0)
        else:
            lax.fori_loop(0, count, body, 0)

    first, pair = {}, 0
    for piece, (number, lanes, order) in enumerate(pieces):
        for index, (owner, high, mids) in enumerate(sources):
            if owner != number:
                continue
            every = slice(None)
            run = lanes_at(accs[number], lanes)
            at = (pl.ds(*high), pl.ds(*mids), every, every, every, run)
            src = (every, every, every, every)
            cross = go(
                ins[index].at[src + (sibling["c"], every, run)], crosses[number].at[at],
                core_sems, (pair,), sibling,
            )
            own = pltpu.make_async_copy(
                ins[index].at[src + (place["c"], every, run)], accs[number].at[at], own_sem.at[pair]
            )
            own.start()
            first.setdefault(piece, []).append((cross, own))
            pair += 1

    def text_copy(block, device):
        return pltpu.make_async_remote_copy(
            src_ref=text_ref.at[block], dst_ref=text_all.at[me], send_sem=text_sems.at[0],
            recv_sem=text_sems.at[1], device_id=device, device_id_type=MESH,
        )

    pltpu.make_async_copy(text_ref.at[own_dp], text_all.at[me], text_sems.at[1]).start()

    def send_text(step, carry):
        there = (me + step) % 128
        text_copy(there // 4, device_at(there)).start()
        return carry

    rings = {}

    def send_opposite(piece):
        number, lanes, order = pieces[piece]
        parts = halves(lanes, piece)
        there = moved(place, LINES[order], 2)
        for way, step in ((0, 1), (1, -1)):
            if parts[way] is not False:
                rings[(way, piece)] = go(
                    block_view(accs[number], there, PLANES[order], parts[way]),
                    slots[way * total + piece], line_sems, (way, piece),
                    moved(place, LINES[order], step),
                )

    for piece, (number, lanes, order) in enumerate(pieces):
        for cross, own in first[piece]:
            own.wait()
            cross.wait_recv()
        run = (slice(None), lanes_at(accs[number], lanes))
        add(number, lanes, place, "xyz", [(crosses[number], run)])
        send_opposite(piece)
        if piece == 2:
            lax.fori_loop(1, 128, send_text, 0)

    rows = text_all.shape[1]
    levels = head_ref.shape[0] // rows
    table_ref[...] = head_ref[...]

    def scatter(block, carry):
        ids = jnp.concatenate([notes_ref[block * 8 + n, 0:1, :] for n in range(8)], 1)
        local = ids - own_vocab * width
        high = jnp.where((local >= 0) & (local < width), local >> 8, -1)
        hot = (lax.broadcasted_iota(jnp.int32, (SPAN_LOW, 1024), 0) == (local & 255)).astype(LOW)
        grad = jnp.concatenate([text_all[block * 8 + n] for n in range(8)], 1).astype(jnp.float32)
        for level in range(0, levels, 2):
            spread[pl.ds(level * rows, 2 * rows), :] = jnp.concatenate(
                [jnp.where(high == level + n, grad, 0.0) for n in range(2)], 0
            ).astype(LOW)
        group = 10 * rows
        for start in range(0, levels * rows, group):
            table_ref[pl.ds(start, group), :] += cols_product(spread[pl.ds(start, group), :], hot)
        return carry

    for piece, (number, lanes, order) in enumerate(pieces):
        parts = halves(lanes, piece)
        for way, step in ((0, 1), (1, -1)):
            there = moved(place, LINES[order], step)
            if parts[way] is not False:
                rings[(way, piece)].wait_recv()
                add(number, parts[way], there, PLANES[order], [(slots[way * total + piece], None)])
            rings[(2 + way, piece)] = go(
                block_view(accs[number], there, PLANES[order], lanes),
                slots[(2 + way) * total + piece], line_sems, (2 + way, piece), there,
            )
    whole = pltpu.make_async_copy(text_all, text_all, text_sems.at[1])
    whole.wait()
    lax.fori_loop(0, 10, scatter, 0)
    for piece, (number, lanes, order) in enumerate(pieces):
        for way in range(2):
            rings[(2 + way, piece)].wait_recv()
        add(
            number, lanes, place, PLANES[order],
            [(slots[(2 + way) * total + piece], None) for way in range(2)],
        )
        for a, b in PLANE_STEPS:
            there = plane_peer(place, PLANES[order], a, b)
            remote(
                block_view(accs[number], there, "", lanes), planes[piece].at[4 * a + b - 1],
                plane_sems.at[0, piece], plane_sems.at[1, piece], there,
            ).start()
    lax.fori_loop(10, 16, scatter, 0)
    home = (place["x"] // 2, place["y"], place["z"], place["x"] % 2)
    square = jnp.zeros((1, 1), jnp.float32)

    def squared(value):
        return jnp.sum(jnp.sum(value * value, 1, keepdims=True), 0, keepdims=True)

    for piece, (number, lanes, order) in enumerate(pieces):
        pltpu.make_async_copy(planes[piece], planes[piece], plane_sems.at[1, piece]).wait()
        where = (slice(None), lanes_at(accs[number], lanes))
        value = accs[number][home + where].astype(jnp.float32)
        for n in range(15):
            value = value + planes[piece][n].astype(jnp.float32)
        outs[number][where] = value
        square = square + squared(value)
    square = square + squared(table_ref[...])

    mine = place["x"] * 2 + place["c"]
    near[mine] = jnp.broadcast_to(square, (8, 128))
    meets = []
    for n in range(1, 8):
        peer = moved(place, "x", n // 2)
        if n % 2:
            peer = moved(peer, "c", 1)
        meets.append(go(near.at[mine], near.at[mine], near_sems, (n - 1,), peer))
    for copy in meets:
        copy.wait_recv()
    spot = place["y"] * 4 + place["z"]
    far[spot] = sum(near[n] for n in range(8))
    meets = []
    for a, b in PLANE_STEPS:
        peer = plane_peer(place, ("y", "z"), a, b)
        meets.append(go(far.at[spot], far.at[spot], far_sems, (4 * a + b - 1,), peer))
    for copy in meets:
        copy.wait_recv()
    square_ref[...] = sum(far[n] for n in range(16))
    for piece in range(total):
        pltpu.make_async_copy(planes[piece], planes[piece], plane_sems.at[0, piece]).wait()
    sent = text_all.at[pl.ds(0, 127)]
    pltpu.make_async_copy(sent, sent, text_sems.at[0]).wait()
    for copy in started:
        copy.wait_send()


def finish_step(arrays, text, notes, head_levels, sources, pieces, width, collective_id):
    shapes, views = {}, []
    for array, (owner, high, mids) in zip(arrays, sources):
        shapes[owner] = array.shape[1:]
        views.append(array.reshape((high[1], mids[1], 4, 2, 2) + array.shape[1:]))
    count, total = len(shapes), len(pieces)
    pairs = sum(owner == piece[0] for piece in pieces for owner, high, mids in sources)
    scratch = [pltpu.VMEM((2, 4, 4, 2) + shapes[n], LOW) for n in range(count)] * 2
    widths = []
    for piece, (number, lanes, order) in enumerate(pieces):
        parts = halves(lanes, piece)
        widths.append([shapes[number][1] if part is None else part for part in
                       [p if p in (None, False) else p[1] for p in (*parts, lanes, lanes)]])
    for way in range(4):
        for piece, (number, lanes, order) in enumerate(pieces):
            wide = widths[piece][way]
            if wide is False:
                scratch.append(pltpu.VMEM((8, 128), LOW))
            else:
                rest = open_shape("".join(PLANES[order]))
                scratch.append(pltpu.VMEM(rest + (shapes[number][0], wide), LOW))
    for piece, (number, lanes, order) in enumerate(pieces):
        scratch.append(pltpu.VMEM((15, shapes[number][0], widths[piece][2]), LOW))
    rows = text.shape[1]
    sems = pltpu.SemaphoreType.DMA
    scratch += [
        pltpu.VMEM((128, rows, 128), LOW),
        pltpu.VMEM((head_levels.shape[0], 1024), LOW),
        pltpu.VMEM((8, 8, 128), jnp.float32),
        pltpu.VMEM((16, 8, 128), jnp.float32),
        sems((pairs,)),
        sems((2, pairs)),
        sems((2, 4, total)),
        sems((2, total)),
        sems((2,)),
        sems((2, 7)),
        sems((2, 15)),
    ]
    local = pl.BlockSpec(memory_space=pltpu.VMEM)
    return pl.pallas_call(
        functools.partial(finish_kernel, sources, pieces, count, width),
        out_shape=[jax.ShapeDtypeStruct(shapes[n], jnp.float32) for n in range(count)]
        + [
            jax.ShapeDtypeStruct(head_levels.shape, jnp.float32),
            jax.ShapeDtypeStruct((8, 128), jnp.float32),
        ],
        in_specs=[pl.BlockSpec(memory_space=pl.ANY)] * len(arrays) + [local] * 3,
        out_specs=[local] * (count + 2),
        scratch_shapes=scratch,
        cost_estimate=LONG,
        compiler_params=pltpu.CompilerParams(
            collective_id=collective_id, has_side_effects=True, vmem_limit_bytes=60 * 1024 * 1024
        ),
    )(*views, text, notes, head_levels)


def thirds(number):
    return [(number, (256 * k, 256), k) for k in range(3)]


GATHER_PIECES = thirds(0) + thirds(1) + [(2, (0, 512), 0), (2, (512, 448), 2), (3, None, 1)]
REDUCE_PIECES = (
    thirds(0)
    + thirds(1)
    + [(2, None, 0), (3, None, 2), (4, None, 1), (5, None, 1), (6, None, 2), (7, None, 2), (8, None, 0)]
)
WHOLE = ((0, 2), (0, 4))
REDUCE_SOURCES = [
    (0, (0, 1), (0, 1)),
    (0, (0, 1), (1, 2)),
    (0, (0, 1), (3, 1)),
    (0, (1, 1), (0, 4)),
] + [(number,) + WHOLE for number in range(1, 9)]


def pack(masters):
    word, position, box, text, down, layout, layout_down, head, vector = [
        m.astype(LOW) for m in masters
    ]
    box = box.reshape(2, 16, 128)
    small = jnp.concatenate(
        [
            jnp.concatenate([box[0], box[1]], 1),
            jnp.pad(
                jnp.concatenate(
                    [
                        layout.T,
                        layout_down[0],
                        layout_down[1],
                        jnp.pad(vector, (0, 192 - vector.shape[0]))[None],
                    ],
                    0,
                ),
                ((0, 7), (0, 64)),
            ),
        ],
        0,
    )
    return [text.T, down, jnp.concatenate([head.T, position], 0), small]


def unpack(gathered):
    text, down, wide, small = gathered
    box = small[:, :16].reshape(128, 2, 8, 2, 128).transpose(3, 1, 0, 2, 4)
    return dict(
        text=text,
        down=down.reshape(3072, 768),
        head=wide[:, :6].reshape(768, 960),
        box=box.reshape(4096, 128),
        layout=small[:, 16:28, :192].reshape(1536, 192),
        layout_down=small[:, 28:34, :192].reshape(768, 192),
        box_proj=small[:, 34:40, :192].reshape(768, 192),
        position=wide[:, 6:].reshape(640, 960),
        vector=small[:, 40, :123].reshape(15744),
    )


def reduce_weights(grads, text, notes, head_levels, width):
    shards = finish_step(
        [
            grads["query"].reshape(16, 48, 768),
            grads["key_value"].reshape(32, 48, 768),
            grads["out"].reshape(16, 48, 768),
            grads["up"].reshape(64, 48, 768),
            grads["down"].reshape(128, 24, 768),
            grads["head"].reshape(128, 6, 960),
            grads["position"].reshape(128, 5, 960),
            grads["layout"].reshape(128, 12, 192),
            grads["layout_down"].reshape(128, 6, 192),
            grads["box_proj"].reshape(128, 6, 192),
            grads["box"].reshape(4, 128, 8, 128).transpose(1, 0, 2, 3).reshape(128, 32, 128),
            grads["vector"].reshape(128, 1, 123),
        ],
        text,
        notes,
        head_levels,
        REDUCE_SOURCES,
        REDUCE_PIECES,
        width,
        4,
    )
    text, down, head, position, layout, layout_down, box_proj, box, vector, table, square = shards
    return table, square, [
        position,
        box.reshape(4, 8, 128),
        text.T,
        down,
        layout.T,
        jnp.stack([layout_down, box_proj]),
        head.T,
        vector[0],
    ]


def on_device(
    token_ids,
    box_coords,
    intersection_flags,
    masked_rows,
    masked_labels,
    *weights,
):
    triples = [tuple(weights[3 * n : 3 * n + 3]) for n in range(9)]
    masters = [entry[0] for entry in triples]
    word_table = masters[0]
    dp = lax.axis_index("dp")
    vocab = lax.axis_index("vocab")
    shard_width = word_table.shape[1]
    table_rows = word_table.shape[0]
    levels = -(-shard_width // SPAN_LOW)

    row_hot = masked_rows[:, :, None] == jnp.arange(64)[None, None, :]
    counted = jnp.sum(jnp.where(row_hot & (intersection_flags == 0)[:, None, :], 1, 0), 2)
    slot_hot = jnp.concatenate(
        [
            jnp.pad(row_hot[0], ((0, 0), (0, 64))),
            jnp.pad(row_hot[1], ((0, 0), (64, 0))),
        ],
        0,
    )
    slot_hot_wide = slot_hot.astype(jnp.float32)
    f32 = jnp.float32

    notes = jnp.concatenate(
        [
            token_ids.reshape(1, 128),
            jnp.concatenate(
                [masked_labels.reshape(1, 16), counted.reshape(1, 16), jnp.zeros((1, 96), jnp.int32)], 1
            ),
        ],
        0,
    )
    table_low = word_table.astype(LOW)
    table_levels = (
        jnp.pad(table_low, ((0, 0), (0, levels * SPAN_LOW - shard_width)))
        .reshape(table_rows, levels, SPAN_LOW)
        .transpose(1, 0, 2)
        .reshape(levels * table_rows, SPAN_LOW)
    )
    table_blocks = (
        jnp.pad(table_low, ((0, 0), (0, 32 * HEAD_BLOCK - shard_width)))
        .reshape(table_rows, 32, HEAD_BLOCK)
        .transpose(1, 0, 2)
    )
    notes_all, found, table_head, gathered = start_step(
        notes, table_levels, table_blocks, pack(masters), GATHER_PIECES, shard_width, 1
    )
    table_head = table_head.reshape(768, HEAD_BLOCK)
    full = unpack(gathered)
    labels_all = notes_all[:, 1, :16].reshape(2048)
    counted_all = notes_all[:, 1, 16:32].reshape(2048).astype(jnp.float32)
    total_count = jnp.sum(counted_all)

    vector = full["vector"].astype(jnp.float32)
    text_vec = vector[:10752].reshape(14, 768)
    layout_vec = vector[10752:13440].reshape(14, 192)
    head_vec = vector[13440:].reshape(3, 768)
    position_own = lax.dynamic_slice_in_dim(full["position"], vocab * 64, 64, 0).astype(f32)
    boxes = box_coords.reshape(4, 128)
    box_index = jnp.stack(
        [
            boxes[0],
            boxes[1],
            boxes[2],
            boxes[3],
            jnp.abs(boxes[3] - boxes[1]),
            jnp.abs(boxes[2] - boxes[0]),
            boxes[0],
            boxes[0],
        ],
        1,
    )
    qkv = (full["text"], (48, 48, 768), (0, 0, 0))
    out_w = (full["text"], (16, 48, 768), (3, 0, 0))
    up_w = (full["text"], (64, 48, 768), (1, 0, 0))
    text_sum, layout_sum, spatial, *kv, query, slot_text, slot_layout = local_call(
        open_kernel,
        [
            found,
            position_own,
            box_index,
            full["box"],
            full["box_proj"],
            qkv,
            full["layout"],
            text_vec,
            layout_vec,
            slot_hot_wide,
        ],
        [
            ((128, 768), f32),
            ((128, 192), f32),
            ((128, 768), LOW),
            ((128, 768), LOW),
            ((128, 768), LOW),
            ((128, 192), LOW),
            ((128, 192), LOW),
            ((16, 1024), LOW),
            ((16, 768), f32),
            ((16, 192), f32),
        ],
        "open_streams",
    )
    query_all = lax.all_gather(query, "vocab", axis=0, tiled=True)
    (partial,) = local_call(score_kernel, [query_all, *kv], [((64, 1280), f32)], "partial_attention")
    partial = lax.all_to_all(partial.reshape(4, 16, 1280), "vocab", 0, 0, tiled=True)
    weights_close = [out_w, up_w, full["down"], full["layout"], full["layout_down"]]
    vectors_close = [text_vec, layout_vec, full["head"], head_vec]
    (att_text, att_layout, log_total, mid_text, mid_layout, pre_text, pre_layout, end_text,
     end_layout, joined, dense, picked) = local_call(
        close_kernel,
        [partial, slot_text, slot_layout] + weights_close + vectors_close,
        [
            ((16, 768), f32),
            ((16, 192), f32),
            ((16, 128), f32),
            ((16, 768), f32),
            ((16, 192), f32),
            ((16, 3072), f32),
            ((16, 768), f32),
            ((16, 768), f32),
            ((16, 192), f32),
            ((16, 1024), LOW),
            ((16, 768), f32),
            ((16, 768), LOW),
        ],
        "close_streams",
    )
    d_picked, table_head_grad, loss = head_step(
        picked,
        table_head,
        (labels_all - vocab * shard_width - dp * HEAD_BLOCK)[None],
        (counted_all / total_count)[None],
        counted_all[None],
        shard_width,
        3,
    )
    loss_total = loss[0, 0]
    table_head_grad = lax.all_to_all(
        table_head_grad.reshape(32, 24, HEAD_BLOCK), "dp", 0, 0, tiled=True
    )
    (back, d_mid_text, d_mid_layout, d_head, d_out, d_up, d_down, d_layout_close, d_layout_down,
     d_text_vec, d_layout_vec, d_head_vec) = local_call(
        close_back_kernel,
        [d_picked, dense, joined, att_text, att_layout, log_total, mid_text, mid_layout]
        + [pre_text, pre_layout, end_text, end_layout]
        + weights_close
        + vectors_close,
        [
            ((16, 1280), f32),
            ((16, 768), f32),
            ((16, 192), f32),
            ((768, 960), LOW),
            ((768, 768), LOW),
            ((3072, 768), LOW),
            ((3072, 768), LOW),
            ((960, 192), LOW),
            ((768, 192), LOW),
            ((14, 768), f32),
            ((14, 192), f32),
            ((3, 768), f32),
        ],
        "close_streams_back",
    )
    back = lax.all_gather(back, "vocab", axis=0, tiled=True)
    d_query, *d_kv = local_call(
        score_back_kernel,
        [back, query_all, *kv],
        [
            ((64, 1024), f32),
            ((128, 768), LOW),
            ((128, 768), LOW),
            ((128, 192), LOW),
            ((128, 192), LOW),
        ],
        "attention_back",
    )
    d_query = lax.all_to_all(d_query.reshape(4, 16, 1024), "vocab", 0, 0, tiled=True)
    (d_query_w, d_kv_w, d_layout_open, d_embedded, d_position, d_box, d_proj, d_text_open,
     d_layout_vec_open) = local_call(
        open_back_kernel,
        [d_query, *d_kv, d_mid_text, d_mid_layout, text_sum, layout_sum, slot_text, slot_layout]
        + [qkv, full["layout"], full["box_proj"], spatial, box_index, text_vec, layout_vec]
        + [slot_hot_wide.T],
        [
            ((768, 768), LOW),
            ((1536, 768), LOW),
            ((576, 192), LOW),
            ((768, 128), LOW),
            ((64, 960), f32),
            ((4096, 128), LOW),
            ((768, 192), LOW),
            ((14, 768), f32),
            ((14, 192), f32),
        ],
        "open_streams_back",
    )
    head_levels = (
        table_head_grad.transpose(1, 0, 2)
        .reshape(table_rows, 32 * HEAD_BLOCK)[:, : levels * SPAN_LOW]
        .reshape(table_rows, levels, SPAN_LOW)
        .transpose(1, 0, 2)
        .reshape(levels * table_rows, SPAN_LOW)
        .astype(f32)
    )
    d_positions = lax.dynamic_update_slice_in_dim(
        jnp.zeros((640, 960), LOW), d_position.astype(LOW), vocab * 64, 0
    )
    table_grad, square, shards = reduce_weights(
        dict(
            query=d_query_w,
            key_value=d_kv_w,
            out=d_out,
            up=d_up,
            down=d_down,
            head=d_head,
            box=d_box,
            layout=jnp.concatenate([d_layout_open, d_layout_close], 0),
            layout_down=d_layout_down,
            box_proj=d_proj,
            position=d_positions,
            vector=jnp.concatenate(
                [
                    (d_text_vec + d_text_open).reshape(10752),
                    (d_layout_vec + d_layout_vec_open).reshape(2688),
                    d_head_vec.reshape(2304),
                ]
            ).astype(LOW),
        ),
        d_embedded.reshape(32, 24, 128),
        notes_all,
        head_levels,
        shard_width,
    )
    table_grad = (
        table_grad.reshape(levels, table_rows, SPAN_LOW)
        .transpose(1, 0, 2)
        .reshape(table_rows, levels * SPAN_LOW)[:, :shard_width]
    )
    all_grads = [table_grad] + shards
    grad_norm = jnp.sqrt(square[0, 0])
    factor = jnp.minimum(1.0, CLIP / grad_norm)
    results = []
    for (master, momentum, average), grad in zip(triples, all_grads):
        clipped = factor * grad
        momentum_next = MOMENTUM * momentum + clipped
        master_next = master - RATE * (clipped + MOMENTUM * momentum_next)
        average_next = AVERAGE_KEEP * average + (1.0 - AVERAGE_KEEP) * master_next
        results += [master_next, momentum_next, average_next]
    return tuple(results + [loss_total, total_count, grad_norm])


TOKEN_SPEC = P(None, AXES)
WEIGHT_SPECS = (
    P("dp", "vocab"),
    P(AXES, None),
    P(None, AXES, None),
    P(None, AXES),
    P(AXES, None),
    P(None, AXES),
    P(None, AXES, None),
    P(None, AXES),
    P(AXES),
)


def solution(mesh):
    weight_specs = tuple(spec for spec in WEIGHT_SPECS for _ in range(3))
    in_specs = (TOKEN_SPEC, P(None, None, AXES), TOKEN_SPEC, TOKEN_SPEC, TOKEN_SPEC) + weight_specs
    out_specs = weight_specs + (P(), P(), P())
    return jax.shard_map(
        on_device, mesh=mesh, in_specs=in_specs, out_specs=out_specs, check_vma=False
    )
```

```python
import functools

import jax
import jax.numpy as jnp
from jax import lax
from jax.experimental import pallas as pl
from jax.experimental.pallas import tpu as pltpu
from jax.sharding import PartitionSpec as P

AXES = ("dp", "vocab")
MESH = pl.DeviceIdType.MESH
LONG = pl.CostEstimate(flops=60_000_000_000, bytes_accessed=200_000_000, transcendentals=0)
ORDERS = (("z", "y", "x"), ("y", "x", "z"), ("x", "z", "y"))


def my_place():
    dp = lax.axis_index("dp")
    vocab = lax.axis_index("vocab")
    return {
        "x": (dp // 16) * 2 + vocab // 2,
        "y": (dp // 4) % 4,
        "z": dp % 4,
        "c": vocab % 2,
    }


def moved(place, dim, step):
    other = dict(place)
    other[dim] = (1 - place["c"]) if dim == "c" else (place[dim] + step + 4) % 4
    return other


def device_of(place):
    return (
        (place["x"] // 2) * 16 + place["y"] * 4 + place["z"],
        (place["x"] % 2) * 2 + place["c"],
    )


def greet(place, steps=(1, 3)):
    barrier = pltpu.get_barrier_semaphore()
    peers = [moved(place, dim, step) for dim in "xyz" for step in steps]
    peers.append(moved(place, "c", 1))
    for peer in peers:
        pl.semaphore_signal(barrier, inc=1, device_id=device_of(peer), device_id_type=MESH)
    pl.semaphore_wait(barrier, len(peers))


def remote(src, dst, send, recv, place):
    return pltpu.make_async_remote_copy(
        src_ref=src,
        dst_ref=dst,
        send_sem=send,
        recv_sem=recv,
        device_id=device_of(place),
        device_id_type=MESH,
    )


def lanes_at(ref, lanes):
    return slice(None) if lanes is None else pl.ds(*lanes)


def block_view(ref, place, dims, lanes, core=None):
    high, low = (pl.ds(0, 2), pl.ds(0, 2)) if "x" in dims else (place["x"] // 2, place["x"] % 2)
    mid = pl.ds(0, 4) if "y" in dims else place["y"]
    deep = pl.ds(0, 4) if "z" in dims else place["z"]
    where = (high, mid, deep, low)
    if core is not None:
        where += (core,)
    return ref.at[where + (slice(None), lanes_at(ref, lanes))]


def halves(lanes, number):
    if lanes is None or lanes[1] < 256:
        return (lanes, False) if number % 2 == 0 else (False, lanes)
    half = lanes[1] // 256 * 128
    return (lanes[0], half), (lanes[0] + half, lanes[1] - half)


def open_shape(dims):
    shape = ()
    if "x" in dims:
        shape += (2,)
    if "y" in dims:
        shape += (4,)
    if "z" in dims:
        shape += (4,)
    if "x" in dims:
        shape += (2,)
    return shape


def chunks_of(dims, place):
    high, mid, deep, low = place["x"] // 2, place["y"], place["z"], place["x"] % 2
    every = slice(None)
    if dims == "":
        return 1, lambda flat: ((high, mid, deep, low), ())
    inner = (every if "y" in dims else mid, every if "z" in dims else deep)
    if "x" in dims and "y" in dims and "z" in dims:
        return 8, lambda flat: ((flat // 4, flat % 4, every, every), (flat // 4, flat % 4))
    if "x" in dims:
        return 2, lambda flat: ((flat,) + inner + (every,), (flat,))
    if "y" in dims and "z" in dims:
        return 4, lambda flat: ((high, flat, every, low), (flat,))
    return 1, lambda flat: ((high,) + inner + (low,), ())


MOMENTUM = 0.9
AVERAGE_KEEP = 0.9
RATE = 1500.0
CLIP = 0.05
LOW = jnp.bfloat16
SPAN_LOW = 256
TOKEN_BLOCK = 1024


HEADS = 12
NORM_EPSILON = 1e-05
ROOT_HALF = 0.5**0.5
PEAK = 0.3989422804014327
WIDTHS = (768, 192)
HEAD_SIZES = (64, 16)
SCALES = (0.125, 0.25)
QUERY_LANES = ((0, 768), (768, 192))
NEGATIVE = -1e30


def plain_product(left, right):
    return jnp.dot(left, right, preferred_element_type=jnp.float32)


def rows_product(left, right):
    return lax.dot_general(
        left, right, (((0,), (0,)), ((), ())), preferred_element_type=jnp.float32
    )


def cols_product(left, right):
    return lax.dot_general(
        left, right, (((1,), (1,)), ((), ())), preferred_element_type=jnp.float32
    )


def exact_product(left, right):
    return jnp.dot(
        left, right, precision=lax.Precision.HIGHEST, preferred_element_type=jnp.float32
    )


def total_rows(values):
    return jnp.sum(values.astype(jnp.float32), 0, keepdims=True)


def normalised(values):
    centred = values - jnp.mean(values, -1, keepdims=True)
    scale = lax.rsqrt(jnp.mean(centred * centred, -1, keepdims=True) + NORM_EPSILON)
    return centred * scale, scale


def norm_apply(values, gain, bias):
    return normalised(values)[0] * gain + bias


def norm_back(values, gain, grad):
    unit, scale = normalised(values)
    inner = grad * gain
    result = scale * (
        inner
        - jnp.mean(inner, -1, keepdims=True)
        - unit * jnp.mean(inner * unit, -1, keepdims=True)
    )
    return result, total_rows(grad * unit), total_rows(grad)


def gelu_value(values):
    return 0.5 * values * (1.0 + lax.erf(values * ROOT_HALF))


def gelu_slope(values):
    return 0.5 * (1.0 + lax.erf(values * ROOT_HALF)) + values * PEAK * jnp.exp(
        -0.5 * values * values
    )


def row_of(ref, row):
    return ref[row : row + 1, :]


def hidden_bias(ref):
    return jnp.concatenate([row_of(ref, row) for row in range(7, 11)], 1)


def head_of(rows, stream):
    lanes = lax.broadcasted_iota(jnp.int32, (rows, WIDTHS[stream]), 1)
    return lanes // HEAD_SIZES[stream]


def stack_heads(values, stream):
    heads = head_of(values.shape[0], stream)
    zero = jnp.zeros_like(values)
    return jnp.concatenate([jnp.where(heads == h, values, zero) for h in range(HEADS)], 0)


def fold_heads(values, stream):
    rows = values.shape[0] // HEADS
    heads = head_of(rows, stream)
    total = jnp.zeros((rows, values.shape[1]), jnp.float32)
    for h in range(HEADS):
        total = total + jnp.where(heads == h, values[h * rows : (h + 1) * rows], 0.0)
    return total


def lane_heads(stream):
    rows = lax.broadcasted_iota(jnp.int32, (128, WIDTHS[stream]), 0)
    return (rows == head_of(128, stream)).astype(jnp.float32)


def head_lanes(stream):
    rows = lax.broadcasted_iota(jnp.int32, (WIDTHS[stream], 128), 0) // HEAD_SIZES[stream]
    return (rows == lax.broadcasted_iota(jnp.int32, (WIDTHS[stream], 128), 1)).astype(jnp.float32)


def stack_columns(values):
    return jnp.concatenate([values[:, h : h + 1] for h in range(HEADS)], 0)


def one_micro_batch(rows):
    row = lax.broadcasted_iota(jnp.int32, (rows, 128), 0)
    key = lax.broadcasted_iota(jnp.int32, (rows, 128), 1)
    return (row // 8) % 2 == key // 64


def coupled_scores(stacks, key_refs):
    return sum(
        cols_product(stacks[n], key_refs[n][...]) * SCALES[n] for n in range(2)
    )


def open_kernel(
    found_ref, position_ref, index_ref, box_ref, proj_ref, qkv_ref, layout_ref,
    text_vec, layout_vec, slot_ref,
    text_sum_ref, layout_sum_ref, spatial_ref, key_text, value_text, key_layout, value_layout,
    query_ref, slot_text, slot_layout,
):
    embedded = found_ref[...].astype(jnp.float32).reshape(768, 128).T
    place = position_ref[...]
    place = jnp.concatenate([place, place], 0)
    text_sum = embedded + place[:, :768]
    text_sum_ref[...] = text_sum
    tables = (0, 1, 0, 1, 2, 3)
    number = lax.broadcasted_iota(jnp.int32, (128, 1024), 1)
    for k in range(6):
        hot = (number == index_ref[:, k : k + 1]).astype(LOW)
        rows = box_ref[pl.ds(1024 * tables[k], 1024), :]
        spatial_ref[:, pl.ds(128 * k, 128)] = plain_product(hot, rows).astype(LOW)
    layout_sum = place[:, 768:] + plain_product(spatial_ref[...], proj_ref[...])
    layout_sum_ref[...] = layout_sum
    query_ref[...] = jnp.zeros_like(query_ref)
    qkv = qkv_ref[...].reshape(2304, 768)
    weights = (qkv, layout_ref[pl.ds(0, 576), :])
    sums, vecs = (text_sum, layout_sum), (text_vec, layout_vec)
    keys, values, slots = (key_text, key_layout), (value_text, value_layout), (slot_text, slot_layout)
    for n in range(2):
        width, weight, vec = WIDTHS[n], weights[n], vecs[n]
        normed = norm_apply(sums[n], row_of(vec, 0), row_of(vec, 1))
        low = normed.astype(LOW)
        keys[n][...] = cols_product(low, weight[width : 2 * width]).astype(LOW)
        values[n][...] = (cols_product(low, weight[2 * width :]) + row_of(vec, 3)).astype(LOW)
        slot = exact_product(slot_ref[...], normed)
        slots[n][...] = slot
        start, size = QUERY_LANES[n]
        query_ref[:, pl.ds(start, size)] = (
            cols_product(slot.astype(LOW), weight[:width]) + row_of(vec, 2)
        ).astype(LOW)


def score_kernel(query_ref, key_text, value_text, key_layout, value_layout, out_ref):
    stacks = [
        stack_heads(query_ref[:, pl.ds(*QUERY_LANES[n])], n) for n in range(2)
    ]
    mask = one_micro_batch(64 * HEADS)
    scores = jnp.where(mask, coupled_scores(stacks, (key_text, key_layout)), NEGATIVE)
    top = jnp.max(scores, -1, keepdims=True)
    powers = jnp.where(mask, jnp.exp(scores - top), 0.0)
    total = jnp.sum(powers, -1, keepdims=True)
    low = powers.astype(LOW)
    out_ref[:, pl.ds(768, 256)] = jnp.zeros((64, 256), jnp.float32)
    for n, values in enumerate((value_text, value_layout)):
        out_ref[:, pl.ds(*QUERY_LANES[n])] = fold_heads(plain_product(low, values[...]), n)
    lane = lax.broadcasted_iota(jnp.int32, (64, 128), 1)
    tops = jnp.zeros((64, 128), jnp.float32)
    totals = jnp.ones((64, 128), jnp.float32)
    for h in range(HEADS):
        tops = jnp.where(lane == h, top[64 * h : 64 * h + 64], tops)
        totals = jnp.where(lane == h, total[64 * h : 64 * h + 64], totals)
    out_ref[:, pl.ds(1024, 128)] = tops
    out_ref[:, pl.ds(1152, 128)] = totals


def close_kernel(
    parts_ref, slot_text, slot_layout, out_w, up_w, down_w, layout_ref, layout_down,
    text_vec, layout_vec, head_ref, head_vec,
    att_text, att_layout, log_ref, mid_text, mid_layout, pre_text, pre_layout,
    end_text, end_layout, joined_ref, dense_ref, pick_ref,
):
    tops = [parts_ref[j, :, pl.ds(1024, 128)] for j in range(4)]
    top = jnp.maximum(jnp.maximum(tops[0], tops[1]), jnp.maximum(tops[2], tops[3]))
    shares = [jnp.exp(item - top) for item in tops]
    total = sum(shares[j] * parts_ref[j, :, pl.ds(1152, 128)] for j in range(4))
    log_ref[...] = top + jnp.log(total)
    shares = [item / total for item in shares]
    joined_ref[...] = jnp.zeros_like(joined_ref)
    streams = (
        (slot_text, text_vec, out_w, up_w, down_w, att_text, mid_text, pre_text, end_text),
        (slot_layout, layout_vec, layout_ref, layout_ref, layout_down, att_layout, mid_layout,
         pre_layout, end_layout),
    )
    for n, (slot, vec, out_r, up_r, down_r, att_r, mid_r, pre_r, end_r) in enumerate(streams):
        width = WIDTHS[n]
        spread = lane_heads(n)
        att = sum(
            parts_ref[j, :, pl.ds(*QUERY_LANES[n])] * exact_product(shares[j], spread)
            for j in range(4)
        )
        att_r[...] = att
        if n == 0:
            out_m, up_m = out_r[...].reshape(768, 768), up_r[...].reshape(3072, 768)
        else:
            out_m, up_m = out_r[pl.ds(576, 192), :], up_r[pl.ds(768, 768), :]
        mid = slot[...] + (cols_product(att.astype(LOW), out_m) + row_of(vec, 4))
        mid_r[...] = mid
        first = norm_apply(mid, row_of(vec, 5), row_of(vec, 6))
        pre = cols_product(first.astype(LOW), up_m) + hidden_bias(vec)
        pre_r[...] = pre
        end = first + (
            plain_product(gelu_value(pre).astype(LOW), down_r[...]) + row_of(vec, 11)
        )
        end_r[...] = end
        joined_ref[:, pl.ds(*QUERY_LANES[n])] = norm_apply(
            end, row_of(vec, 12), row_of(vec, 13)
        ).astype(LOW)
    dense = cols_product(joined_ref[:, pl.ds(0, 960)], head_ref[...]) + row_of(head_vec, 0)
    dense_ref[...] = dense
    pick_ref[...] = norm_apply(
        gelu_value(dense), row_of(head_vec, 1), row_of(head_vec, 2)
    ).astype(LOW)


def close_back_kernel(
    grad_ref, dense_ref, joined_ref, att_text, att_layout, log_ref, mid_text, mid_layout,
    pre_text, pre_layout, end_text, end_layout, out_w, up_w, down_w, layout_ref, layout_down,
    text_vec, layout_vec, head_ref, head_vec,
    back_ref, d_mid_text, d_mid_layout, d_head, d_out, d_up, d_down, d_layout, d_layout_down,
    d_text_vec, d_layout_vec, d_head_vec,
):
    dense = dense_ref[...]
    d_active, d_gain, d_shift = norm_back(gelu_value(dense), row_of(head_vec, 1), grad_ref[...])
    d_dense = (d_active * gelu_slope(dense)).astype(LOW)
    d_head_vec[0:1, :] = total_rows(d_dense)
    d_head_vec[1:2, :] = d_gain
    d_head_vec[2:3, :] = d_shift
    d_head[...] = rows_product(d_dense, joined_ref[:, pl.ds(0, 960)]).astype(LOW)
    d_joined = plain_product(d_dense, head_ref[...])
    back_ref[:, pl.ds(768, 256)] = jnp.zeros((16, 256), jnp.float32)
    delta = jnp.zeros((16, 128), jnp.float32)
    streams = (
        (text_vec, out_w, up_w, down_w, att_text, mid_text, pre_text, end_text,
         d_mid_text, d_out, d_up, d_down, d_text_vec),
        (layout_vec, layout_ref, layout_ref, layout_down, att_layout, mid_layout, pre_layout,
         end_layout, d_mid_layout, d_layout, d_layout, d_layout_down, d_layout_vec),
    )
    for n, (vec, out_r, up_r, down_r, att_r, mid_r, pre_r, end_r, d_mid_r, d_out_r, d_up_r,
            d_down_r, d_vec) in enumerate(streams):
        width = WIDTHS[n]
        if n == 0:
            out_m, up_m = out_r[...].reshape(768, 768), up_r[...].reshape(3072, 768)
        else:
            out_m, up_m = out_r[pl.ds(576, 192), :], up_r[pl.ds(768, 768), :]
        d_end, d_gain2, d_shift2 = norm_back(
            end_r[...], row_of(vec, 12), d_joined[:, QUERY_LANES[n][0] : sum(QUERY_LANES[n])]
        )
        d_branch2 = d_end.astype(LOW)
        mid, pre = mid_r[...], pre_r[...]
        low = gelu_value(pre).astype(LOW)
        d_pre = (cols_product(d_branch2, down_r[...]) * gelu_slope(pre)).astype(LOW)
        first_low = norm_apply(mid, row_of(vec, 5), row_of(vec, 6)).astype(LOW)
        for k in range(4):
            part = slice(width * k, width * (k + 1))
            d_down_r[pl.ds(width * k, width), :] = rows_product(low[:, part], d_branch2).astype(LOW)
            up_at = pl.ds(width * k, width) if n == 0 else pl.ds(192 + width * k, width)
            d_up_r[up_at, :] = rows_product(d_pre[:, part], first_low).astype(LOW)
            d_vec[7 + k : 8 + k, :] = total_rows(d_pre[:, part])
        d_first = d_end + plain_product(d_pre, up_m)
        d_mid, d_gain1, d_shift1 = norm_back(mid, row_of(vec, 5), d_first)
        d_mid_r[...] = d_mid
        d_branch1 = d_mid.astype(LOW)
        att = att_r[...]
        d_out_r[pl.ds(0, width), :] = rows_product(d_branch1, att.astype(LOW)).astype(LOW)
        d_att = plain_product(d_branch1, out_m).astype(LOW).astype(jnp.float32)
        back_ref[:, pl.ds(*QUERY_LANES[n])] = d_att
        delta = delta + exact_product(d_att * att, head_lanes(n))
        d_vec[0:4, :] = jnp.zeros((4, width), jnp.float32)
        for row, value in (
            (4, total_rows(d_branch1)),
            (5, d_gain1),
            (6, d_shift1),
            (11, total_rows(d_branch2)),
            (12, d_gain2),
            (13, d_shift2),
        ):
            d_vec[row : row + 1, :] = value
    back_ref[:, pl.ds(1024, 128)] = log_ref[...]
    back_ref[:, pl.ds(1152, 128)] = delta


def score_back_kernel(
    back_ref, query_ref, key_text, value_text, key_layout, value_layout,
    d_query, d_key_text, d_value_text, d_key_layout, d_value_layout,
):
    keys, values = (key_text, key_layout), (value_text, value_layout)
    stacks = [stack_heads(query_ref[:, pl.ds(*QUERY_LANES[n])], n) for n in range(2)]
    grads = [stack_heads(back_ref[:, pl.ds(*QUERY_LANES[n])], n).astype(LOW) for n in range(2)]
    logs = stack_columns(back_ref[:, pl.ds(1024, 128)])
    delta = stack_columns(back_ref[:, pl.ds(1152, 128)])
    mask = one_micro_batch(64 * HEADS)
    probs = jnp.where(mask, jnp.exp(jnp.where(mask, coupled_scores(stacks, keys) - logs, 0.0)), 0.0)
    d_probs = sum(cols_product(grads[n], values[n][...]) for n in range(2))
    d_scores = (probs * (d_probs - delta)).astype(LOW)
    low = probs.astype(LOW)
    d_query[:, pl.ds(768, 256)] = jnp.zeros((64, 256), jnp.float32)
    d_keys, d_values = (d_key_text, d_key_layout), (d_value_text, d_value_layout)
    for n in range(2):
        d_query[:, pl.ds(*QUERY_LANES[n])] = (
            fold_heads(plain_product(d_scores, keys[n][...]), n) * SCALES[n]
        )
        d_keys[n][...] = (rows_product(d_scores, stacks[n]) * SCALES[n]).astype(LOW)
        d_values[n][...] = rows_product(low, grads[n]).astype(LOW)


def open_back_kernel(
    parts_ref, d_key_text, d_value_text, d_key_layout, d_value_layout, d_mid_text, d_mid_layout,
    text_sum, layout_sum, slot_text, slot_layout, qkv_ref, layout_ref, proj_ref, spatial_ref,
    index_ref, text_vec, layout_vec, slot_turned,
    d_query_w, d_kv_w, d_layout, d_embedded, d_position, d_box, d_proj, d_text_vec, d_layout_vec,
):
    qkv = qkv_ref[...].reshape(2304, 768)
    streams = (
        (qkv, d_key_text, d_value_text, d_mid_text, text_sum, slot_text, text_vec, d_text_vec),
        (layout_ref[pl.ds(0, 576), :], d_key_layout, d_value_layout, d_mid_layout, layout_sum,
         slot_layout, layout_vec, d_layout_vec),
    )
    lows = []
    for n, (weight, d_key_r, d_value_r, d_mid_r, sum_r, slot_r, vec, d_vec) in enumerate(streams):
        width = WIDTHS[n]
        lanes = pl.ds(*QUERY_LANES[n])
        d_query = sum(parts_ref[j, :, lanes] for j in range(4)).astype(LOW)
        d_key, d_value = d_key_r[...], d_value_r[...]
        d_slot = d_mid_r[...] + plain_product(d_query, weight[:width])
        d_normed = (
            plain_product(d_key, weight[width : 2 * width])
            + plain_product(d_value, weight[2 * width :])
            + exact_product(slot_turned[...], d_slot)
        )
        sums = sum_r[...]
        low = norm_apply(sums, row_of(vec, 0), row_of(vec, 1)).astype(LOW)
        d_sum, d_gain, d_shift = norm_back(sums, row_of(vec, 0), d_normed)
        d_vec[...] = jnp.zeros_like(d_vec)
        for row, value in ((0, d_gain), (1, d_shift), (2, total_rows(d_query)), (3, total_rows(d_value))):
            d_vec[row : row + 1, :] = value
        slot_low = slot_r[...].astype(LOW)
        grads = (rows_product(d_query, slot_low), rows_product(d_key, low), rows_product(d_value, low))
        if n == 0:
            d_query_w[...] = grads[0].astype(LOW)
            d_kv_w[pl.ds(0, 768), :] = grads[1].astype(LOW)
            d_kv_w[pl.ds(768, 768), :] = grads[2].astype(LOW)
        else:
            for k in range(3):
                d_layout[pl.ds(192 * k, 192), :] = grads[k].astype(LOW)
        d_low = d_sum.astype(LOW)
        lows.append(d_low)
        wide = d_low.astype(jnp.float32)
        d_position[:, lanes] = wide[:64] + wide[64:]
        if n == 0:
            d_embedded[...] = wide.T.astype(LOW)
    d_spatial = cols_product(lows[1], proj_ref[...]).astype(LOW)
    d_proj[...] = rows_product(spatial_ref[...], lows[1]).astype(LOW)
    number = lax.broadcasted_iota(jnp.int32, (128, 1024), 1)
    for table, users in enumerate(((0, 2), (1, 3), (4,), (5,))):
        total = 0.0
        for k in users:
            hot = (number == index_ref[:, k : k + 1]).astype(LOW)
            total = total + rows_product(hot, d_spatial[:, 128 * k : 128 * k + 128])
        d_box[pl.ds(1024 * table, 1024), :] = total.astype(LOW)


def local_call(kernel, inputs, outputs, name):
    specs, arrays = [], []

    def spec(shape, index):
        return pl.BlockSpec(shape, lambda step: index, pipeline_mode=pl.Buffered(1))

    for item in inputs:
        array, shape, index = item if isinstance(item, tuple) else (item, item.shape, None)
        specs.append(spec(shape, index or (0,) * len(shape)))
        arrays.append(array)
    return pl.pallas_call(
        kernel,
        name=name,
        grid=(1,),
        out_shape=[jax.ShapeDtypeStruct(shape, dtype) for shape, dtype in outputs],
        in_specs=specs,
        out_specs=[spec(shape, (0,) * len(shape)) for shape, dtype in outputs],
        compiler_params=pltpu.CompilerParams(vmem_limit_bytes=56 * 1024 * 1024),
    )(*arrays)


PLANES = (("y", "z"), ("x", "z"), ("x", "y"))
LINES = ("x", "y", "z")
HEAD_BLOCK = 512
PLANE_STEPS = [(a, b) for a in range(4) for b in range(4) if (a, b) != (0, 0)]


def plane_peer(place, plane, a, b):
    return moved(moved(place, plane[0], a), plane[1], b)


def head_peers(place):
    peers = [
        plane_peer(place, plane, a, b)
        for plane in PLANES
        for a, b in PLANE_STEPS
        if (a and b) or plane == ("y", "z")
    ]
    peers += [moved(place, "x", step) for step in (1, 2, 3)]
    peers += [moved(moved(place, "x", step), "c", 1) for step in range(4)]
    return peers


def merge_logs(logs):
    top = logs[0]
    for item in logs[1:]:
        top = jnp.maximum(top, item)
    total = jnp.exp(logs[0] - top)
    for item in logs[1:]:
        total = total + jnp.exp(item - top)
    return top + jnp.log(total)


def head_kernel(
    limit_width, pick_ref, table_ref, label_ref, weight_ref, count_ref,
    grad_ref, d_table_ref, loss_ref,
    picked, table, logits, d_logits, part, acc, cross, near, far, line_in, plane_in, own_sem,
    plane_send, plane_recv, line_send, line_recv, pass_send, pass_recv,
    near_send, near_recv, far_send, far_recv, core_send, core_recv,
    back_send, back_recv, last_send, last_recv,
):
    place = my_place()
    sibling = moved(place, "c", 1)
    barrier = pltpu.get_barrier_semaphore()
    peers = head_peers(place)
    for peer in peers:
        pl.semaphore_signal(barrier, inc=1, device_id=device_of(peer), device_id_type=MESH)
    own = pltpu.make_async_copy(
        pick_ref, block_view(picked, place, "", None, place["c"]), own_sem
    )
    own.start()
    pl.semaphore_wait(barrier, len(peers))
    sends = []

    def go(copy):
        copy.start()
        sends.append(copy)
        return copy

    def third(k):
        return (256 * k, 256)

    flights = {}
    for k in range(3):
        here = block_view(picked, place, "", third(k), place["c"])
        for a, b in PLANE_STEPS:
            n = 4 * a + b - 1
            flights[(k, n)] = go(
                remote(
                    pick_ref.at[:, pl.ds(*third(k))], here, plane_send.at[k, n],
                    plane_recv.at[k, n], plane_peer(place, PLANES[k], a, b),
                )
            )
    table[...] = table_ref[...].astype(jnp.float32).T.astype(LOW)
    own.wait()
    lines, passes = {}, []

    def hand_over(k, n, where):
        passes.append(go(remote(where, where, pass_send.at[k, n], pass_recv.at[k, n], sibling)))

    for k in range(3):
        for a, b in PLANE_STEPS:
            flights[(k, 4 * a + b - 1)].wait_recv()
        sheet = block_view(picked, place, PLANES[k], third(k), place["c"])
        for step in (1, 2, 3):
            lines[(k, step)] = go(
                remote(
                    sheet, sheet, line_send.at[k, step - 1], line_recv.at[k, step - 1],
                    moved(place, LINES[k], step),
                )
            )
        hand_over(k, 0, sheet)
    for step in (1, 3, 2):
        for k in range(3):
            lines[(k, step)].wait_recv()
            origin = moved(place, LINES[k], -step)
            hand_over(k, step, block_view(picked, origin, PLANES[k], third(k), place["c"]))
    for copy in passes:
        copy.wait_recv()

    limit = limit_width - lax.axis_index("dp") * HEAD_BLOCK
    row = lax.broadcasted_iota(jnp.int32, (HEAD_BLOCK, 256), 0)
    valid = row < limit
    mine = place["x"] * 2 + place["c"]
    for chunk in range(8):
        high, mid = chunk // 4, chunk % 4
        lanes = pl.ds(256 * chunk, 256)
        values = cols_product(table[...], picked[high, mid].reshape(256, 768))
        values = jnp.where(valid, values, NEGATIVE)
        logits[:, lanes] = values
        top = jnp.max(values, 0, keepdims=True)
        total = jnp.sum(jnp.where(valid, jnp.exp(values - top), 0.0), 0, keepdims=True)
        hot = valid & (row == label_ref[:, lanes])
        near[mine, 0, :, lanes] = top + jnp.log(jnp.maximum(total, 1e-30))
        near[mine, 1, :, lanes] = jnp.sum(jnp.where(hot, values, 0.0), 0, keepdims=True)
    meets = []
    for n in range(1, 8):
        peer = moved(place, "x", n // 2)
        if n % 2:
            peer = moved(peer, "c", 1)
        meets.append(
            go(remote(near.at[mine], near.at[mine], near_send.at[n - 1], near_recv.at[n - 1], peer))
        )
    for copy in meets:
        copy.wait_recv()
    spot = place["y"] * 4 + place["z"]
    far[spot, 0] = merge_logs([near[n, 0] for n in range(8)])
    far[spot, 1] = sum(near[n, 1] for n in range(8))
    meets = []
    for a, b in PLANE_STEPS:
        n = 4 * a + b - 1
        peer = plane_peer(place, ("y", "z"), a, b)
        meets.append(go(remote(far.at[spot], far.at[spot], far_send.at[n], far_recv.at[n], peer)))
    for copy in meets:
        copy.wait_recv()
    log_total = merge_logs([far[n, 0] for n in range(16)])
    target = sum(far[n, 1] for n in range(16))
    loss = jnp.sum(count_ref[...] * (log_total - target), 1, keepdims=True)
    loss_ref[...] = jnp.broadcast_to(loss, loss_ref.shape)

    crossings = []
    for chunk in range(8):
        high, mid = chunk // 4, chunk % 4
        lanes = pl.ds(256 * chunk, 256)
        here = slice(256 * chunk, 256 * chunk + 256)
        hot = (valid & (row == label_ref[:, lanes])).astype(jnp.float32)
        powers = jnp.where(valid, jnp.exp(logits[:, lanes] - log_total[:, here]), 0.0)
        low = (weight_ref[:, lanes] * (powers - hot)).astype(LOW)
        d_logits[:, lanes] = low
        part[high, mid] = rows_product(low, table[...]).astype(LOW).reshape(4, 2, 2, 16, 768)
        crossings.append(
            go(
                remote(
                    part.at[high, mid, :, :, sibling["c"]], cross.at[high, mid],
                    core_send.at[chunk], core_recv.at[chunk], sibling,
                )
            )
        )
    for chunk in range(8):
        high, mid = chunk // 4, chunk % 4
        crossings[chunk].wait_recv()
        acc[high, mid] = part[high, mid, :, :, place["c"]] + cross[high, mid]

    legs = {}
    for k in range(3):
        for step in (1, 3, 2):
            there = moved(place, LINES[k], step)
            legs[(k, step)] = go(
                remote(
                    block_view(acc, there, PLANES[k], third(k)), line_in[k].at[step - 1],
                    back_send.at[k, step - 1], back_recv.at[k, step - 1], there,
                )
            )
    d_table = jnp.zeros((HEAD_BLOCK, 768), jnp.float32)
    for chunk in range(8):
        d_table = d_table + plain_product(
            d_logits[:, pl.ds(256 * chunk, 256)], picked[chunk // 4, chunk % 4].reshape(256, 768)
        )
    d_table_ref[...] = d_table.T.astype(LOW)
    ends = {}
    for k in range(3):
        for step in (1, 2, 3):
            legs[(k, step)].wait_recv()
        count, chunk_of = chunks_of("".join(PLANES[k]), place)
        for flat in range(count):
            block, inner = chunk_of(flat)
            where = block + (slice(None), pl.ds(*third(k)))
            total = acc[where].astype(jnp.float32)
            for step in (1, 2, 3):
                total = total + line_in[k][(step - 1,) + inner].astype(jnp.float32)
            acc[where] = total.astype(LOW)
        for a, b in PLANE_STEPS:
            n = 4 * a + b - 1
            there = plane_peer(place, PLANES[k], a, b)
            ends[(k, n)] = go(
                remote(
                    block_view(acc, there, "", third(k)), plane_in.at[k, n],
                    last_send.at[k, n], last_recv.at[k, n], there,
                )
            )
    home = (place["x"] // 2, place["y"], place["z"], place["x"] % 2)
    for k in range(3):
        total = acc[home + (slice(None), pl.ds(*third(k)))].astype(jnp.float32)
        for n in range(15):
            ends[(k, n)].wait_recv()
            total = total + plane_in[k, n].astype(jnp.float32)
        grad_ref[:, pl.ds(*third(k))] = total
    for copy in sends:
        copy.wait_send()


def head_step(picked, table, labels, weights, counts, width, collective_id):
    sems = pltpu.SemaphoreType.DMA
    everyone = (2, 4, 4, 2, 2, 16, 768)
    half = (2, 4, 4, 2, 16, 768)
    line_slots = [
        pltpu.VMEM((3,) + open_shape("".join(PLANES[k])) + (16, 256), LOW) for k in range(3)
    ]

    def kernel(*refs):
        head_kernel(width, *refs[:17], refs[17:20], *refs[20:])

    return pl.pallas_call(
        kernel,
        out_shape=[
            jax.ShapeDtypeStruct((16, 768), jnp.float32),
            jax.ShapeDtypeStruct((768, HEAD_BLOCK), LOW),
            jax.ShapeDtypeStruct((8, 128), jnp.float32),
        ],
        in_specs=[pl.BlockSpec(memory_space=pltpu.VMEM)] * 5,
        out_specs=[pl.BlockSpec(memory_space=pltpu.VMEM)] * 3,
        scratch_shapes=[
            pltpu.VMEM(everyone, LOW),
            pltpu.VMEM((HEAD_BLOCK, 768), LOW),
            pltpu.VMEM((HEAD_BLOCK, 2048), jnp.float32),
            pltpu.VMEM((HEAD_BLOCK, 2048), LOW),
            pltpu.VMEM(everyone, LOW),
            pltpu.VMEM(half, LOW),
            pltpu.VMEM(half, LOW),
            pltpu.VMEM((8, 2, 1, 2048), jnp.float32),
            pltpu.VMEM((16, 2, 1, 2048), jnp.float32),
        ]
        + line_slots
        + [
            pltpu.VMEM((3, 15, 16, 256), LOW),
            sems(()),
            sems((3, 15)),
            sems((3, 15)),
            sems((3, 3)),
            sems((3, 3)),
            sems((3, 4)),
            sems((3, 4)),
            sems((7,)),
            sems((7,)),
            sems((15,)),
            sems((15,)),
            sems((8,)),
            sems((8,)),
            sems((3, 3)),
            sems((3, 3)),
            sems((3, 15)),
            sems((3, 15)),
        ],
        compiler_params=pltpu.CompilerParams(
            collective_id=collective_id, has_side_effects=True, vmem_limit_bytes=56 * 1024 * 1024
        ),
    )(picked, table, labels, weights, counts)


def greet_groups(place, extra):
    barrier = pltpu.get_barrier_semaphore()
    dp, vocab = device_of(place)

    def signal(device):
        pl.semaphore_signal(barrier, inc=1, device_id=device, device_id_type=MESH)

    def group(step, carry):
        signal(((dp + step) % 32, vocab))
        return carry

    lax.fori_loop(1, 32, group, 0)
    for step in (1, 2, 3):
        signal((dp, (vocab + step) % 4))
    for peer in extra:
        signal(device_of(peer))
    pl.semaphore_wait(barrier, 34 + len(extra))


def beyond(place):
    return moved(place, "x", 2 * (place["x"] % 2) - 1)


def start_kernel(
    pieces, count, width, notes_ref, levels_ref, blocks_ref, *refs
):
    ins, refs = refs[:count], refs[count:]
    notes_out, found_out, table_out = refs[:3]
    outs, refs = refs[3 : 3 + count], refs[3 + count :]
    notes_all, found, found_in, merged = refs[:4]
    note_sems, spread_sems, found_sems, vocab_sems, table_sems = refs[4:9]
    own_sem, ring_send, ring_recv, pass_send, pass_recv = refs[9:]
    place = my_place()
    sibling = moved(place, "c", 1)
    own_dp, own_vocab = device_of(place)
    greet_groups(place, [beyond(place)])

    def to_device(src, dst, sems, device):
        return pltpu.make_async_remote_copy(
            src_ref=src, dst_ref=dst, send_sem=sems.at[0], recv_sem=sems.at[1],
            device_id=device, device_id_type=MESH,
        )

    rings, passes = {}, []

    def spot(number, origin, dims, lanes):
        return block_view(outs[number], origin, dims, lanes, place["c"])

    def send(phase, way, piece, src, dst, target):
        copy = remote(
            src, dst, ring_send.at[phase, way, piece], ring_recv.at[phase, way, piece], target
        )
        copy.start()
        rings[(phase, way, piece)] = copy

    def hand_over(phase, way, piece, where):
        copy = remote(
            where, where, pass_send.at[phase, way, piece], pass_recv.at[phase, way, piece], sibling
        )
        copy.start()
        passes.append(copy)

    def begin(phase, piece):
        number, lanes, order = pieces[piece]
        dim, dims = ORDERS[order][phase], ORDERS[order][:phase]
        where = spot(number, place, dims, lanes)
        src = ins[number].at[:, lanes_at(ins[number], lanes)] if phase == 0 else where
        for way, step in ((0, 1), (1, -1)):
            send(phase, way, piece, src, where, moved(place, dim, step))

    def forward(phase):
        for piece, (number, lanes, order) in enumerate(pieces):
            dim, dims = ORDERS[order][phase], ORDERS[order][:phase]
            parts = halves(lanes, piece)
            for way, step in ((0, 1), (1, -1)):
                rings[(phase, way, piece)].wait_recv()
                origin = moved(place, dim, -step)
                if parts[way] is not False:
                    onward = spot(number, origin, dims, parts[way])
                    send(phase, 2 + way, piece, onward, onward, moved(place, dim, step))
                if phase == 2:
                    hand_over(phase, way, piece, spot(number, origin, dims, lanes))

    def conclude(phase):
        for piece, (number, lanes, order) in enumerate(pieces):
            dim, dims = ORDERS[order][phase], ORDERS[order][:phase]
            parts = halves(lanes, piece)
            for way in range(2):
                if parts[way] is not False:
                    rings[(phase, 2 + way, piece)].wait_recv()
            if phase == 0:
                begin(1, piece)
            elif phase == 1:
                begin(2, piece)
                hand_over(1, 0, piece, spot(number, place, ORDERS[order][:2], lanes))
            else:
                hand_over(2, 2, piece, spot(number, moved(place, dim, 2), dims, lanes))

    own_copies = []
    for piece in range(len(pieces)):
        begin(0, piece)
    for number in range(count):
        copy = pltpu.make_async_copy(
            ins[number], spot(number, place, "", None), own_sem.at[number]
        )
        copy.start()
        own_copies.append(copy)
    own_notes = notes_all.at[own_dp, own_vocab]
    pltpu.make_async_copy(notes_ref, own_notes, note_sems.at[1]).start()
    for step in (1, 2, 3):
        to_device(notes_ref, own_notes, note_sems, (own_dp, (own_vocab + step) % 4)).start()
    pltpu.make_async_copy(
        blocks_ref.at[own_dp], table_out.at[own_dp], table_sems.at[1]
    ).start()

    def send_block(step, carry):
        other = (own_dp + step) % 32
        to_device(
            blocks_ref.at[other], table_out.at[own_dp], table_sems, (other, own_vocab)
        ).start()
        return carry

    lax.fori_loop(1, 32, send_block, 0)

    group_notes = notes_all.at[own_dp]
    pltpu.make_async_copy(group_notes, group_notes, note_sems.at[1]).wait()

    def send_notes(step, carry):
        to_device(
            group_notes, group_notes, spread_sems, ((own_dp + step) % 32, own_vocab)
        ).start()
        return carry

    lax.fori_loop(1, 32, send_notes, 0)
    for copy in own_copies:
        copy.wait()
    forward(0)
    rows = found.shape[2]
    levels = levels_ref.shape[0] // rows

    def pick(step, carry):
        ids = jnp.concatenate(
            [notes_all[step * 2 + n // 4, n % 4, 0:1, :] for n in range(8)], 1
        )
        local = ids - own_vocab * width
        high = jnp.where((local >= 0) & (local < width), local >> 8, -1)
        low = local & 255
        hot = (lax.broadcasted_iota(jnp.int32, (SPAN_LOW, 1024), 0) == low).astype(LOW)
        total = jnp.zeros((rows, 1024), jnp.float32)
        group = 5
        for first in range(0, levels, group):
            values = jnp.dot(
                levels_ref[pl.ds(first * rows, group * rows), :],
                hot,
                preferred_element_type=jnp.float32,
            )
            for level in range(group):
                total = total + jnp.where(
                    high == first + level, values[level * rows : (level + 1) * rows], 0.0
                )
        total = total.astype(LOW)
        for n in range(8):
            found[step * 2 + n // 4, n % 4] = total[:, 128 * n : 128 * n + 128]
        return carry

    arrived = notes_all.at[pl.ds(0, 31)]
    pltpu.make_async_copy(arrived, arrived, spread_sems.at[1]).wait()
    conclude(0)
    lax.fori_loop(0, 3, pick, 0)
    forward(1)
    lax.fori_loop(3, 6, pick, 0)
    conclude(1)
    lax.fori_loop(6, 16, pick, 0)
    swaps = []
    for step in (1, 2, 3):
        there = (own_vocab + step) % 4
        copy = pltpu.make_async_remote_copy(
            src_ref=found.at[:, there], dst_ref=found_in.at[own_vocab],
            send_sem=vocab_sems.at[0, step - 1], recv_sem=vocab_sems.at[1, step - 1],
            device_id=(own_dp, there), device_id_type=MESH,
        )
        copy.start()
        swaps.append(copy)
    forward(2)
    total = found[:, own_vocab]
    for step in (1, 2, 3):
        swaps[step - 1].wait_recv()
        total = total + found_in[(own_vocab - step + 4) % 4]
    merged[...] = total
    pltpu.make_async_copy(merged.at[own_dp], found_out.at[own_dp], found_sems.at[1]).start()

    def send_found(step, carry):
        there = (own_dp + step) % 32
        to_device(
            merged.at[there], found_out.at[own_dp], found_sems, (there, own_vocab)
        ).start()
        return carry

    lax.fori_loop(1, 32, send_found, 0)
    conclude(2)
    notes_out[...] = notes_all[...]
    pltpu.make_async_copy(found_out, found_out, found_sems.at[1]).wait()
    pltpu.make_async_copy(table_out, table_out, table_sems.at[1]).wait()
    for sems, ref in (
        (note_sems, notes_all.at[0, pl.ds(0, 3)]),
        (spread_sems, arrived),
        (found_sems, merged.at[pl.ds(0, 31)]),
        (table_sems, blocks_ref.at[pl.ds(0, 31)]),
    ):
        pltpu.make_async_copy(ref, ref, sems.at[0]).wait()
    for copy in swaps:
        copy.wait_send()
    for copy in rings.values():
        copy.wait_send()
    for copy in passes:
        copy.wait()


def start_step(notes, levels, blocks, arrays, pieces, width, collective_id):
    count, total = len(arrays), len(pieces)
    sems = pltpu.SemaphoreType.DMA
    anywhere = pl.BlockSpec(memory_space=pl.ANY)
    local = pl.BlockSpec(memory_space=pltpu.VMEM)
    rows = blocks.shape[1]
    notes_all, found, table, *outs = pl.pallas_call(
        functools.partial(start_kernel, pieces, count, width),
        out_shape=[
            jax.ShapeDtypeStruct((32, 4) + notes.shape, jnp.int32),
            jax.ShapeDtypeStruct((32, rows, 128), LOW),
            jax.ShapeDtypeStruct(blocks.shape, LOW),
        ]
        + [jax.ShapeDtypeStruct((2, 4, 4, 2, 2) + a.shape, a.dtype) for a in arrays],
        in_specs=[local, local, anywhere] + [anywhere] * count,
        out_specs=[local, anywhere, anywhere] + [anywhere] * count,
        scratch_shapes=[
            pltpu.VMEM((32, 4) + notes.shape, jnp.int32),
            pltpu.VMEM((32, 4, rows, 128), LOW),
            pltpu.VMEM((4, 32, rows, 128), LOW),
            pltpu.VMEM((32, rows, 128), LOW),
            sems((2,)),
            sems((2,)),
            sems((2,)),
            sems((2, 3)),
            sems((2,)),
            sems((count,)),
            sems((3, 4, total)),
            sems((3, 4, total)),
            sems((3, 3, total)),
            sems((3, 3, total)),
        ],
        cost_estimate=LONG,
        compiler_params=pltpu.CompilerParams(
            collective_id=collective_id, has_side_effects=True, vmem_limit_bytes=40 * 1024 * 1024
        ),
    )(notes, levels, blocks, *arrays)
    return notes_all, found, table, [o.reshape((128,) + a.shape) for o, a in zip(outs, arrays)]


def finish_kernel(sources, pieces, count, width, *refs):
    total = len(pieces)
    ins, refs = refs[: len(sources)], refs[len(sources) :]
    text_ref, notes_ref, head_ref, refs = refs[0], refs[1], refs[2], refs[3:]
    outs, table_ref, square_ref, refs = refs[:count], refs[count], refs[count + 1], refs[count + 2 :]
    accs, crosses, refs = refs[:count], refs[count : 2 * count], refs[2 * count :]
    slots, refs = refs[: 12 * total], refs[12 * total :]
    text_all, spread, near, far = refs[:4]
    own_sem, core_sems, ring_sems, text_sems, vocab_sems, near_sems, far_sems = refs[4:]
    place = my_place()
    sibling = moved(place, "c", 1)
    own_dp, own_vocab = device_of(place)
    across = moved(moved(place, "x", 2), "c", 1)
    greet_groups(place, [beyond(place), moved(beyond(place), "c", 1), across])
    started = []

    def go(src, dst, sems, index, target):
        copy = remote(src, dst, sems.at[(0,) + index], sems.at[(1,) + index], target)
        copy.start()
        started.append(copy)
        return copy

    def add(number, lanes, at, dims, others):
        acc = accs[number]
        count, chunk = chunks_of(dims, at)

        def body(flat, carry):
            block, inner = chunk(flat)
            where = block + (slice(None), lanes_at(acc, lanes))
            parts = [
                other[inner] if index is None else other[block + index] for other, index in others
            ]
            if len(parts) == 1:
                acc[where] = acc[where] + parts[0]
            else:
                wide = [part.astype(jnp.float32) for part in [acc[where]] + parts]
                acc[where] = sum(wide).astype(acc.dtype)
            return carry

        if count == 1:
            body(0, 0)
        else:
            lax.fori_loop(0, count, body, 0)

    first, pair = {}, 0
    for piece, (number, lanes, order) in enumerate(pieces):
        for index, (owner, high, mids) in enumerate(sources):
            if owner != number:
                continue
            every = slice(None)
            run = lanes_at(accs[number], lanes)
            at = (pl.ds(*high), pl.ds(*mids), every, every, every, run)
            src = (every, every, every, every)
            cross = go(
                ins[index].at[src + (sibling["c"], every, run)], crosses[number].at[at],
                core_sems, (pair,), sibling,
            )
            own = pltpu.make_async_copy(
                ins[index].at[src + (place["c"], every, run)], accs[number].at[at], own_sem.at[pair]
            )
            own.start()
            first.setdefault(piece, []).append((cross, own))
            pair += 1

    own_text = text_all.at[own_dp, own_vocab]
    pltpu.make_async_copy(text_ref.at[own_dp], own_text, text_sems.at[1]).start()

    def send_text(step, carry):
        there = (own_dp + step) % 32
        pltpu.make_async_remote_copy(
            src_ref=text_ref.at[there], dst_ref=own_text, send_sem=text_sems.at[0],
            recv_sem=text_sems.at[1], device_id=(there, own_vocab), device_id_type=MESH,
        ).start()
        return carry

    rings = {}

    def slot(phase, way, piece):
        return slots[(phase * 4 + way) * total + piece]

    def send(phase, way, piece, src, step):
        number, lanes, order = pieces[piece]
        rings[(phase, way, piece)] = go(
            src, slot(phase, way, piece), ring_sems, (phase, way, piece),
            moved(place, ORDERS[order][phase], step),
        )

    def begin(phase, piece):
        number, lanes, order = pieces[piece]
        dim, rest = ORDERS[order][phase], ORDERS[order][phase + 1 :]
        parts = halves(lanes, piece)
        there = moved(place, dim, 2)
        for way, step in ((0, 1), (1, -1)):
            if parts[way] is not False:
                send(phase, way, piece, block_view(accs[number], there, rest, parts[way]), step)

    def pass_on(phase):
        for piece, (number, lanes, order) in enumerate(pieces):
            dim, rest = ORDERS[order][phase], ORDERS[order][phase + 1 :]
            parts = halves(lanes, piece)
            for way, step in ((0, 1), (1, -1)):
                there = moved(place, dim, step)
                if parts[way] is not False:
                    rings[(phase, way, piece)].wait_recv()
                    add(number, parts[way], there, rest, [(slot(phase, way, piece), None)])
                send(phase, 2 + way, piece, block_view(accs[number], there, rest, lanes), step)

    def take_in(phase):
        for piece, (number, lanes, order) in enumerate(pieces):
            rest = ORDERS[order][phase + 1 :]
            for way in range(2):
                rings[(phase, 2 + way, piece)].wait_recv()
            others = [slot(phase, 2 + way, piece) for way in range(2)]
            if phase < 2:
                add(number, lanes, place, rest, [(other, None) for other in others])
                begin(phase + 1, piece)
            else:
                where = (slice(None), lanes_at(accs[number], lanes))
                value = accs[number][home + where].astype(jnp.float32)
                for other in others:
                    value = value + other[...].astype(jnp.float32)
                outs[number][where] = value

    home = (place["x"] // 2, place["y"], place["z"], place["x"] % 2)
    for piece, (number, lanes, order) in enumerate(pieces):
        for cross, own in first[piece]:
            own.wait()
            cross.wait_recv()
        run = (slice(None), lanes_at(accs[number], lanes))
        add(number, lanes, place, "xyz", [(crosses[number], run)])
        begin(0, piece)
        if piece == 2:
            lax.fori_loop(1, 32, send_text, 0)

    rows = text_all.shape[2]
    levels = head_ref.shape[0] // rows
    table_ref[...] = head_ref[...]

    def scatter(block, carry):
        ids = jnp.concatenate(
            [notes_ref[block * 2 + n // 4, n % 4, 0:1, :] for n in range(8)], 1
        )
        local = ids - own_vocab * width
        high = jnp.where((local >= 0) & (local < width), local >> 8, -1)
        hot = (lax.broadcasted_iota(jnp.int32, (SPAN_LOW, 1024), 0) == (local & 255)).astype(LOW)
        grad = jnp.concatenate(
            [text_all[block * 2 + n // 4, n % 4] for n in range(8)], 1
        ).astype(jnp.float32)
        for level in range(0, levels, 2):
            spread[pl.ds(level * rows, 2 * rows), :] = jnp.concatenate(
                [jnp.where(high == level + n, grad, 0.0) for n in range(2)], 0
            ).astype(LOW)
        group = 10 * rows
        for start in range(0, levels * rows, group):
            table_ref[pl.ds(start, group), :] += cols_product(spread[pl.ds(start, group), :], hot)
        return carry

    own_column = text_all.at[:, own_vocab]
    pltpu.make_async_copy(own_column, own_column, text_sems.at[1]).wait()
    swaps = []
    for step in (1, 2, 3):
        copy = pltpu.make_async_remote_copy(
            src_ref=own_column, dst_ref=own_column, send_sem=vocab_sems.at[0, step - 1],
            recv_sem=vocab_sems.at[1, step - 1], device_id=(own_dp, (own_vocab + step) % 4),
            device_id_type=MESH,
        )
        copy.start()
        swaps.append(copy)
    pass_on(0)
    for copy in swaps:
        copy.wait_recv()
    lax.fori_loop(0, 7, scatter, 0)
    take_in(0)
    lax.fori_loop(7, 10, scatter, 0)
    pass_on(1)
    lax.fori_loop(10, 12, scatter, 0)
    take_in(1)
    lax.fori_loop(12, 14, scatter, 0)
    pass_on(2)
    lax.fori_loop(14, 16, scatter, 0)
    take_in(2)
    square = jnp.zeros((1, 1), jnp.float32)

    def squared(value):
        return jnp.sum(jnp.sum(value * value, 1, keepdims=True), 0, keepdims=True)

    for out in outs:
        square = square + squared(out[...])
    square = square + squared(table_ref[...])

    mine = place["x"] * 2 + place["c"]
    near[mine] = jnp.broadcast_to(square, (8, 128))
    meets = []
    for n in range(1, 8):
        peer = moved(place, "x", n // 2)
        if n % 2:
            peer = moved(peer, "c", 1)
        meets.append(go(near.at[mine], near.at[mine], near_sems, (n - 1,), peer))
    for copy in meets:
        copy.wait_recv()
    spot = place["y"] * 4 + place["z"]
    far[spot] = sum(near[n] for n in range(8))
    meets = []
    for a, b in PLANE_STEPS:
        peer = plane_peer(place, ("y", "z"), a, b)
        meets.append(go(far.at[spot], far.at[spot], far_sems, (4 * a + b - 1,), peer))
    for copy in meets:
        copy.wait_recv()
    square_ref[...] = sum(far[n] for n in range(16))
    sent = text_ref.at[pl.ds(0, 31)]
    pltpu.make_async_copy(sent, sent, text_sems.at[0]).wait()
    for copy in swaps:
        copy.wait_send()
    for copy in started:
        copy.wait_send()


def finish_step(arrays, text, notes, head_levels, sources, pieces, width, collective_id):
    shapes, views = {}, []
    for array, (owner, high, mids) in zip(arrays, sources):
        shapes[owner] = array.shape[1:]
        views.append(array.reshape((high[1], mids[1], 4, 2, 2) + array.shape[1:]))
    count, total = len(shapes), len(pieces)
    pairs = sum(owner == piece[0] for piece in pieces for owner, high, mids in sources)
    scratch = [pltpu.VMEM((2, 4, 4, 2) + shapes[n], LOW) for n in range(count)] * 2
    widths = []
    for piece, (number, lanes, order) in enumerate(pieces):
        parts = halves(lanes, piece)
        widths.append([shapes[number][1] if part is None else part for part in
                       [p if p in (None, False) else p[1] for p in (*parts, lanes, lanes)]])
    for phase in range(3):
        for way in range(4):
            for piece, (number, lanes, order) in enumerate(pieces):
                wide = widths[piece][way]
                if wide is False:
                    scratch.append(pltpu.VMEM((8, 128), LOW))
                else:
                    rest = open_shape(ORDERS[order][phase + 1 :])
                    scratch.append(pltpu.VMEM(rest + (shapes[number][0], wide), LOW))
    rows = text.shape[1]
    sems = pltpu.SemaphoreType.DMA
    scratch += [
        pltpu.VMEM((32, 4, rows, 128), LOW),
        pltpu.VMEM((head_levels.shape[0], 1024), LOW),
        pltpu.VMEM((8, 8, 128), jnp.float32),
        pltpu.VMEM((16, 8, 128), jnp.float32),
        sems((pairs,)),
        sems((2, pairs)),
        sems((2, 3, 4, total)),
        sems((2,)),
        sems((2, 3)),
        sems((2, 7)),
        sems((2, 15)),
    ]
    local = pl.BlockSpec(memory_space=pltpu.VMEM)
    return pl.pallas_call(
        functools.partial(finish_kernel, sources, pieces, count, width),
        out_shape=[jax.ShapeDtypeStruct(shapes[n], jnp.float32) for n in range(count)]
        + [
            jax.ShapeDtypeStruct(head_levels.shape, jnp.float32),
            jax.ShapeDtypeStruct((8, 128), jnp.float32),
        ],
        in_specs=[pl.BlockSpec(memory_space=pl.ANY)] * len(arrays) + [local] * 3,
        out_specs=[local] * (count + 2),
        scratch_shapes=scratch,
        cost_estimate=LONG,
        compiler_params=pltpu.CompilerParams(
            collective_id=collective_id, has_side_effects=True, vmem_limit_bytes=60 * 1024 * 1024
        ),
    )(*views, text, notes, head_levels)


def thirds(number):
    return [(number, (256 * k, 256), k) for k in range(3)]


GATHER_PIECES = thirds(0) + thirds(1) + [(2, (0, 512), 0), (2, (512, 512), 1), (3, (0, 256), 2)]
REDUCE_PIECES = (
    thirds(0)
    + thirds(1)
    + [(2, None, 0), (3, None, 2), (4, None, 1), (5, None, 1), (6, None, 2), (7, None, 2), (8, None, 0)]
)
WHOLE = ((0, 2), (0, 4))
REDUCE_SOURCES = [
    (0, (0, 1), (0, 1)),
    (0, (0, 1), (1, 2)),
    (0, (0, 1), (3, 1)),
    (0, (1, 1), (0, 4)),
] + [(number,) + WHOLE for number in range(1, 9)]


def pack(masters):
    word, position, box, text, down, layout, layout_down, head, vector = [
        m.astype(LOW) for m in masters
    ]
    box = box.reshape(2, 16, 128)
    small = jnp.concatenate(
        [
            jnp.concatenate([box[0], box[1]], 1),
            filled(layout.T, 16, 256),
            filled(layout_down[0], 8, 256),
            filled(layout_down[1], 8, 256),
            filled(vector[None], 8, 256),
        ],
        0,
    )
    wide = jnp.concatenate([filled(head.T, 8, 1024), filled(position, 8, 1024)], 0)
    return [text.T, down, wide, small]


def filled(values, rows, width):
    lead = [(0, 0)] * (values.ndim - 2)
    return jnp.pad(
        values, lead + [(0, rows - values.shape[-2]), (0, width - values.shape[-1])]
    )


def unpack(gathered):
    text, down, wide, small = gathered
    box = small[:, :16].reshape(128, 2, 8, 2, 128).transpose(3, 1, 0, 2, 4)
    return dict(
        text=text,
        down=down.reshape(3072, 768),
        head=wide[:, :6, :960].reshape(768, 960),
        box=box.reshape(4096, 128),
        layout=small[:, 16:28, :192].reshape(1536, 192),
        layout_down=small[:, 32:38, :192].reshape(768, 192),
        box_proj=small[:, 40:46, :192].reshape(768, 192),
        position=wide[:52, 8:13, :960].reshape(260, 960),
        vector=small[:, 48, :123].reshape(15744),
    )


def reduce_weights(grads, text, notes, head_levels, width):
    shards = finish_step(
        [
            grads["query"].reshape(16, 48, 768),
            grads["key_value"].reshape(32, 48, 768),
            grads["out"].reshape(16, 48, 768),
            grads["up"].reshape(64, 48, 768),
            grads["down"].reshape(128, 24, 768),
            grads["head"].reshape(128, 6, 960),
            grads["position"].reshape(128, 5, 960),
            grads["layout"].reshape(128, 12, 192),
            grads["layout_down"].reshape(128, 6, 192),
            grads["box_proj"].reshape(128, 6, 192),
            grads["box"].reshape(4, 128, 8, 128).transpose(1, 0, 2, 3).reshape(128, 32, 128),
            grads["vector"].reshape(128, 1, 123),
        ],
        text,
        notes,
        head_levels,
        REDUCE_SOURCES,
        REDUCE_PIECES,
        width,
        4,
    )
    text, down, head, position, layout, layout_down, box_proj, box, vector, table, square = shards
    return table, square, [
        position,
        box.reshape(4, 8, 128),
        text.T,
        down,
        layout.T,
        jnp.stack([layout_down, box_proj]),
        head.T,
        vector[0],
    ]


def on_device(
    token_ids,
    box_coords,
    intersection_flags,
    masked_rows,
    masked_labels,
    *weights,
):
    triples = [tuple(weights[3 * n : 3 * n + 3]) for n in range(9)]
    masters = [entry[0] for entry in triples]
    word_table = masters[0]
    dp = lax.axis_index("dp")
    vocab = lax.axis_index("vocab")
    shard_width = word_table.shape[1]
    table_rows = word_table.shape[0]
    levels = -(-shard_width // SPAN_LOW)

    row_hot = masked_rows[:, :, None] == jnp.arange(64)[None, None, :]
    counted = jnp.sum(jnp.where(row_hot & (intersection_flags == 0)[:, None, :], 1, 0), 2)
    slot_hot = jnp.concatenate(
        [
            jnp.pad(row_hot[0], ((0, 0), (0, 64))),
            jnp.pad(row_hot[1], ((0, 0), (64, 0))),
        ],
        0,
    )
    slot_hot_wide = slot_hot.astype(jnp.float32)
    f32 = jnp.float32

    notes = jnp.concatenate(
        [
            token_ids.reshape(1, 128),
            jnp.concatenate(
                [masked_labels.reshape(1, 16), counted.reshape(1, 16), jnp.zeros((1, 96), jnp.int32)], 1
            ),
        ],
        0,
    )
    table_low = word_table.astype(LOW)
    table_levels = (
        jnp.pad(table_low, ((0, 0), (0, levels * SPAN_LOW - shard_width)))
        .reshape(table_rows, levels, SPAN_LOW)
        .transpose(1, 0, 2)
        .reshape(levels * table_rows, SPAN_LOW)
    )
    table_blocks = (
        jnp.pad(table_low, ((0, 0), (0, 32 * HEAD_BLOCK - shard_width)))
        .reshape(table_rows, 32, HEAD_BLOCK)
        .transpose(1, 0, 2)
    )
    notes_all, found, table_head, gathered = start_step(
        notes, table_levels, table_blocks, pack(masters), GATHER_PIECES, shard_width, 1
    )
    table_head = table_head.reshape(768, HEAD_BLOCK)
    full = unpack(gathered)
    notes_rows = notes_all.reshape(128, 2, 128)
    labels_all = notes_rows[:, 1, :16].reshape(2048)
    counted_all = notes_rows[:, 1, 16:32].reshape(2048).astype(jnp.float32)
    total_count = jnp.sum(counted_all)

    vector = full["vector"].astype(jnp.float32)
    text_vec = vector[:10752].reshape(14, 768)
    layout_vec = vector[10752:13440].reshape(14, 192)
    head_vec = vector[13440:].reshape(3, 768)
    position_own = lax.dynamic_slice_in_dim(full["position"], vocab * 64, 64, 0).astype(f32)
    boxes = box_coords.reshape(4, 128)
    box_index = jnp.stack(
        [
            boxes[0],
            boxes[1],
            boxes[2],
            boxes[3],
            jnp.abs(boxes[3] - boxes[1]),
            jnp.abs(boxes[2] - boxes[0]),
            boxes[0],
            boxes[0],
        ],
        1,
    )
    qkv = (full["text"], (48, 48, 768), (0, 0, 0))
    out_w = (full["text"], (16, 48, 768), (3, 0, 0))
    up_w = (full["text"], (64, 48, 768), (1, 0, 0))
    text_sum, layout_sum, spatial, *kv, query, slot_text, slot_layout = local_call(
        open_kernel,
        [
            found,
            position_own,
            box_index,
            full["box"],
            full["box_proj"],
            qkv,
            full["layout"],
            text_vec,
            layout_vec,
            slot_hot_wide,
        ],
        [
            ((128, 768), f32),
            ((128, 192), f32),
            ((128, 768), LOW),
            ((128, 768), LOW),
            ((128, 768), LOW),
            ((128, 192), LOW),
            ((128, 192), LOW),
            ((16, 1024), LOW),
            ((16, 768), f32),
            ((16, 192), f32),
        ],
        "open_streams",
    )
    query_all = lax.all_to_all(
        jnp.broadcast_to(query[None], (4, 16, 1024)), "vocab", 0, 0, tiled=True
    ).reshape(64, 1024)
    (partial,) = local_call(score_kernel, [query_all, *kv], [((64, 1280), f32)], "partial_attention")
    partial = lax.all_to_all(partial.reshape(4, 16, 1280), "vocab", 0, 0, tiled=True)
    weights_close = [out_w, up_w, full["down"], full["layout"], full["layout_down"]]
    vectors_close = [text_vec, layout_vec, full["head"], head_vec]
    (att_text, att_layout, log_total, mid_text, mid_layout, pre_text, pre_layout, end_text,
     end_layout, joined, dense, picked) = local_call(
        close_kernel,
        [partial, slot_text, slot_layout] + weights_close + vectors_close,
        [
            ((16, 768), f32),
            ((16, 192), f32),
            ((16, 128), f32),
            ((16, 768), f32),
            ((16, 192), f32),
            ((16, 3072), f32),
            ((16, 768), f32),
            ((16, 768), f32),
            ((16, 192), f32),
            ((16, 1024), LOW),
            ((16, 768), f32),
            ((16, 768), LOW),
        ],
        "close_streams",
    )
    d_picked, table_head_grad, loss = head_step(
        picked,
        table_head,
        (labels_all - vocab * shard_width - dp * HEAD_BLOCK)[None],
        (counted_all / total_count)[None],
        counted_all[None],
        shard_width,
        3,
    )
    loss_total = loss[0, 0]
    table_head_grad = lax.all_to_all(
        table_head_grad.reshape(32, 24, HEAD_BLOCK), "dp", 0, 0, tiled=True
    )
    (back, d_mid_text, d_mid_layout, d_head, d_out, d_up, d_down, d_layout_close, d_layout_down,
     d_text_vec, d_layout_vec, d_head_vec) = local_call(
        close_back_kernel,
        [d_picked, dense, joined, att_text, att_layout, log_total, mid_text, mid_layout]
        + [pre_text, pre_layout, end_text, end_layout]
        + weights_close
        + vectors_close,
        [
            ((16, 1280), f32),
            ((16, 768), f32),
            ((16, 192), f32),
            ((768, 960), LOW),
            ((768, 768), LOW),
            ((3072, 768), LOW),
            ((3072, 768), LOW),
            ((960, 192), LOW),
            ((768, 192), LOW),
            ((14, 768), f32),
            ((14, 192), f32),
            ((3, 768), f32),
        ],
        "close_streams_back",
    )
    back = lax.all_to_all(
        jnp.broadcast_to(back[None], (4, 16, 1280)), "vocab", 0, 0, tiled=True
    ).reshape(64, 1280)
    d_query, *d_kv = local_call(
        score_back_kernel,
        [back, query_all, *kv],
        [
            ((64, 1024), f32),
            ((128, 768), LOW),
            ((128, 768), LOW),
            ((128, 192), LOW),
            ((128, 192), LOW),
        ],
        "attention_back",
    )
    d_query = lax.all_to_all(d_query.reshape(4, 16, 1024), "vocab", 0, 0, tiled=True)
    (d_query_w, d_kv_w, d_layout_open, d_embedded, d_position, d_box, d_proj, d_text_open,
     d_layout_vec_open) = local_call(
        open_back_kernel,
        [d_query, *d_kv, d_mid_text, d_mid_layout, text_sum, layout_sum, slot_text, slot_layout]
        + [qkv, full["layout"], full["box_proj"], spatial, box_index, text_vec, layout_vec]
        + [slot_hot_wide.T],
        [
            ((768, 768), LOW),
            ((1536, 768), LOW),
            ((576, 192), LOW),
            ((768, 128), LOW),
            ((64, 960), f32),
            ((4096, 128), LOW),
            ((768, 192), LOW),
            ((14, 768), f32),
            ((14, 192), f32),
        ],
        "open_streams_back",
    )
    head_levels = (
        table_head_grad.transpose(1, 0, 2)
        .reshape(table_rows, 32 * HEAD_BLOCK)[:, : levels * SPAN_LOW]
        .reshape(table_rows, levels, SPAN_LOW)
        .transpose(1, 0, 2)
        .reshape(levels * table_rows, SPAN_LOW)
        .astype(f32)
    )
    d_positions = lax.dynamic_update_slice_in_dim(
        jnp.zeros((640, 960), LOW), d_position.astype(LOW), vocab * 64, 0
    )
    table_grad, square, shards = reduce_weights(
        dict(
            query=d_query_w,
            key_value=d_kv_w,
            out=d_out,
            up=d_up,
            down=d_down,
            head=d_head,
            box=d_box,
            layout=jnp.concatenate([d_layout_open, d_layout_close], 0),
            layout_down=d_layout_down,
            box_proj=d_proj,
            position=d_positions,
            vector=jnp.concatenate(
                [
                    (d_text_vec + d_text_open).reshape(10752),
                    (d_layout_vec + d_layout_vec_open).reshape(2688),
                    d_head_vec.reshape(2304),
                ]
            ).astype(LOW),
        ),
        d_embedded.reshape(32, 24, 128),
        notes_all,
        head_levels,
        shard_width,
    )
    table_grad = (
        table_grad.reshape(levels, table_rows, SPAN_LOW)
        .transpose(1, 0, 2)
        .reshape(table_rows, levels * SPAN_LOW)[:, :shard_width]
    )
    all_grads = [table_grad] + shards
    grad_norm = jnp.sqrt(square[0, 0])
    factor = jnp.minimum(1.0, CLIP / grad_norm)
    results = []
    for (master, momentum, average), grad in zip(triples, all_grads):
        clipped = factor * grad
        momentum_next = MOMENTUM * momentum + clipped
        master_next = master - RATE * (clipped + MOMENTUM * momentum_next)
        average_next = AVERAGE_KEEP * average + (1.0 - AVERAGE_KEEP) * master_next
        results += [master_next, momentum_next, average_next]
    return tuple(results + [loss_total, total_count, grad_norm])


TOKEN_SPEC = P(None, AXES)
WEIGHT_SPECS = (
    P("dp", "vocab"),
    P(AXES, None),
    P(None, AXES, None),
    P(None, AXES),
    P(AXES, None),
    P(None, AXES),
    P(None, AXES, None),
    P(None, AXES),
    P(AXES),
)


def solution(mesh):
    weight_specs = tuple(spec for spec in WEIGHT_SPECS for _ in range(3))
    in_specs = (TOKEN_SPEC, P(None, None, AXES), TOKEN_SPEC, TOKEN_SPEC, TOKEN_SPEC) + weight_specs
    out_specs = weight_specs + (P(), P(), P())
    return jax.shard_map(
        on_device, mesh=mesh, in_specs=in_specs, out_specs=out_specs, check_vma=False
    )
```

```python
import functools

import jax
import jax.numpy as jnp
from jax import lax
from jax.experimental import pallas as pl
from jax.experimental.pallas import tpu as pltpu
from jax.sharding import PartitionSpec as P

AXES = ("dp", "vocab")
MESH = pl.DeviceIdType.MESH
LONG = pl.CostEstimate(flops=60_000_000_000, bytes_accessed=200_000_000, transcendentals=0)
ORDERS = (("z", "y", "x"), ("y", "x", "z"), ("x", "z", "y"))


def my_place():
    dp = lax.axis_index("dp")
    vocab = lax.axis_index("vocab")
    return {
        "x": (dp // 16) * 2 + vocab // 2,
        "y": (dp // 4) % 4,
        "z": dp % 4,
        "c": vocab % 2,
    }


def moved(place, dim, step):
    other = dict(place)
    other[dim] = (1 - place["c"]) if dim == "c" else (place[dim] + step + 4) % 4
    return other


def device_of(place):
    return (
        (place["x"] // 2) * 16 + place["y"] * 4 + place["z"],
        (place["x"] % 2) * 2 + place["c"],
    )


def greet(place, steps=(1, 3)):
    barrier = pltpu.get_barrier_semaphore()
    peers = [moved(place, dim, step) for dim in "xyz" for step in steps]
    peers.append(moved(place, "c", 1))
    for peer in peers:
        pl.semaphore_signal(barrier, inc=1, device_id=device_of(peer), device_id_type=MESH)
    pl.semaphore_wait(barrier, len(peers))


def remote(src, dst, send, recv, place):
    return pltpu.make_async_remote_copy(
        src_ref=src,
        dst_ref=dst,
        send_sem=send,
        recv_sem=recv,
        device_id=device_of(place),
        device_id_type=MESH,
    )


def lanes_at(ref, lanes):
    return slice(None) if lanes is None else pl.ds(*lanes)


def block_view(ref, place, dims, lanes, core=None):
    high, low = (pl.ds(0, 2), pl.ds(0, 2)) if "x" in dims else (place["x"] // 2, place["x"] % 2)
    mid = pl.ds(0, 4) if "y" in dims else place["y"]
    deep = pl.ds(0, 4) if "z" in dims else place["z"]
    where = (high, mid, deep, low)
    if core is not None:
        where += (core,)
    return ref.at[where + (slice(None), lanes_at(ref, lanes))]


def halves(lanes, number):
    if lanes is None or lanes[1] < 256:
        return (lanes, False) if number % 2 == 0 else (False, lanes)
    half = lanes[1] // 256 * 128
    return (lanes[0], half), (lanes[0] + half, lanes[1] - half)


def open_shape(dims):
    shape = ()
    if "x" in dims:
        shape += (2,)
    if "y" in dims:
        shape += (4,)
    if "z" in dims:
        shape += (4,)
    if "x" in dims:
        shape += (2,)
    return shape


def chunks_of(dims, place):
    high, mid, deep, low = place["x"] // 2, place["y"], place["z"], place["x"] % 2
    every = slice(None)
    if dims == "":
        return 1, lambda flat: ((high, mid, deep, low), ())
    inner = (every if "y" in dims else mid, every if "z" in dims else deep)
    if "x" in dims and "y" in dims and "z" in dims:
        return 8, lambda flat: ((flat // 4, flat % 4, every, every), (flat // 4, flat % 4))
    if "x" in dims:
        return 2, lambda flat: ((flat,) + inner + (every,), (flat,))
    if "y" in dims and "z" in dims:
        return 4, lambda flat: ((high, flat, every, low), (flat,))
    return 1, lambda flat: ((high,) + inner + (low,), ())


MOMENTUM = 0.9
AVERAGE_KEEP = 0.9
RATE = 1500.0
CLIP = 0.05
LOW = jnp.bfloat16
SPAN_LOW = 256
TOKEN_BLOCK = 1024


HEADS = 12
NORM_EPSILON = 1e-05
ROOT_HALF = 0.5**0.5
PEAK = 0.3989422804014327
WIDTHS = (768, 192)
HEAD_SIZES = (64, 16)
SCALES = (0.125, 0.25)
QUERY_LANES = ((0, 768), (768, 192))
NEGATIVE = -1e30


def plain_product(left, right):
    return jnp.dot(left, right, preferred_element_type=jnp.float32)


def rows_product(left, right):
    return lax.dot_general(
        left, right, (((0,), (0,)), ((), ())), preferred_element_type=jnp.float32
    )


def cols_product(left, right):
    return lax.dot_general(
        left, right, (((1,), (1,)), ((), ())), preferred_element_type=jnp.float32
    )


def exact_product(left, right):
    return jnp.dot(
        left, right, precision=lax.Precision.HIGHEST, preferred_element_type=jnp.float32
    )


def total_rows(values):
    return jnp.sum(values.astype(jnp.float32), 0, keepdims=True)


def normalised(values):
    centred = values - jnp.mean(values, -1, keepdims=True)
    scale = lax.rsqrt(jnp.mean(centred * centred, -1, keepdims=True) + NORM_EPSILON)
    return centred * scale, scale


def norm_apply(values, gain, bias):
    return normalised(values)[0] * gain + bias


def norm_back(values, gain, grad):
    unit, scale = normalised(values)
    inner = grad * gain
    result = scale * (
        inner
        - jnp.mean(inner, -1, keepdims=True)
        - unit * jnp.mean(inner * unit, -1, keepdims=True)
    )
    return result, total_rows(grad * unit), total_rows(grad)


def gelu_value(values):
    return 0.5 * values * (1.0 + lax.erf(values * ROOT_HALF))


def gelu_slope(values):
    return 0.5 * (1.0 + lax.erf(values * ROOT_HALF)) + values * PEAK * jnp.exp(
        -0.5 * values * values
    )


def row_of(ref, row):
    return ref[row : row + 1, :]


def hidden_bias(ref):
    return jnp.concatenate([row_of(ref, row) for row in range(7, 11)], 1)


def head_of(rows, stream):
    lanes = lax.broadcasted_iota(jnp.int32, (rows, WIDTHS[stream]), 1)
    return lanes // HEAD_SIZES[stream]


def stack_heads(values, stream):
    heads = head_of(values.shape[0], stream)
    zero = jnp.zeros_like(values)
    return jnp.concatenate([jnp.where(heads == h, values, zero) for h in range(HEADS)], 0)


def fold_heads(values, stream):
    rows = values.shape[0] // HEADS
    heads = head_of(rows, stream)
    total = jnp.zeros((rows, values.shape[1]), jnp.float32)
    for h in range(HEADS):
        total = total + jnp.where(heads == h, values[h * rows : (h + 1) * rows], 0.0)
    return total


def lane_heads(stream):
    rows = lax.broadcasted_iota(jnp.int32, (128, WIDTHS[stream]), 0)
    return (rows == head_of(128, stream)).astype(jnp.float32)


def head_lanes(stream):
    rows = lax.broadcasted_iota(jnp.int32, (WIDTHS[stream], 128), 0) // HEAD_SIZES[stream]
    return (rows == lax.broadcasted_iota(jnp.int32, (WIDTHS[stream], 128), 1)).astype(jnp.float32)


def stack_columns(values):
    return jnp.concatenate([values[:, h : h + 1] for h in range(HEADS)], 0)


def one_micro_batch(rows):
    row = lax.broadcasted_iota(jnp.int32, (rows, 128), 0)
    key = lax.broadcasted_iota(jnp.int32, (rows, 128), 1)
    return (row // 8) % 2 == key // 64


def coupled_scores(stacks, key_refs):
    return sum(
        cols_product(stacks[n], key_refs[n][...]) * SCALES[n] for n in range(2)
    )


def open_kernel(
    found_ref, position_ref, index_ref, box_ref, proj_ref, qkv_ref, layout_ref,
    text_vec, layout_vec, slot_ref,
    text_sum_ref, layout_sum_ref, spatial_ref, key_text, value_text, key_layout, value_layout,
    query_ref, slot_text, slot_layout,
):
    embedded = found_ref[...].astype(jnp.float32).reshape(768, 128).T
    place = position_ref[...]
    place = jnp.concatenate([place, place], 0)
    text_sum = embedded + place[:, :768]
    text_sum_ref[...] = text_sum
    tables = (0, 1, 0, 1, 2, 3)
    number = lax.broadcasted_iota(jnp.int32, (128, 1024), 1)
    for k in range(6):
        hot = (number == index_ref[:, k : k + 1]).astype(LOW)
        rows = box_ref[pl.ds(1024 * tables[k], 1024), :]
        spatial_ref[:, pl.ds(128 * k, 128)] = plain_product(hot, rows).astype(LOW)
    layout_sum = place[:, 768:] + plain_product(spatial_ref[...], proj_ref[...])
    layout_sum_ref[...] = layout_sum
    query_ref[...] = jnp.zeros_like(query_ref)
    qkv = qkv_ref[...].reshape(2304, 768)
    weights = (qkv, layout_ref[pl.ds(0, 576), :])
    sums, vecs = (text_sum, layout_sum), (text_vec, layout_vec)
    keys, values, slots = (key_text, key_layout), (value_text, value_layout), (slot_text, slot_layout)
    for n in range(2):
        width, weight, vec = WIDTHS[n], weights[n], vecs[n]
        normed = norm_apply(sums[n], row_of(vec, 0), row_of(vec, 1))
        low = normed.astype(LOW)
        keys[n][...] = cols_product(low, weight[width : 2 * width]).astype(LOW)
        values[n][...] = (cols_product(low, weight[2 * width :]) + row_of(vec, 3)).astype(LOW)
        slot = exact_product(slot_ref[...], normed)
        slots[n][...] = slot
        start, size = QUERY_LANES[n]
        query_ref[:, pl.ds(start, size)] = (
            cols_product(slot.astype(LOW), weight[:width]) + row_of(vec, 2)
        ).astype(LOW)


def score_kernel(query_ref, key_text, value_text, key_layout, value_layout, out_ref):
    stacks = [
        stack_heads(query_ref[:, pl.ds(*QUERY_LANES[n])], n) for n in range(2)
    ]
    mask = one_micro_batch(64 * HEADS)
    scores = jnp.where(mask, coupled_scores(stacks, (key_text, key_layout)), NEGATIVE)
    top = jnp.max(scores, -1, keepdims=True)
    powers = jnp.where(mask, jnp.exp(scores - top), 0.0)
    total = jnp.sum(powers, -1, keepdims=True)
    low = powers.astype(LOW)
    out_ref[:, pl.ds(768, 256)] = jnp.zeros((64, 256), jnp.float32)
    for n, values in enumerate((value_text, value_layout)):
        out_ref[:, pl.ds(*QUERY_LANES[n])] = fold_heads(plain_product(low, values[...]), n)
    lane = lax.broadcasted_iota(jnp.int32, (64, 128), 1)
    tops = jnp.zeros((64, 128), jnp.float32)
    totals = jnp.ones((64, 128), jnp.float32)
    for h in range(HEADS):
        tops = jnp.where(lane == h, top[64 * h : 64 * h + 64], tops)
        totals = jnp.where(lane == h, total[64 * h : 64 * h + 64], totals)
    out_ref[:, pl.ds(1024, 128)] = tops
    out_ref[:, pl.ds(1152, 128)] = totals


def close_kernel(
    parts_ref, slot_text, slot_layout, out_w, up_w, down_w, layout_ref, layout_down,
    text_vec, layout_vec, head_ref, head_vec,
    att_text, att_layout, log_ref, mid_text, mid_layout, pre_text, pre_layout,
    end_text, end_layout, joined_ref, dense_ref, pick_ref,
):
    tops = [parts_ref[j, :, pl.ds(1024, 128)] for j in range(4)]
    top = jnp.maximum(jnp.maximum(tops[0], tops[1]), jnp.maximum(tops[2], tops[3]))
    shares = [jnp.exp(item - top) for item in tops]
    total = sum(shares[j] * parts_ref[j, :, pl.ds(1152, 128)] for j in range(4))
    log_ref[...] = top + jnp.log(total)
    shares = [item / total for item in shares]
    joined_ref[...] = jnp.zeros_like(joined_ref)
    streams = (
        (slot_text, text_vec, out_w, up_w, down_w, att_text, mid_text, pre_text, end_text),
        (slot_layout, layout_vec, layout_ref, layout_ref, layout_down, att_layout, mid_layout,
         pre_layout, end_layout),
    )
    for n, (slot, vec, out_r, up_r, down_r, att_r, mid_r, pre_r, end_r) in enumerate(streams):
        width = WIDTHS[n]
        spread = lane_heads(n)
        att = sum(
            parts_ref[j, :, pl.ds(*QUERY_LANES[n])] * exact_product(shares[j], spread)
            for j in range(4)
        )
        att_r[...] = att
        if n == 0:
            out_m, up_m = out_r[...].reshape(768, 768), up_r[...].reshape(3072, 768)
        else:
            out_m, up_m = out_r[pl.ds(576, 192), :], up_r[pl.ds(768, 768), :]
        mid = slot[...] + (cols_product(att.astype(LOW), out_m) + row_of(vec, 4))
        mid_r[...] = mid
        first = norm_apply(mid, row_of(vec, 5), row_of(vec, 6))
        pre = cols_product(first.astype(LOW), up_m) + hidden_bias(vec)
        pre_r[...] = pre
        end = first + (
            plain_product(gelu_value(pre).astype(LOW), down_r[...]) + row_of(vec, 11)
        )
        end_r[...] = end
        joined_ref[:, pl.ds(*QUERY_LANES[n])] = norm_apply(
            end, row_of(vec, 12), row_of(vec, 13)
        ).astype(LOW)
    dense = cols_product(joined_ref[:, pl.ds(0, 960)], head_ref[...]) + row_of(head_vec, 0)
    dense_ref[...] = dense
    pick_ref[...] = norm_apply(
        gelu_value(dense), row_of(head_vec, 1), row_of(head_vec, 2)
    ).astype(LOW)


def close_back_kernel(
    grad_ref, dense_ref, joined_ref, att_text, att_layout, log_ref, mid_text, mid_layout,
    pre_text, pre_layout, end_text, end_layout, out_w, up_w, down_w, layout_ref, layout_down,
    text_vec, layout_vec, head_ref, head_vec,
    back_ref, d_mid_text, d_mid_layout, d_head, d_out, d_up, d_down, d_layout, d_layout_down,
    d_text_vec, d_layout_vec, d_head_vec,
):
    dense = dense_ref[...]
    d_active, d_gain, d_shift = norm_back(gelu_value(dense), row_of(head_vec, 1), grad_ref[...])
    d_dense = (d_active * gelu_slope(dense)).astype(LOW)
    d_head_vec[0:1, :] = total_rows(d_dense)
    d_head_vec[1:2, :] = d_gain
    d_head_vec[2:3, :] = d_shift
    d_head[...] = rows_product(d_dense, joined_ref[:, pl.ds(0, 960)]).astype(LOW)
    d_joined = plain_product(d_dense, head_ref[...])
    back_ref[:, pl.ds(768, 256)] = jnp.zeros((16, 256), jnp.float32)
    delta = jnp.zeros((16, 128), jnp.float32)
    streams = (
        (text_vec, out_w, up_w, down_w, att_text, mid_text, pre_text, end_text,
         d_mid_text, d_out, d_up, d_down, d_text_vec),
        (layout_vec, layout_ref, layout_ref, layout_down, att_layout, mid_layout, pre_layout,
         end_layout, d_mid_layout, d_layout, d_layout, d_layout_down, d_layout_vec),
    )
    for n, (vec, out_r, up_r, down_r, att_r, mid_r, pre_r, end_r, d_mid_r, d_out_r, d_up_r,
            d_down_r, d_vec) in enumerate(streams):
        width = WIDTHS[n]
        if n == 0:
            out_m, up_m = out_r[...].reshape(768, 768), up_r[...].reshape(3072, 768)
        else:
            out_m, up_m = out_r[pl.ds(576, 192), :], up_r[pl.ds(768, 768), :]
        d_end, d_gain2, d_shift2 = norm_back(
            end_r[...], row_of(vec, 12), d_joined[:, QUERY_LANES[n][0] : sum(QUERY_LANES[n])]
        )
        d_branch2 = d_end.astype(LOW)
        mid, pre = mid_r[...], pre_r[...]
        low = gelu_value(pre).astype(LOW)
        d_pre = (cols_product(d_branch2, down_r[...]) * gelu_slope(pre)).astype(LOW)
        first_low = norm_apply(mid, row_of(vec, 5), row_of(vec, 6)).astype(LOW)
        for k in range(4):
            part = slice(width * k, width * (k + 1))
            d_down_r[pl.ds(width * k, width), :] = rows_product(low[:, part], d_branch2).astype(LOW)
            up_at = pl.ds(width * k, width) if n == 0 else pl.ds(192 + width * k, width)
            d_up_r[up_at, :] = rows_product(d_pre[:, part], first_low).astype(LOW)
            d_vec[7 + k : 8 + k, :] = total_rows(d_pre[:, part])
        d_first = d_end + plain_product(d_pre, up_m)
        d_mid, d_gain1, d_shift1 = norm_back(mid, row_of(vec, 5), d_first)
        d_mid_r[...] = d_mid
        d_branch1 = d_mid.astype(LOW)
        att = att_r[...]
        d_out_r[pl.ds(0, width), :] = rows_product(d_branch1, att.astype(LOW)).astype(LOW)
        d_att = plain_product(d_branch1, out_m).astype(LOW).astype(jnp.float32)
        back_ref[:, pl.ds(*QUERY_LANES[n])] = d_att
        delta = delta + exact_product(d_att * att, head_lanes(n))
        d_vec[0:4, :] = jnp.zeros((4, width), jnp.float32)
        for row, value in (
            (4, total_rows(d_branch1)),
            (5, d_gain1),
            (6, d_shift1),
            (11, total_rows(d_branch2)),
            (12, d_gain2),
            (13, d_shift2),
        ):
            d_vec[row : row + 1, :] = value
    back_ref[:, pl.ds(1024, 128)] = log_ref[...]
    back_ref[:, pl.ds(1152, 128)] = delta


def score_back_kernel(
    back_ref, query_ref, key_text, value_text, key_layout, value_layout,
    d_query, d_key_text, d_value_text, d_key_layout, d_value_layout,
):
    keys, values = (key_text, key_layout), (value_text, value_layout)
    stacks = [stack_heads(query_ref[:, pl.ds(*QUERY_LANES[n])], n) for n in range(2)]
    grads = [stack_heads(back_ref[:, pl.ds(*QUERY_LANES[n])], n).astype(LOW) for n in range(2)]
    logs = stack_columns(back_ref[:, pl.ds(1024, 128)])
    delta = stack_columns(back_ref[:, pl.ds(1152, 128)])
    mask = one_micro_batch(64 * HEADS)
    probs = jnp.where(mask, jnp.exp(jnp.where(mask, coupled_scores(stacks, keys) - logs, 0.0)), 0.0)
    d_probs = sum(cols_product(grads[n], values[n][...]) for n in range(2))
    d_scores = (probs * (d_probs - delta)).astype(LOW)
    low = probs.astype(LOW)
    d_query[:, pl.ds(768, 256)] = jnp.zeros((64, 256), jnp.float32)
    d_keys, d_values = (d_key_text, d_key_layout), (d_value_text, d_value_layout)
    for n in range(2):
        d_query[:, pl.ds(*QUERY_LANES[n])] = (
            fold_heads(plain_product(d_scores, keys[n][...]), n) * SCALES[n]
        )
        d_keys[n][...] = (rows_product(d_scores, stacks[n]) * SCALES[n]).astype(LOW)
        d_values[n][...] = rows_product(low, grads[n]).astype(LOW)


def open_back_kernel(
    parts_ref, d_key_text, d_value_text, d_key_layout, d_value_layout, d_mid_text, d_mid_layout,
    text_sum, layout_sum, slot_text, slot_layout, qkv_ref, layout_ref, proj_ref, spatial_ref,
    index_ref, text_vec, layout_vec, slot_turned,
    d_query_w, d_kv_w, d_layout, d_embedded, d_position, d_box, d_proj, d_text_vec, d_layout_vec,
):
    qkv = qkv_ref[...].reshape(2304, 768)
    streams = (
        (qkv, d_key_text, d_value_text, d_mid_text, text_sum, slot_text, text_vec, d_text_vec),
        (layout_ref[pl.ds(0, 576), :], d_key_layout, d_value_layout, d_mid_layout, layout_sum,
         slot_layout, layout_vec, d_layout_vec),
    )
    lows = []
    for n, (weight, d_key_r, d_value_r, d_mid_r, sum_r, slot_r, vec, d_vec) in enumerate(streams):
        width = WIDTHS[n]
        lanes = pl.ds(*QUERY_LANES[n])
        d_query = sum(parts_ref[j, :, lanes] for j in range(4)).astype(LOW)
        d_key, d_value = d_key_r[...], d_value_r[...]
        d_slot = d_mid_r[...] + plain_product(d_query, weight[:width])
        d_normed = (
            plain_product(d_key, weight[width : 2 * width])
            + plain_product(d_value, weight[2 * width :])
            + exact_product(slot_turned[...], d_slot)
        )
        sums = sum_r[...]
        low = norm_apply(sums, row_of(vec, 0), row_of(vec, 1)).astype(LOW)
        d_sum, d_gain, d_shift = norm_back(sums, row_of(vec, 0), d_normed)
        d_vec[...] = jnp.zeros_like(d_vec)
        for row, value in ((0, d_gain), (1, d_shift), (2, total_rows(d_query)), (3, total_rows(d_value))):
            d_vec[row : row + 1, :] = value
        slot_low = slot_r[...].astype(LOW)
        grads = (rows_product(d_query, slot_low), rows_product(d_key, low), rows_product(d_value, low))
        if n == 0:
            d_query_w[...] = grads[0].astype(LOW)
            d_kv_w[pl.ds(0, 768), :] = grads[1].astype(LOW)
            d_kv_w[pl.ds(768, 768), :] = grads[2].astype(LOW)
        else:
            for k in range(3):
                d_layout[pl.ds(192 * k, 192), :] = grads[k].astype(LOW)
        d_low = d_sum.astype(LOW)
        lows.append(d_low)
        wide = d_low.astype(jnp.float32)
        d_position[:, lanes] = wide[:64] + wide[64:]
        if n == 0:
            d_embedded[...] = wide.T.astype(LOW)
    d_spatial = cols_product(lows[1], proj_ref[...]).astype(LOW)
    d_proj[...] = rows_product(spatial_ref[...], lows[1]).astype(LOW)
    number = lax.broadcasted_iota(jnp.int32, (128, 1024), 1)
    for table, users in enumerate(((0, 2), (1, 3), (4,), (5,))):
        total = 0.0
        for k in users:
            hot = (number == index_ref[:, k : k + 1]).astype(LOW)
            total = total + rows_product(hot, d_spatial[:, 128 * k : 128 * k + 128])
        d_box[pl.ds(1024 * table, 1024), :] = total.astype(LOW)


def local_call(kernel, inputs, outputs, name):
    specs, arrays = [], []

    def spec(shape, index):
        return pl.BlockSpec(shape, lambda step: index, pipeline_mode=pl.Buffered(1))

    for item in inputs:
        array, shape, index = item if isinstance(item, tuple) else (item, item.shape, None)
        specs.append(spec(shape, index or (0,) * len(shape)))
        arrays.append(array)
    return pl.pallas_call(
        kernel,
        name=name,
        grid=(1,),
        out_shape=[jax.ShapeDtypeStruct(shape, dtype) for shape, dtype in outputs],
        in_specs=specs,
        out_specs=[spec(shape, (0,) * len(shape)) for shape, dtype in outputs],
        compiler_params=pltpu.CompilerParams(vmem_limit_bytes=56 * 1024 * 1024),
    )(*arrays)


PLANES = (("y", "z"), ("x", "z"), ("x", "y"))
LINES = ("x", "y", "z")
HEAD_BLOCK = 512
PLANE_STEPS = [(a, b) for a in range(4) for b in range(4) if (a, b) != (0, 0)]


def plane_peer(place, plane, a, b):
    return moved(moved(place, plane[0], a), plane[1], b)


def head_peers(place):
    peers = [
        plane_peer(place, plane, a, b)
        for plane in PLANES
        for a, b in PLANE_STEPS
        if (a and b) or plane == ("y", "z")
    ]
    peers += [moved(place, "x", step) for step in (1, 2, 3)]
    peers += [moved(moved(place, "x", step), "c", 1) for step in range(4)]
    return peers


def merge_logs(logs):
    top = logs[0]
    for item in logs[1:]:
        top = jnp.maximum(top, item)
    total = jnp.exp(logs[0] - top)
    for item in logs[1:]:
        total = total + jnp.exp(item - top)
    return top + jnp.log(total)


def head_kernel(
    limit_width, pick_ref, table_ref, label_ref, weight_ref, count_ref,
    grad_ref, d_table_ref, loss_ref,
    picked, table, logits, d_logits, part, acc, cross, near, far, line_in, plane_in, own_sem,
    plane_send, plane_recv, line_send, line_recv, pass_send, pass_recv,
    near_send, near_recv, far_send, far_recv, core_send, core_recv,
    back_send, back_recv, last_send, last_recv,
):
    place = my_place()
    sibling = moved(place, "c", 1)
    barrier = pltpu.get_barrier_semaphore()
    peers = head_peers(place)
    for peer in peers:
        pl.semaphore_signal(barrier, inc=1, device_id=device_of(peer), device_id_type=MESH)
    own = pltpu.make_async_copy(
        pick_ref, block_view(picked, place, "", None, place["c"]), own_sem
    )
    own.start()
    pl.semaphore_wait(barrier, len(peers))
    sends = []

    def go(copy):
        copy.start()
        sends.append(copy)
        return copy

    def third(k):
        return (256 * k, 256)

    flights = {}
    for k in range(3):
        here = block_view(picked, place, "", third(k), place["c"])
        for a, b in PLANE_STEPS:
            n = 4 * a + b - 1
            flights[(k, n)] = go(
                remote(
                    pick_ref.at[:, pl.ds(*third(k))], here, plane_send.at[k, n],
                    plane_recv.at[k, n], plane_peer(place, PLANES[k], a, b),
                )
            )
    table[...] = table_ref[...].astype(jnp.float32).T.astype(LOW)
    own.wait()
    lines, passes = {}, []

    def hand_over(k, n, where):
        passes.append(go(remote(where, where, pass_send.at[k, n], pass_recv.at[k, n], sibling)))

    for k in range(3):
        for a, b in PLANE_STEPS:
            flights[(k, 4 * a + b - 1)].wait_recv()
        sheet = block_view(picked, place, PLANES[k], third(k), place["c"])
        for step in (1, 2, 3):
            lines[(k, step)] = go(
                remote(
                    sheet, sheet, line_send.at[k, step - 1], line_recv.at[k, step - 1],
                    moved(place, LINES[k], step),
                )
            )
        hand_over(k, 0, sheet)
    for step in (1, 3, 2):
        for k in range(3):
            lines[(k, step)].wait_recv()
            origin = moved(place, LINES[k], -step)
            hand_over(k, step, block_view(picked, origin, PLANES[k], third(k), place["c"]))
    for copy in passes:
        copy.wait_recv()

    limit = limit_width - lax.axis_index("dp") * HEAD_BLOCK
    row = lax.broadcasted_iota(jnp.int32, (HEAD_BLOCK, 256), 0)
    valid = row < limit
    mine = place["x"] * 2 + place["c"]
    for chunk in range(8):
        high, mid = chunk // 4, chunk % 4
        lanes = pl.ds(256 * chunk, 256)
        values = cols_product(table[...], picked[high, mid].reshape(256, 768))
        values = jnp.where(valid, values, NEGATIVE)
        logits[:, lanes] = values
        top = jnp.max(values, 0, keepdims=True)
        total = jnp.sum(jnp.where(valid, jnp.exp(values - top), 0.0), 0, keepdims=True)
        hot = valid & (row == label_ref[:, lanes])
        near[mine, 0, :, lanes] = top + jnp.log(jnp.maximum(total, 1e-30))
        near[mine, 1, :, lanes] = jnp.sum(jnp.where(hot, values, 0.0), 0, keepdims=True)
    meets = []
    for n in range(1, 8):
        peer = moved(place, "x", n // 2)
        if n % 2:
            peer = moved(peer, "c", 1)
        meets.append(
            go(remote(near.at[mine], near.at[mine], near_send.at[n - 1], near_recv.at[n - 1], peer))
        )
    for copy in meets:
        copy.wait_recv()
    spot = place["y"] * 4 + place["z"]
    far[spot, 0] = merge_logs([near[n, 0] for n in range(8)])
    far[spot, 1] = sum(near[n, 1] for n in range(8))
    meets = []
    for a, b in PLANE_STEPS:
        n = 4 * a + b - 1
        peer = plane_peer(place, ("y", "z"), a, b)
        meets.append(go(remote(far.at[spot], far.at[spot], far_send.at[n], far_recv.at[n], peer)))
    for copy in meets:
        copy.wait_recv()
    log_total = merge_logs([far[n, 0] for n in range(16)])
    target = sum(far[n, 1] for n in range(16))
    loss = jnp.sum(count_ref[...] * (log_total - target), 1, keepdims=True)
    loss_ref[...] = jnp.broadcast_to(loss, loss_ref.shape)

    crossings = []
    for chunk in range(8):
        high, mid = chunk // 4, chunk % 4
        lanes = pl.ds(256 * chunk, 256)
        here = slice(256 * chunk, 256 * chunk + 256)
        hot = (valid & (row == label_ref[:, lanes])).astype(jnp.float32)
        powers = jnp.where(valid, jnp.exp(logits[:, lanes] - log_total[:, here]), 0.0)
        low = (weight_ref[:, lanes] * (powers - hot)).astype(LOW)
        d_logits[:, lanes] = low
        part[high, mid] = rows_product(low, table[...]).astype(LOW).reshape(4, 2, 2, 16, 768)
        crossings.append(
            go(
                remote(
                    part.at[high, mid, :, :, sibling["c"]], cross.at[high, mid],
                    core_send.at[chunk], core_recv.at[chunk], sibling,
                )
            )
        )
    for chunk in range(8):
        high, mid = chunk // 4, chunk % 4
        crossings[chunk].wait_recv()
        acc[high, mid] = part[high, mid, :, :, place["c"]] + cross[high, mid]

    legs = {}
    for k in range(3):
        for step in (1, 3, 2):
            there = moved(place, LINES[k], step)
            legs[(k, step)] = go(
                remote(
                    block_view(acc, there, PLANES[k], third(k)), line_in[k].at[step - 1],
                    back_send.at[k, step - 1], back_recv.at[k, step - 1], there,
                )
            )
    d_table = jnp.zeros((HEAD_BLOCK, 768), jnp.float32)
    for chunk in range(8):
        d_table = d_table + plain_product(
            d_logits[:, pl.ds(256 * chunk, 256)], picked[chunk // 4, chunk % 4].reshape(256, 768)
        )
    d_table_ref[...] = d_table.T.astype(LOW)
    ends = {}
    for k in range(3):
        for step in (1, 2, 3):
            legs[(k, step)].wait_recv()
        count, chunk_of = chunks_of("".join(PLANES[k]), place)
        for flat in range(count):
            block, inner = chunk_of(flat)
            where = block + (slice(None), pl.ds(*third(k)))
            total = acc[where].astype(jnp.float32)
            for step in (1, 2, 3):
                total = total + line_in[k][(step - 1,) + inner].astype(jnp.float32)
            acc[where] = total.astype(LOW)
        for a, b in PLANE_STEPS:
            n = 4 * a + b - 1
            there = plane_peer(place, PLANES[k], a, b)
            ends[(k, n)] = go(
                remote(
                    block_view(acc, there, "", third(k)), plane_in.at[k, n],
                    last_send.at[k, n], last_recv.at[k, n], there,
                )
            )
    home = (place["x"] // 2, place["y"], place["z"], place["x"] % 2)
    for k in range(3):
        total = acc[home + (slice(None), pl.ds(*third(k)))].astype(jnp.float32)
        for n in range(15):
            ends[(k, n)].wait_recv()
            total = total + plane_in[k, n].astype(jnp.float32)
        grad_ref[:, pl.ds(*third(k))] = total
    for copy in sends:
        copy.wait_send()


def head_step(picked, table, labels, weights, counts, width, collective_id):
    sems = pltpu.SemaphoreType.DMA
    everyone = (2, 4, 4, 2, 2, 16, 768)
    half = (2, 4, 4, 2, 16, 768)
    line_slots = [
        pltpu.VMEM((3,) + open_shape("".join(PLANES[k])) + (16, 256), LOW) for k in range(3)
    ]

    def kernel(*refs):
        head_kernel(width, *refs[:17], refs[17:20], *refs[20:])

    return pl.pallas_call(
        kernel,
        out_shape=[
            jax.ShapeDtypeStruct((16, 768), jnp.float32),
            jax.ShapeDtypeStruct((768, HEAD_BLOCK), LOW),
            jax.ShapeDtypeStruct((8, 128), jnp.float32),
        ],
        in_specs=[pl.BlockSpec(memory_space=pltpu.VMEM)] * 5,
        out_specs=[pl.BlockSpec(memory_space=pltpu.VMEM)] * 3,
        scratch_shapes=[
            pltpu.VMEM(everyone, LOW),
            pltpu.VMEM((HEAD_BLOCK, 768), LOW),
            pltpu.VMEM((HEAD_BLOCK, 2048), jnp.float32),
            pltpu.VMEM((HEAD_BLOCK, 2048), LOW),
            pltpu.VMEM(everyone, LOW),
            pltpu.VMEM(half, LOW),
            pltpu.VMEM(half, LOW),
            pltpu.VMEM((8, 2, 1, 2048), jnp.float32),
            pltpu.VMEM((16, 2, 1, 2048), jnp.float32),
        ]
        + line_slots
        + [
            pltpu.VMEM((3, 15, 16, 256), LOW),
            sems(()),
            sems((3, 15)),
            sems((3, 15)),
            sems((3, 3)),
            sems((3, 3)),
            sems((3, 4)),
            sems((3, 4)),
            sems((7,)),
            sems((7,)),
            sems((15,)),
            sems((15,)),
            sems((8,)),
            sems((8,)),
            sems((3, 3)),
            sems((3, 3)),
            sems((3, 15)),
            sems((3, 15)),
        ],
        compiler_params=pltpu.CompilerParams(
            collective_id=collective_id, has_side_effects=True, vmem_limit_bytes=56 * 1024 * 1024
        ),
    )(picked, table, labels, weights, counts)


def greet_groups(place, extra):
    barrier = pltpu.get_barrier_semaphore()
    dp, vocab = device_of(place)

    def signal(device):
        pl.semaphore_signal(barrier, inc=1, device_id=device, device_id_type=MESH)

    def group(step, carry):
        signal(((dp + step) % 32, vocab))
        return carry

    lax.fori_loop(1, 32, group, 0)
    for step in (1, 2, 3):
        signal((dp, (vocab + step) % 4))
    for peer in extra:
        signal(device_of(peer))
    pl.semaphore_wait(barrier, 34 + len(extra))


def beyond(place):
    return moved(place, "x", 2 * (place["x"] % 2) - 1)


def start_kernel(
    pieces, count, width, notes_ref, levels_ref, blocks_ref, *refs
):
    ins, refs = refs[:count], refs[count:]
    notes_out, found_out, table_out = refs[:3]
    outs, refs = refs[3 : 3 + count], refs[3 + count :]
    notes_all, found, found_in, merged = refs[:4]
    note_sems, spread_sems, found_sems, vocab_sems, table_sems = refs[4:9]
    own_sem, ring_send, ring_recv, pass_send, pass_recv = refs[9:]
    place = my_place()
    sibling = moved(place, "c", 1)
    own_dp, own_vocab = device_of(place)
    greet_groups(place, [beyond(place)])

    def to_device(src, dst, sems, device):
        return pltpu.make_async_remote_copy(
            src_ref=src, dst_ref=dst, send_sem=sems.at[0], recv_sem=sems.at[1],
            device_id=device, device_id_type=MESH,
        )

    rings, passes = {}, []

    def spot(number, origin, dims, lanes):
        return block_view(outs[number], origin, dims, lanes, place["c"])

    def send(phase, way, piece, src, dst, target):
        copy = remote(
            src, dst, ring_send.at[phase, way, piece], ring_recv.at[phase, way, piece], target
        )
        copy.start()
        rings[(phase, way, piece)] = copy

    def hand_over(phase, way, piece, where):
        copy = remote(
            where, where, pass_send.at[phase, way, piece], pass_recv.at[phase, way, piece], sibling
        )
        copy.start()
        passes.append(copy)

    def begin(phase, piece):
        number, lanes, order = pieces[piece]
        dim, dims = ORDERS[order][phase], ORDERS[order][:phase]
        where = spot(number, place, dims, lanes)
        src = ins[number].at[:, lanes_at(ins[number], lanes)] if phase == 0 else where
        for way, step in ((0, 1), (1, -1)):
            send(phase, way, piece, src, where, moved(place, dim, step))

    def forward(phase):
        for piece, (number, lanes, order) in enumerate(pieces):
            dim, dims = ORDERS[order][phase], ORDERS[order][:phase]
            parts = halves(lanes, piece)
            for way, step in ((0, 1), (1, -1)):
                rings[(phase, way, piece)].wait_recv()
                origin = moved(place, dim, -step)
                if parts[way] is not False:
                    onward = spot(number, origin, dims, parts[way])
                    send(phase, 2 + way, piece, onward, onward, moved(place, dim, step))
                if phase == 2:
                    hand_over(phase, way, piece, spot(number, origin, dims, lanes))

    def conclude(phase):
        for piece, (number, lanes, order) in enumerate(pieces):
            dim, dims = ORDERS[order][phase], ORDERS[order][:phase]
            parts = halves(lanes, piece)
            for way in range(2):
                if parts[way] is not False:
                    rings[(phase, 2 + way, piece)].wait_recv()
            if phase == 0:
                begin(1, piece)
            elif phase == 1:
                begin(2, piece)
                hand_over(1, 0, piece, spot(number, place, ORDERS[order][:2], lanes))
            else:
                hand_over(2, 2, piece, spot(number, moved(place, dim, 2), dims, lanes))

    own_copies = []
    for piece in range(len(pieces)):
        begin(0, piece)
    for number in range(count):
        copy = pltpu.make_async_copy(
            ins[number], spot(number, place, "", None), own_sem.at[number]
        )
        copy.start()
        own_copies.append(copy)
    own_notes = notes_all.at[own_dp, own_vocab]
    pltpu.make_async_copy(notes_ref, own_notes, note_sems.at[1]).start()
    for step in (1, 2, 3):
        to_device(notes_ref, own_notes, note_sems, (own_dp, (own_vocab + step) % 4)).start()
    pltpu.make_async_copy(
        blocks_ref.at[own_dp], table_out.at[own_dp], table_sems.at[1]
    ).start()

    def send_block(step, carry):
        other = (own_dp + step) % 32
        to_device(
            blocks_ref.at[other], table_out.at[own_dp], table_sems, (other, own_vocab)
        ).start()
        return carry

    lax.fori_loop(1, 32, send_block, 0)

    group_notes = notes_all.at[own_dp]
    pltpu.make_async_copy(group_notes, group_notes, note_sems.at[1]).wait()

    def send_notes(step, carry):
        to_device(
            group_notes, group_notes, spread_sems, ((own_dp + step) % 32, own_vocab)
        ).start()
        return carry

    lax.fori_loop(1, 32, send_notes, 0)
    for copy in own_copies:
        copy.wait()
    forward(0)
    rows = found.shape[2]
    levels = levels_ref.shape[0] // rows

    def pick(step, carry):
        ids = jnp.concatenate(
            [notes_all[step * 2 + n // 4, n % 4, 0:1, :] for n in range(8)], 1
        )
        local = ids - own_vocab * width
        high = jnp.where((local >= 0) & (local < width), local >> 8, -1)
        low = local & 255
        hot = (lax.broadcasted_iota(jnp.int32, (SPAN_LOW, 1024), 0) == low).astype(LOW)
        total = jnp.zeros((rows, 1024), jnp.float32)
        group = 5
        for first in range(0, levels, group):
            values = jnp.dot(
                levels_ref[pl.ds(first * rows, group * rows), :],
                hot,
                preferred_element_type=jnp.float32,
            )
            for level in range(group):
                total = total + jnp.where(
                    high == first + level, values[level * rows : (level + 1) * rows], 0.0
                )
        total = total.astype(LOW)
        for n in range(8):
            found[step * 2 + n // 4, n % 4] = total[:, 128 * n : 128 * n + 128]
        return carry

    arrived = notes_all.at[pl.ds(0, 31)]
    pltpu.make_async_copy(arrived, arrived, spread_sems.at[1]).wait()
    conclude(0)
    lax.fori_loop(0, 3, pick, 0)
    forward(1)
    lax.fori_loop(3, 6, pick, 0)
    conclude(1)
    lax.fori_loop(6, 16, pick, 0)
    swaps = []
    for step in (1, 2, 3):
        there = (own_vocab + step) % 4
        copy = pltpu.make_async_remote_copy(
            src_ref=found.at[:, there], dst_ref=found_in.at[own_vocab],
            send_sem=vocab_sems.at[0, step - 1], recv_sem=vocab_sems.at[1, step - 1],
            device_id=(own_dp, there), device_id_type=MESH,
        )
        copy.start()
        swaps.append(copy)
    forward(2)
    total = found[:, own_vocab]
    for step in (1, 2, 3):
        swaps[step - 1].wait_recv()
        total = total + found_in[(own_vocab - step + 4) % 4]
    merged[...] = total
    pltpu.make_async_copy(merged.at[own_dp], found_out.at[own_dp], found_sems.at[1]).start()

    def send_found(step, carry):
        there = (own_dp + step) % 32
        to_device(
            merged.at[there], found_out.at[own_dp], found_sems, (there, own_vocab)
        ).start()
        return carry

    lax.fori_loop(1, 32, send_found, 0)
    conclude(2)
    notes_out[...] = notes_all[...]
    pltpu.make_async_copy(found_out, found_out, found_sems.at[1]).wait()
    pltpu.make_async_copy(table_out, table_out, table_sems.at[1]).wait()
    for sems, ref in (
        (note_sems, notes_all.at[0, pl.ds(0, 3)]),
        (spread_sems, arrived),
        (found_sems, merged.at[pl.ds(0, 31)]),
        (table_sems, blocks_ref.at[pl.ds(0, 31)]),
    ):
        pltpu.make_async_copy(ref, ref, sems.at[0]).wait()
    for copy in swaps:
        copy.wait_send()
    for copy in rings.values():
        copy.wait_send()
    for copy in passes:
        copy.wait()


def start_step(notes, levels, blocks, arrays, pieces, width, collective_id):
    count, total = len(arrays), len(pieces)
    sems = pltpu.SemaphoreType.DMA
    anywhere = pl.BlockSpec(memory_space=pl.ANY)
    local = pl.BlockSpec(memory_space=pltpu.VMEM)
    rows = blocks.shape[1]
    notes_all, found, table, *outs = pl.pallas_call(
        functools.partial(start_kernel, pieces, count, width),
        out_shape=[
            jax.ShapeDtypeStruct((32, 4) + notes.shape, jnp.int32),
            jax.ShapeDtypeStruct((32, rows, 128), LOW),
            jax.ShapeDtypeStruct(blocks.shape, LOW),
        ]
        + [jax.ShapeDtypeStruct((2, 4, 4, 2, 2) + a.shape, a.dtype) for a in arrays],
        in_specs=[local, local, anywhere] + [anywhere] * count,
        out_specs=[local, anywhere, anywhere] + [anywhere] * count,
        scratch_shapes=[
            pltpu.VMEM((32, 4) + notes.shape, jnp.int32),
            pltpu.VMEM((32, 4, rows, 128), LOW),
            pltpu.VMEM((4, 32, rows, 128), LOW),
            pltpu.VMEM((32, rows, 128), LOW),
            sems((2,)),
            sems((2,)),
            sems((2,)),
            sems((2, 3)),
            sems((2,)),
            sems((count,)),
            sems((3, 4, total)),
            sems((3, 4, total)),
            sems((3, 3, total)),
            sems((3, 3, total)),
        ],
        cost_estimate=LONG,
        compiler_params=pltpu.CompilerParams(
            collective_id=collective_id, has_side_effects=True, vmem_limit_bytes=40 * 1024 * 1024
        ),
    )(notes, levels, blocks, *arrays)
    return notes_all, found, table, [o.reshape((128,) + a.shape) for o, a in zip(outs, arrays)]


def finish_kernel(sources, pieces, count, width, *refs):
    total = len(pieces)
    ins, refs = refs[: len(sources)], refs[len(sources) :]
    text_ref, notes_ref, head_ref, refs = refs[0], refs[1], refs[2], refs[3:]
    outs, table_ref, square_ref, refs = refs[:count], refs[count], refs[count + 1], refs[count + 2 :]
    accs, crosses, refs = refs[:count], refs[count : 2 * count], refs[2 * count :]
    slots, refs = refs[: 12 * total], refs[12 * total :]
    text_all, spread, near, far = refs[:4]
    own_sem, core_sems, ring_sems, text_sems, vocab_sems, near_sems, far_sems = refs[4:]
    place = my_place()
    sibling = moved(place, "c", 1)
    own_dp, own_vocab = device_of(place)
    across = moved(moved(place, "x", 2), "c", 1)
    greet_groups(place, [beyond(place), moved(beyond(place), "c", 1), across])
    started = []

    def go(src, dst, sems, index, target):
        copy = remote(src, dst, sems.at[(0,) + index], sems.at[(1,) + index], target)
        copy.start()
        started.append(copy)
        return copy

    def add(number, lanes, at, dims, others):
        acc = accs[number]
        count, chunk = chunks_of(dims, at)

        def body(flat, carry):
            block, inner = chunk(flat)
            where = block + (slice(None), lanes_at(acc, lanes))
            parts = [
                other[inner] if index is None else other[block + index] for other, index in others
            ]
            if len(parts) == 1:
                acc[where] = acc[where] + parts[0]
            else:
                wide = [part.astype(jnp.float32) for part in [acc[where]] + parts]
                acc[where] = sum(wide).astype(acc.dtype)
            return carry

        if count == 1:
            body(0, 0)
        else:
            lax.fori_loop(0, count, body, 0)

    first, pair = {}, 0
    for piece, (number, lanes, order) in enumerate(pieces):
        for index, (owner, high, mids) in enumerate(sources):
            if owner != number:
                continue
            every = slice(None)
            run = lanes_at(accs[number], lanes)
            at = (pl.ds(*high), pl.ds(*mids), every, every, every, run)
            src = (every, every, every, every)
            cross = go(
                ins[index].at[src + (sibling["c"], every, run)], crosses[number].at[at],
                core_sems, (pair,), sibling,
            )
            own = pltpu.make_async_copy(
                ins[index].at[src + (place["c"], every, run)], accs[number].at[at], own_sem.at[pair]
            )
            own.start()
            first.setdefault(piece, []).append((cross, own))
            pair += 1

    own_text = text_all.at[own_dp, own_vocab]
    pltpu.make_async_copy(text_ref.at[own_dp], own_text, text_sems.at[1]).start()

    def send_text(step, carry):
        there = (own_dp + step) % 32
        pltpu.make_async_remote_copy(
            src_ref=text_ref.at[there], dst_ref=own_text, send_sem=text_sems.at[0],
            recv_sem=text_sems.at[1], device_id=(there, own_vocab), device_id_type=MESH,
        ).start()
        return carry

    rings = {}

    def slot(phase, way, piece):
        return slots[(phase * 4 + way) * total + piece]

    def send(phase, way, piece, src, step):
        number, lanes, order = pieces[piece]
        rings[(phase, way, piece)] = go(
            src, slot(phase, way, piece), ring_sems, (phase, way, piece),
            moved(place, ORDERS[order][phase], step),
        )

    def begin(phase, piece):
        number, lanes, order = pieces[piece]
        dim, rest = ORDERS[order][phase], ORDERS[order][phase + 1 :]
        parts = halves(lanes, piece)
        there = moved(place, dim, 2)
        for way, step in ((0, 1), (1, -1)):
            if parts[way] is not False:
                send(phase, way, piece, block_view(accs[number], there, rest, parts[way]), step)

    def pass_on(phase):
        for piece, (number, lanes, order) in enumerate(pieces):
            dim, rest = ORDERS[order][phase], ORDERS[order][phase + 1 :]
            parts = halves(lanes, piece)
            for way, step in ((0, 1), (1, -1)):
                there = moved(place, dim, step)
                if parts[way] is not False:
                    rings[(phase, way, piece)].wait_recv()
                    add(number, parts[way], there, rest, [(slot(phase, way, piece), None)])
                send(phase, 2 + way, piece, block_view(accs[number], there, rest, lanes), step)

    def take_in(phase):
        for piece, (number, lanes, order) in enumerate(pieces):
            rest = ORDERS[order][phase + 1 :]
            for way in range(2):
                rings[(phase, 2 + way, piece)].wait_recv()
            others = [slot(phase, 2 + way, piece) for way in range(2)]
            if phase < 2:
                add(number, lanes, place, rest, [(other, None) for other in others])
                begin(phase + 1, piece)
            else:
                where = (slice(None), lanes_at(accs[number], lanes))
                value = accs[number][home + where].astype(jnp.float32)
                for other in others:
                    value = value + other[...].astype(jnp.float32)
                outs[number][where] = value

    home = (place["x"] // 2, place["y"], place["z"], place["x"] % 2)
    for piece, (number, lanes, order) in enumerate(pieces):
        for cross, own in first[piece]:
            own.wait()
            cross.wait_recv()
        run = (slice(None), lanes_at(accs[number], lanes))
        add(number, lanes, place, "xyz", [(crosses[number], run)])
        begin(0, piece)
        if piece == 2:
            lax.fori_loop(1, 32, send_text, 0)

    rows = text_all.shape[2]
    levels = head_ref.shape[0] // rows
    table_ref[...] = head_ref[...]

    def scatter(block, carry):
        ids = jnp.concatenate(
            [notes_ref[block * 2 + n // 4, n % 4, 0:1, :] for n in range(8)], 1
        )
        local = ids - own_vocab * width
        high = jnp.where((local >= 0) & (local < width), local >> 8, -1)
        hot = (lax.broadcasted_iota(jnp.int32, (SPAN_LOW, 1024), 0) == (local & 255)).astype(LOW)
        grad = jnp.concatenate(
            [text_all[block * 2 + n // 4, n % 4] for n in range(8)], 1
        ).astype(jnp.float32)
        for level in range(0, levels, 2):
            spread[pl.ds(level * rows, 2 * rows), :] = jnp.concatenate(
                [jnp.where(high == level + n, grad, 0.0) for n in range(2)], 0
            ).astype(LOW)
        group = 10 * rows
        for start in range(0, levels * rows, group):
            table_ref[pl.ds(start, group), :] += cols_product(spread[pl.ds(start, group), :], hot)
        return carry

    own_column = text_all.at[:, own_vocab]
    pltpu.make_async_copy(own_column, own_column, text_sems.at[1]).wait()
    swaps = []
    for step in (1, 2, 3):
        copy = pltpu.make_async_remote_copy(
            src_ref=own_column, dst_ref=own_column, send_sem=vocab_sems.at[0, step - 1],
            recv_sem=vocab_sems.at[1, step - 1], device_id=(own_dp, (own_vocab + step) % 4),
            device_id_type=MESH,
        )
        copy.start()
        swaps.append(copy)
    pass_on(0)
    for copy in swaps:
        copy.wait_recv()
    lax.fori_loop(0, 7, scatter, 0)
    take_in(0)
    lax.fori_loop(7, 10, scatter, 0)
    pass_on(1)
    lax.fori_loop(10, 12, scatter, 0)
    take_in(1)
    lax.fori_loop(12, 14, scatter, 0)
    pass_on(2)
    lax.fori_loop(14, 16, scatter, 0)
    take_in(2)
    square = jnp.zeros((1, 1), jnp.float32)

    def squared(value):
        return jnp.sum(jnp.sum(value * value, 1, keepdims=True), 0, keepdims=True)

    for out in outs:
        square = square + squared(out[...])
    square = square + squared(table_ref[...])

    mine = place["x"] * 2 + place["c"]
    near[mine] = jnp.broadcast_to(square, (8, 128))
    meets = []
    for n in range(1, 8):
        peer = moved(place, "x", n // 2)
        if n % 2:
            peer = moved(peer, "c", 1)
        meets.append(go(near.at[mine], near.at[mine], near_sems, (n - 1,), peer))
    for copy in meets:
        copy.wait_recv()
    spot = place["y"] * 4 + place["z"]
    far[spot] = sum(near[n] for n in range(8))
    meets = []
    for a, b in PLANE_STEPS:
        peer = plane_peer(place, ("y", "z"), a, b)
        meets.append(go(far.at[spot], far.at[spot], far_sems, (4 * a + b - 1,), peer))
    for copy in meets:
        copy.wait_recv()
    square_ref[...] = sum(far[n] for n in range(16))
    sent = text_ref.at[pl.ds(0, 31)]
    pltpu.make_async_copy(sent, sent, text_sems.at[0]).wait()
    for copy in swaps:
        copy.wait_send()
    for copy in started:
        copy.wait_send()


def finish_step(arrays, text, notes, head_levels, sources, pieces, width, collective_id):
    shapes, views = {}, []
    for array, (owner, high, mids) in zip(arrays, sources):
        shapes[owner] = array.shape[1:]
        views.append(array.reshape((high[1], mids[1], 4, 2, 2) + array.shape[1:]))
    count, total = len(shapes), len(pieces)
    pairs = sum(owner == piece[0] for piece in pieces for owner, high, mids in sources)
    scratch = [pltpu.VMEM((2, 4, 4, 2) + shapes[n], LOW) for n in range(count)] * 2
    widths = []
    for piece, (number, lanes, order) in enumerate(pieces):
        parts = halves(lanes, piece)
        widths.append([shapes[number][1] if part is None else part for part in
                       [p if p in (None, False) else p[1] for p in (*parts, lanes, lanes)]])
    for phase in range(3):
        for way in range(4):
            for piece, (number, lanes, order) in enumerate(pieces):
                wide = widths[piece][way]
                if wide is False:
                    scratch.append(pltpu.VMEM((8, 128), LOW))
                else:
                    rest = open_shape(ORDERS[order][phase + 1 :])
                    scratch.append(pltpu.VMEM(rest + (shapes[number][0], wide), LOW))
    rows = text.shape[1]
    sems = pltpu.SemaphoreType.DMA
    scratch += [
        pltpu.VMEM((32, 4, rows, 128), LOW),
        pltpu.VMEM((head_levels.shape[0], 1024), LOW),
        pltpu.VMEM((8, 8, 128), jnp.float32),
        pltpu.VMEM((16, 8, 128), jnp.float32),
        sems((pairs,)),
        sems((2, pairs)),
        sems((2, 3, 4, total)),
        sems((2,)),
        sems((2, 3)),
        sems((2, 7)),
        sems((2, 15)),
    ]
    local = pl.BlockSpec(memory_space=pltpu.VMEM)
    return pl.pallas_call(
        functools.partial(finish_kernel, sources, pieces, count, width),
        out_shape=[jax.ShapeDtypeStruct(shapes[n], jnp.float32) for n in range(count)]
        + [
            jax.ShapeDtypeStruct(head_levels.shape, jnp.float32),
            jax.ShapeDtypeStruct((8, 128), jnp.float32),
        ],
        in_specs=[pl.BlockSpec(memory_space=pl.ANY)] * len(arrays) + [local] * 3,
        out_specs=[local] * (count + 2),
        scratch_shapes=scratch,
        cost_estimate=LONG,
        compiler_params=pltpu.CompilerParams(
            collective_id=collective_id, has_side_effects=True, vmem_limit_bytes=60 * 1024 * 1024
        ),
    )(*views, text, notes, head_levels)


def thirds(number):
    return [(number, (256 * k, 256), k) for k in range(3)]


GATHER_PIECES = thirds(0) + thirds(1) + [(2, (0, 512), 0), (2, (512, 512), 1), (3, (0, 256), 2)]
REDUCE_PIECES = (
    thirds(0)
    + thirds(1)
    + [(2, None, 0), (3, None, 2), (4, None, 1), (5, None, 1), (6, None, 2), (7, None, 2), (8, None, 0)]
)
WHOLE = ((0, 2), (0, 4))
REDUCE_SOURCES = [
    (0, (0, 1), (0, 1)),
    (0, (0, 1), (1, 2)),
    (0, (0, 1), (3, 1)),
    (0, (1, 1), (0, 4)),
] + [(number,) + WHOLE for number in range(1, 9)]


def pack(masters):
    word, position, box, text, down, layout, layout_down, head, vector = [
        m.astype(LOW) for m in masters
    ]
    box = box.reshape(2, 16, 128)
    small = jnp.concatenate(
        [
            jnp.concatenate([box[0], box[1]], 1),
            filled(layout.T, 16, 256),
            filled(layout_down[0], 8, 256),
            filled(layout_down[1], 8, 256),
            filled(vector[None], 8, 256),
        ],
        0,
    )
    wide = jnp.concatenate([filled(head.T, 8, 1024), filled(position, 8, 1024)], 0)
    return [text.T, down, wide, small]


def filled(values, rows, width):
    lead = [(0, 0)] * (values.ndim - 2)
    return jnp.pad(
        values, lead + [(0, rows - values.shape[-2]), (0, width - values.shape[-1])]
    )


def unpack(gathered):
    text, down, wide, small = gathered
    box = small[:, :16].reshape(128, 2, 8, 2, 128).transpose(3, 1, 0, 2, 4)
    return dict(
        text=text,
        down=down.reshape(3072, 768),
        head=wide[:, :6, :960].reshape(768, 960),
        box=box.reshape(4096, 128),
        layout=small[:, 16:28, :192].reshape(1536, 192),
        layout_down=small[:, 32:38, :192].reshape(768, 192),
        box_proj=small[:, 40:46, :192].reshape(768, 192),
        position=wide[:52, 8:13, :960].reshape(260, 960),
        vector=small[:, 48, :123].reshape(15744),
    )


def reduce_weights(grads, text, notes, head_levels, width):
    shards = finish_step(
        [
            grads["query"].reshape(16, 48, 768),
            grads["key_value"].reshape(32, 48, 768),
            grads["out"].reshape(16, 48, 768),
            grads["up"].reshape(64, 48, 768),
            grads["down"].reshape(128, 24, 768),
            grads["head"].reshape(128, 6, 960),
            grads["position"].reshape(128, 5, 960),
            grads["layout"].reshape(128, 12, 192),
            grads["layout_down"].reshape(128, 6, 192),
            grads["box_proj"].reshape(128, 6, 192),
            grads["box"].reshape(4, 128, 8, 128).transpose(1, 0, 2, 3).reshape(128, 32, 128),
            grads["vector"].reshape(128, 1, 123),
        ],
        text,
        notes,
        head_levels,
        REDUCE_SOURCES,
        REDUCE_PIECES,
        width,
        4,
    )
    text, down, head, position, layout, layout_down, box_proj, box, vector, table, square = shards
    return table, square, [
        position,
        box.reshape(4, 8, 128),
        text.T,
        down,
        layout.T,
        jnp.stack([layout_down, box_proj]),
        head.T,
        vector[0],
    ]


def on_device(
    token_ids,
    box_coords,
    intersection_flags,
    masked_rows,
    masked_labels,
    *weights,
):
    triples = [tuple(weights[3 * n : 3 * n + 3]) for n in range(9)]
    masters = [entry[0] for entry in triples]
    word_table = masters[0]
    dp = lax.axis_index("dp")
    vocab = lax.axis_index("vocab")
    shard_width = word_table.shape[1]
    table_rows = word_table.shape[0]
    levels = -(-shard_width // SPAN_LOW)

    row_hot = masked_rows[:, :, None] == jnp.arange(64)[None, None, :]
    counted = jnp.sum(jnp.where(row_hot & (intersection_flags == 0)[:, None, :], 1, 0), 2)
    slot_hot = jnp.concatenate(
        [
            jnp.pad(row_hot[0], ((0, 0), (0, 64))),
            jnp.pad(row_hot[1], ((0, 0), (64, 0))),
        ],
        0,
    )
    slot_hot_wide = slot_hot.astype(jnp.float32)
    f32 = jnp.float32

    notes = jnp.concatenate(
        [
            token_ids.reshape(1, 128),
            jnp.concatenate(
                [masked_labels.reshape(1, 16), counted.reshape(1, 16), jnp.zeros((1, 96), jnp.int32)], 1
            ),
        ],
        0,
    )
    table_low = word_table.astype(LOW)
    table_levels = (
        jnp.pad(table_low, ((0, 0), (0, levels * SPAN_LOW - shard_width)))
        .reshape(table_rows, levels, SPAN_LOW)
        .transpose(1, 0, 2)
        .reshape(levels * table_rows, SPAN_LOW)
    )
    table_blocks = (
        jnp.pad(table_low, ((0, 0), (0, 32 * HEAD_BLOCK - shard_width)))
        .reshape(table_rows, 32, HEAD_BLOCK)
        .transpose(1, 0, 2)
    )
    notes_all, found, table_head, gathered = start_step(
        notes, table_levels, table_blocks, pack(masters), GATHER_PIECES, shard_width, 1
    )
    table_head = table_head.reshape(768, HEAD_BLOCK)
    full = unpack(gathered)
    notes_rows = notes_all.reshape(128, 2, 128)
    labels_all = notes_rows[:, 1, :16].reshape(2048)
    counted_all = notes_rows[:, 1, 16:32].reshape(2048).astype(jnp.float32)
    total_count = jnp.sum(counted_all)

    vector = full["vector"].astype(jnp.float32)
    text_vec = vector[:10752].reshape(14, 768)
    layout_vec = vector[10752:13440].reshape(14, 192)
    head_vec = vector[13440:].reshape(3, 768)
    position_own = lax.dynamic_slice_in_dim(full["position"], vocab * 64, 64, 0).astype(f32)
    boxes = box_coords.reshape(4, 128)
    box_index = jnp.stack(
        [
            boxes[0],
            boxes[1],
            boxes[2],
            boxes[3],
            jnp.abs(boxes[3] - boxes[1]),
            jnp.abs(boxes[2] - boxes[0]),
            boxes[0],
            boxes[0],
        ],
        1,
    )
    qkv = (full["text"], (48, 48, 768), (0, 0, 0))
    out_w = (full["text"], (16, 48, 768), (3, 0, 0))
    up_w = (full["text"], (64, 48, 768), (1, 0, 0))
    text_sum, layout_sum, spatial, *kv, query, slot_text, slot_layout = local_call(
        open_kernel,
        [
            found,
            position_own,
            box_index,
            full["box"],
            full["box_proj"],
            qkv,
            full["layout"],
            text_vec,
            layout_vec,
            slot_hot_wide,
        ],
        [
            ((128, 768), f32),
            ((128, 192), f32),
            ((128, 768), LOW),
            ((128, 768), LOW),
            ((128, 768), LOW),
            ((128, 192), LOW),
            ((128, 192), LOW),
            ((16, 1024), LOW),
            ((16, 768), f32),
            ((16, 192), f32),
        ],
        "open_streams",
    )
    query_all = lax.all_to_all(
        jnp.broadcast_to(query[None], (4, 16, 1024)), "vocab", 0, 0, tiled=True
    ).reshape(64, 1024)
    (partial,) = local_call(score_kernel, [query_all, *kv], [((64, 1280), f32)], "partial_attention")
    partial = lax.all_to_all(partial.reshape(4, 16, 1280), "vocab", 0, 0, tiled=True)
    weights_close = [out_w, up_w, full["down"], full["layout"], full["layout_down"]]
    vectors_close = [text_vec, layout_vec, full["head"], head_vec]
    (att_text, att_layout, log_total, mid_text, mid_layout, pre_text, pre_layout, end_text,
     end_layout, joined, dense, picked) = local_call(
        close_kernel,
        [partial, slot_text, slot_layout] + weights_close + vectors_close,
        [
            ((16, 768), f32),
            ((16, 192), f32),
            ((16, 128), f32),
            ((16, 768), f32),
            ((16, 192), f32),
            ((16, 3072), f32),
            ((16, 768), f32),
            ((16, 768), f32),
            ((16, 192), f32),
            ((16, 1024), LOW),
            ((16, 768), f32),
            ((16, 768), LOW),
        ],
        "close_streams",
    )
    d_picked, table_head_grad, loss = head_step(
        picked,
        table_head,
        (labels_all - vocab * shard_width - dp * HEAD_BLOCK)[None],
        (counted_all / total_count)[None],
        counted_all[None],
        shard_width,
        3,
    )
    loss_total = loss[0, 0]
    table_head_grad = lax.all_to_all(
        table_head_grad.reshape(32, 24, HEAD_BLOCK), "dp", 0, 0, tiled=True
    )
    (back, d_mid_text, d_mid_layout, d_head, d_out, d_up, d_down, d_layout_close, d_layout_down,
     d_text_vec, d_layout_vec, d_head_vec) = local_call(
        close_back_kernel,
        [d_picked, dense, joined, att_text, att_layout, log_total, mid_text, mid_layout]
        + [pre_text, pre_layout, end_text, end_layout]
        + weights_close
        + vectors_close,
        [
            ((16, 1280), f32),
            ((16, 768), f32),
            ((16, 192), f32),
            ((768, 960), LOW),
            ((768, 768), LOW),
            ((3072, 768), LOW),
            ((3072, 768), LOW),
            ((960, 192), LOW),
            ((768, 192), LOW),
            ((14, 768), f32),
            ((14, 192), f32),
            ((3, 768), f32),
        ],
        "close_streams_back",
    )
    back = lax.all_gather(back, "vocab", axis=0, tiled=True)
    d_query, *d_kv = local_call(
        score_back_kernel,
        [back, query_all, *kv],
        [
            ((64, 1024), f32),
            ((128, 768), LOW),
            ((128, 768), LOW),
            ((128, 192), LOW),
            ((128, 192), LOW),
        ],
        "attention_back",
    )
    d_query = lax.all_to_all(d_query.reshape(4, 16, 1024), "vocab", 0, 0, tiled=True)
    (d_query_w, d_kv_w, d_layout_open, d_embedded, d_position, d_box, d_proj, d_text_open,
     d_layout_vec_open) = local_call(
        open_back_kernel,
        [d_query, *d_kv, d_mid_text, d_mid_layout, text_sum, layout_sum, slot_text, slot_layout]
        + [qkv, full["layout"], full["box_proj"], spatial, box_index, text_vec, layout_vec]
        + [slot_hot_wide.T],
        [
            ((768, 768), LOW),
            ((1536, 768), LOW),
            ((576, 192), LOW),
            ((768, 128), LOW),
            ((64, 960), f32),
            ((4096, 128), LOW),
            ((768, 192), LOW),
            ((14, 768), f32),
            ((14, 192), f32),
        ],
        "open_streams_back",
    )
    head_levels = (
        table_head_grad.transpose(1, 0, 2)
        .reshape(table_rows, 32 * HEAD_BLOCK)[:, : levels * SPAN_LOW]
        .reshape(table_rows, levels, SPAN_LOW)
        .transpose(1, 0, 2)
        .reshape(levels * table_rows, SPAN_LOW)
        .astype(f32)
    )
    d_positions = lax.dynamic_update_slice_in_dim(
        jnp.zeros((640, 960), LOW), d_position.astype(LOW), vocab * 64, 0
    )
    table_grad, square, shards = reduce_weights(
        dict(
            query=d_query_w,
            key_value=d_kv_w,
            out=d_out,
            up=d_up,
            down=d_down,
            head=d_head,
            box=d_box,
            layout=jnp.concatenate([d_layout_open, d_layout_close], 0),
            layout_down=d_layout_down,
            box_proj=d_proj,
            position=d_positions,
            vector=jnp.concatenate(
                [
                    (d_text_vec + d_text_open).reshape(10752),
                    (d_layout_vec + d_layout_vec_open).reshape(2688),
                    d_head_vec.reshape(2304),
                ]
            ).astype(LOW),
        ),
        d_embedded.reshape(32, 24, 128),
        notes_all,
        head_levels,
        shard_width,
    )
    table_grad = (
        table_grad.reshape(levels, table_rows, SPAN_LOW)
        .transpose(1, 0, 2)
        .reshape(table_rows, levels * SPAN_LOW)[:, :shard_width]
    )
    all_grads = [table_grad] + shards
    grad_norm = jnp.sqrt(square[0, 0])
    factor = jnp.minimum(1.0, CLIP / grad_norm)
    results = []
    for (master, momentum, average), grad in zip(triples, all_grads):
        clipped = factor * grad
        momentum_next = MOMENTUM * momentum + clipped
        master_next = master - RATE * (clipped + MOMENTUM * momentum_next)
        average_next = AVERAGE_KEEP * average + (1.0 - AVERAGE_KEEP) * master_next
        results += [master_next, momentum_next, average_next]
    return tuple(results + [loss_total, total_count, grad_norm])


TOKEN_SPEC = P(None, AXES)
WEIGHT_SPECS = (
    P("dp", "vocab"),
    P(AXES, None),
    P(None, AXES, None),
    P(None, AXES),
    P(AXES, None),
    P(None, AXES),
    P(None, AXES, None),
    P(None, AXES),
    P(AXES),
)


def solution(mesh):
    weight_specs = tuple(spec for spec in WEIGHT_SPECS for _ in range(3))
    in_specs = (TOKEN_SPEC, P(None, None, AXES), TOKEN_SPEC, TOKEN_SPEC, TOKEN_SPEC) + weight_specs
    out_specs = weight_specs + (P(), P(), P())
    return jax.shard_map(
        on_device, mesh=mesh, in_specs=in_specs, out_specs=out_specs, check_vma=False
    )
```
